32 devices in a mesh: sub: 8 (over z, y), grp: 4 (over x, core).
Axes of the slice: x: 2, y: 2, z: 4, core: 2. Of those that a mesh axis runs over, the one named last changes fastest.
Arguments:
- coarse: float32 [768, 128], P(('sub', 'grp')), may hold values from -6 to 6
- corner_idx: int32 [32, 24], P(('sub', 'grp')), may hold values from 0 to 767, as said below
- coupling: bfloat16 [49152, 24], P(('sub', 'grp')), may hold values from -1.25 to 1.25
- force: bfloat16 [16384, 3, 128], P(('sub', 'grp')), may hold values from -6 to 6
- panel_inv: bfloat16 [128, 384, 384], P(('sub', 'grp')), as said below
- panel_nodes: int32 [32, 4], P(('sub', 'grp')), may hold values from 64 to 128, as said below
- strain_disp: bfloat16 [6, 24, 4096], P(None, None, ('sub', 'grp')), may hold values from -1.25 to 1.25
- modulus: float32 [4096], P(('sub', 'grp')), may hold values from 0.5 to 4
- connect: int32 [8, 4096], P(None, ('sub', 'grp')), may hold values from 0 to 511, as said below
- interface: int32 [32, 224], P(('sub', 'grp')), may hold values from 0 to 511, as said below
- nodal_volume: float32 [16384], P(('sub', 'grp')), may hold values from 4 to 16
Outputs:
- displacement: bfloat16 [16384, 3, 128], P(('sub', 'grp'))
- nodal_stress: bfloat16 [16384, 6, 128], P(('sub', 'grp'))
The draws below stay inside these ranges and needn't reach their ends.
Inputs may be any that keep to these rules, and one draw needn't show every extreme that they name: `corner_idx`: the rows of subdomain (s, g) lie in the coarse blocks of subdomains (s', g') with |s' - s| <= 1 that exist, including blocks of all grp indices; they come in triples of consecutive rows. `panel_nodes`: every subdomain has one panel with exactly 128 live nodes and one with 64. `connect`: every entry is a live node of its subdomain (slot j < panel_nodes of its panel). `interface`: each row holds 224 distinct live nodes as eight lists: sub-lo (64), sub-hi (64), grp-lo (32), grp-hi (32), then edges ll, lh, hl, hh (8 each; first letter the sub side, second the grp side). Entry k of a list of (s, g) is the same physical node as entry k of the facing list of each neighbour: sub-hi with sub-lo of (s + 1, g), grp-hi with grp-lo of (s, g + 1); edge (x, y) with the edge of the neighbour across it that has the opposite letter on each side crossed. `panel_inv`: given inverses of the padded panels.
All inputs are finite; a program needn't handle non-finite values.
Results may differ from the reference program's by a relative error of at most 0.0058.
Values sent between devices are 32-bit elements; how exact they have to be, the bound alone decides.
No kernel may reach another device: no remote copies, remote signals or barrier semaphores. Data moves between devices by JAX's collectives and lax.ppermute only.
A program may use at most 64 MiB of HBM per device.

```python
import math
import jax
import jax.numpy as jnp
import numpy as np
from jax import lax

PNODES = 128
PW = 384
NP = 4
NN = 512
NE = 128
NL = 128
NIS = 64
NIG = 32
NED = 8
NIF = 224
NCL = 24
CPD = 24
SUBDOMAINS = 32
NODES = 16384
DOFS = 49152
NELEMS = 4096
NCOARSE = 768
N_SUB = 8
N_GRP = 4


def live_counts(key):
    base_key = jax.random.fold_in(key, 101)
    key_counts, key_full, key_empty = jax.random.split(base_key, 3)
    counts = jax.random.randint(key_counts, (SUBDOMAINS, NP), PNODES // 2, PNODES + 1)
    fullest = jax.random.randint(key_full, (SUBDOMAINS,), 0, NP)
    emptiest = (fullest + jax.random.randint(key_empty, (SUBDOMAINS,), 1, NP)) % NP
    panel_ids = jnp.arange(NP)[None, :]
    counts = jnp.where(panel_ids == fullest[:, None], PNODES, counts)
    counts = jnp.where(panel_ids == emptiest[:, None], PNODES // 2, counts)
    return counts.astype(jnp.int32)


def live_order(key):
    counts = live_counts(key)
    node_ids = jnp.arange(NN)
    live_mask = (node_ids % PNODES)[None, :] < jnp.take(counts, node_ids // PNODES, axis=1)
    row_keys = jax.random.split(jax.random.fold_in(key, 202), SUBDOMAINS)
    priority = jax.vmap(lambda k: jax.random.permutation(k, NN))(row_keys)
    priority = priority + jnp.where(live_mask, 0, NN)
    live_first = jnp.argsort(priority, axis=1).astype(jnp.int32)
    return (live_first, jnp.sum(counts, axis=1))


def draw_panel_nodes(key, part):
    return live_counts(key)


def draw_interface(key, part):
    live_first, total_live = live_order(key)
    return live_first[:, :NIF]


def draw_connect(key, part):
    live_first, total_live = live_order(key)
    picked = jax.random.randint(jax.random.fold_in(key, 303), (8, SUBDOMAINS, NE), 0, total_live[None, :, None])
    chosen = jnp.take_along_axis(jnp.broadcast_to(live_first[None], (8, SUBDOMAINS, NN)), picked, axis=2)
    return chosen.reshape(8, SUBDOMAINS * NE).astype(jnp.int32)


def draw_corner_idx(key, part):
    key_grp, key_step, key_node = jax.random.split(jax.random.fold_in(key, 404), 3)
    domain = jnp.arange(SUBDOMAINS)
    sub_pos = (domain // N_GRP)[:, None]
    grp_pos = (domain % N_GRP)[:, None]
    rand_grp = jax.random.randint(key_grp, (SUBDOMAINS, 8), 0, N_GRP)
    rand_step = jax.random.randint(key_step, (SUBDOMAINS, 8), -1, 2)
    node_pick = jax.random.randint(key_node, (SUBDOMAINS, 8), 0, CPD // 3)
    corner_slot = jnp.arange(8)[None, :]
    owner_sub = jnp.clip(sub_pos + rand_step, 0, N_SUB - 1)
    owner_sub = jnp.where(corner_slot == 0, jnp.maximum(sub_pos - 1, 0), owner_sub)
    owner_sub = jnp.where(corner_slot == 1, jnp.minimum(sub_pos + 1, N_SUB - 1), owner_sub)
    owner_sub = jnp.where((corner_slot >= 2) & (corner_slot <= 4), sub_pos, owner_sub)
    owner_grp = rand_grp
    owner_grp = jnp.where(corner_slot == 2, (grp_pos + 2) % N_GRP, owner_grp)
    owner_grp = jnp.where(corner_slot == 3, (grp_pos + 1) % N_GRP, owner_grp)
    owner_grp = jnp.where(corner_slot == 4, (grp_pos + N_GRP - 1) % N_GRP, owner_grp)
    first_dof = (owner_sub * N_GRP + owner_grp) * CPD + 3 * node_pick
    return (first_dof[:, :, None] + jnp.arange(3)[None, None, :]).reshape(SUBDOMAINS, NCL).astype(jnp.int32)


def draw_panel_inv(key, part):
    key_off, key_diag = jax.random.split(jax.random.fold_in(key, 505))
    full_shape = (SUBDOMAINS * NP, PW, PW)
    random_part = jnp.clip(jax.random.normal(key_off, full_shape, jnp.float32), -4.0, 4.0) * (0.5 / math.sqrt(PW))
    diag_part = jax.random.uniform(key_diag, (SUBDOMAINS * NP, PW), jnp.float32, 1.0, 3.0)
    return (random_part + jnp.eye(PW, dtype=jnp.float32)[None] * diag_part[:, None, :]).astype(jnp.bfloat16)


def block_scale(own_key, dims, cuts, least, high):
    factor_of = 1.0
    for position, shards_of in cuts:
        draws = jax.random.uniform(jax.random.fold_in(jax.random.fold_in(own_key, 6), position), (shards_of,), jnp.float32, least / len(cuts), high / len(cuts))
        factor_of = factor_of * jnp.repeat(jnp.exp(draws), dims[position] // shards_of).reshape((-1,) + (1,) * (len(dims) - 1 - position))
    return factor_of


def gaussian(rng, shape, spread, bound, cuts=(), kind=jnp.bfloat16):
    gain = block_scale(rng, shape, cuts, -0.22, 0.18) if cuts else 1.0
    array = jax.random.normal(rng, shape, jnp.float32) * spread * gain
    return jnp.minimum(jnp.maximum(array, -bound), bound).astype(kind)


def setup_inputs(seed: int = 0) -> dict:
    splits = jax.random.split(jax.random.key(seed), 12)
    return {
        "coarse": gaussian(splits[0], (NCOARSE, NL), 1.0, 6.0, ((0, 32),), jnp.float32),
        "corner_idx": draw_corner_idx(jax.random.fold_in(splits[11], 71), 0),
        "coupling": gaussian(splits[2], (DOFS, NCL), NCL ** -0.5, 1.25, ((0, 32),)),
        "force": gaussian(splits[3], (NODES, 3, NL), 1.0, 6.0, ((0, 32),)),
        "panel_inv": draw_panel_inv(jax.random.fold_in(splits[11], 71), 0),
        "panel_nodes": draw_panel_nodes(jax.random.fold_in(splits[11], 71), 0),
        "strain_disp": gaussian(splits[6], (6, 24, NELEMS), 24 ** -0.5, 1.25, ((2, 32),)),
        "modulus": jnp.clip(jnp.exp(math.log(4.0) - 2.0794415 * jax.random.uniform(splits[7], (NELEMS,), jnp.float32) ** block_scale(splits[7], (NELEMS,), ((0, 32),), -0.2, 0.2)), 0.5, 4.0),
        "connect": draw_connect(jax.random.fold_in(splits[11], 71), 0),
        "interface": draw_interface(jax.random.fold_in(splits[11], 71), 0),
        "nodal_volume": jnp.clip(jnp.exp(math.log(16.0) - 1.3862944 * jax.random.uniform(splits[10], (NODES,), jnp.float32) ** block_scale(splits[10], (NODES,), ((0, 32),), -0.2, 0.2)), 4.0, 16.0),
    }


POISSON = 0.3


def iso_matrix():
    lame_first = POISSON / ((1.0 + POISSON) * (1.0 - 2.0 * POISSON))
    shear_mod = 0.5 / (1.0 + POISSON)
    upper_block = jnp.full((3, 3), lame_first, jnp.float32) + jnp.eye(3, dtype=jnp.float32) * (2.0 * shear_mod)
    shear_block = jnp.eye(3, dtype=jnp.float32) * shear_mod
    zero_block = jnp.zeros((3, 3), jnp.float32)
    return jnp.concatenate([jnp.concatenate([upper_block, zero_block], 1), jnp.concatenate([zero_block, shear_block], 1)], 0)


def row_span(first_row, row_count):
    return np.arange(first_row, first_row + row_count)


def shifted(values, step_sub, step_grp):
    padding = [(1, 1), (1, 1)] + [(0, 0)] * (values.ndim - 2)
    padded = jnp.pad(values, padding)
    padded = lax.slice_in_dim(padded, 1 - step_sub, 1 - step_sub + N_SUB, axis=0)
    return lax.slice_in_dim(padded, 1 - step_grp, 1 - step_grp + N_GRP, axis=1)


def pick_rows(partial_rows, node_ids):
    return partial_rows[node_ids]


def put_rows(partial_rows, node_ids, new_rows):
    return partial_rows.at[node_ids].set(new_rows)


def reference(coarse, corner_idx, coupling, force, panel_inv, panel_nodes, strain_disp, modulus, connect, interface, nodal_volume):
    elastic = iso_matrix()
    corner_values = coarse[corner_idx]
    coupling_all = coupling.reshape(SUBDOMAINS, 3 * NN, NCL)
    force_all = force.reshape(SUBDOMAINS, 3 * NN, NL)
    inverse_all = panel_inv.reshape(SUBDOMAINS, NP, PW, PW)
    strain_all = jnp.moveaxis(strain_disp.reshape(6, 24, SUBDOMAINS, NE), 2, 0)
    modulus_all = modulus.reshape(SUBDOMAINS, NE)
    connect_all = jnp.moveaxis(connect.reshape(8, SUBDOMAINS, NE), 1, 0)

    def one_domain(pieces):
        values, coupled, load_rows, inverse, counts, strain_map, moduli, nodes_of = pieces
        correction = jnp.dot(coupled.astype(jnp.float32), values, precision=lax.Precision.HIGHEST)
        live_mask = jnp.arange(PW)[None, :] < 3 * counts[:, None]
        reduced = (load_rows.astype(jnp.float32) - correction).reshape(NP, PW, NL)
        reduced = jnp.where(live_mask[:, :, None], reduced, 0.0).astype(jnp.bfloat16)
        solved = jnp.einsum("prc,pcl->prl", inverse.astype(jnp.float32), reduced.astype(jnp.float32), precision=lax.Precision.HIGHEST)
        displaced = jnp.where(live_mask[:, :, None], solved, 0.0).astype(jnp.bfloat16).reshape(NN, 3 * NL)
        element = displaced[nodes_of.T].reshape(NE, 24, NL)
        strain = jnp.einsum("ije,ejl->eil", strain_map.astype(jnp.float32), element.astype(jnp.float32), precision=lax.Precision.HIGHEST)
        stress = jnp.einsum("ik,ekl->eil", elastic, strain, precision=lax.Precision.HIGHEST) * moduli[:, None, None]
        partial_value = jnp.zeros((NN, 6, NL), jnp.float32)
        for corner in range(8):
            partial_value = partial_value.at[nodes_of[corner]].add(stress)
        return displaced.reshape(NN, 3, NL), partial_value

    displacement, partials = lax.map(one_domain, (corner_values, coupling_all, force_all, inverse_all, panel_nodes, strain_all, modulus_all, connect_all))
    iface_rows = jax.vmap(pick_rows)(partials, interface).reshape(N_SUB, N_GRP, NIF, 6, NL)
    sub_lo = row_span(0, NIS)
    sub_hi = row_span(NIS, NIS)
    grp_lo = row_span(2 * NIS, NIG)
    grp_hi = row_span(2 * NIS + NIG, NIG)
    start_edge = 2 * NIS + 2 * NIG
    edge_ll = row_span(start_edge, NED)
    edge_lh = row_span(start_edge + NED, NED)
    edge_hl = row_span(start_edge + 2 * NED, NED)
    edge_hh = row_span(start_edge + 3 * NED, NED)
    pairings = [
        (np.concatenate([sub_hi, edge_hl, edge_hh]), np.concatenate([sub_lo, edge_ll, edge_lh]), 1, 0),
        (np.concatenate([sub_lo, edge_ll, edge_lh]), np.concatenate([sub_hi, edge_hl, edge_hh]), -1, 0),
        (np.concatenate([grp_hi, edge_lh, edge_hh]), np.concatenate([grp_lo, edge_ll, edge_hl]), 0, 1),
        (np.concatenate([grp_lo, edge_ll, edge_hl]), np.concatenate([grp_hi, edge_lh, edge_hh]), 0, -1),
        (edge_hh, edge_ll, 1, 1),
        (edge_hl, edge_lh, 1, -1),
        (edge_lh, edge_hl, -1, 1),
        (edge_ll, edge_hh, -1, -1),
    ]
    totals = iface_rows
    for sender, receiver, step_sub, step_grp in pairings:
        totals = totals.at[:, :, receiver].add(shifted(iface_rows[:, :, sender], step_sub, step_grp))
    totals = totals.reshape(SUBDOMAINS, NIF, 6, NL)
    summed = jax.vmap(put_rows)(partials, interface, totals)
    stress_out = (summed / nodal_volume.reshape(SUBDOMAINS, NN)[:, :, None, None]).astype(jnp.bfloat16)
    return displacement.reshape(NODES, 3, NL), stress_out.reshape(NODES, 6, NL)
```

```python
import functools

import jax
import jax.numpy as jnp
from jax import lax
from jax.experimental import pallas as pl
from jax.experimental.pallas import tpu as pltpu
from jax.sharding import PartitionSpec as P

NIS = 64
NIG = 32
NED = 8
EDGES = 2 * NIS + 2 * NIG
NIF = EDGES + 4 * NED
CORNERS = 8
COMPS = 6
LANES = 128

POISSON = 0.3
LAME = POISSON / ((1.0 + POISSON) * (1.0 - 2.0 * POISSON))
SHEAR = 0.5 / (1.0 + POISSON)

F32 = jnp.float32
BF16 = jnp.bfloat16
VMEM_LIMIT = 24 * 1024 * 1024


def split_two(x):
    high = x.astype(BF16)
    return high, (x - high.astype(F32)).astype(BF16)


def dot_nt(a, b):
    return lax.dot_general(a, b, (((1,), (1,)), ((), ())), preferred_element_type=F32)


def dot_tn(a, b):
    return lax.dot_general(a, b, (((0,), (0,)), ((), ())), preferred_element_type=F32)


def column(row):
    return jnp.broadcast_to(row, (LANES, LANES)).T


def scaled_strain_map(strain_ref, modulus_ref, out_ref):
    modulus = modulus_ref[...]
    rows = [strain_ref[i].astype(F32) for i in range(COMPS)]
    trace = (rows[0] + rows[1] + rows[2]) * LAME
    for i in range(COMPS):
        value = trace + rows[i] * (2.0 * SHEAR) if i < 3 else rows[i] * SHEAR
        out_ref[24 * i : 24 * (i + 1), :] = value * modulus


def main_kernel(
    corner_idx,
    panel_nodes,
    nearby,
    coupling,
    force,
    inverse,
    strain_map,
    modulus,
    connect,
    interface,
    disp,
    stress,
    sub_lo,
    sub_hi,
    grp_lo,
    grp_hi,
    corners,
    loads,
    solved,
    disp_t,
    onehot,
    elem_t,
    scaled,
    ids,
):
    panels, panel_rows, _ = inverse.shape
    nodes = force.shape[1]
    panel_size = panel_rows // 3

    scaled_strain_map(strain_map, modulus, scaled)
    node_of = lax.broadcasted_iota(jnp.int32, (nodes, LANES), 0)
    for a in range(CORNERS):
        hit = connect[a : a + 1, :] == node_of
        onehot[:, a * LANES : (a + 1) * LANES] = jnp.where(hit, 1.0, 0.0).astype(BF16)
    ids[...] = jnp.full(ids.shape, -1.0, F32)
    ids[0:1, 0:NIF] = interface[...].astype(F32)
    connect_f = connect[...].astype(F32)
    face = []
    for half in range(2):
        id_col = column(ids[0:1, half * LANES : (half + 1) * LANES])
        count = jnp.zeros((LANES, LANES), F32)
        for a in range(CORNERS):
            count = count + jnp.where(connect_f[a : a + 1, :] == id_col, 1.0, 0.0)
        face.append(count)
    face = jnp.concatenate(face, axis=0)[:NIF].astype(BF16)
    face = jnp.concatenate([face, face], axis=1)

    for c in range(3):
        loads[pl.ds(c, nodes, stride=3), :] = force[c].astype(F32)

    for k in range(corner_idx.shape[1]):
        corners[k : k + 1, :] = nearby[pl.ds(corner_idx[0, k], 1), :]
    values = corners[...]
    high = values.astype(BF16).astype(F32)
    middle = (values - high).astype(BF16).astype(F32)
    low = values - high - middle
    values = jnp.concatenate([high, middle, low], axis=0).astype(BF16)
    coupled = coupling[...].astype(F32)
    coupled = jnp.concatenate([coupled, coupled, coupled], axis=0).astype(BF16)

    row_of = lax.broadcasted_iota(jnp.int32, (panel_rows, LANES), 0)
    for p in range(panels):
        start = p * panel_rows
        live = row_of < 3 * panel_nodes[0, p]
        correction = dot_tn(coupled[:, start : start + panel_rows], values)
        reduced = loads[start : start + panel_rows, :] - correction
        reduced = jnp.where(live, reduced, 0.0).astype(BF16)
        result = jnp.dot(inverse[p], reduced, preferred_element_type=F32)
        solved[start : start + panel_rows, :] = jnp.where(live, result, 0.0)
        for c in range(3):
            part = solved[pl.ds(start + c, panel_size, stride=3), :].astype(BF16)
            disp[c, p * panel_size : (p + 1) * panel_size, :] = part
            disp_t[c * LANES : (c + 1) * LANES, p * panel_size : (p + 1) * panel_size] = (
                part.astype(F32).T.astype(BF16)
            )

    for c in range(3):
        elem_t[c] = jnp.dot(
            disp_t[c * LANES : (c + 1) * LANES, :], onehot[...], preferred_element_type=F32
        )
    step = 32
    for start in range(0, LANES, step):
        sums = [None] * COMPS
        for a in range(CORNERS):
            for c in range(3):
                x = elem_t[c, start : start + step, a * LANES : (a + 1) * LANES]
                for i in range(COMPS):
                    r = 24 * i + 3 * a + c
                    term = scaled[r : r + 1, :] * x
                    sums[i] = term if sums[i] is None else sums[i] + term
        for i in range(COMPS):
            high, low = split_two(sums[i])
            stress[i * LANES + start : i * LANES + start + step, 0:LANES] = high
            stress[i * LANES + start : i * LANES + start + step, LANES : 2 * LANES] = low

    rows = dot_nt(face, stress[...])
    for i in range(COMPS):
        part = rows[:, i * LANES : (i + 1) * LANES]
        sub_lo[i] = part[:NIS]
        sub_hi[i] = part[NIS : 2 * NIS]
        edge = [part[EDGES + NED * k : EDGES + NED * (k + 1)] for k in range(4)]
        grp_lo[i] = jnp.concatenate([part[2 * NIS : 2 * NIS + NIG], edge[0], edge[2]], axis=0)
        grp_hi[i] = jnp.concatenate([part[2 * NIS + NIG : EDGES], edge[1], edge[3]], axis=0)


def partial_kernel(connect, volume, stress, partial, inverse_volume):
    nodes = partial.shape[1]
    node_of = lax.broadcasted_iota(jnp.int32, (nodes, LANES), 0)
    count = jnp.zeros((nodes, LANES), F32)
    for a in range(CORNERS):
        count = count + jnp.where(connect[a : a + 1, :] == node_of, 1.0, 0.0)
    count = count.astype(BF16)
    count = jnp.concatenate([count, count], axis=1)
    for i in range(COMPS):
        partial[i] = dot_nt(count, stress[i * LANES : (i + 1) * LANES, :])
    for k in range(nodes // LANES):
        inverse_volume[k * LANES : (k + 1) * LANES, :] = column(1.0 / volume[k : k + 1, :])


def edge_kernel(grp_lo, grp_hi, from_lo, from_hi, edge_lo, edge_hi):
    split = NIG + NED
    edge_lo[:, 0:NED, :] = grp_lo[:, NIG:split, :] + from_lo[:, NIG:split, :]
    edge_lo[:, NED:, :] = grp_hi[:, NIG:split, :] + from_hi[:, NIG:split, :]
    edge_hi[:, 0:NED, :] = grp_lo[:, split:, :] + from_lo[:, split:, :]
    edge_hi[:, NED:, :] = grp_hi[:, split:, :] + from_hi[:, split:, :]


def finish_kernel(
    interface, partial, inverse_volume, sub_lo, sub_hi, grp_lo, grp_hi, edge_lo, edge_hi, out, ids, received
):
    nodes = partial.shape[1]
    split = NIG + NED
    ids[...] = jnp.full(ids.shape, -1, jnp.int32)
    ids[0:1, 0:NIF] = interface[...]
    node_of = lax.broadcasted_iota(jnp.int32, (nodes, 2 * LANES), 0)
    placing = jnp.where(ids[0:1, :] == node_of, 1.0, 0.0).astype(BF16)
    for i in range(COMPS):
        lo, hi, low_edge, high_edge = grp_lo[i], grp_hi[i], edge_lo[i], edge_hi[i]
        rows = jnp.concatenate(
            [
                sub_lo[i],
                sub_hi[i],
                lo[:NIG],
                hi[:NIG],
                lo[NIG:split] + low_edge[:NED],
                hi[NIG:split] + low_edge[NED:],
                lo[split:] + high_edge[:NED],
                hi[split:] + high_edge[NED:],
                jnp.zeros((2 * LANES - NIF, LANES), F32),
            ],
            axis=0,
        )
        high, low = split_two(rows)
        received[0, :, i * LANES : (i + 1) * LANES] = high
        received[1, :, i * LANES : (i + 1) * LANES] = low
    scale = inverse_volume[...]
    for i in range(0, COMPS, 2):
        cols = slice(i * LANES, (i + 2) * LANES)
        added = jnp.dot(placing, received[0, :, cols], preferred_element_type=F32)
        added = added + jnp.dot(placing, received[1, :, cols], preferred_element_type=F32)
        out[i] = ((partial[i] + added[:, :LANES]) * scale).astype(BF16)
        out[i + 1] = ((partial[i + 1] + added[:, LANES:]) * scale).astype(BF16)


def vmem(count):
    return [pl.BlockSpec(memory_space=pltpu.VMEM)] * count


def smem(count):
    return [pl.BlockSpec(memory_space=pltpu.SMEM)] * count


def array(shape, dtype=F32):
    return jax.ShapeDtypeStruct(shape, dtype)


def call(kernel, name, out_shape, in_specs, scratch=(), cost=None):
    return pl.pallas_call(
        kernel,
        name=name,
        out_shape=out_shape,
        in_specs=in_specs,
        out_specs=vmem(len(out_shape)),
        scratch_shapes=list(scratch),
        compiler_params=pltpu.CompilerParams(vmem_limit_bytes=VMEM_LIMIT),
        cost_estimate=cost,
    )


def shift(block, axis, up):
    count = lax.axis_size(axis)
    pairs = [(i, i + 1) if up else (i + 1, i) for i in range(count - 1)]
    return lax.ppermute(block, axis, pairs)


def shards(
    coarse,
    corner_idx,
    coupling,
    force,
    panel_inv,
    panel_nodes,
    strain_disp,
    modulus,
    connect,
    interface,
    nodal_volume,
):
    nodes, _, loads = force.shape
    nearby = lax.all_gather(coarse, ("sub", "grp"), axis=0, tiled=True)
    force_t = jnp.transpose(force, (1, 0, 2))
    coupling_t = coupling.T
    disp, stress, sub_lo, sub_hi, grp_lo, grp_hi = call(
        main_kernel,
        "solve_and_stress",
        (
            array((3, nodes, loads), BF16),
            array((COMPS * loads, 2 * LANES), BF16),
            array((COMPS, NIS, loads)),
            array((COMPS, NIS, loads)),
            array((COMPS, NIG + 2 * NED, loads)),
            array((COMPS, NIG + 2 * NED, loads)),
        ),
        smem(2) + vmem(8),
        (
            pltpu.VMEM((corner_idx.shape[1], loads), F32),
            pltpu.VMEM((3 * nodes, loads), F32),
            pltpu.VMEM((3 * nodes, loads), F32),
            pltpu.VMEM((3 * loads, nodes), BF16),
            pltpu.VMEM((nodes, CORNERS * LANES), BF16),
            pltpu.VMEM((3, loads, CORNERS * LANES), F32),
            pltpu.VMEM((COMPS * 24, LANES), F32),
            pltpu.VMEM((8, 2 * LANES), F32),
        ),
        pl.CostEstimate(flops=1500000000, bytes_accessed=4000000, transcendentals=0),
    )(
        corner_idx,
        panel_nodes,
        nearby,
        coupling_t,
        force_t,
        panel_inv,
        strain_disp,
        modulus.reshape(1, -1),
        connect,
        interface,
    )
    from_sub_lo = shift(sub_hi, "sub", True)
    from_sub_hi = shift(sub_lo, "sub", False)
    from_grp_lo = shift(grp_hi, "grp", True)
    from_grp_hi = shift(grp_lo, "grp", False)
    partial, inverse_volume = call(
        partial_kernel,
        "assemble_nodes",
        (array((COMPS, nodes, loads)), array((nodes, LANES))),
        vmem(3),
        cost=pl.CostEstimate(flops=400000000, bytes_accessed=2000000, transcendentals=0),
    )(connect, nodal_volume.reshape(-1, LANES), stress)
    edge_lo, edge_hi = call(
        edge_kernel,
        "sum_edges",
        (array((COMPS, 2 * NED, loads)), array((COMPS, 2 * NED, loads))),
        vmem(4),
    )(grp_lo, grp_hi, from_grp_lo, from_grp_hi)
    from_edge_lo = shift(edge_hi, "sub", True)
    from_edge_hi = shift(edge_lo, "sub", False)
    (nodal,) = call(
        finish_kernel,
        "add_received",
        (array((COMPS, nodes, loads), BF16),),
        vmem(9),
        (
            pltpu.VMEM((8, 2 * LANES), jnp.int32),
            pltpu.VMEM((2, 2 * LANES, COMPS * LANES), BF16),
        ),
    )(
        interface,
        partial,
        inverse_volume,
        from_sub_lo,
        from_sub_hi,
        from_grp_lo,
        from_grp_hi,
        from_edge_lo,
        from_edge_hi,
    )
    return jnp.transpose(disp, (1, 0, 2)), jnp.transpose(nodal, (1, 0, 2))


def solution(mesh):
    owner = ("sub", "grp")
    placed = (
        P(owner, None),
        P(owner, None),
        P(owner, None),
        P(owner, None, None),
        P(owner, None, None),
        P(owner, None),
        P(None, None, owner),
        P(owner),
        P(None, owner),
        P(owner, None),
        P(owner),
    )
    return jax.shard_map(
        shards,
        mesh=mesh,
        in_specs=placed,
        out_specs=(P(owner, None, None), P(owner, None, None)),
        check_vma=False,
    )
```

```python
import jax
import jax.numpy as jnp
from jax import lax
from jax.experimental import pallas as pl
from jax.experimental.pallas import tpu as pltpu
from jax.sharding import PartitionSpec as P

NIS = 64
NIG = 32
NED = 8
EDGES = 2 * NIS + 2 * NIG
NIF = EDGES + 4 * NED
CORNERS = 8
COMPS = 6
LANES = 128
TERM = 32

POISSON = 0.3
LAME = POISSON / ((1.0 + POISSON) * (1.0 - 2.0 * POISSON))
SHEAR = 0.5 / (1.0 + POISSON)

F32 = jnp.float32
BF16 = jnp.bfloat16
VMEM_LIMIT = 24 * 1024 * 1024


def split_two(x):
    high = x.astype(BF16)
    return high, (x - high.astype(F32)).astype(BF16)


def dot(a, b):
    return jnp.dot(a, b, preferred_element_type=F32)


def dot_nt(a, b):
    return lax.dot_general(a, b, (((1,), (1,)), ((), ())), preferred_element_type=F32)


def column(row):
    return jnp.broadcast_to(row, (LANES, LANES)).T


def prepare_kernel(
    blocks,
    corner_idx,
    panel_nodes,
    coupling,
    force,
    panel_inv,
    strain_disp,
    modulus,
    connect,
    interface,
    volume,
    coarse,
    inverse,
    coupled,
    loads,
    live,
    select,
    onehot,
    face,
    scaled,
    count,
    placing,
    inverse_volume,
    own,
    corner_v,
    panel_v,
    coupling_v,
    force_v,
    strain_v,
    modulus_v,
    connect_v,
    interface_v,
    volume_v,
    ids,
    sems,
):
    pairs = [
        (connect, connect_v),
        (interface, interface_v),
        (corner_idx, corner_v),
        (panel_nodes, panel_v),
        (volume, volume_v),
        (modulus, modulus_v),
        (strain_disp, strain_v),
        (coupling, coupling_v),
        (force, force_v),
        (panel_inv, inverse),
        (coarse, own),
    ]
    copies = [pltpu.make_async_copy(src, dst, sems.at[k]) for k, (src, dst) in enumerate(pairs)]
    for copy in copies:
        copy.start()
    panels, panel_rows, _ = inverse.shape
    nodes = force_v.shape[1]
    q = corner_idx.shape[1]

    copies[0].wait()
    node_of = lax.broadcasted_iota(jnp.int32, (nodes, LANES), 0)
    total = jnp.zeros((nodes, LANES), F32)
    for a in range(CORNERS):
        hit = jnp.where(connect_v[a : a + 1, :] == node_of, 1.0, 0.0)
        onehot[:, a * LANES : (a + 1) * LANES] = hit.astype(BF16)
        total = total + hit
    total = total.astype(BF16)
    count[:, :LANES] = total
    count[:, LANES:] = total

    copies[1].wait()
    ids[...] = jnp.full(ids.shape, -1.0, F32)
    ids[0:1, 0:NIF] = interface_v[...].astype(F32)
    node_of = lax.broadcasted_iota(jnp.int32, (nodes, 2 * LANES), 0)
    placing[...] = jnp.where(ids[0:1, :].astype(jnp.int32) == node_of, 1.0, 0.0).astype(BF16)
    connect_f = connect_v[...].astype(F32)
    for half in range(2):
        id_col = column(ids[0:1, half * LANES : (half + 1) * LANES])
        rows = jnp.zeros((LANES, LANES), F32)
        for a in range(CORNERS):
            rows = rows + jnp.where(connect_f[a : a + 1, :] == id_col, 1.0, 0.0)
        rows = rows.astype(BF16)[: min(LANES, NIF - half * LANES)]
        face[half * LANES : half * LANES + rows.shape[0], :LANES] = rows
        face[half * LANES : half * LANES + rows.shape[0], LANES:] = rows

    copies[2].wait()
    ids[0:1, 0:q] = corner_v[...].astype(F32)
    wanted = column(ids[0:1, :LANES])[:TERM]
    lane = lax.broadcasted_iota(jnp.int32, (TERM, LANES), 1)
    entry = lax.broadcasted_iota(jnp.int32, (TERM, LANES), 0)
    for b in range(3):
        row = (lax.axis_index("sub") - 1 + b) * blocks + lane
        hit = (wanted == row.astype(F32)) & (lane < blocks) & (entry < q)
        select[:, b * LANES : (b + 1) * LANES] = jnp.where(hit, 1.0, 0.0).astype(BF16)

    copies[3].wait()
    row_of = lax.broadcasted_iota(jnp.int32, (panel_rows, LANES), 0)
    for p in range(panels):
        alive = row_of < 3 * panel_v[0:1, p : p + 1]
        live[p * panel_rows : (p + 1) * panel_rows, :] = jnp.where(alive, 1.0, 0.0)

    copies[4].wait()
    for k in range(nodes // LANES):
        inverse_volume[k * LANES : (k + 1) * LANES, :] = column(1.0 / volume_v[k : k + 1, :])

    copies[5].wait()
    copies[6].wait()
    factor = modulus_v[...]
    rows = [strain_v[i].astype(F32) for i in range(COMPS)]
    trace = (rows[0] + rows[1] + rows[2]) * LAME
    for i in range(COMPS):
        value = trace + rows[i] * (2.0 * SHEAR) if i < 3 else rows[i] * SHEAR
        scaled[24 * i : 24 * (i + 1), :] = value * factor

    copies[7].wait()
    for k in range(coupling_v.shape[1] // LANES):
        part = coupling_v[:, k * LANES : (k + 1) * LANES].astype(F32)
        gap = jnp.zeros((TERM - q, LANES), F32)
        stack = jnp.concatenate([part, gap] * 3 + [jnp.zeros((LANES - 3 * TERM, LANES), F32)], axis=0)
        rows = slice(k * LANES, (k + 1) * LANES)
        coupled[rows, :] = (stack.T * live[rows, :]).astype(BF16)

    copies[8].wait()
    for c in range(3):
        loads[pl.ds(c, nodes, stride=3), :] = force_v[c].astype(F32)
    loads[...] = loads[...] * live[...]
    copies[9].wait()
    copies[10].wait()


def merge_kernel(bit, own, other, out):
    rows = own.shape[0]
    place = (lax.axis_index("grp") >> bit) & 1
    out[pl.ds(pl.multiple_of(place * rows, 8), rows), :] = own[...]
    out[pl.ds(pl.multiple_of((1 - place) * rows, 8), rows), :] = other[...]


def solve_kernel(
    below,
    here,
    above,
    inverse,
    coupled,
    loads,
    live,
    select,
    onehot,
    face,
    scaled,
    disp,
    stress,
    sub_hi,
    terms,
    solved,
    disp_t,
    elem_t,
):
    panels, panel_rows, _ = inverse.shape
    panel_size = panel_rows // 3
    rows = here.shape[0]

    terms[...] = jnp.zeros(terms.shape, BF16)
    for b, block in enumerate((below, here, above)):
        x = block[...]
        high = x.astype(BF16)
        rest = x - high.astype(F32)
        middle = rest.astype(BF16)
        low = (rest - middle.astype(F32)).astype(BF16)
        for t, value in enumerate((high, middle, low)):
            terms[t, b * LANES : b * LANES + rows, :] = value
    picked = [dot(select[...], terms[t]) for t in range(3)]
    picked.append(jnp.zeros((LANES - 3 * TERM, LANES), F32))
    values = jnp.concatenate(picked, axis=0).astype(BF16)

    for p in range(panels):
        start = p * panel_rows
        span = slice(start, start + panel_rows)
        reduced = (loads[span, :] - dot(coupled[span, :], values)).astype(BF16)
        solved[span, :] = dot(inverse[p], reduced) * live[span, :]
        for c in range(3):
            part = solved[pl.ds(start + c, panel_size, stride=3), :].astype(BF16)
            disp[c, p * panel_size : (p + 1) * panel_size, :] = part
            disp_t[c * LANES : (c + 1) * LANES, p * panel_size : (p + 1) * panel_size] = (
                part.astype(F32).T.astype(BF16)
            )

    for c in range(3):
        elem_t[c] = dot(disp_t[c * LANES : (c + 1) * LANES, :], onehot[...])
    step = 32
    for start in range(0, LANES, step):
        sums = [None] * COMPS
        for a in range(CORNERS):
            for c in range(3):
                x = elem_t[c, start : start + step, a * LANES : (a + 1) * LANES]
                for i in range(COMPS):
                    r = 24 * i + 3 * a + c
                    term = scaled[r : r + 1, :] * x
                    sums[i] = term if sums[i] is None else sums[i] + term
        for i in range(COMPS):
            high, low = split_two(sums[i])
            stress[i * LANES + start : i * LANES + start + step, 0:LANES] = high
            stress[i * LANES + start : i * LANES + start + step, LANES : 2 * LANES] = low

    rows = dot_nt(face[NIS : 2 * NIS, :], stress[...])
    for i in range(COMPS):
        sub_hi[i] = rows[:, i * LANES : (i + 1) * LANES]


def face_kernel(face, stress, sub_lo, grp_lo, grp_hi):
    low = dot_nt(face[:NIS, :], stress[...])
    rows = dot_nt(face[2 * NIS :, :], stress[...])
    base = EDGES - 2 * NIS
    for i in range(COMPS):
        part = rows[:, i * LANES : (i + 1) * LANES]
        edge = [part[base + NED * k : base + NED * (k + 1)] for k in range(4)]
        first = low[:, i * LANES : (i + 1) * LANES]
        sub_lo[i] = jnp.concatenate([first, edge[0], edge[1]], axis=0)
        grp_lo[i] = jnp.concatenate([part[:NIG], edge[0], edge[2]], axis=0)
        grp_hi[i] = jnp.concatenate([part[NIG:base], edge[1], edge[3]], axis=0)


def edge_kernel(sub_lo, grp_lo, grp_hi, from_lo, from_hi, _, sub_out, edge_hi):
    split = NIG + NED
    sub_out[:, :NIS, :] = sub_lo[:, :NIS, :]
    sub_out[:, NIS : NIS + NED, :] = grp_lo[:, NIG:split, :] + from_lo[:, NIG:split, :]
    sub_out[:, NIS + NED :, :] = grp_hi[:, NIG:split, :] + from_hi[:, NIG:split, :]
    edge_hi[:, 0:NED, :] = grp_lo[:, split:, :] + from_lo[:, split:, :]
    edge_hi[:, NED:, :] = grp_hi[:, split:, :] + from_hi[:, split:, :]


def partial_kernel(count, stress, disp, partial, disp_out):
    disp_out[...] = disp[...]
    for i in range(COMPS):
        partial[i] = dot_nt(count[...], stress[i * LANES : (i + 1) * LANES, :])


def finish_kernel(
    placing, partial, inverse_volume, sub_lo, sub_hi, grp_lo, grp_hi, edge_lo, out, received
):
    split = NIG + NED
    for i in range(COMPS):
        lo, hi, low_edge, high = grp_lo[i], grp_hi[i], edge_lo[i], sub_hi[i]
        rows = jnp.concatenate(
            [
                sub_lo[i],
                high[:NIS],
                lo[:NIG],
                hi[:NIG],
                lo[NIG:split] + low_edge[:NED],
                hi[NIG:split] + low_edge[NED:],
                lo[split:] + high[NIS : NIS + NED],
                hi[split:] + high[NIS + NED :],
                jnp.zeros((2 * LANES - NIF, LANES), F32),
            ],
            axis=0,
        )
        first, second = split_two(rows)
        received[0, :, i * LANES : (i + 1) * LANES] = first
        received[1, :, i * LANES : (i + 1) * LANES] = second
    scale = inverse_volume[...]
    for i in range(0, COMPS, 2):
        cols = slice(i * LANES, (i + 2) * LANES)
        added = dot(placing[...], received[0, :, cols]) + dot(placing[...], received[1, :, cols])
        out[i] = ((partial[i] + added[:, :LANES]) * scale).astype(BF16)
        out[i + 1] = ((partial[i + 1] + added[:, LANES:]) * scale).astype(BF16)


def vmem(count):
    return [pl.BlockSpec(memory_space=pltpu.VMEM)] * count


def array(shape, dtype=F32):
    return jax.ShapeDtypeStruct(shape, dtype)


def call(kernel, name, out_shape, in_specs, scratch=(), flops=0, moved=0):
    return pl.pallas_call(
        kernel,
        name=name,
        out_shape=out_shape,
        in_specs=in_specs,
        out_specs=vmem(len(out_shape)),
        scratch_shapes=list(scratch),
        compiler_params=pltpu.CompilerParams(vmem_limit_bytes=VMEM_LIMIT),
        cost_estimate=pl.CostEstimate(flops=flops, bytes_accessed=moved, transcendentals=0),
    )


def shift(block, axis, up):
    count = lax.axis_size(axis)
    pairs = [(i, i + 1) if up else (i + 1, i) for i in range(count - 1)]
    return lax.ppermute(block, axis, pairs)


def in_hbm(*arrays):
    return [pltpu.with_memory_space_constraint(x, pltpu.HBM) for x in arrays]


def gather_group(block, own):
    count = lax.axis_size("grp")
    bit = 0
    while 1 << bit < count:
        other = lax.ppermute(block, "grp", [(i, i ^ (1 << bit)) for i in range(count)])
        rows, lanes = block.shape

        def merge(own, received, out, bit=bit):
            merge_kernel(bit, own, received, out)

        (block,) = call(merge, "merge_blocks", (array((2 * rows, lanes)),), vmem(2))(own, other)
        own = block
        bit += 1
    return block


def shards(
    coarse,
    corner_idx,
    coupling,
    force,
    panel_inv,
    panel_nodes,
    strain_disp,
    modulus,
    connect,
    interface,
    nodal_volume,
):
    nodes, _, cases = force.shape
    dofs = 3 * nodes
    q = corner_idx.shape[1]
    blocks = coarse.shape[0] * lax.axis_size("grp")

    def prepare(*refs):
        prepare_kernel(blocks, *refs)

    prepared = call(
        prepare,
        "prepare",
        (
            array(panel_inv.shape, BF16),
            array((dofs, LANES), BF16),
            array((dofs, cases)),
            array((dofs, LANES)),
            array((TERM, 3 * LANES), BF16),
            array((nodes, CORNERS * LANES), BF16),
            array((NIF, 2 * LANES), BF16),
            array((COMPS * 24, LANES)),
            array((nodes, 2 * LANES), BF16),
            array((nodes, 2 * LANES), BF16),
            array((nodes, LANES)),
            array(coarse.shape),
        ),
        [pl.BlockSpec(memory_space=pltpu.HBM)] * 11,
        (
            pltpu.VMEM((1, q), jnp.int32),
            pltpu.VMEM(panel_nodes.shape, jnp.int32),
            pltpu.VMEM((q, dofs), BF16),
            pltpu.VMEM((3, nodes, cases), BF16),
            pltpu.VMEM(strain_disp.shape, BF16),
            pltpu.VMEM((1, LANES), F32),
            pltpu.VMEM(connect.shape, jnp.int32),
            pltpu.VMEM(interface.shape, jnp.int32),
            pltpu.VMEM((nodes // LANES, LANES), F32),
            pltpu.VMEM((8, 2 * LANES), F32),
            pltpu.SemaphoreType.DMA((11,)),
        ),
        flops=200000000,
        moved=8000000,
    )(
        *in_hbm(
            corner_idx,
            panel_nodes,
            coupling.T,
            jnp.transpose(force, (1, 0, 2)),
            panel_inv,
            strain_disp,
            modulus.reshape(1, -1),
            connect,
            interface,
            nodal_volume.reshape(-1, LANES),
            coarse,
        )
    )
    *operands, count, placing, inverse_volume, own = prepared

    here = gather_group(coarse, own)
    below = shift(here, "sub", True)
    above = shift(here, "sub", False)
    disp, stress, sub_hi = call(
        solve_kernel,
        "solve_and_stress",
        (
            array((3, nodes, cases), BF16),
            array((COMPS * cases, 2 * LANES), BF16),
            array((COMPS, NIS, cases)),
        ),
        vmem(11),
        (
            pltpu.VMEM((3, 3 * LANES, cases), BF16),
            pltpu.VMEM((dofs, cases), F32),
            pltpu.VMEM((3 * cases, nodes), BF16),
            pltpu.VMEM((3, cases, CORNERS * LANES), F32),
        ),
        flops=1500000000,
        moved=4000000,
    )(below, here, above, *operands)
    from_sub_lo = shift(sub_hi, "sub", True)
    sub_lo, grp_lo, grp_hi = call(
        face_kernel,
        "interface_rows",
        (
            array((COMPS, NIS + 2 * NED, cases)),
            array((COMPS, NIG + 2 * NED, cases)),
            array((COMPS, NIG + 2 * NED, cases)),
        ),
        vmem(2),
        flops=100000000,
        moved=1000000,
    )(operands[6], stress)
    from_grp_lo = shift(grp_hi, "grp", True)
    from_grp_hi = shift(grp_lo, "grp", False)
    sub_lo, edge_hi = call(
        edge_kernel,
        "sum_edges",
        (array(sub_lo.shape), array((COMPS, 2 * NED, cases))),
        vmem(5) + [pl.BlockSpec(memory_space=pl.ANY)],
    )(sub_lo, grp_lo, grp_hi, from_grp_lo, from_grp_hi, from_sub_lo)
    from_edge_lo = shift(edge_hi, "sub", True)
    from_sub_hi = shift(sub_lo, "sub", False)
    partial, disp = call(
        partial_kernel,
        "assemble_nodes",
        (array((COMPS, nodes, cases)), array(disp.shape, BF16)),
        vmem(3),
        flops=400000000,
        moved=2000000,
    )(count, stress, disp)
    (nodal,) = call(
        finish_kernel,
        "add_received",
        (array((COMPS, nodes, cases), BF16),),
        vmem(8),
        (pltpu.VMEM((2, 2 * LANES, COMPS * cases), BF16),),
        flops=800000000,
        moved=3000000,
    )(
        placing,
        partial,
        inverse_volume,
        from_sub_lo,
        from_sub_hi,
        from_grp_lo,
        from_grp_hi,
        from_edge_lo,
    )
    return jnp.transpose(disp, (1, 0, 2)), jnp.transpose(nodal, (1, 0, 2))


def solution(mesh):
    owner = ("sub", "grp")
    placed = (
        P(owner, None),
        P(owner, None),
        P(owner, None),
        P(owner, None, None),
        P(owner, None, None),
        P(owner, None),
        P(None, None, owner),
        P(owner),
        P(None, owner),
        P(owner, None),
        P(owner),
    )
    return jax.shard_map(
        shards,
        mesh=mesh,
        in_specs=placed,
        out_specs=(P(owner, None, None), P(owner, None, None)),
        check_vma=False,
    )
```

```python
import jax
import jax.numpy as jnp
from jax import lax
from jax.experimental import pallas as pl
from jax.experimental.pallas import tpu as pltpu
from jax.sharding import PartitionSpec as P

NIS = 64
NIG = 32
NED = 8
EDGES = 2 * NIS + 2 * NIG
NIF = EDGES + 4 * NED
CORNERS = 8
COMPS = 6
LANES = 128
TERM = 32

POISSON = 0.3
LAME = POISSON / ((1.0 + POISSON) * (1.0 - 2.0 * POISSON))
SHEAR = 0.5 / (1.0 + POISSON)

F32 = jnp.float32
BF16 = jnp.bfloat16
VMEM_LIMIT = 24 * 1024 * 1024


def split_two(x):
    high = x.astype(BF16)
    return high, (x - high.astype(F32)).astype(BF16)


def dot(a, b):
    return jnp.dot(a, b, preferred_element_type=F32)


def dot_nt(a, b):
    return lax.dot_general(a, b, (((1,), (1,)), ((), ())), preferred_element_type=F32)


def column(row):
    return jnp.broadcast_to(row, (LANES, LANES)).T


def swap_lanes(x, distance):
    lane = lax.broadcasted_iota(jnp.int32, x.shape, 1)
    after = pltpu.roll(x, LANES - distance, 1)
    before = pltpu.roll(x, distance, 1)
    return jnp.where((lane & distance) == 0, after, before)


def order_lists(ids):
    sub_even = (lax.axis_index("sub") & 1) == 0
    grp_even = (lax.axis_index("grp") & 1) == 0
    first, second = ids[:, :LANES], ids[:, LANES:]
    ids[:, :LANES] = jnp.where(sub_even, swap_lanes(first, NIS), first)
    lane = lax.broadcasted_iota(jnp.int32, second.shape, 1)
    groups = jnp.where(grp_even, swap_lanes(second, NIG), second)
    edges = jnp.where(sub_even, swap_lanes(second, 2 * NED), second)
    edges = jnp.where(grp_even, swap_lanes(edges, NED), edges)
    ids[:, LANES:] = jnp.where(lane < 2 * NIG, groups, edges)


def prepare_kernel(
    blocks,
    corner_idx,
    panel_nodes,
    coupling,
    force,
    panel_inv,
    strain_disp,
    modulus,
    connect,
    interface,
    volume,
    inverse,
    coupled,
    loads,
    live,
    select,
    onehot,
    face,
    scaled,
    count,
    placing,
    inverse_volume,
    corner_v,
    panel_v,
    coupling_v,
    force_v,
    strain_v,
    modulus_v,
    connect_v,
    interface_v,
    volume_v,
    ids,
    sems,
):
    pairs = [
        (connect, connect_v),
        (interface, interface_v),
        (corner_idx, corner_v),
        (panel_nodes, panel_v),
        (volume, volume_v),
        (modulus, modulus_v),
        (strain_disp, strain_v),
        (coupling, coupling_v),
        (force, force_v),
        (panel_inv, inverse),
    ]
    copies = [pltpu.make_async_copy(src, dst, sems.at[k]) for k, (src, dst) in enumerate(pairs)]
    for copy in copies:
        copy.start()
    panels, panel_rows, _ = inverse.shape
    nodes = force_v.shape[1]
    q = corner_idx.shape[1]

    copies[0].wait()
    node_of = lax.broadcasted_iota(jnp.int32, (nodes, LANES), 0)
    total = jnp.zeros((nodes, LANES), F32)
    for a in range(CORNERS):
        hit = jnp.where(connect_v[a : a + 1, :] == node_of, 1.0, 0.0)
        onehot[:, a * LANES : (a + 1) * LANES] = hit.astype(BF16)
        total = total + hit
    total = total.astype(BF16)
    count[:, :LANES] = total
    count[:, LANES:] = total

    copies[1].wait()
    ids[...] = jnp.full(ids.shape, -1.0, F32)
    ids[0:1, 0:NIF] = interface_v[...].astype(F32)
    order_lists(ids)
    node_of = lax.broadcasted_iota(jnp.int32, (nodes, 2 * LANES), 0)
    placing[...] = jnp.where(ids[0:1, :].astype(jnp.int32) == node_of, 1.0, 0.0).astype(BF16)
    connect_f = connect_v[...].astype(F32)
    for half in range(2):
        id_col = column(ids[0:1, half * LANES : (half + 1) * LANES])
        rows = jnp.zeros((LANES, LANES), F32)
        for a in range(CORNERS):
            rows = rows + jnp.where(connect_f[a : a + 1, :] == id_col, 1.0, 0.0)
        rows = rows.astype(BF16)[: min(LANES, NIF - half * LANES)]
        face[half * LANES : half * LANES + rows.shape[0], :LANES] = rows
        face[half * LANES : half * LANES + rows.shape[0], LANES:] = rows

    copies[2].wait()
    ids[0:1, 0:q] = corner_v[...].astype(F32)
    wanted = column(ids[0:1, :LANES])[:TERM]
    lane = lax.broadcasted_iota(jnp.int32, (TERM, LANES), 1)
    entry = lax.broadcasted_iota(jnp.int32, (TERM, LANES), 0)
    s = lax.axis_index("sub")
    aside = 1 - 2 * (s & 1)
    for b, owner in enumerate((s, s + aside, s - aside)):
        row = owner * blocks + lane
        hit = (wanted == row.astype(F32)) & (lane < blocks) & (entry < q)
        select[:, b * LANES : (b + 1) * LANES] = jnp.where(hit, 1.0, 0.0).astype(BF16)

    copies[3].wait()
    row_of = lax.broadcasted_iota(jnp.int32, (panel_rows, LANES), 0)
    for p in range(panels):
        alive = row_of < 3 * panel_v[0:1, p : p + 1]
        live[p * panel_rows : (p + 1) * panel_rows, :] = jnp.where(alive, 1.0, 0.0)

    copies[4].wait()
    for k in range(nodes // LANES):
        inverse_volume[k * LANES : (k + 1) * LANES, :] = column(1.0 / volume_v[k : k + 1, :])

    copies[5].wait()
    copies[6].wait()
    factor = modulus_v[...]
    rows = [strain_v[i].astype(F32) for i in range(COMPS)]
    trace = (rows[0] + rows[1] + rows[2]) * LAME
    for i in range(COMPS):
        value = trace + rows[i] * (2.0 * SHEAR) if i < 3 else rows[i] * SHEAR
        scaled[24 * i : 24 * (i + 1), :] = value * factor

    copies[7].wait()
    for k in range(coupling_v.shape[1] // LANES):
        part = coupling_v[:, k * LANES : (k + 1) * LANES].astype(F32)
        gap = jnp.zeros((TERM - q, LANES), F32)
        stack = jnp.concatenate([part, gap] * 3 + [jnp.zeros((LANES - 3 * TERM, LANES), F32)], axis=0)
        rows = slice(k * LANES, (k + 1) * LANES)
        coupled[rows, :] = (stack.T * live[rows, :]).astype(BF16)

    copies[8].wait()
    for c in range(3):
        loads[pl.ds(c, nodes, stride=3), :] = force_v[c].astype(F32)
    loads[...] = loads[...] * live[...]
    copies[9].wait()


def load_kernel(coarse, own, sem):
    copy = pltpu.make_async_copy(coarse, own, sem)
    copy.start()
    copy.wait()


def merge_kernel(bit, own, other, out):
    rows = own.shape[0]
    place = (lax.axis_index("grp") >> bit) & 1
    out[pl.ds(pl.multiple_of(place * rows, 8), rows), :] = own[...]
    out[pl.ds(pl.multiple_of((1 - place) * rows, 8), rows), :] = other[...]


def solve_kernel(
    here,
    beside,
    beyond,
    inverse,
    coupled,
    loads,
    live,
    select,
    onehot,
    face,
    scaled,
    disp,
    stress,
    sub_a,
    sub_b,
    grp_a,
    grp_b,
    terms,
    solved,
    disp_t,
    elem_t,
):
    panels, panel_rows, _ = inverse.shape
    panel_size = panel_rows // 3
    rows = here.shape[0]

    terms[...] = jnp.zeros(terms.shape, BF16)
    for b, block in enumerate((here, beside, beyond)):
        x = block[...]
        high = x.astype(BF16)
        rest = x - high.astype(F32)
        middle = rest.astype(BF16)
        low = (rest - middle.astype(F32)).astype(BF16)
        for t, value in enumerate((high, middle, low)):
            terms[t, b * LANES : b * LANES + rows, :] = value
    picked = [dot(select[...], terms[t]) for t in range(3)]
    picked.append(jnp.zeros((LANES - 3 * TERM, LANES), F32))
    values = jnp.concatenate(picked, axis=0).astype(BF16)

    for p in range(panels):
        start = p * panel_rows
        span = slice(start, start + panel_rows)
        reduced = (loads[span, :] - dot(coupled[span, :], values)).astype(BF16)
        solved[span, :] = dot(inverse[p], reduced) * live[span, :]
        for c in range(3):
            part = solved[pl.ds(start + c, panel_size, stride=3), :].astype(BF16)
            disp[c, p * panel_size : (p + 1) * panel_size, :] = part
            disp_t[c * LANES : (c + 1) * LANES, p * panel_size : (p + 1) * panel_size] = (
                part.astype(F32).T.astype(BF16)
            )

    for c in range(3):
        elem_t[c] = dot(disp_t[c * LANES : (c + 1) * LANES, :], onehot[...])
    step = 32
    for start in range(0, LANES, step):
        sums = [None] * COMPS
        for a in range(CORNERS):
            for c in range(3):
                x = elem_t[c, start : start + step, a * LANES : (a + 1) * LANES]
                for i in range(COMPS):
                    r = 24 * i + 3 * a + c
                    term = scaled[r : r + 1, :] * x
                    sums[i] = term if sums[i] is None else sums[i] + term
        for i in range(COMPS):
            high, low = split_two(sums[i])
            stress[i * LANES + start : i * LANES + start + step, 0:LANES] = high
            stress[i * LANES + start : i * LANES + start + step, LANES : 2 * LANES] = low

    rows = dot_nt(face[...], stress[...])
    for i in range(COMPS):
        part = rows[:, i * LANES : (i + 1) * LANES]
        edge = [part[EDGES + NED * k : EDGES + NED * (k + 1)] for k in range(4)]
        sub_a[i] = part[:NIS]
        sub_b[i] = part[NIS : 2 * NIS]
        grp_a[i] = jnp.concatenate([part[2 * NIS : 2 * NIS + NIG], edge[0], edge[2]], axis=0)
        grp_b[i] = jnp.concatenate([part[2 * NIS + NIG : EDGES], edge[1], edge[3]], axis=0)


def edge_kernel(sub_a, sub_b, grp_a, grp_b, from_a, from_b, out_a, out_b):
    split = NIG + NED
    out_a[:, :NIS, :] = sub_a[...]
    out_b[:, :NIS, :] = sub_b[...]
    out_a[:, NIS : NIS + NED, :] = grp_a[:, NIG:split, :] + from_a[:, NIG:split, :]
    out_a[:, NIS + NED :, :] = grp_b[:, NIG:split, :] + from_b[:, NIG:split, :]
    out_b[:, NIS : NIS + NED, :] = grp_a[:, split:, :] + from_a[:, split:, :]
    out_b[:, NIS + NED :, :] = grp_b[:, split:, :] + from_b[:, split:, :]


def partial_kernel(count, stress, disp, partial, disp_out):
    disp_out[...] = disp[...]
    for i in range(COMPS):
        partial[i] = dot_nt(count[...], stress[i * LANES : (i + 1) * LANES, :])


def finish_kernel(
    placing, partial, inverse_volume, sub_a, sub_b, grp_a, grp_b, out, received
):
    split = NIG + NED
    for i in range(COMPS):
        low, high, sub, last = grp_a[i], grp_b[i], sub_a[i], sub_b[i]
        rows = jnp.concatenate(
            [
                sub[:NIS],
                last[:NIS],
                low[:NIG],
                high[:NIG],
                low[NIG:split] + sub[NIS : NIS + NED],
                high[NIG:split] + sub[NIS + NED :],
                low[split:] + last[NIS : NIS + NED],
                high[split:] + last[NIS + NED :],
                jnp.zeros((2 * LANES - NIF, LANES), F32),
            ],
            axis=0,
        )
        first, second = split_two(rows)
        received[0, :, i * LANES : (i + 1) * LANES] = first
        received[1, :, i * LANES : (i + 1) * LANES] = second
    scale = inverse_volume[...]
    for i in range(0, COMPS, 2):
        cols = slice(i * LANES, (i + 2) * LANES)
        added = dot(placing[...], received[0, :, cols]) + dot(placing[...], received[1, :, cols])
        out[i] = ((partial[i] + added[:, :LANES]) * scale).astype(BF16)
        out[i + 1] = ((partial[i + 1] + added[:, LANES:]) * scale).astype(BF16)


def vmem(count):
    return [pl.BlockSpec(memory_space=pltpu.VMEM)] * count


def array(shape, dtype=F32):
    return jax.ShapeDtypeStruct(shape, dtype)


def call(kernel, name, out_shape, in_specs, scratch=(), flops=0, moved=0):
    return pl.pallas_call(
        kernel,
        name=name,
        out_shape=out_shape,
        in_specs=in_specs,
        out_specs=vmem(len(out_shape)),
        scratch_shapes=list(scratch),
        compiler_params=pltpu.CompilerParams(vmem_limit_bytes=VMEM_LIMIT),
        cost_estimate=pl.CostEstimate(flops=flops, bytes_accessed=moved, transcendentals=0),
    )


def exchange(block, axis, first):
    count = lax.axis_size(axis)
    pairs = []
    for i in range(first, count - 1, 2):
        pairs += [(i, i + 1), (i + 1, i)]
    return lax.ppermute(block, axis, pairs)


def in_hbm(*arrays):
    return [pltpu.with_memory_space_constraint(x, pltpu.HBM) for x in arrays]


def gather_group(block, own):
    count = lax.axis_size("grp")
    bit = 0
    while 1 << bit < count:
        other = lax.ppermute(block, "grp", [(i, i ^ (1 << bit)) for i in range(count)])
        rows, lanes = block.shape

        def merge(own, received, out, bit=bit):
            merge_kernel(bit, own, received, out)

        (block,) = call(merge, "merge_blocks", (array((2 * rows, lanes)),), vmem(2))(own, other)
        own = block
        bit += 1
    return block


def shards(
    coarse,
    corner_idx,
    coupling,
    force,
    panel_inv,
    panel_nodes,
    strain_disp,
    modulus,
    connect,
    interface,
    nodal_volume,
):
    nodes, _, cases = force.shape
    dofs = 3 * nodes
    q = corner_idx.shape[1]
    blocks = coarse.shape[0] * lax.axis_size("grp")

    def prepare(*refs):
        prepare_kernel(blocks, *refs)

    prepared = call(
        prepare,
        "prepare",
        (
            array(panel_inv.shape, BF16),
            array((dofs, LANES), BF16),
            array((dofs, cases)),
            array((dofs, LANES)),
            array((TERM, 3 * LANES), BF16),
            array((nodes, CORNERS * LANES), BF16),
            array((NIF, 2 * LANES), BF16),
            array((COMPS * 24, LANES)),
            array((nodes, 2 * LANES), BF16),
            array((nodes, 2 * LANES), BF16),
            array((nodes, LANES)),
        ),
        [pl.BlockSpec(memory_space=pltpu.HBM)] * 10,
        (
            pltpu.VMEM((1, q), jnp.int32),
            pltpu.VMEM(panel_nodes.shape, jnp.int32),
            pltpu.VMEM((q, dofs), BF16),
            pltpu.VMEM((3, nodes, cases), BF16),
            pltpu.VMEM(strain_disp.shape, BF16),
            pltpu.VMEM((1, LANES), F32),
            pltpu.VMEM(connect.shape, jnp.int32),
            pltpu.VMEM(interface.shape, jnp.int32),
            pltpu.VMEM((nodes // LANES, LANES), F32),
            pltpu.VMEM((8, 2 * LANES), F32),
            pltpu.SemaphoreType.DMA((10,)),
        ),
        flops=200000000,
        moved=8000000,
    )(
        *in_hbm(
            corner_idx,
            panel_nodes,
            coupling.T,
            jnp.transpose(force, (1, 0, 2)),
            panel_inv,
            strain_disp,
            modulus.reshape(1, -1),
            connect,
            interface,
            nodal_volume.reshape(-1, LANES),
        )
    )
    *operands, count, placing, inverse_volume = prepared

    (own,) = call(
        load_kernel,
        "load_own",
        (array(coarse.shape),),
        [pl.BlockSpec(memory_space=pltpu.HBM)],
        (pltpu.SemaphoreType.DMA,),
    )(*in_hbm(coarse))
    here = gather_group(coarse, own)
    beyond = exchange(here, "sub", 1)
    beside = exchange(here, "sub", 0)
    disp, stress, sub_a, sub_b, grp_a, grp_b = call(
        solve_kernel,
        "solve_and_stress",
        (
            array((3, nodes, cases), BF16),
            array((COMPS * cases, 2 * LANES), BF16),
            array((COMPS, NIS, cases)),
            array((COMPS, NIS, cases)),
            array((COMPS, NIG + 2 * NED, cases)),
            array((COMPS, NIG + 2 * NED, cases)),
        ),
        vmem(11),
        (
            pltpu.VMEM((3, 3 * LANES, cases), BF16),
            pltpu.VMEM((dofs, cases), F32),
            pltpu.VMEM((3 * cases, nodes), BF16),
            pltpu.VMEM((3, cases, CORNERS * LANES), F32),
        ),
        flops=1500000000,
        moved=4000000,
    )(here, beside, beyond, *operands)
    from_grp_a = exchange(grp_a, "grp", 0)
    from_grp_b = exchange(grp_b, "grp", 1)
    sub_a, sub_b = call(
        edge_kernel,
        "sum_edges",
        (array((COMPS, NIS + 2 * NED, cases)), array((COMPS, NIS + 2 * NED, cases))),
        vmem(6),
    )(sub_a, sub_b, grp_a, grp_b, from_grp_a, from_grp_b)
    from_sub_a = exchange(sub_a, "sub", 0)
    from_sub_b = exchange(sub_b, "sub", 1)
    partial, disp = call(
        partial_kernel,
        "assemble_nodes",
        (array((COMPS, nodes, cases)), array(disp.shape, BF16)),
        vmem(3),
        flops=400000000,
        moved=2000000,
    )(count, stress, disp)
    (nodal,) = call(
        finish_kernel,
        "add_received",
        (array((COMPS, nodes, cases), BF16),),
        vmem(7),
        (pltpu.VMEM((2, 2 * LANES, COMPS * cases), BF16),),
        flops=800000000,
        moved=3000000,
    )(
        placing,
        partial,
        inverse_volume,
        from_sub_a,
        from_sub_b,
        from_grp_a,
        from_grp_b,
    )
    return jnp.transpose(disp, (1, 0, 2)), jnp.transpose(nodal, (1, 0, 2))


def solution(mesh):
    owner = ("sub", "grp")
    placed = (
        P(owner, None),
        P(owner, None),
        P(owner, None),
        P(owner, None, None),
        P(owner, None, None),
        P(owner, None),
        P(None, None, owner),
        P(owner),
        P(None, owner),
        P(owner, None),
        P(owner),
    )
    return jax.shard_map(
        shards,
        mesh=mesh,
        in_specs=placed,
        out_specs=(P(owner, None, None), P(owner, None, None)),
        check_vma=False,
    )
```

```python
import jax
import jax.numpy as jnp
from jax import lax
from jax.experimental import pallas as pl
from jax.experimental.pallas import tpu as pltpu
from jax.sharding import PartitionSpec as P

NIS = 64
NIG = 32
NED = 8
EDGES = 2 * NIS + 2 * NIG
NIF = EDGES + 4 * NED
CORNERS = 8
COMPS = 6
LANES = 128
TERM = 32

POISSON = 0.3
LAME = POISSON / ((1.0 + POISSON) * (1.0 - 2.0 * POISSON))
SHEAR = 0.5 / (1.0 + POISSON)

F32 = jnp.float32
BF16 = jnp.bfloat16
VMEM_LIMIT = 24 * 1024 * 1024


def split_two(x):
    high = x.astype(BF16)
    return high, (x - high.astype(F32)).astype(BF16)


def dot(a, b):
    return jnp.dot(a, b, preferred_element_type=F32)


def dot_nt(a, b):
    return lax.dot_general(a, b, (((1,), (1,)), ((), ())), preferred_element_type=F32)


def column(row):
    return jnp.broadcast_to(row, (LANES, LANES)).T


def swap_lanes(x, distance):
    lane = lax.broadcasted_iota(jnp.int32, x.shape, 1)
    after = pltpu.roll(x, LANES - distance, 1)
    before = pltpu.roll(x, distance, 1)
    return jnp.where((lane & distance) == 0, after, before)


def order_lists(ids):
    sub_even = (lax.axis_index("sub") & 1) == 0
    grp_even = (lax.axis_index("grp") & 1) == 0
    first, second = ids[:, :LANES], ids[:, LANES:]
    ids[:, :LANES] = jnp.where(sub_even, swap_lanes(first, NIS), first)
    lane = lax.broadcasted_iota(jnp.int32, second.shape, 1)
    groups = jnp.where(grp_even, swap_lanes(second, NIG), second)
    edges = jnp.where(sub_even, swap_lanes(second, 2 * NED), second)
    edges = jnp.where(grp_even, swap_lanes(edges, NED), edges)
    ids[:, LANES:] = jnp.where(lane < 2 * NIG, groups, edges)


def prepare_kernel(
    blocks,
    corner_idx,
    panel_nodes,
    coupling,
    force,
    panel_inv,
    strain_disp,
    modulus,
    connect,
    interface,
    volume,
    inverse,
    coupled,
    loads,
    live,
    select,
    onehot,
    face,
    scaled,
    count,
    placing,
    inverse_volume,
    corner_v,
    panel_v,
    coupling_v,
    force_v,
    strain_v,
    modulus_v,
    connect_v,
    interface_v,
    volume_v,
    ids,
    sems,
):
    pairs = [
        (connect, connect_v),
        (interface, interface_v),
        (corner_idx, corner_v),
        (panel_nodes, panel_v),
        (volume, volume_v),
        (modulus, modulus_v),
        (strain_disp, strain_v),
        (coupling, coupling_v),
        (force, force_v),
        (panel_inv, inverse),
    ]
    copies = [pltpu.make_async_copy(src, dst, sems.at[k]) for k, (src, dst) in enumerate(pairs)]
    for copy in copies:
        copy.start()
    panels, panel_rows, _ = inverse.shape
    nodes = force_v.shape[1]
    q = corner_idx.shape[1]

    copies[0].wait()
    node_of = lax.broadcasted_iota(jnp.int32, (nodes, LANES), 0)
    total = jnp.zeros((nodes, LANES), F32)
    for a in range(CORNERS):
        hit = jnp.where(connect_v[a : a + 1, :] == node_of, 1.0, 0.0)
        onehot[:, a * LANES : (a + 1) * LANES] = hit.astype(BF16)
        total = total + hit
    total = total.astype(BF16)
    count[:, :LANES] = total
    count[:, LANES:] = total

    copies[1].wait()
    ids[...] = jnp.full(ids.shape, -1.0, F32)
    ids[0:1, 0:NIF] = interface_v[...].astype(F32)
    order_lists(ids)
    node_of = lax.broadcasted_iota(jnp.int32, (nodes, 2 * LANES), 0)
    placing[...] = jnp.where(ids[0:1, :].astype(jnp.int32) == node_of, 1.0, 0.0).astype(BF16)
    connect_f = connect_v[...].astype(F32)
    for half in range(2):
        id_col = column(ids[0:1, half * LANES : (half + 1) * LANES])
        rows = jnp.zeros((LANES, LANES), F32)
        for a in range(CORNERS):
            rows = rows + jnp.where(connect_f[a : a + 1, :] == id_col, 1.0, 0.0)
        rows = rows.astype(BF16)[: min(LANES, NIF - half * LANES)]
        face[half * LANES : half * LANES + rows.shape[0], :LANES] = rows
        face[half * LANES : half * LANES + rows.shape[0], LANES:] = rows

    copies[2].wait()
    ids[0:1, 0:q] = corner_v[...].astype(F32)
    wanted = column(ids[0:1, :LANES])[:TERM]
    lane = lax.broadcasted_iota(jnp.int32, (TERM, LANES), 1)
    entry = lax.broadcasted_iota(jnp.int32, (TERM, LANES), 0)
    s = lax.axis_index("sub")
    aside = 1 - 2 * (s & 1)
    for b, owner in enumerate((s, s + aside, s - aside)):
        row = owner * blocks + lane
        hit = (wanted == row.astype(F32)) & (lane < blocks) & (entry < q)
        select[:, b * LANES : (b + 1) * LANES] = jnp.where(hit, 1.0, 0.0).astype(BF16)

    copies[3].wait()
    row_of = lax.broadcasted_iota(jnp.int32, (panel_rows, LANES), 0)
    for p in range(panels):
        alive = row_of < 3 * panel_v[0:1, p : p + 1]
        live[p * panel_rows : (p + 1) * panel_rows, :] = jnp.where(alive, 1.0, 0.0)

    copies[4].wait()
    for k in range(nodes // LANES):
        inverse_volume[k * LANES : (k + 1) * LANES, :] = column(1.0 / volume_v[k : k + 1, :])

    copies[5].wait()
    copies[6].wait()
    factor = modulus_v[...]
    rows = [strain_v[i].astype(F32) for i in range(COMPS)]
    trace = (rows[0] + rows[1] + rows[2]) * LAME
    for i in range(COMPS):
        value = trace + rows[i] * (2.0 * SHEAR) if i < 3 else rows[i] * SHEAR
        scaled[24 * i : 24 * (i + 1), :] = value * factor

    copies[7].wait()
    for k in range(coupling_v.shape[1] // LANES):
        part = coupling_v[:, k * LANES : (k + 1) * LANES].astype(F32)
        gap = jnp.zeros((TERM - q, LANES), F32)
        stack = jnp.concatenate([part, gap] * 3 + [jnp.zeros((LANES - 3 * TERM, LANES), F32)], axis=0)
        rows = slice(k * LANES, (k + 1) * LANES)
        coupled[rows, :] = (stack.T * live[rows, :]).astype(BF16)

    copies[8].wait()
    for c in range(3):
        loads[pl.ds(c, nodes, stride=3), :] = force_v[c].astype(F32)
    loads[...] = loads[...] * live[...]
    copies[9].wait()


def load_kernel(coarse, own, sem):
    copy = pltpu.make_async_copy(coarse, own, sem)
    copy.start()
    copy.wait()


def merge_kernel(bit, own, other, out):
    rows = own.shape[0]
    place = (lax.axis_index("grp") >> bit) & 1
    out[pl.ds(pl.multiple_of(place * rows, 8), rows), :] = own[...]
    out[pl.ds(pl.multiple_of((1 - place) * rows, 8), rows), :] = other[...]


def solve_kernel(
    here,
    beside,
    beyond,
    inverse,
    coupled,
    loads,
    live,
    select,
    onehot,
    face,
    scaled,
    disp,
    stress,
    sub_a,
    sub_b,
    grp_a,
    grp_b,
    terms,
    solved,
    disp_t,
    elem_t,
):
    panels, panel_rows, _ = inverse.shape
    panel_size = panel_rows // 3
    rows = here.shape[0]

    terms[...] = jnp.zeros(terms.shape, BF16)
    for b, block in enumerate((here, beside, beyond)):
        x = block[...]
        high = x.astype(BF16)
        rest = x - high.astype(F32)
        middle = rest.astype(BF16)
        low = (rest - middle.astype(F32)).astype(BF16)
        for t, value in enumerate((high, middle, low)):
            terms[t, b * LANES : b * LANES + rows, :] = value
    picked = [dot(select[...], terms[t]) for t in range(3)]
    picked.append(jnp.zeros((LANES - 3 * TERM, LANES), F32))
    values = jnp.concatenate(picked, axis=0).astype(BF16)

    for p in range(panels):
        start = p * panel_rows
        span = slice(start, start + panel_rows)
        reduced = (loads[span, :] - dot(coupled[span, :], values)).astype(BF16)
        solved[span, :] = dot(inverse[p], reduced) * live[span, :]
        for c in range(3):
            part = solved[pl.ds(start + c, panel_size, stride=3), :].astype(BF16)
            disp[c, p * panel_size : (p + 1) * panel_size, :] = part
            disp_t[c * LANES : (c + 1) * LANES, p * panel_size : (p + 1) * panel_size] = (
                part.astype(F32).T.astype(BF16)
            )

    for c in range(3):
        elem_t[c] = dot(disp_t[c * LANES : (c + 1) * LANES, :], onehot[...])
    step = 32
    for start in range(0, LANES, step):
        sums = [None] * COMPS
        for a in range(CORNERS):
            for c in range(3):
                x = elem_t[c, start : start + step, a * LANES : (a + 1) * LANES]
                for i in range(COMPS):
                    r = 24 * i + 3 * a + c
                    term = scaled[r : r + 1, :] * x
                    sums[i] = term if sums[i] is None else sums[i] + term
        for i in range(COMPS):
            high, low = split_two(sums[i])
            stress[i * LANES + start : i * LANES + start + step, 0:LANES] = high
            stress[i * LANES + start : i * LANES + start + step, LANES : 2 * LANES] = low

    rows = dot_nt(face[...], stress[...])
    for i in range(COMPS):
        part = rows[:, i * LANES : (i + 1) * LANES]
        edge = [part[EDGES + NED * k : EDGES + NED * (k + 1)] for k in range(4)]
        sub_a[i] = part[:NIS]
        sub_b[i] = part[NIS : 2 * NIS]
        grp_a[i] = jnp.concatenate([part[2 * NIS : 2 * NIS + NIG], edge[0], edge[2]], axis=0)
        grp_b[i] = jnp.concatenate([part[2 * NIS + NIG : EDGES], edge[1], edge[3]], axis=0)


def edge_kernel(grp_a, grp_b, from_a, from_b, edge_a, edge_b):
    split = NIG + NED
    edge_a[:, :NED, :] = grp_a[:, NIG:split, :] + from_a[:, NIG:split, :]
    edge_a[:, NED:, :] = grp_b[:, NIG:split, :] + from_b[:, NIG:split, :]
    edge_b[:, :NED, :] = grp_a[:, split:, :] + from_a[:, split:, :]
    edge_b[:, NED:, :] = grp_b[:, split:, :] + from_b[:, split:, :]


def partial_kernel(count, stress, disp, partial, disp_out):
    disp_out[...] = disp[...]
    for i in range(COMPS):
        partial[i] = dot_nt(count[...], stress[i * LANES : (i + 1) * LANES, :])


def finish_kernel(
    placing, partial, inverse_volume, sub_a, sub_b, grp_a, grp_b, edge_a, edge_b, out, received
):
    split = NIG + NED
    for i in range(COMPS):
        low, high, first, second = grp_a[i], grp_b[i], edge_a[i], edge_b[i]
        rows = jnp.concatenate(
            [
                sub_a[i],
                sub_b[i],
                low[:NIG],
                high[:NIG],
                low[NIG:split] + first[:NED],
                high[NIG:split] + first[NED:],
                low[split:] + second[:NED],
                high[split:] + second[NED:],
                jnp.zeros((2 * LANES - NIF, LANES), F32),
            ],
            axis=0,
        )
        first, second = split_two(rows)
        received[0, :, i * LANES : (i + 1) * LANES] = first
        received[1, :, i * LANES : (i + 1) * LANES] = second
    scale = inverse_volume[...]
    for i in range(0, COMPS, 2):
        cols = slice(i * LANES, (i + 2) * LANES)
        added = dot(placing[...], received[0, :, cols]) + dot(placing[...], received[1, :, cols])
        out[i] = ((partial[i] + added[:, :LANES]) * scale).astype(BF16)
        out[i + 1] = ((partial[i + 1] + added[:, LANES:]) * scale).astype(BF16)


def vmem(count):
    return [pl.BlockSpec(memory_space=pltpu.VMEM)] * count


def array(shape, dtype=F32):
    return jax.ShapeDtypeStruct(shape, dtype)


def call(kernel, name, out_shape, in_specs, scratch=(), flops=0, moved=0):
    return pl.pallas_call(
        kernel,
        name=name,
        out_shape=out_shape,
        in_specs=in_specs,
        out_specs=vmem(len(out_shape)),
        scratch_shapes=list(scratch),
        compiler_params=pltpu.CompilerParams(vmem_limit_bytes=VMEM_LIMIT),
        cost_estimate=pl.CostEstimate(flops=flops, bytes_accessed=moved, transcendentals=0),
    )


def exchange(block, axis, first):
    count = lax.axis_size(axis)
    pairs = []
    for i in range(first, count - 1, 2):
        pairs += [(i, i + 1), (i + 1, i)]
    return lax.ppermute(block, axis, pairs)


def in_hbm(*arrays):
    return [pltpu.with_memory_space_constraint(x, pltpu.HBM) for x in arrays]


def gather_group(block, own):
    count = lax.axis_size("grp")
    bit = 0
    while 1 << bit < count:
        other = lax.ppermute(block, "grp", [(i, i ^ (1 << bit)) for i in range(count)])
        rows, lanes = block.shape

        def merge(own, received, out, bit=bit):
            merge_kernel(bit, own, received, out)

        (block,) = call(merge, "merge_blocks", (array((2 * rows, lanes)),), vmem(2))(own, other)
        own = block
        bit += 1
    return block


def shards(
    coarse,
    corner_idx,
    coupling,
    force,
    panel_inv,
    panel_nodes,
    strain_disp,
    modulus,
    connect,
    interface,
    nodal_volume,
):
    nodes, _, cases = force.shape
    dofs = 3 * nodes
    q = corner_idx.shape[1]
    blocks = coarse.shape[0] * lax.axis_size("grp")

    def prepare(*refs):
        prepare_kernel(blocks, *refs)

    prepared = call(
        prepare,
        "prepare",
        (
            array(panel_inv.shape, BF16),
            array((dofs, LANES), BF16),
            array((dofs, cases)),
            array((dofs, LANES)),
            array((TERM, 3 * LANES), BF16),
            array((nodes, CORNERS * LANES), BF16),
            array((NIF, 2 * LANES), BF16),
            array((COMPS * 24, LANES)),
            array((nodes, 2 * LANES), BF16),
            array((nodes, 2 * LANES), BF16),
            array((nodes, LANES)),
        ),
        [pl.BlockSpec(memory_space=pltpu.HBM)] * 10,
        (
            pltpu.VMEM((1, q), jnp.int32),
            pltpu.VMEM(panel_nodes.shape, jnp.int32),
            pltpu.VMEM((q, dofs), BF16),
            pltpu.VMEM((3, nodes, cases), BF16),
            pltpu.VMEM(strain_disp.shape, BF16),
            pltpu.VMEM((1, LANES), F32),
            pltpu.VMEM(connect.shape, jnp.int32),
            pltpu.VMEM(interface.shape, jnp.int32),
            pltpu.VMEM((nodes // LANES, LANES), F32),
            pltpu.VMEM((8, 2 * LANES), F32),
            pltpu.SemaphoreType.DMA((10,)),
        ),
        flops=200000000,
        moved=8000000,
    )(
        *in_hbm(
            corner_idx,
            panel_nodes,
            coupling.T,
            jnp.transpose(force, (1, 0, 2)),
            panel_inv,
            strain_disp,
            modulus.reshape(1, -1),
            connect,
            interface,
            nodal_volume.reshape(-1, LANES),
        )
    )
    *operands, count, placing, inverse_volume = prepared

    (own,) = call(
        load_kernel,
        "load_own",
        (array(coarse.shape),),
        [pl.BlockSpec(memory_space=pltpu.HBM)],
        (pltpu.SemaphoreType.DMA,),
    )(*in_hbm(coarse))
    here = gather_group(coarse, own)
    beyond = exchange(here, "sub", 1)
    beside = exchange(here, "sub", 0)
    disp, stress, sub_a, sub_b, grp_a, grp_b = call(
        solve_kernel,
        "solve_and_stress",
        (
            array((3, nodes, cases), BF16),
            array((COMPS * cases, 2 * LANES), BF16),
            array((COMPS, NIS, cases)),
            array((COMPS, NIS, cases)),
            array((COMPS, NIG + 2 * NED, cases)),
            array((COMPS, NIG + 2 * NED, cases)),
        ),
        vmem(11),
        (
            pltpu.VMEM((3, 3 * LANES, cases), BF16),
            pltpu.VMEM((dofs, cases), F32),
            pltpu.VMEM((3 * cases, nodes), BF16),
            pltpu.VMEM((3, cases, CORNERS * LANES), F32),
        ),
        flops=1500000000,
        moved=4000000,
    )(here, beside, beyond, *operands)
    from_grp_a = exchange(grp_a, "grp", 0)
    from_grp_b = exchange(grp_b, "grp", 1)
    edge_a, edge_b = call(
        edge_kernel,
        "sum_edges",
        (array((COMPS, 2 * NED, cases)), array((COMPS, 2 * NED, cases))),
        vmem(4),
    )(grp_a, grp_b, from_grp_a, from_grp_b)
    from_sub_b = exchange(sub_b, "sub", 1)
    from_sub_a = exchange(sub_a, "sub", 0)
    from_edge_b = exchange(edge_b, "sub", 1)
    from_edge_a = exchange(edge_a, "sub", 0)
    partial, disp = call(
        partial_kernel,
        "assemble_nodes",
        (array((COMPS, nodes, cases)), array(disp.shape, BF16)),
        vmem(3),
        flops=400000000,
        moved=2000000,
    )(count, stress, disp)
    (nodal,) = call(
        finish_kernel,
        "add_received",
        (array((COMPS, nodes, cases), BF16),),
        vmem(9),
        (pltpu.VMEM((2, 2 * LANES, COMPS * cases), BF16),),
        flops=800000000,
        moved=3000000,
    )(
        placing,
        partial,
        inverse_volume,
        from_sub_a,
        from_sub_b,
        from_grp_a,
        from_grp_b,
        from_edge_a,
        from_edge_b,
    )
    return jnp.transpose(disp, (1, 0, 2)), jnp.transpose(nodal, (1, 0, 2))


def solution(mesh):
    owner = ("sub", "grp")
    placed = (
        P(owner, None),
        P(owner, None),
        P(owner, None),
        P(owner, None, None),
        P(owner, None, None),
        P(owner, None),
        P(None, None, owner),
        P(owner),
        P(None, owner),
        P(owner, None),
        P(owner),
    )
    return jax.shard_map(
        shards,
        mesh=mesh,
        in_specs=placed,
        out_specs=(P(owner, None, None), P(owner, None, None)),
        check_vma=False,
    )
```

```python
import jax
import jax.numpy as jnp
from jax import lax
from jax.experimental import pallas as pl
from jax.experimental.pallas import tpu as pltpu
from jax.sharding import PartitionSpec as P

NIS = 64
NIG = 32
NED = 8
EDGES = 2 * NIS + 2 * NIG
NIF = EDGES + 4 * NED
CORNERS = 8
COMPS = 6
LANES = 128
TERM = 32

POISSON = 0.3
LAME = POISSON / ((1.0 + POISSON) * (1.0 - 2.0 * POISSON))
SHEAR = 0.5 / (1.0 + POISSON)

F32 = jnp.float32
BF16 = jnp.bfloat16
VMEM_LIMIT = 24 * 1024 * 1024


def split_two(x):
    high = x.astype(BF16)
    return high, (x - high.astype(F32)).astype(BF16)


def dot(a, b):
    return jnp.dot(a, b, preferred_element_type=F32)


def dot_nt(a, b):
    return lax.dot_general(a, b, (((1,), (1,)), ((), ())), preferred_element_type=F32)


def column(row):
    return jnp.broadcast_to(row, (LANES, LANES)).T


def swap_lanes(x, distance):
    lane = lax.broadcasted_iota(jnp.int32, x.shape, 1)
    after = pltpu.roll(x, LANES - distance, 1)
    before = pltpu.roll(x, distance, 1)
    return jnp.where((lane & distance) == 0, after, before)


def order_lists(ids):
    sub_even = (lax.axis_index("sub") & 1) == 0
    grp_even = (lax.axis_index("grp") & 1) == 0
    first, second = ids[:, :LANES], ids[:, LANES:]
    ids[:, :LANES] = jnp.where(sub_even, swap_lanes(first, NIS), first)
    lane = lax.broadcasted_iota(jnp.int32, second.shape, 1)
    groups = jnp.where(grp_even, swap_lanes(second, NIG), second)
    edges = jnp.where(sub_even, swap_lanes(second, 2 * NED), second)
    edges = jnp.where(grp_even, swap_lanes(edges, NED), edges)
    ids[:, LANES:] = jnp.where(lane < 2 * NIG, groups, edges)


def start_copies(pairs, sems):
    copies = [pltpu.make_async_copy(src, dst, sems.at[k]) for k, (src, dst) in enumerate(pairs)]
    for copy in copies:
        copy.start()
    return copies


def prepare_lists(
    block_rows,
    members,
    corner_idx,
    connect,
    interface,
    strain_disp,
    modulus,
    volume,
    select,
    onehot,
    face,
    scaled,
    count,
    placing,
    inverse_volume,
    corner_v,
    connect_v,
    interface_v,
    strain_v,
    modulus_v,
    volume_v,
    ids,
    sems,
):
    copies = start_copies(
        [
            (connect, connect_v),
            (interface, interface_v),
            (corner_idx, corner_v),
            (modulus, modulus_v),
            (strain_disp, strain_v),
            (volume, volume_v),
        ],
        sems,
    )
    nodes = onehot.shape[0]
    q = corner_idx.shape[1]

    copies[0].wait()
    node_of = lax.broadcasted_iota(jnp.int32, (nodes, LANES), 0)
    total = jnp.zeros((nodes, LANES), F32)
    for a in range(CORNERS):
        hit = jnp.where(connect_v[a : a + 1, :] == node_of, 1.0, 0.0)
        onehot[:, a * LANES : (a + 1) * LANES] = hit.astype(BF16)
        total = total + hit
    total = total.astype(BF16)
    count[:, :LANES] = total
    count[:, LANES:] = total

    copies[1].wait()
    ids[...] = jnp.full(ids.shape, -1.0, F32)
    ids[0:1, 0:NIF] = interface_v[...].astype(F32)
    order_lists(ids)
    node_of = lax.broadcasted_iota(jnp.int32, (nodes, 2 * LANES), 0)
    placing[...] = jnp.where(ids[0:1, :].astype(jnp.int32) == node_of, 1.0, 0.0).astype(BF16)
    connect_f = connect_v[...].astype(F32)
    for half in range(2):
        id_col = column(ids[0:1, half * LANES : (half + 1) * LANES])
        rows = jnp.zeros((LANES, LANES), F32)
        for a in range(CORNERS):
            rows = rows + jnp.where(connect_f[a : a + 1, :] == id_col, 1.0, 0.0)
        rows = rows.astype(BF16)[: min(LANES, NIF - half * LANES)]
        face[half * LANES : half * LANES + rows.shape[0], :LANES] = rows
        face[half * LANES : half * LANES + rows.shape[0], LANES:] = rows

    copies[2].wait()
    ids[0:1, 0:q] = corner_v[...].astype(F32)
    wanted = column(ids[0:1, :LANES])[:TERM]
    lane = lax.broadcasted_iota(jnp.int32, (TERM, 3 * LANES), 1)
    entry = lax.broadcasted_iota(jnp.int32, (TERM, LANES), 0)
    s, g = lax.axis_index("sub"), lax.axis_index("grp")
    aside = 1 - 2 * (s & 1)
    row = jnp.full((TERM, 3 * LANES), -1, jnp.int32)
    base = 0
    for member in range(members):
        distance, bits, turn = members // 2, member, 0
        while distance:
            turn += (bits & 1) * distance
            distance, bits = distance // 2, bits >> 1
        for owner in (s, s + aside, s - aside):
            first = (owner * members + (g ^ turn)) * block_rows
            row = jnp.where((lane >= base) & (lane < base + block_rows), first - base + lane, row)
            base += block_rows
    for b in range(3):
        cols = slice(b * LANES, (b + 1) * LANES)
        hit = (wanted == row[:, cols].astype(F32)) & (entry < q)
        select[:, cols] = jnp.where(hit, 1.0, 0.0).astype(BF16)

    copies[3].wait()
    copies[4].wait()
    factor = modulus_v[...]
    rows = [strain_v[i].astype(F32) for i in range(COMPS)]
    trace = (rows[0] + rows[1] + rows[2]) * LAME
    for i in range(COMPS):
        value = trace + rows[i] * (2.0 * SHEAR) if i < 3 else rows[i] * SHEAR
        scaled[24 * i : 24 * (i + 1), :] = value * factor

    copies[5].wait()
    for k in range(nodes // LANES):
        inverse_volume[k * LANES : (k + 1) * LANES, :] = column(1.0 / volume_v[k : k + 1, :])


def prepare_panels(
    panel_nodes,
    coupling,
    force,
    panel_inv,
    inverse,
    coupled,
    loads,
    live,
    panel_v,
    coupling_v,
    force_v,
    sems,
):
    copies = start_copies(
        [
            (panel_nodes, panel_v),
            (coupling, coupling_v),
            (force, force_v),
            (panel_inv, inverse),
        ],
        sems,
    )
    panels, panel_rows, _ = inverse.shape
    nodes = force_v.shape[1]
    q = coupling_v.shape[0]

    copies[0].wait()
    row_of = lax.broadcasted_iota(jnp.int32, (panel_rows, LANES), 0)
    for p in range(panels):
        alive = row_of < 3 * panel_v[0:1, p : p + 1]
        live[p * panel_rows : (p + 1) * panel_rows, :] = jnp.where(alive, 1.0, 0.0)

    copies[1].wait()
    for k in range(coupling_v.shape[1] // LANES):
        part = coupling_v[:, k * LANES : (k + 1) * LANES].astype(F32)
        gap = jnp.zeros((TERM - q, LANES), F32)
        stack = jnp.concatenate([part, gap] * 3 + [jnp.zeros((LANES - 3 * TERM, LANES), F32)], axis=0)
        rows = slice(k * LANES, (k + 1) * LANES)
        coupled[rows, :] = (stack.T * live[rows, :]).astype(BF16)

    copies[2].wait()
    for c in range(3):
        loads[pl.ds(c, nodes, stride=3), :] = force_v[c].astype(F32)
    loads[...] = loads[...] * live[...]
    copies[3].wait()


def load_kernel(coarse, own, sem):
    copy = pltpu.make_async_copy(coarse, own, sem)
    copy.start()
    copy.wait()


def join_kernel(*refs):
    *parts, out = refs
    start = 0
    for part in parts:
        out[start : start + part.shape[0], :] = part[...]
        start += part.shape[0]


def solve_kernel(
    near,
    across,
    inverse,
    coupled,
    loads,
    live,
    select,
    onehot,
    face,
    scaled,
    disp,
    stress,
    sub_a,
    terms,
    solved,
    disp_t,
    elem_t,
):
    panels, panel_rows, _ = inverse.shape
    panel_size = panel_rows // 3
    rows = near.shape[0]

    terms[:, 2 * rows :, :] = jnp.zeros((3, terms.shape[1] - 2 * rows, terms.shape[2]), BF16)
    for b, block in enumerate((near, across)):
        x = block[...]
        high = x.astype(BF16)
        rest = x - high.astype(F32)
        middle = rest.astype(BF16)
        low = (rest - middle.astype(F32)).astype(BF16)
        for t, value in enumerate((high, middle, low)):
            terms[t, b * rows : (b + 1) * rows, :] = value
    picked = [dot(select[...], terms[t]) for t in range(3)]
    picked.append(jnp.zeros((LANES - 3 * TERM, LANES), F32))
    values = jnp.concatenate(picked, axis=0).astype(BF16)

    for p in range(panels):
        start = p * panel_rows
        span = slice(start, start + panel_rows)
        reduced = (loads[span, :] - dot(coupled[span, :], values)).astype(BF16)
        solved[span, :] = dot(inverse[p], reduced) * live[span, :]
        for c in range(3):
            part = solved[pl.ds(start + c, panel_size, stride=3), :].astype(BF16)
            disp[c, p * panel_size : (p + 1) * panel_size, :] = part
            disp_t[c * LANES : (c + 1) * LANES, p * panel_size : (p + 1) * panel_size] = (
                part.astype(F32).T.astype(BF16)
            )

    for c in range(3):
        elem_t[c] = dot(disp_t[c * LANES : (c + 1) * LANES, :], onehot[...])
    step = 32
    for start in range(0, LANES, step):
        sums = [None] * COMPS
        for a in range(CORNERS):
            for c in range(3):
                x = elem_t[c, start : start + step, a * LANES : (a + 1) * LANES]
                for i in range(COMPS):
                    r = 24 * i + 3 * a + c
                    term = scaled[r : r + 1, :] * x
                    sums[i] = term if sums[i] is None else sums[i] + term
        for i in range(COMPS):
            high, low = split_two(sums[i])
            stress[i * LANES + start : i * LANES + start + step, 0:LANES] = high
            stress[i * LANES + start : i * LANES + start + step, LANES : 2 * LANES] = low

    rows = dot_nt(face[:NIS, :], stress[...])
    for i in range(COMPS):
        sub_a[i] = rows[:, i * LANES : (i + 1) * LANES]


def face_kernel(face, stress, sub_b, grp_a, grp_b):
    base = EDGES - NIS
    rows = dot_nt(face[NIS:, :], stress[...])
    for i in range(COMPS):
        part = rows[:, i * LANES : (i + 1) * LANES]
        edge = [part[base + NED * k : base + NED * (k + 1)] for k in range(4)]
        sub_b[i] = part[:NIS]
        grp_a[i] = jnp.concatenate([part[NIS : NIS + NIG], edge[0], edge[2]], axis=0)
        grp_b[i] = jnp.concatenate([part[NIS + NIG : base], edge[1], edge[3]], axis=0)


def edge_kernel(grp_a, grp_b, from_a, from_b, _, edge_a, edge_b):
    split = NIG + NED
    edge_a[:, :NED, :] = grp_a[:, NIG:split, :] + from_a[:, NIG:split, :]
    edge_a[:, NED:, :] = grp_b[:, NIG:split, :] + from_b[:, NIG:split, :]
    edge_b[:, :NED, :] = grp_a[:, split:, :] + from_a[:, split:, :]
    edge_b[:, NED:, :] = grp_b[:, split:, :] + from_b[:, split:, :]


def partial_kernel(count, stress, disp, partial, disp_out):
    disp_out[...] = disp[...]
    for i in range(COMPS):
        partial[i] = dot_nt(count[...], stress[i * LANES : (i + 1) * LANES, :])


def finish_kernel(
    placing, partial, inverse_volume, sub_a, sub_b, grp_a, grp_b, edge_a, edge_b, out, received
):
    split = NIG + NED
    for i in range(COMPS):
        low, high, first, second = grp_a[i], grp_b[i], edge_a[i], edge_b[i]
        rows = jnp.concatenate(
            [
                sub_a[i],
                sub_b[i],
                low[:NIG],
                high[:NIG],
                low[NIG:split] + first[:NED],
                high[NIG:split] + first[NED:],
                low[split:] + second[:NED],
                high[split:] + second[NED:],
                jnp.zeros((2 * LANES - NIF, LANES), F32),
            ],
            axis=0,
        )
        first, second = split_two(rows)
        received[0, :, i * LANES : (i + 1) * LANES] = first
        received[1, :, i * LANES : (i + 1) * LANES] = second
    scale = inverse_volume[...]
    for i in range(0, COMPS, 2):
        cols = slice(i * LANES, (i + 2) * LANES)
        added = dot(placing[...], received[0, :, cols]) + dot(placing[...], received[1, :, cols])
        out[i] = ((partial[i] + added[:, :LANES]) * scale).astype(BF16)
        out[i + 1] = ((partial[i + 1] + added[:, LANES:]) * scale).astype(BF16)


def vmem(count):
    return [pl.BlockSpec(memory_space=pltpu.VMEM)] * count


def anywhere(count):
    return [pl.BlockSpec(memory_space=pl.ANY)] * count


def hbm(count):
    return [pl.BlockSpec(memory_space=pltpu.HBM)] * count


def array(shape, dtype=F32):
    return jax.ShapeDtypeStruct(shape, dtype)


def call(kernel, name, out_shape, in_specs, scratch=(), flops=0, moved=0):
    return pl.pallas_call(
        kernel,
        name=name,
        out_shape=out_shape,
        in_specs=in_specs,
        out_specs=vmem(len(out_shape)),
        scratch_shapes=list(scratch),
        compiler_params=pltpu.CompilerParams(vmem_limit_bytes=VMEM_LIMIT),
        cost_estimate=pl.CostEstimate(flops=flops, bytes_accessed=moved, transcendentals=0),
    )


def exchange(block, axis, first):
    count = lax.axis_size(axis)
    pairs = []
    for i in range(first, count - 1, 2):
        pairs += [(i, i + 1), (i + 1, i)]
    return lax.ppermute(block, axis, pairs)


def in_hbm(*arrays):
    return [pltpu.with_memory_space_constraint(x, pltpu.HBM) for x in arrays]


def gather_near(coarse, ahead):
    (own,) = call(
        load_kernel,
        "load_own",
        (array(coarse.shape),),
        [pl.BlockSpec(memory_space=pltpu.HBM)],
        (pltpu.SemaphoreType.DMA,),
    )(*in_hbm(coarse))
    beyond = exchange(coarse, "sub", 1)
    beside = exchange(coarse, "sub", 0)
    parts = [own, beside, beyond]
    distance = lax.axis_size("grp") // 2
    while distance:
        rows = sum(x.shape[0] for x in parts)
        before, ahead = ahead[:1], ahead[1:]

        def join(*refs, skip=len(before)):
            join_kernel(*refs[: len(refs) - 1 - skip], refs[-1])

        (block,) = call(
            join,
            "join_blocks",
            (array((rows, parts[0].shape[1])),),
            vmem(len(parts)) + anywhere(len(before)),
        )(*parts, *before)
        pairs = [(i, i ^ distance) for i in range(lax.axis_size("grp"))]
        parts = [block, lax.ppermute(block, "grp", pairs)]
        distance //= 2
    return parts


def shards(
    coarse,
    corner_idx,
    coupling,
    force,
    panel_inv,
    panel_nodes,
    strain_disp,
    modulus,
    connect,
    interface,
    nodal_volume,
):
    nodes, _, cases = force.shape
    dofs = 3 * nodes
    q = corner_idx.shape[1]

    def lists(*refs):
        prepare_lists(coarse.shape[0], lax.axis_size("grp"), *refs)

    select, onehot, face, scaled, count, placing, inverse_volume = call(
        lists,
        "prepare_lists",
        (
            array((TERM, 3 * LANES), BF16),
            array((nodes, CORNERS * LANES), BF16),
            array((NIF, 2 * LANES), BF16),
            array((COMPS * 24, LANES)),
            array((nodes, 2 * LANES), BF16),
            array((nodes, 2 * LANES), BF16),
            array((nodes, LANES)),
        ),
        hbm(6),
        (
            pltpu.VMEM((1, q), jnp.int32),
            pltpu.VMEM(connect.shape, jnp.int32),
            pltpu.VMEM(interface.shape, jnp.int32),
            pltpu.VMEM(strain_disp.shape, BF16),
            pltpu.VMEM((1, LANES), F32),
            pltpu.VMEM((nodes // LANES, LANES), F32),
            pltpu.VMEM((8, 2 * LANES), F32),
            pltpu.SemaphoreType.DMA((6,)),
        ),
        flops=100000000,
        moved=4000000,
    )(
        *in_hbm(
            corner_idx,
            connect,
            interface,
            strain_disp,
            modulus.reshape(1, -1),
            nodal_volume.reshape(-1, LANES),
        )
    )
    inverse, coupled, loads, live = call(
        prepare_panels,
        "prepare_panels",
        (
            array(panel_inv.shape, BF16),
            array((dofs, LANES), BF16),
            array((dofs, cases)),
            array((dofs, LANES)),
        ),
        hbm(4),
        (
            pltpu.VMEM(panel_nodes.shape, jnp.int32),
            pltpu.VMEM((q, dofs), BF16),
            pltpu.VMEM((3, nodes, cases), BF16),
            pltpu.SemaphoreType.DMA((4,)),
        ),
        flops=100000000,
        moved=4000000,
    )(*in_hbm(panel_nodes, coupling.T, jnp.transpose(force, (1, 0, 2)), panel_inv))

    near = gather_near(coarse, [select, live])
    disp, stress, sub_a = call(
        solve_kernel,
        "solve_and_stress",
        (
            array((3, nodes, cases), BF16),
            array((COMPS * cases, 2 * LANES), BF16),
            array((COMPS, NIS, cases)),
        ),
        vmem(10),
        (
            pltpu.VMEM((3, 3 * LANES, cases), BF16),
            pltpu.VMEM((dofs, cases), F32),
            pltpu.VMEM((3 * cases, nodes), BF16),
            pltpu.VMEM((3, cases, CORNERS * LANES), F32),
        ),
        flops=1500000000,
        moved=4000000,
    )(*near, inverse, coupled, loads, live, select, onehot, face, scaled)
    from_sub_a = exchange(sub_a, "sub", 0)
    sub_b, grp_a, grp_b = call(
        face_kernel,
        "interface_rows",
        (
            array((COMPS, NIS, cases)),
            array((COMPS, NIG + 2 * NED, cases)),
            array((COMPS, NIG + 2 * NED, cases)),
        ),
        vmem(2),
        flops=100000000,
        moved=1000000,
    )(face, stress)
    from_grp_a = exchange(grp_a, "grp", 0)
    from_grp_b = exchange(grp_b, "grp", 1)
    edge_a, edge_b = call(
        edge_kernel,
        "sum_edges",
        (array((COMPS, 2 * NED, cases)), array((COMPS, 2 * NED, cases))),
        vmem(4) + anywhere(1),
    )(grp_a, grp_b, from_grp_a, from_grp_b, from_sub_a)
    from_sub_b = exchange(sub_b, "sub", 1)
    from_edge_b = exchange(edge_b, "sub", 1)
    from_edge_a = exchange(edge_a, "sub", 0)
    partial, disp = call(
        partial_kernel,
        "assemble_nodes",
        (array((COMPS, nodes, cases)), array(disp.shape, BF16)),
        vmem(3),
        flops=400000000,
        moved=2000000,
    )(count, stress, disp)
    (nodal,) = call(
        finish_kernel,
        "add_received",
        (array((COMPS, nodes, cases), BF16),),
        vmem(9),
        (pltpu.VMEM((2, 2 * LANES, COMPS * cases), BF16),),
        flops=800000000,
        moved=3000000,
    )(
        placing,
        partial,
        inverse_volume,
        from_sub_a,
        from_sub_b,
        from_grp_a,
        from_grp_b,
        from_edge_a,
        from_edge_b,
    )
    return jnp.transpose(disp, (1, 0, 2)), jnp.transpose(nodal, (1, 0, 2))


def solution(mesh):
    owner = ("sub", "grp")
    placed = (
        P(owner, None),
        P(owner, None),
        P(owner, None),
        P(owner, None, None),
        P(owner, None, None),
        P(owner, None),
        P(None, None, owner),
        P(owner),
        P(None, owner),
        P(owner, None),
        P(owner),
    )
    return jax.shard_map(
        shards,
        mesh=mesh,
        in_specs=placed,
        out_specs=(P(owner, None, None), P(owner, None, None)),
        check_vma=False,
    )
```

```python
import jax
import jax.numpy as jnp
from jax import lax
from jax.experimental import pallas as pl
from jax.experimental.pallas import tpu as pltpu
from jax.sharding import PartitionSpec as P

NIS = 64
NIG = 32
NED = 8
EDGES = 2 * NIS + 2 * NIG
NIF = EDGES + 4 * NED
CORNERS = 8
COMPS = 6
LANES = 128
TERM = 32

POISSON = 0.3
LAME = POISSON / ((1.0 + POISSON) * (1.0 - 2.0 * POISSON))
SHEAR = 0.5 / (1.0 + POISSON)

F32 = jnp.float32
BF16 = jnp.bfloat16
VMEM_LIMIT = 24 * 1024 * 1024


def split_two(x):
    high = x.astype(BF16)
    return high, (x - high.astype(F32)).astype(BF16)


def dot(a, b):
    return jnp.dot(a, b, preferred_element_type=F32)


def dot_nt(a, b):
    return lax.dot_general(a, b, (((1,), (1,)), ((), ())), preferred_element_type=F32)


def column(row):
    return jnp.broadcast_to(row, (LANES, LANES)).T


def swap_lanes(x, distance):
    lane = lax.broadcasted_iota(jnp.int32, x.shape, 1)
    after = pltpu.roll(x, LANES - distance, 1)
    before = pltpu.roll(x, distance, 1)
    return jnp.where((lane & distance) == 0, after, before)


def order_lists(ids):
    sub_even = (lax.axis_index("sub") & 1) == 0
    grp_even = (lax.axis_index("grp") & 1) == 0
    first, second = ids[:, :LANES], ids[:, LANES:]
    ids[:, :LANES] = jnp.where(sub_even, swap_lanes(first, NIS), first)
    lane = lax.broadcasted_iota(jnp.int32, second.shape, 1)
    groups = jnp.where(grp_even, swap_lanes(second, NIG), second)
    edges = jnp.where(sub_even, swap_lanes(second, 2 * NED), second)
    edges = jnp.where(grp_even, swap_lanes(edges, NED), edges)
    ids[:, LANES:] = jnp.where(lane < 2 * NIG, groups, edges)


def start_copies(pairs, sems):
    copies = [pltpu.make_async_copy(src, dst, sems.at[k]) for k, (src, dst) in enumerate(pairs)]
    for copy in copies:
        copy.start()
    return copies


def prepare_lists(
    block_rows,
    members,
    corner_idx,
    connect,
    interface,
    strain_disp,
    modulus,
    volume,
    coarse,
    own,
    select,
    onehot,
    face,
    scaled,
    count,
    placing,
    placing_last,
    inverse_volume,
    corner_v,
    connect_v,
    interface_v,
    strain_v,
    modulus_v,
    volume_v,
    ids,
    sems,
):
    copies = start_copies(
        [
            (connect, connect_v),
            (interface, interface_v),
            (corner_idx, corner_v),
            (modulus, modulus_v),
            (strain_disp, strain_v),
            (volume, volume_v),
            (coarse, own),
        ],
        sems,
    )
    nodes = onehot.shape[0]
    q = corner_idx.shape[1]

    copies[0].wait()
    node_of = lax.broadcasted_iota(jnp.int32, (nodes, LANES), 0)
    total = jnp.zeros((nodes, LANES), F32)
    for a in range(CORNERS):
        hit = jnp.where(connect_v[a : a + 1, :] == node_of, 1.0, 0.0)
        onehot[:, a * LANES : (a + 1) * LANES] = hit.astype(BF16)
        total = total + hit
    total = total.astype(BF16)
    count[:, :LANES] = total
    count[:, LANES:] = total

    copies[1].wait()
    ids[...] = jnp.full(ids.shape, -1.0, F32)
    ids[0:1, 0:NIF] = interface_v[...].astype(F32)
    order_lists(ids)
    node_of = lax.broadcasted_iota(jnp.int32, (nodes, 2 * LANES), 0)
    placing[...] = jnp.where(ids[0:1, :].astype(jnp.int32) == node_of, 1.0, 0.0).astype(BF16)
    lane = lax.broadcasted_iota(jnp.int32, (8, LANES), 1)
    faces = pltpu.roll(ids[:, :LANES], NIS, 1)
    late = jnp.where(lane < NIS, faces, jnp.where(lane < NIS + 4 * NED, ids[:, LANES:], -1.0))
    hit = jnp.where(late[0:1, :].astype(jnp.int32) == node_of[:, :LANES], 1.0, 0.0).astype(BF16)
    placing_last[:, :LANES] = hit
    placing_last[:, LANES:] = hit
    connect_f = connect_v[...].astype(F32)
    for half in range(2):
        id_col = column(ids[0:1, half * LANES : (half + 1) * LANES])
        rows = jnp.zeros((LANES, LANES), F32)
        for a in range(CORNERS):
            rows = rows + jnp.where(connect_f[a : a + 1, :] == id_col, 1.0, 0.0)
        rows = rows.astype(BF16)[: min(LANES, NIF - half * LANES)]
        face[half * LANES : half * LANES + rows.shape[0], :LANES] = rows
        face[half * LANES : half * LANES + rows.shape[0], LANES:] = rows

    copies[2].wait()
    ids[0:1, 0:q] = corner_v[...].astype(F32)
    wanted = column(ids[0:1, :LANES])[:TERM]
    lane = lax.broadcasted_iota(jnp.int32, (TERM, 3 * LANES), 1)
    entry = lax.broadcasted_iota(jnp.int32, (TERM, LANES), 0)
    s, g = lax.axis_index("sub"), lax.axis_index("grp")
    aside = 1 - 2 * (s & 1)
    row = jnp.full((TERM, 3 * LANES), -1, jnp.int32)
    base = 0
    for member in range(members):
        distance, bits, turn = members // 2, member, 0
        while distance:
            turn += (bits & 1) * distance
            distance, bits = distance // 2, bits >> 1
        for owner in (s, s + aside, s - aside):
            first = (owner * members + (g ^ turn)) * block_rows
            row = jnp.where((lane >= base) & (lane < base + block_rows), first - base + lane, row)
            base += block_rows
    for b in range(3):
        cols = slice(b * LANES, (b + 1) * LANES)
        hit = (wanted == row[:, cols].astype(F32)) & (entry < q)
        select[:, cols] = jnp.where(hit, 1.0, 0.0).astype(BF16)

    copies[3].wait()
    copies[4].wait()
    factor = modulus_v[...]
    rows = [strain_v[i].astype(F32) for i in range(COMPS)]
    trace = (rows[0] + rows[1] + rows[2]) * LAME
    for i in range(COMPS):
        value = trace + rows[i] * (2.0 * SHEAR) if i < 3 else rows[i] * SHEAR
        scaled[24 * i : 24 * (i + 1)] = jnp.broadcast_to((value * factor)[:, None, :], (24, 8, LANES))

    copies[5].wait()
    for k in range(nodes // LANES):
        inverse_volume[k * LANES : (k + 1) * LANES, :] = column(1.0 / volume_v[k : k + 1, :])
    copies[6].wait()


def prepare_panels(
    panel_nodes,
    coupling,
    force,
    panel_inv,
    inverse,
    coupled,
    loads,
    live,
    panel_v,
    coupling_v,
    force_v,
    sems,
):
    copies = start_copies(
        [
            (panel_nodes, panel_v),
            (coupling, coupling_v),
            (force, force_v),
            (panel_inv, inverse),
        ],
        sems,
    )
    panels, panel_rows, _ = inverse.shape
    nodes = force_v.shape[1]
    q = coupling_v.shape[0]

    copies[0].wait()
    row_of = lax.broadcasted_iota(jnp.int32, (panel_rows, LANES), 0)
    for p in range(panels):
        alive = row_of < 3 * panel_v[0:1, p : p + 1]
        live[p * panel_rows : (p + 1) * panel_rows, :] = jnp.where(alive, 1.0, 0.0)

    copies[1].wait()
    for k in range(coupling_v.shape[1] // LANES):
        part = coupling_v[:, k * LANES : (k + 1) * LANES].astype(F32)
        gap = jnp.zeros((TERM - q, LANES), F32)
        stack = jnp.concatenate([part, gap] * 3 + [jnp.zeros((LANES - 3 * TERM, LANES), F32)], axis=0)
        rows = slice(k * LANES, (k + 1) * LANES)
        coupled[rows, :] = (stack.T * live[rows, :]).astype(BF16)

    copies[2].wait()
    for c in range(3):
        loads[pl.ds(c, nodes, stride=3), :] = force_v[c].astype(F32)
    loads[...] = loads[...] * live[...]
    copies[3].wait()


def join_kernel(*refs):
    *parts, out = refs
    start = 0
    for part in parts:
        out[start : start + part.shape[0], :] = part[...]
        start += part.shape[0]


def solve_kernel(
    near,
    across,
    inverse,
    coupled,
    loads,
    live,
    select,
    onehot,
    face,
    scaled,
    disp,
    stress,
    sub_a,
    sub_b,
    grp_a,
    grp_b,
    terms,
    solved,
    disp_t,
    elem_t,
):
    panels, panel_rows, _ = inverse.shape
    panel_size = panel_rows // 3
    rows = near.shape[0]

    terms[:, 2 * rows :, :] = jnp.zeros((3, terms.shape[1] - 2 * rows, terms.shape[2]), BF16)
    for b, block in enumerate((near, across)):
        x = block[...]
        high = x.astype(BF16)
        rest = x - high.astype(F32)
        middle = rest.astype(BF16)
        low = (rest - middle.astype(F32)).astype(BF16)
        for t, value in enumerate((high, middle, low)):
            terms[t, b * rows : (b + 1) * rows, :] = value
    picked = [dot(select[...], terms[t]) for t in range(3)]
    picked.append(jnp.zeros((LANES - 3 * TERM, LANES), F32))
    values = jnp.concatenate(picked, axis=0).astype(BF16)

    for p in range(panels):
        start = p * panel_rows
        span = slice(start, start + panel_rows)
        reduced = (loads[span, :] - dot(coupled[span, :], values)).astype(BF16)
        solved[span, :] = dot(inverse[p], reduced) * live[span, :]
        for c in range(3):
            part = solved[pl.ds(start + c, panel_size, stride=3), :].astype(BF16)
            disp[c, p * panel_size : (p + 1) * panel_size, :] = part
            disp_t[c * LANES : (c + 1) * LANES, p * panel_size : (p + 1) * panel_size] = (
                part.astype(F32).T.astype(BF16)
            )

    elem_t[...] = dot(disp_t[...], onehot[...])
    step = 32
    for start in range(0, LANES, step):
        sums = [None] * COMPS
        for a in range(CORNERS):
            for c in range(3):
                x = elem_t[c * LANES + start : c * LANES + start + step, a * LANES : (a + 1) * LANES]
                x = x.reshape(step // 8, 8, LANES)
                for i in range(COMPS):
                    term = scaled[24 * i + 3 * a + c] * x
                    sums[i] = term if sums[i] is None else sums[i] + term
        sums = [x.reshape(step, LANES) for x in sums]
        for i in range(COMPS):
            high, low = split_two(sums[i])
            stress[i * LANES + start : i * LANES + start + step, 0:LANES] = high
            stress[i * LANES + start : i * LANES + start + step, LANES : 2 * LANES] = low

    rows = dot_nt(face[...], stress[...])
    for i in range(COMPS):
        part = rows[:, i * LANES : (i + 1) * LANES]
        edge = [part[EDGES + NED * k : EDGES + NED * (k + 1)] for k in range(4)]
        sub_a[i] = part[:NIS]
        sub_b[i] = part[NIS : 2 * NIS]
        grp_a[i] = jnp.concatenate([part[2 * NIS : 2 * NIS + NIG], edge[0], edge[2]], axis=0)
        grp_b[i] = jnp.concatenate([part[2 * NIS + NIG : EDGES], edge[1], edge[3]], axis=0)


def edge_kernel(grp_a, grp_b, from_a, from_b, _, edge_b, edge_a):
    split = NIG + NED
    edge_a[:, :NED, :] = grp_a[:, NIG:split, :] + from_a[:, NIG:split, :]
    edge_a[:, NED:, :] = grp_b[:, NIG:split, :] + from_b[:, NIG:split, :]
    edge_b[:, :NED, :] = grp_a[:, split:, :] + from_a[:, split:, :]
    edge_b[:, NED:, :] = grp_b[:, split:, :] + from_b[:, split:, :]


def partial_kernel(
    count, stress, disp, placing, sub_a, grp_a, grp_b, partial, disp_out, received
):
    disp_out[...] = disp[...]
    split = NIG + NED
    gap = jnp.zeros((NIS, LANES), F32)
    for i in range(COMPS):
        low, high = grp_a[i], grp_b[i]
        rows = [sub_a[i], gap, low[:NIG], high[:NIG], low[NIG:split], high[NIG:split], low[split:], high[split:]]
        rows.append(jnp.zeros((2 * LANES - NIF, LANES), F32))
        first, second = split_two(jnp.concatenate(rows, axis=0))
        received[: 2 * LANES, i * LANES : (i + 1) * LANES] = first
        received[2 * LANES :, i * LANES : (i + 1) * LANES] = second
    for i in range(0, COMPS, 2):
        cols = slice(i * LANES, (i + 2) * LANES)
        own = dot_nt(count[...], stress[cols, :])
        added = dot(placing[...], received[: 2 * LANES, cols]) + dot(placing[...], received[2 * LANES :, cols])
        total = own + added
        partial[i] = total[:, :LANES]
        partial[i + 1] = total[:, LANES:]


def finish_kernel(placing, partial, inverse_volume, sub_b, edge_b, edge_a, out, received, nodal, sems):
    rows = NIS + 4 * NED
    for i in range(COMPS):
        cols = slice(i * LANES, (i + 1) * LANES)
        parts = jnp.concatenate([sub_b[i], edge_a[i], edge_b[i], jnp.zeros((LANES - rows, LANES), F32)], axis=0)
        first, second = split_two(parts)
        received[:LANES, cols] = first
        received[LANES:, cols] = second
    scale = inverse_volume[...]
    copies = []
    for i in range(0, COMPS, 2):
        added = dot(placing[...], received[:, i * LANES : (i + 2) * LANES])
        nodal[i] = ((partial[i] + added[:, :LANES]) * scale).astype(BF16)
        nodal[i + 1] = ((partial[i + 1] + added[:, LANES:]) * scale).astype(BF16)
        copy = pltpu.make_async_copy(nodal.at[pl.ds(i, 2)], out.at[pl.ds(i, 2)], sems.at[i // 2])
        copy.start()
        copies.append(copy)
    for copy in copies:
        copy.wait()


def vmem(count):
    return [pl.BlockSpec(memory_space=pltpu.VMEM)] * count


def anywhere(count):
    return [pl.BlockSpec(memory_space=pl.ANY)] * count


def hbm(count):
    return [pl.BlockSpec(memory_space=pltpu.HBM)] * count


def array(shape, dtype=F32):
    return jax.ShapeDtypeStruct(shape, dtype)


def call(kernel, name, out_shape, in_specs, scratch=(), flops=0, moved=0, out_specs=None):
    return pl.pallas_call(
        kernel,
        name=name,
        out_shape=out_shape,
        in_specs=in_specs,
        out_specs=out_specs or vmem(len(out_shape)),
        scratch_shapes=list(scratch),
        compiler_params=pltpu.CompilerParams(vmem_limit_bytes=VMEM_LIMIT),
        cost_estimate=pl.CostEstimate(flops=flops, bytes_accessed=moved, transcendentals=0),
    )


def exchange(block, axis, first):
    count = lax.axis_size(axis)
    pairs = []
    for i in range(first, count - 1, 2):
        pairs += [(i, i + 1), (i + 1, i)]
    return lax.ppermute(block, axis, pairs)


def in_hbm(*arrays):
    return [pltpu.with_memory_space_constraint(x, pltpu.HBM) for x in arrays]


def gather_near(coarse, own, ahead):
    beyond = exchange(coarse, "sub", 1)
    beside = exchange(coarse, "sub", 0)
    parts = [own, beside, beyond]
    distance = lax.axis_size("grp") // 2
    while distance:
        rows = sum(x.shape[0] for x in parts)
        before, ahead = ahead[:1], ahead[1:]

        def join(*refs, skip=len(before)):
            join_kernel(*refs[: len(refs) - 1 - skip], refs[-1])

        (block,) = call(
            join,
            "join_blocks",
            (array((rows, parts[0].shape[1])),),
            vmem(len(parts)) + anywhere(len(before)),
        )(*parts, *before)
        pairs = [(i, i ^ distance) for i in range(lax.axis_size("grp"))]
        parts = [block, lax.ppermute(block, "grp", pairs)]
        distance //= 2
    return parts


def shards(
    coarse,
    corner_idx,
    coupling,
    force,
    panel_inv,
    panel_nodes,
    strain_disp,
    modulus,
    connect,
    interface,
    nodal_volume,
):
    nodes, _, cases = force.shape
    dofs = 3 * nodes
    q = corner_idx.shape[1]

    def lists(*refs):
        prepare_lists(coarse.shape[0], lax.axis_size("grp"), *refs)

    own, select, onehot, face, scaled, count, placing, placing_last, inverse_volume = call(
        lists,
        "prepare_lists",
        (
            array(coarse.shape),
            array((TERM, 3 * LANES), BF16),
            array((nodes, CORNERS * LANES), BF16),
            array((NIF, 2 * LANES), BF16),
            array((COMPS * 24, 8, LANES)),
            array((nodes, 2 * LANES), BF16),
            array((nodes, 2 * LANES), BF16),
            array((nodes, 2 * LANES), BF16),
            array((nodes, LANES)),
        ),
        hbm(7),
        (
            pltpu.VMEM((1, q), jnp.int32),
            pltpu.VMEM(connect.shape, jnp.int32),
            pltpu.VMEM(interface.shape, jnp.int32),
            pltpu.VMEM(strain_disp.shape, BF16),
            pltpu.VMEM((1, LANES), F32),
            pltpu.VMEM((nodes // LANES, LANES), F32),
            pltpu.VMEM((8, 2 * LANES), F32),
            pltpu.SemaphoreType.DMA((7,)),
        ),
        flops=100000000,
        moved=4000000,
    )(
        *in_hbm(
            corner_idx,
            connect,
            interface,
            strain_disp,
            modulus.reshape(1, -1),
            nodal_volume.reshape(-1, LANES),
            coarse,
        )
    )
    inverse, coupled, loads, live = call(
        prepare_panels,
        "prepare_panels",
        (
            array(panel_inv.shape, BF16),
            array((dofs, LANES), BF16),
            array((dofs, cases)),
            array((dofs, LANES)),
        ),
        hbm(4),
        (
            pltpu.VMEM(panel_nodes.shape, jnp.int32),
            pltpu.VMEM((q, dofs), BF16),
            pltpu.VMEM((3, nodes, cases), BF16),
            pltpu.SemaphoreType.DMA((4,)),
        ),
        flops=100000000,
        moved=4000000,
    )(*in_hbm(panel_nodes, coupling.T, jnp.transpose(force, (1, 0, 2)), panel_inv))

    near = gather_near(coarse, own, [select, live])
    disp, stress, sub_a, sub_b, grp_a, grp_b = call(
        solve_kernel,
        "solve_and_stress",
        (
            array((3, nodes, cases), BF16),
            array((COMPS * cases, 2 * LANES), BF16),
            array((COMPS, NIS, cases)),
            array((COMPS, NIS, cases)),
            array((COMPS, NIG + 2 * NED, cases)),
            array((COMPS, NIG + 2 * NED, cases)),
        ),
        vmem(10),
        (
            pltpu.VMEM((3, 3 * LANES, cases), BF16),
            pltpu.VMEM((dofs, cases), F32),
            pltpu.VMEM((3 * cases, nodes), BF16),
            pltpu.VMEM((3 * cases, CORNERS * LANES), F32),
        ),
        flops=1500000000,
        moved=4000000,
    )(*near, inverse, coupled, loads, live, select, onehot, face, scaled)
    from_sub_a = exchange(sub_a, "sub", 0)
    from_grp_a = exchange(grp_a, "grp", 0)
    from_grp_b = exchange(grp_b, "grp", 1)
    edge_b, edge_a = call(
        edge_kernel,
        "sum_edges",
        (array((COMPS, 2 * NED, cases)), array((COMPS, 2 * NED, cases))),
        vmem(4) + anywhere(1),
    )(grp_a, grp_b, from_grp_a, from_grp_b, from_sub_a)
    from_sub_b = exchange(sub_b, "sub", 1)
    from_edge_b = exchange(edge_b, "sub", 1)
    from_edge_a = exchange(edge_a, "sub", 0)
    partial, disp = call(
        partial_kernel,
        "assemble_nodes",
        (array((COMPS, nodes, cases)), array(disp.shape, BF16)),
        vmem(7),
        (pltpu.VMEM((4 * LANES, COMPS * cases), BF16),),
        flops=400000000,
        moved=2000000,
    )(count, stress, disp, placing, from_sub_a, from_grp_a, from_grp_b)
    (nodal,) = call(
        finish_kernel,
        "add_last",
        (array((COMPS, nodes, cases), BF16),),
        vmem(6),
        (
            pltpu.VMEM((2 * LANES, COMPS * cases), BF16),
            pltpu.VMEM((COMPS, nodes, cases), BF16),
            pltpu.SemaphoreType.DMA((COMPS // 2,)),
        ),
        flops=400000000,
        moved=3000000,
        out_specs=hbm(1),
    )(placing_last, partial, inverse_volume, from_sub_b, from_edge_b, from_edge_a)
    return jnp.transpose(disp, (1, 0, 2)), jnp.transpose(nodal, (1, 0, 2))


def solution(mesh):
    owner = ("sub", "grp")
    placed = (
        P(owner, None),
        P(owner, None),
        P(owner, None),
        P(owner, None, None),
        P(owner, None, None),
        P(owner, None),
        P(None, None, owner),
        P(owner),
        P(None, owner),
        P(owner, None),
        P(owner),
    )
    return jax.shard_map(
        shards,
        mesh=mesh,
        in_specs=placed,
        out_specs=(P(owner, None, None), P(owner, None, None)),
        check_vma=False,
    )
```

```python
import jax
import jax.numpy as jnp
from jax import lax
from jax.experimental import pallas as pl
from jax.experimental.pallas import tpu as pltpu
from jax.sharding import PartitionSpec as P

NIS = 64
NIG = 32
NED = 8
EDGES = 2 * NIS + 2 * NIG
NIF = EDGES + 4 * NED
CORNERS = 8
COMPS = 6
LANES = 128
TERM = 32

POISSON = 0.3
LAME = POISSON / ((1.0 + POISSON) * (1.0 - 2.0 * POISSON))
SHEAR = 0.5 / (1.0 + POISSON)

F32 = jnp.float32
BF16 = jnp.bfloat16
VMEM_LIMIT = 24 * 1024 * 1024


def split_two(x):
    high = x.astype(BF16)
    return high, (x - high.astype(F32)).astype(BF16)


def dot(a, b):
    return jnp.dot(a, b, preferred_element_type=F32)


def dot_nt(a, b):
    return lax.dot_general(a, b, (((1,), (1,)), ((), ())), preferred_element_type=F32)


def column(row):
    return jnp.broadcast_to(row, (LANES, LANES)).T


def swap_lanes(x, distance):
    lane = lax.broadcasted_iota(jnp.int32, x.shape, 1)
    after = pltpu.roll(x, LANES - distance, 1)
    before = pltpu.roll(x, distance, 1)
    return jnp.where((lane & distance) == 0, after, before)


def order_lists(ids):
    sub_even = (lax.axis_index("sub") & 1) == 0
    grp_even = (lax.axis_index("grp") & 1) == 0
    first, second = ids[:, :LANES], ids[:, LANES:]
    ids[:, :LANES] = jnp.where(sub_even, swap_lanes(first, NIS), first)
    lane = lax.broadcasted_iota(jnp.int32, second.shape, 1)
    groups = jnp.where(grp_even, swap_lanes(second, NIG), second)
    edges = jnp.where(sub_even, swap_lanes(second, 2 * NED), second)
    edges = jnp.where(grp_even, swap_lanes(edges, NED), edges)
    ids[:, LANES:] = jnp.where(lane < 2 * NIG, groups, edges)


def start_copies(pairs, sems):
    copies = [pltpu.make_async_copy(src, dst, sems.at[k]) for k, (src, dst) in enumerate(pairs)]
    for copy in copies:
        copy.start()
    return copies


def prepare_lists(
    block_rows,
    members,
    corner_idx,
    connect,
    interface,
    strain_disp,
    modulus,
    volume,
    coarse,
    own,
    select,
    onehot,
    face,
    scaled,
    count,
    placing,
    placing_last,
    inverse_volume,
    corner_v,
    connect_v,
    interface_v,
    strain_v,
    modulus_v,
    volume_v,
    ids,
    sems,
):
    copies = start_copies(
        [
            (connect, connect_v),
            (interface, interface_v),
            (corner_idx, corner_v),
            (modulus, modulus_v),
            (strain_disp, strain_v),
            (volume, volume_v),
            (coarse, own),
        ],
        sems,
    )
    nodes = onehot.shape[0]
    q = corner_idx.shape[1]

    copies[0].wait()
    node_of = lax.broadcasted_iota(jnp.int32, (nodes, LANES), 0)
    total = jnp.zeros((nodes, LANES), F32)
    for a in range(CORNERS):
        hit = jnp.where(connect_v[a : a + 1, :] == node_of, 1.0, 0.0)
        onehot[:, a * LANES : (a + 1) * LANES] = hit.astype(BF16)
        total = total + hit
    total = total.astype(BF16)
    count[:, :LANES] = total
    count[:, LANES:] = total

    copies[1].wait()
    ids[...] = jnp.full(ids.shape, -1.0, F32)
    ids[0:1, 0:NIF] = interface_v[...].astype(F32)
    order_lists(ids)
    node_of = lax.broadcasted_iota(jnp.int32, (nodes, 2 * LANES), 0)
    placing[...] = jnp.where(ids[0:1, :].astype(jnp.int32) == node_of, 1.0, 0.0).astype(BF16)
    lane = lax.broadcasted_iota(jnp.int32, (8, LANES), 1)
    faces = pltpu.roll(ids[:, :LANES], NIS, 1)
    late = jnp.where(lane < NIS, faces, jnp.where(lane < NIS + 4 * NED, ids[:, LANES:], -1.0))
    hit = jnp.where(late[0:1, :].astype(jnp.int32) == node_of[:, :LANES], 1.0, 0.0).astype(BF16)
    placing_last[:, :LANES] = hit
    placing_last[:, LANES:] = hit
    connect_f = connect_v[...].astype(F32)
    for half in range(2):
        id_col = column(ids[0:1, half * LANES : (half + 1) * LANES])
        rows = jnp.zeros((LANES, LANES), F32)
        for a in range(CORNERS):
            rows = rows + jnp.where(connect_f[a : a + 1, :] == id_col, 1.0, 0.0)
        rows = rows.astype(BF16)[: min(LANES, NIF - half * LANES)]
        face[half * LANES : half * LANES + rows.shape[0], :LANES] = rows
        face[half * LANES : half * LANES + rows.shape[0], LANES:] = rows

    copies[2].wait()
    ids[0:1, 0:q] = corner_v[...].astype(F32)
    wanted = column(ids[0:1, :LANES])[:TERM]
    lane = lax.broadcasted_iota(jnp.int32, (TERM, 3 * LANES), 1)
    entry = lax.broadcasted_iota(jnp.int32, (TERM, LANES), 0)
    s, g = lax.axis_index("sub"), lax.axis_index("grp")
    aside = 1 - 2 * (s & 1)
    row = jnp.full((TERM, 3 * LANES), -1, jnp.int32)
    base = 0
    for member in range(members):
        distance, bits, turn = members // 2, member, 0
        while distance:
            turn += (bits & 1) * distance
            distance, bits = distance // 2, bits >> 1
        for owner in (s, s + aside, s - aside):
            first = (owner * members + (g ^ turn)) * block_rows
            row = jnp.where((lane >= base) & (lane < base + block_rows), first - base + lane, row)
            base += block_rows
    for b in range(3):
        cols = slice(b * LANES, (b + 1) * LANES)
        hit = (wanted == row[:, cols].astype(F32)) & (entry < q)
        select[:, cols] = jnp.where(hit, 1.0, 0.0).astype(BF16)

    copies[3].wait()
    copies[4].wait()
    factor = modulus_v[...]
    rows = [strain_v[i].astype(F32) for i in range(COMPS)]
    trace = (rows[0] + rows[1] + rows[2]) * LAME
    for i in range(COMPS):
        value = trace + rows[i] * (2.0 * SHEAR) if i < 3 else rows[i] * SHEAR
        scaled[24 * i : 24 * (i + 1)] = jnp.broadcast_to((value * factor)[:, None, :], (24, 8, LANES))

    copies[5].wait()
    for k in range(nodes // LANES):
        inverse_volume[k * LANES : (k + 1) * LANES, :] = column(1.0 / volume_v[k : k + 1, :])
    copies[6].wait()


def prepare_panels(
    panel_nodes,
    coupling,
    force,
    panel_inv,
    inverse,
    coupled,
    loads,
    live,
    panel_v,
    coupling_v,
    force_v,
    sems,
):
    copies = start_copies(
        [
            (panel_nodes, panel_v),
            (coupling, coupling_v),
            (force, force_v),
            (panel_inv, inverse),
        ],
        sems,
    )
    panels, panel_rows, _ = inverse.shape
    nodes = force_v.shape[1]
    q = coupling_v.shape[0]

    copies[0].wait()
    row_of = lax.broadcasted_iota(jnp.int32, (panel_rows, LANES), 0)
    for p in range(panels):
        alive = row_of < 3 * panel_v[0:1, p : p + 1]
        live[p * panel_rows : (p + 1) * panel_rows, :] = jnp.where(alive, 1.0, 0.0)

    copies[1].wait()
    for k in range(coupling_v.shape[1] // LANES):
        part = coupling_v[:, k * LANES : (k + 1) * LANES].astype(F32)
        gap = jnp.zeros((TERM - q, LANES), F32)
        stack = jnp.concatenate([part, gap] * 3 + [jnp.zeros((LANES - 3 * TERM, LANES), F32)], axis=0)
        rows = slice(k * LANES, (k + 1) * LANES)
        coupled[rows, :] = (stack.T * live[rows, :]).astype(BF16)

    copies[2].wait()
    for c in range(3):
        loads[pl.ds(c, nodes, stride=3), :] = force_v[c].astype(F32)
    loads[...] = loads[...] * live[...]
    copies[3].wait()


def join_kernel(*refs):
    *parts, out = refs
    start = 0
    for part in parts:
        out[start : start + part.shape[0], :] = part[...]
        start += part.shape[0]


def solve_kernel(
    near,
    across,
    inverse,
    coupled,
    loads,
    live,
    select,
    onehot,
    face,
    scaled,
    disp,
    stress,
    sub_a,
    sub_b,
    grp_a,
    grp_b,
    terms,
    solved,
    disp_t,
    elem_t,
):
    panels, panel_rows, _ = inverse.shape
    panel_size = panel_rows // 3
    rows = near.shape[0]

    terms[:, 2 * rows :, :] = jnp.zeros((3, terms.shape[1] - 2 * rows, terms.shape[2]), BF16)
    for b, block in enumerate((near, across)):
        x = block[...]
        high = x.astype(BF16)
        rest = x - high.astype(F32)
        middle = rest.astype(BF16)
        low = (rest - middle.astype(F32)).astype(BF16)
        for t, value in enumerate((high, middle, low)):
            terms[t, b * rows : (b + 1) * rows, :] = value
    picked = [dot(select[...], terms[t]) for t in range(3)]
    picked.append(jnp.zeros((LANES - 3 * TERM, LANES), F32))
    values = jnp.concatenate(picked, axis=0).astype(BF16)

    for p in range(panels):
        start = p * panel_rows
        span = slice(start, start + panel_rows)
        reduced = (loads[span, :] - dot(coupled[span, :], values)).astype(BF16)
        solved[span, :] = dot(inverse[p], reduced) * live[span, :]
        for c in range(3):
            part = solved[pl.ds(start + c, panel_size, stride=3), :].astype(BF16)
            disp[c, p * panel_size : (p + 1) * panel_size, :] = part
            disp_t[c * LANES : (c + 1) * LANES, p * panel_size : (p + 1) * panel_size] = (
                part.astype(F32).T.astype(BF16)
            )

    elem_t[...] = dot(disp_t[...], onehot[...])
    step = 32
    for start in range(0, LANES, step):
        sums = [None] * COMPS
        for a in range(CORNERS):
            for c in range(3):
                x = elem_t[c * LANES + start : c * LANES + start + step, a * LANES : (a + 1) * LANES]
                x = x.reshape(step // 8, 8, LANES)
                for i in range(COMPS):
                    term = scaled[24 * i + 3 * a + c] * x
                    sums[i] = term if sums[i] is None else sums[i] + term
        sums = [x.reshape(step, LANES) for x in sums]
        for i in range(COMPS):
            high, low = split_two(sums[i])
            stress[i * LANES + start : i * LANES + start + step, 0:LANES] = high
            stress[i * LANES + start : i * LANES + start + step, LANES : 2 * LANES] = low

    rows = dot_nt(face[...], stress[...])
    for i in range(COMPS):
        part = rows[:, i * LANES : (i + 1) * LANES]
        edge = [part[EDGES + NED * k : EDGES + NED * (k + 1)] for k in range(4)]
        sub_a[i] = part[:NIS]
        sub_b[i] = part[NIS : 2 * NIS]
        grp_a[i] = jnp.concatenate([part[2 * NIS : 2 * NIS + NIG], edge[0], edge[2]], axis=0)
        grp_b[i] = jnp.concatenate([part[2 * NIS + NIG : EDGES], edge[1], edge[3]], axis=0)


def edge_kernel(grp_a, grp_b, from_a, from_b, edge_b, edge_a):
    split = NIG + NED
    edge_a[:, :NED, :] = grp_a[:, NIG:split, :] + from_a[:, NIG:split, :]
    edge_a[:, NED:, :] = grp_b[:, NIG:split, :] + from_b[:, NIG:split, :]
    edge_b[:, :NED, :] = grp_a[:, split:, :] + from_a[:, split:, :]
    edge_b[:, NED:, :] = grp_b[:, split:, :] + from_b[:, split:, :]


def partial_kernel(
    count, stress, disp, placing, sub_a, grp_a, grp_b, partial, disp_out, received
):
    disp_out[...] = disp[...]
    split = NIG + NED
    gap = jnp.zeros((NIS, LANES), F32)
    for i in range(COMPS):
        low, high = grp_a[i], grp_b[i]
        rows = [sub_a[i], gap, low[:NIG], high[:NIG], low[NIG:split], high[NIG:split], low[split:], high[split:]]
        rows.append(jnp.zeros((2 * LANES - NIF, LANES), F32))
        first, second = split_two(jnp.concatenate(rows, axis=0))
        received[: 2 * LANES, i * LANES : (i + 1) * LANES] = first
        received[2 * LANES :, i * LANES : (i + 1) * LANES] = second
    for i in range(0, COMPS, 2):
        cols = slice(i * LANES, (i + 2) * LANES)
        own = dot_nt(count[...], stress[cols, :])
        added = dot(placing[...], received[: 2 * LANES, cols]) + dot(placing[...], received[2 * LANES :, cols])
        total = own + added
        partial[i] = total[:, :LANES]
        partial[i + 1] = total[:, LANES:]


def finish_kernel(placing, partial, inverse_volume, sub_b, edge_b, edge_a, out, received, nodal, sems):
    rows = NIS + 4 * NED
    for i in range(COMPS):
        cols = slice(i * LANES, (i + 1) * LANES)
        parts = jnp.concatenate([sub_b[i], edge_a[i], edge_b[i], jnp.zeros((LANES - rows, LANES), F32)], axis=0)
        first, second = split_two(parts)
        received[:LANES, cols] = first
        received[LANES:, cols] = second
    scale = inverse_volume[...]
    copies = []
    for i in range(0, COMPS, 2):
        added = dot(placing[...], received[:, i * LANES : (i + 2) * LANES])
        nodal[i] = ((partial[i] + added[:, :LANES]) * scale).astype(BF16)
        nodal[i + 1] = ((partial[i + 1] + added[:, LANES:]) * scale).astype(BF16)
        copy = pltpu.make_async_copy(nodal.at[pl.ds(i, 2)], out.at[pl.ds(i, 2)], sems.at[i // 2])
        copy.start()
        copies.append(copy)
    for copy in copies:
        copy.wait()


def vmem(count):
    return [pl.BlockSpec(memory_space=pltpu.VMEM)] * count


def anywhere(count):
    return [pl.BlockSpec(memory_space=pl.ANY)] * count


def hbm(count):
    return [pl.BlockSpec(memory_space=pltpu.HBM)] * count


def array(shape, dtype=F32):
    return jax.ShapeDtypeStruct(shape, dtype)


def call(kernel, name, out_shape, in_specs, scratch=(), flops=0, moved=0, out_specs=None):
    return pl.pallas_call(
        kernel,
        name=name,
        out_shape=out_shape,
        in_specs=in_specs,
        out_specs=out_specs or vmem(len(out_shape)),
        scratch_shapes=list(scratch),
        compiler_params=pltpu.CompilerParams(vmem_limit_bytes=VMEM_LIMIT),
        cost_estimate=pl.CostEstimate(flops=flops, bytes_accessed=moved, transcendentals=0),
    )


def exchange(block, axis, first):
    count = lax.axis_size(axis)
    pairs = []
    for i in range(first, count - 1, 2):
        pairs += [(i, i + 1), (i + 1, i)]
    return lax.ppermute(block, axis, pairs)


def in_hbm(*arrays):
    return [pltpu.with_memory_space_constraint(x, pltpu.HBM) for x in arrays]


def gather_near(coarse, own, ahead):
    beyond = exchange(coarse, "sub", 1)
    beside = exchange(coarse, "sub", 0)
    parts = [own, beside, beyond]
    distance = lax.axis_size("grp") // 2
    while distance:
        rows = sum(x.shape[0] for x in parts)
        before, ahead = ahead[:1], ahead[1:]

        def join(*refs, skip=len(before)):
            join_kernel(*refs[: len(refs) - 1 - skip], refs[-1])

        (block,) = call(
            join,
            "join_blocks",
            (array((rows, parts[0].shape[1])),),
            vmem(len(parts)) + anywhere(len(before)),
        )(*parts, *before)
        pairs = [(i, i ^ distance) for i in range(lax.axis_size("grp"))]
        parts = [block, lax.ppermute(block, "grp", pairs)]
        distance //= 2
    return parts


def shards(
    coarse,
    corner_idx,
    coupling,
    force,
    panel_inv,
    panel_nodes,
    strain_disp,
    modulus,
    connect,
    interface,
    nodal_volume,
):
    nodes, _, cases = force.shape
    dofs = 3 * nodes
    q = corner_idx.shape[1]

    def lists(*refs):
        prepare_lists(coarse.shape[0], lax.axis_size("grp"), *refs)

    own, select, onehot, face, scaled, count, placing, placing_last, inverse_volume = call(
        lists,
        "prepare_lists",
        (
            array(coarse.shape),
            array((TERM, 3 * LANES), BF16),
            array((nodes, CORNERS * LANES), BF16),
            array((NIF, 2 * LANES), BF16),
            array((COMPS * 24, 8, LANES)),
            array((nodes, 2 * LANES), BF16),
            array((nodes, 2 * LANES), BF16),
            array((nodes, 2 * LANES), BF16),
            array((nodes, LANES)),
        ),
        hbm(7),
        (
            pltpu.VMEM((1, q), jnp.int32),
            pltpu.VMEM(connect.shape, jnp.int32),
            pltpu.VMEM(interface.shape, jnp.int32),
            pltpu.VMEM(strain_disp.shape, BF16),
            pltpu.VMEM((1, LANES), F32),
            pltpu.VMEM((nodes // LANES, LANES), F32),
            pltpu.VMEM((8, 2 * LANES), F32),
            pltpu.SemaphoreType.DMA((7,)),
        ),
        flops=100000000,
        moved=4000000,
    )(
        *in_hbm(
            corner_idx,
            connect,
            interface,
            strain_disp,
            modulus.reshape(1, -1),
            nodal_volume.reshape(-1, LANES),
            coarse,
        )
    )
    inverse, coupled, loads, live = call(
        prepare_panels,
        "prepare_panels",
        (
            array(panel_inv.shape, BF16),
            array((dofs, LANES), BF16),
            array((dofs, cases)),
            array((dofs, LANES)),
        ),
        hbm(4),
        (
            pltpu.VMEM(panel_nodes.shape, jnp.int32),
            pltpu.VMEM((q, dofs), BF16),
            pltpu.VMEM((3, nodes, cases), BF16),
            pltpu.SemaphoreType.DMA((4,)),
        ),
        flops=100000000,
        moved=4000000,
    )(*in_hbm(panel_nodes, coupling.T, jnp.transpose(force, (1, 0, 2)), panel_inv))

    near = gather_near(coarse, own, [select, live])
    disp, stress, sub_a, sub_b, grp_a, grp_b = call(
        solve_kernel,
        "solve_and_stress",
        (
            array((3, nodes, cases), BF16),
            array((COMPS * cases, 2 * LANES), BF16),
            array((COMPS, NIS, cases)),
            array((COMPS, NIS, cases)),
            array((COMPS, NIG + 2 * NED, cases)),
            array((COMPS, NIG + 2 * NED, cases)),
        ),
        vmem(10),
        (
            pltpu.VMEM((3, 3 * LANES, cases), BF16),
            pltpu.VMEM((dofs, cases), F32),
            pltpu.VMEM((3 * cases, nodes), BF16),
            pltpu.VMEM((3 * cases, CORNERS * LANES), F32),
        ),
        flops=1500000000,
        moved=4000000,
    )(*near, inverse, coupled, loads, live, select, onehot, face, scaled)
    from_sub_a = exchange(sub_a, "sub", 0)
    from_grp_a = exchange(grp_a, "grp", 0)
    from_grp_b = exchange(grp_b, "grp", 1)
    edge_b, edge_a = call(
        edge_kernel,
        "sum_edges",
        (array((COMPS, 2 * NED, cases)), array((COMPS, 2 * NED, cases))),
        vmem(4),
    )(grp_a, grp_b, from_grp_a, from_grp_b)
    from_sub_b = exchange(sub_b, "sub", 1)
    from_edge_b = exchange(edge_b, "sub", 1)
    from_edge_a = exchange(edge_a, "sub", 0)
    partial, disp = call(
        partial_kernel,
        "assemble_nodes",
        (array((COMPS, nodes, cases)), array(disp.shape, BF16)),
        vmem(7),
        (pltpu.VMEM((4 * LANES, COMPS * cases), BF16),),
        flops=400000000,
        moved=2000000,
    )(count, stress, disp, placing, from_sub_a, from_grp_a, from_grp_b)
    (nodal,) = call(
        finish_kernel,
        "add_last",
        (array((COMPS, nodes, cases), BF16),),
        vmem(6),
        (
            pltpu.VMEM((2 * LANES, COMPS * cases), BF16),
            pltpu.VMEM((COMPS, nodes, cases), BF16),
            pltpu.SemaphoreType.DMA((COMPS // 2,)),
        ),
        flops=400000000,
        moved=3000000,
        out_specs=hbm(1),
    )(placing_last, partial, inverse_volume, from_sub_b, from_edge_b, from_edge_a)
    return jnp.transpose(disp, (1, 0, 2)), jnp.transpose(nodal, (1, 0, 2))


def solution(mesh):
    owner = ("sub", "grp")
    placed = (
        P(owner, None),
        P(owner, None),
        P(owner, None),
        P(owner, None, None),
        P(owner, None, None),
        P(owner, None),
        P(None, None, owner),
        P(owner),
        P(None, owner),
        P(owner, None),
        P(owner),
    )
    return jax.shard_map(
        shards,
        mesh=mesh,
        in_specs=placed,
        out_specs=(P(owner, None, None), P(owner, None, None)),
        check_vma=False,
    )
```

```python
import jax
import jax.numpy as jnp
from jax import lax
from jax.experimental import pallas as pl
from jax.experimental.pallas import tpu as pltpu
from jax.sharding import PartitionSpec as P

NIS = 64
NIG = 32
NED = 8
EDGES = 2 * NIS + 2 * NIG
NIF = EDGES + 4 * NED
CORNERS = 8
COMPS = 6
LANES = 128
TERM = 32

POISSON = 0.3
LAME = POISSON / ((1.0 + POISSON) * (1.0 - 2.0 * POISSON))
SHEAR = 0.5 / (1.0 + POISSON)

F32 = jnp.float32
BF16 = jnp.bfloat16
VMEM_LIMIT = 24 * 1024 * 1024


def split_two(x):
    high = x.astype(BF16)
    return high, (x - high.astype(F32)).astype(BF16)


def dot(a, b):
    return jnp.dot(a, b, preferred_element_type=F32)


def dot_nt(a, b):
    return lax.dot_general(a, b, (((1,), (1,)), ((), ())), preferred_element_type=F32)


def column(row):
    return jnp.broadcast_to(row, (LANES, LANES)).T


def swap_lanes(x, distance):
    lane = lax.broadcasted_iota(jnp.int32, x.shape, 1)
    after = pltpu.roll(x, LANES - distance, 1)
    before = pltpu.roll(x, distance, 1)
    return jnp.where((lane & distance) == 0, after, before)


def order_lists(ids):
    sub_even = (lax.axis_index("sub") & 1) == 0
    grp_even = (lax.axis_index("grp") & 1) == 0
    first, second = ids[:, :LANES], ids[:, LANES:]
    ids[:, :LANES] = jnp.where(sub_even, swap_lanes(first, NIS), first)
    lane = lax.broadcasted_iota(jnp.int32, second.shape, 1)
    groups = jnp.where(grp_even, swap_lanes(second, NIG), second)
    edges = jnp.where(sub_even, swap_lanes(second, 2 * NED), second)
    edges = jnp.where(grp_even, swap_lanes(edges, NED), edges)
    ids[:, LANES:] = jnp.where(lane < 2 * NIG, groups, edges)


def start_copies(pairs, sems):
    copies = [pltpu.make_async_copy(src, dst, sems.at[k]) for k, (src, dst) in enumerate(pairs)]
    for copy in copies:
        copy.start()
    return copies


def prepare_lists(
    block_rows,
    members,
    corner_idx,
    connect,
    interface,
    strain_disp,
    modulus,
    volume,
    coarse,
    own,
    select,
    onehot,
    face,
    scaled,
    count,
    placing,
    placing_last,
    inverse_volume,
    corner_v,
    connect_v,
    interface_v,
    strain_v,
    modulus_v,
    volume_v,
    ids,
    sems,
):
    copies = start_copies(
        [
            (connect, connect_v),
            (interface, interface_v),
            (corner_idx, corner_v),
            (modulus, modulus_v),
            (strain_disp, strain_v),
            (volume, volume_v),
            (coarse, own),
        ],
        sems,
    )
    nodes = onehot.shape[0]
    q = corner_idx.shape[1]

    copies[0].wait()
    node_of = lax.broadcasted_iota(jnp.int32, (nodes, LANES), 0)
    total = jnp.zeros((nodes, LANES), F32)
    for a in range(CORNERS):
        hit = jnp.where(connect_v[a : a + 1, :] == node_of, 1.0, 0.0)
        onehot[:, a * LANES : (a + 1) * LANES] = hit.astype(BF16)
        total = total + hit
    total = total.astype(BF16)
    count[:, :LANES] = total
    count[:, LANES:] = total

    copies[1].wait()
    ids[...] = jnp.full(ids.shape, -1.0, F32)
    ids[0:1, 0:NIF] = interface_v[...].astype(F32)
    order_lists(ids)
    lane = lax.broadcasted_iota(jnp.int32, (8, LANES), 1)
    last = jnp.where((lane >= NIS) & (lane < NIS + 4 * NED), ids[:, LANES:], -1.0)
    for index, (row, target) in enumerate(((ids[0:1, LANES:], placing), (ids[0:1, :LANES], placing_last), (last[0:1], placing_last))):
        hit = jnp.where(row.astype(jnp.int32) == node_of, 1.0, 0.0).astype(BF16)
        if index == 0:
            target[:, :LANES] = hit
            target[:, LANES:] = hit
        else:
            target[:, (index - 1) * LANES : index * LANES] = hit
    connect_f = connect_v[...].astype(F32)
    for half in range(2):
        id_col = column(ids[0:1, half * LANES : (half + 1) * LANES])
        rows = jnp.zeros((LANES, LANES), F32)
        for a in range(CORNERS):
            rows = rows + jnp.where(connect_f[a : a + 1, :] == id_col, 1.0, 0.0)
        rows = rows.astype(BF16)[: min(LANES, NIF - half * LANES)]
        face[half * LANES : half * LANES + rows.shape[0], :LANES] = rows
        face[half * LANES : half * LANES + rows.shape[0], LANES:] = rows

    copies[2].wait()
    ids[0:1, 0:q] = corner_v[...].astype(F32)
    wanted = column(ids[0:1, :LANES])[:TERM]
    lane = lax.broadcasted_iota(jnp.int32, (TERM, 3 * LANES), 1)
    entry = lax.broadcasted_iota(jnp.int32, (TERM, LANES), 0)
    s, g = lax.axis_index("sub"), lax.axis_index("grp")
    aside = 1 - 2 * (s & 1)
    row = jnp.full((TERM, 3 * LANES), -1, jnp.int32)
    base = 0
    for member in range(members):
        distance, bits, turn = members // 2, member, 0
        while distance:
            turn += (bits & 1) * distance
            distance, bits = distance // 2, bits >> 1
        for owner in (s, s + aside, s - aside):
            first = (owner * members + (g ^ turn)) * block_rows
            row = jnp.where((lane >= base) & (lane < base + block_rows), first - base + lane, row)
            base += block_rows
    for b in range(3):
        cols = slice(b * LANES, (b + 1) * LANES)
        hit = (wanted == row[:, cols].astype(F32)) & (entry < q)
        select[:, cols] = jnp.where(hit, 1.0, 0.0).astype(BF16)

    copies[3].wait()
    copies[4].wait()
    factor = modulus_v[...]
    rows = [strain_v[i].astype(F32) for i in range(COMPS)]
    trace = (rows[0] + rows[1] + rows[2]) * LAME
    for i in range(COMPS):
        value = trace + rows[i] * (2.0 * SHEAR) if i < 3 else rows[i] * SHEAR
        scaled[24 * i : 24 * (i + 1)] = jnp.broadcast_to((value * factor)[:, None, :], (24, 8, LANES))

    copies[5].wait()
    for k in range(nodes // LANES):
        inverse_volume[k * LANES : (k + 1) * LANES, :] = column(1.0 / volume_v[k : k + 1, :])
    copies[6].wait()


def prepare_panels(
    panel_nodes,
    coupling,
    force,
    panel_inv,
    inverse,
    coupled,
    loads,
    live,
    panel_v,
    coupling_v,
    force_v,
    sems,
):
    copies = start_copies(
        [
            (panel_nodes, panel_v),
            (coupling, coupling_v),
            (force, force_v),
            (panel_inv, inverse),
        ],
        sems,
    )
    panels, panel_rows, _ = inverse.shape
    nodes = force_v.shape[1]
    q = coupling_v.shape[0]

    copies[0].wait()
    row_of = lax.broadcasted_iota(jnp.int32, (panel_rows, LANES), 0)
    for p in range(panels):
        alive = row_of < 3 * panel_v[0:1, p : p + 1]
        live[p * panel_rows : (p + 1) * panel_rows, :] = jnp.where(alive, 1.0, 0.0)

    copies[1].wait()
    for k in range(coupling_v.shape[1] // LANES):
        part = coupling_v[:, k * LANES : (k + 1) * LANES].astype(F32)
        gap = jnp.zeros((TERM - q, LANES), F32)
        stack = jnp.concatenate([part, gap] * 3 + [jnp.zeros((LANES - 3 * TERM, LANES), F32)], axis=0)
        rows = slice(k * LANES, (k + 1) * LANES)
        coupled[rows, :] = (stack.T * live[rows, :]).astype(BF16)

    copies[2].wait()
    for c in range(3):
        loads[pl.ds(c, nodes, stride=3), :] = force_v[c].astype(F32)
    loads[...] = loads[...] * live[...]
    copies[3].wait()


def join_kernel(*refs):
    *parts, out = refs
    start = 0
    for part in parts:
        out[start : start + part.shape[0], :] = part[...]
        start += part.shape[0]


def solve_kernel(
    near,
    across,
    inverse,
    coupled,
    loads,
    live,
    select,
    onehot,
    face,
    scaled,
    disp,
    stress,
    sub_a,
    sub_b,
    grp_a,
    grp_b,
    terms,
    solved,
    disp_t,
    elem_t,
):
    panels, panel_rows, _ = inverse.shape
    panel_size = panel_rows // 3
    rows = near.shape[0]

    terms[:, 2 * rows :, :] = jnp.zeros((3, terms.shape[1] - 2 * rows, terms.shape[2]), BF16)
    for b, block in enumerate((near, across)):
        x = block[...]
        high = x.astype(BF16)
        rest = x - high.astype(F32)
        middle = rest.astype(BF16)
        low = (rest - middle.astype(F32)).astype(BF16)
        for t, value in enumerate((high, middle, low)):
            terms[t, b * rows : (b + 1) * rows, :] = value
    picked = [dot(select[...], terms[t]) for t in range(3)]
    picked.append(jnp.zeros((LANES - 3 * TERM, LANES), F32))
    values = jnp.concatenate(picked, axis=0).astype(BF16)

    for p in range(panels):
        start = p * panel_rows
        span = slice(start, start + panel_rows)
        reduced = (loads[span, :] - dot(coupled[span, :], values)).astype(BF16)
        solved[span, :] = dot(inverse[p], reduced) * live[span, :]
        for c in range(3):
            part = solved[pl.ds(start + c, panel_size, stride=3), :].astype(BF16)
            disp[c, p * panel_size : (p + 1) * panel_size, :] = part
            disp_t[c * LANES : (c + 1) * LANES, p * panel_size : (p + 1) * panel_size] = (
                part.astype(F32).T.astype(BF16)
            )

    elem_t[...] = dot(disp_t[...], onehot[...])
    step = 32
    for start in range(0, LANES, step):
        sums = [None] * COMPS
        for a in range(CORNERS):
            for c in range(3):
                x = elem_t[c * LANES + start : c * LANES + start + step, a * LANES : (a + 1) * LANES]
                x = x.reshape(step // 8, 8, LANES)
                for i in range(COMPS):
                    term = scaled[24 * i + 3 * a + c] * x
                    sums[i] = term if sums[i] is None else sums[i] + term
        sums = [x.reshape(step, LANES) for x in sums]
        for i in range(COMPS):
            high, low = split_two(sums[i])
            stress[i * LANES + start : i * LANES + start + step, 0:LANES] = high
            stress[i * LANES + start : i * LANES + start + step, LANES : 2 * LANES] = low

    rows = dot_nt(face[...], stress[...])
    for i in range(COMPS):
        part = rows[:, i * LANES : (i + 1) * LANES]
        edge = [part[EDGES + NED * k : EDGES + NED * (k + 1)] for k in range(4)]
        sub_a[i] = part[:NIS]
        sub_b[i] = part[NIS : 2 * NIS]
        grp_a[i] = jnp.concatenate([part[2 * NIS : 2 * NIS + NIG], edge[0], edge[2]], axis=0)
        grp_b[i] = jnp.concatenate([part[2 * NIS + NIG : EDGES], edge[1], edge[3]], axis=0)


def edge_kernel(grp_a, grp_b, from_a, from_b, edge_b, edge_a):
    split = NIG + NED
    edge_a[:, :NED, :] = grp_a[:, NIG:split, :] + from_a[:, NIG:split, :]
    edge_a[:, NED:, :] = grp_b[:, NIG:split, :] + from_b[:, NIG:split, :]
    edge_b[:, :NED, :] = grp_a[:, split:, :] + from_a[:, split:, :]
    edge_b[:, NED:, :] = grp_b[:, split:, :] + from_b[:, split:, :]


def partial_kernel(
    count, stress, disp, placing, grp_a, grp_b, partial, disp_out, received
):
    disp_out[...] = disp[...]
    split = NIG + NED
    for i in range(COMPS):
        low, high = grp_a[i], grp_b[i]
        rows = [low[:NIG], high[:NIG], low[NIG:split], high[NIG:split], low[split:], high[split:]]
        rows.append(jnp.zeros((2 * LANES - NIF, LANES), F32))
        first, second = split_two(jnp.concatenate(rows, axis=0))
        received[:LANES, i * LANES : (i + 1) * LANES] = first
        received[LANES:, i * LANES : (i + 1) * LANES] = second
    for i in range(0, COMPS, 2):
        cols = slice(i * LANES, (i + 2) * LANES)
        own = dot_nt(count[...], stress[cols, :])
        total = own + dot(placing[...], received[:, cols])
        partial[i] = total[:, :LANES]
        partial[i + 1] = total[:, LANES:]


def finish_kernel(
    placing, partial, inverse_volume, sub_a, sub_b, edge_b, edge_a, out, received, nodal, sems
):
    gap = jnp.zeros((NIS, LANES), F32)
    for i in range(COMPS):
        cols = slice(i * LANES, (i + 1) * LANES)
        tail = jnp.zeros((2 * LANES - NIF, LANES), F32)
        rows = jnp.concatenate([sub_a[i], sub_b[i], gap, edge_a[i], edge_b[i], tail], axis=0)
        first, second = split_two(rows)
        received[: 2 * LANES, cols] = first
        received[2 * LANES :, cols] = second
    scale = inverse_volume[...]
    copies = []
    for i in range(0, COMPS, 2):
        cols = slice(i * LANES, (i + 2) * LANES)
        added = dot(placing[...], received[: 2 * LANES, cols]) + dot(placing[...], received[2 * LANES :, cols])
        nodal[i] = ((partial[i] + added[:, :LANES]) * scale).astype(BF16)
        nodal[i + 1] = ((partial[i + 1] + added[:, LANES:]) * scale).astype(BF16)
        copy = pltpu.make_async_copy(nodal.at[pl.ds(i, 2)], out.at[pl.ds(i, 2)], sems.at[i // 2])
        copy.start()
        copies.append(copy)
    for copy in copies:
        copy.wait()


def vmem(count):
    return [pl.BlockSpec(memory_space=pltpu.VMEM)] * count


def anywhere(count):
    return [pl.BlockSpec(memory_space=pl.ANY)] * count


def hbm(count):
    return [pl.BlockSpec(memory_space=pltpu.HBM)] * count


def array(shape, dtype=F32):
    return jax.ShapeDtypeStruct(shape, dtype)


def call(kernel, name, out_shape, in_specs, scratch=(), flops=0, moved=0, out_specs=None):
    return pl.pallas_call(
        kernel,
        name=name,
        out_shape=out_shape,
        in_specs=in_specs,
        out_specs=out_specs or vmem(len(out_shape)),
        scratch_shapes=list(scratch),
        compiler_params=pltpu.CompilerParams(vmem_limit_bytes=VMEM_LIMIT),
        cost_estimate=pl.CostEstimate(flops=flops, bytes_accessed=moved, transcendentals=0),
    )


def exchange(block, axis, first):
    count = lax.axis_size(axis)
    pairs = []
    for i in range(first, count - 1, 2):
        pairs += [(i, i + 1), (i + 1, i)]
    return lax.ppermute(block, axis, pairs)


def in_hbm(*arrays):
    return [pltpu.with_memory_space_constraint(x, pltpu.HBM) for x in arrays]


def gather_near(coarse, own, ahead):
    beyond = exchange(coarse, "sub", 1)
    beside = exchange(coarse, "sub", 0)
    parts = [own, beside, beyond]
    distance = lax.axis_size("grp") // 2
    while distance:
        rows = sum(x.shape[0] for x in parts)
        before, ahead = ahead[:1], ahead[1:]

        def join(*refs, skip=len(before)):
            join_kernel(*refs[: len(refs) - 1 - skip], refs[-1])

        (block,) = call(
            join,
            "join_blocks",
            (array((rows, parts[0].shape[1])),),
            vmem(len(parts)) + anywhere(len(before)),
        )(*parts, *before)
        pairs = [(i, i ^ distance) for i in range(lax.axis_size("grp"))]
        parts = [block, lax.ppermute(block, "grp", pairs)]
        distance //= 2
    return parts


def shards(
    coarse,
    corner_idx,
    coupling,
    force,
    panel_inv,
    panel_nodes,
    strain_disp,
    modulus,
    connect,
    interface,
    nodal_volume,
):
    nodes, _, cases = force.shape
    dofs = 3 * nodes
    q = corner_idx.shape[1]

    def lists(*refs):
        prepare_lists(coarse.shape[0], lax.axis_size("grp"), *refs)

    own, select, onehot, face, scaled, count, placing, placing_last, inverse_volume = call(
        lists,
        "prepare_lists",
        (
            array(coarse.shape),
            array((TERM, 3 * LANES), BF16),
            array((nodes, CORNERS * LANES), BF16),
            array((NIF, 2 * LANES), BF16),
            array((COMPS * 24, 8, LANES)),
            array((nodes, 2 * LANES), BF16),
            array((nodes, 2 * LANES), BF16),
            array((nodes, 2 * LANES), BF16),
            array((nodes, LANES)),
        ),
        hbm(7),
        (
            pltpu.VMEM((1, q), jnp.int32),
            pltpu.VMEM(connect.shape, jnp.int32),
            pltpu.VMEM(interface.shape, jnp.int32),
            pltpu.VMEM(strain_disp.shape, BF16),
            pltpu.VMEM((1, LANES), F32),
            pltpu.VMEM((nodes // LANES, LANES), F32),
            pltpu.VMEM((8, 2 * LANES), F32),
            pltpu.SemaphoreType.DMA((7,)),
        ),
        flops=100000000,
        moved=4000000,
    )(
        *in_hbm(
            corner_idx,
            connect,
            interface,
            strain_disp,
            modulus.reshape(1, -1),
            nodal_volume.reshape(-1, LANES),
            coarse,
        )
    )
    inverse, coupled, loads, live = call(
        prepare_panels,
        "prepare_panels",
        (
            array(panel_inv.shape, BF16),
            array((dofs, LANES), BF16),
            array((dofs, cases)),
            array((dofs, LANES)),
        ),
        hbm(4),
        (
            pltpu.VMEM(panel_nodes.shape, jnp.int32),
            pltpu.VMEM((q, dofs), BF16),
            pltpu.VMEM((3, nodes, cases), BF16),
            pltpu.SemaphoreType.DMA((4,)),
        ),
        flops=100000000,
        moved=4000000,
    )(*in_hbm(panel_nodes, coupling.T, jnp.transpose(force, (1, 0, 2)), panel_inv))

    near = gather_near(coarse, own, [select, live])
    disp, stress, sub_a, sub_b, grp_a, grp_b = call(
        solve_kernel,
        "solve_and_stress",
        (
            array((3, nodes, cases), BF16),
            array((COMPS * cases, 2 * LANES), BF16),
            array((COMPS, NIS, cases)),
            array((COMPS, NIS, cases)),
            array((COMPS, NIG + 2 * NED, cases)),
            array((COMPS, NIG + 2 * NED, cases)),
        ),
        vmem(10),
        (
            pltpu.VMEM((3, 3 * LANES, cases), BF16),
            pltpu.VMEM((dofs, cases), F32),
            pltpu.VMEM((3 * cases, nodes), BF16),
            pltpu.VMEM((3 * cases, CORNERS * LANES), F32),
        ),
        flops=1500000000,
        moved=4000000,
    )(*near, inverse, coupled, loads, live, select, onehot, face, scaled)
    from_sub_a = exchange(sub_a, "sub", 0)
    from_grp_a = exchange(grp_a, "grp", 0)
    from_grp_b = exchange(grp_b, "grp", 1)
    edge_b, edge_a = call(
        edge_kernel,
        "sum_edges",
        (array((COMPS, 2 * NED, cases)), array((COMPS, 2 * NED, cases))),
        vmem(4),
    )(grp_a, grp_b, from_grp_a, from_grp_b)
    from_sub_b = exchange(sub_b, "sub", 1)
    from_edge_b = exchange(edge_b, "sub", 1)
    from_edge_a = exchange(edge_a, "sub", 0)
    partial, disp = call(
        partial_kernel,
        "assemble_nodes",
        (array((COMPS, nodes, cases)), array(disp.shape, BF16)),
        vmem(6),
        (pltpu.VMEM((2 * LANES, COMPS * cases), BF16),),
        flops=400000000,
        moved=2000000,
    )(count, stress, disp, placing, from_grp_a, from_grp_b)
    (nodal,) = call(
        finish_kernel,
        "add_last",
        (array((COMPS, nodes, cases), BF16),),
        vmem(7),
        (
            pltpu.VMEM((4 * LANES, COMPS * cases), BF16),
            pltpu.VMEM((COMPS, nodes, cases), BF16),
            pltpu.SemaphoreType.DMA((COMPS // 2,)),
        ),
        flops=400000000,
        moved=3000000,
        out_specs=hbm(1),
    )(placing_last, partial, inverse_volume, from_sub_a, from_sub_b, from_edge_b, from_edge_a)
    return jnp.transpose(disp, (1, 0, 2)), jnp.transpose(nodal, (1, 0, 2))


def solution(mesh):
    owner = ("sub", "grp")
    placed = (
        P(owner, None),
        P(owner, None),
        P(owner, None),
        P(owner, None, None),
        P(owner, None, None),
        P(owner, None),
        P(None, None, owner),
        P(owner),
        P(None, owner),
        P(owner, None),
        P(owner),
    )
    return jax.shard_map(
        shards,
        mesh=mesh,
        in_specs=placed,
        out_specs=(P(owner, None, None), P(owner, None, None)),
        check_vma=False,
    )
```

```python
import jax
import jax.numpy as jnp
from jax import lax
from jax.experimental import pallas as pl
from jax.experimental.pallas import tpu as pltpu
from jax.sharding import PartitionSpec as P

NIS = 64
NIG = 32
NED = 8
EDGES = 2 * NIS + 2 * NIG
NIF = EDGES + 4 * NED
CORNERS = 8
COMPS = 6
LANES = 128
TERM = 32
TERMS = ((0, 0), (0, 1), (0, 2), (1, 0), (1, 1), (2, 0))

POISSON = 0.3
LAME = POISSON / ((1.0 + POISSON) * (1.0 - 2.0 * POISSON))
SHEAR = 0.5 / (1.0 + POISSON)

F32 = jnp.float32
BF16 = jnp.bfloat16
VMEM_LIMIT = 24 * 1024 * 1024


def split_two(x):
    high = x.astype(BF16)
    return high, (x - high.astype(F32)).astype(BF16)


def split_three(x):
    high = x.astype(BF16)
    rest = x - high.astype(F32)
    middle = rest.astype(BF16)
    return high, middle, (rest - middle.astype(F32)).astype(BF16)


def dot(a, b):
    return jnp.dot(a, b, preferred_element_type=F32)


def dot_nt(a, b):
    return lax.dot_general(a, b, (((1,), (1,)), ((), ())), preferred_element_type=F32)


def column(row):
    return jnp.broadcast_to(row, (LANES, LANES)).T


def swap_lanes(x, distance):
    lane = lax.broadcasted_iota(jnp.int32, x.shape, 1)
    after = pltpu.roll(x, LANES - distance, 1)
    before = pltpu.roll(x, distance, 1)
    return jnp.where((lane & distance) == 0, after, before)


def order_lists(ids):
    sub_even = (lax.axis_index("sub") & 1) == 0
    grp_even = (lax.axis_index("grp") & 1) == 0
    first, second = ids[:, :LANES], ids[:, LANES:]
    ids[:, :LANES] = jnp.where(sub_even, swap_lanes(first, NIS), first)
    lane = lax.broadcasted_iota(jnp.int32, second.shape, 1)
    groups = jnp.where(grp_even, swap_lanes(second, NIG), second)
    edges = jnp.where(sub_even, swap_lanes(second, 2 * NED), second)
    edges = jnp.where(grp_even, swap_lanes(edges, NED), edges)
    ids[:, LANES:] = jnp.where(lane < 2 * NIG, groups, edges)


def start_copies(pairs, sems):
    copies = [pltpu.make_async_copy(src, dst, sems.at[k]) for k, (src, dst) in enumerate(pairs)]
    for copy in copies:
        copy.start()
    return copies


def prepare_lists(
    block_rows,
    members,
    corner_idx,
    connect,
    interface,
    strain_disp,
    modulus,
    volume,
    coarse,
    own,
    select,
    onehot,
    face,
    scaled,
    count,
    placing,
    placing_last,
    inverse_volume,
    corner_v,
    connect_v,
    interface_v,
    strain_v,
    modulus_v,
    volume_v,
    ids,
    sems,
):
    copies = start_copies(
        [
            (connect, connect_v),
            (interface, interface_v),
            (corner_idx, corner_v),
            (modulus, modulus_v),
            (strain_disp, strain_v),
            (volume, volume_v),
            (coarse, own),
        ],
        sems,
    )
    nodes = onehot.shape[0]
    q = corner_idx.shape[1]

    copies[0].wait()
    node_of = lax.broadcasted_iota(jnp.int32, (nodes, LANES), 0)
    total = jnp.zeros((nodes, LANES), F32)
    for a in range(CORNERS):
        hit = jnp.where(connect_v[a : a + 1, :] == node_of, 1.0, 0.0)
        onehot[:, a * LANES : (a + 1) * LANES] = hit.astype(BF16)
        total = total + hit
    total = total.astype(BF16)
    count[:, :LANES] = total
    count[:, LANES:] = total

    copies[1].wait()
    ids[...] = jnp.full(ids.shape, -1.0, F32)
    ids[0:1, 0:NIF] = interface_v[...].astype(F32)
    order_lists(ids)
    lane = lax.broadcasted_iota(jnp.int32, (8, LANES), 1)
    last = jnp.where((lane >= NIS) & (lane < NIS + 4 * NED), ids[:, LANES:], -1.0)
    for index, (row, target) in enumerate(((ids[0:1, LANES:], placing), (ids[0:1, :LANES], placing_last), (last[0:1], placing_last))):
        hit = jnp.where(row.astype(jnp.int32) == node_of, 1.0, 0.0).astype(BF16)
        if index == 0:
            target[:, :LANES] = hit
            target[:, LANES:] = hit
        else:
            target[:, (index - 1) * LANES : index * LANES] = hit
    connect_f = connect_v[...].astype(F32)
    for half in range(2):
        id_col = column(ids[0:1, half * LANES : (half + 1) * LANES])
        rows = jnp.zeros((LANES, LANES), F32)
        for a in range(CORNERS):
            rows = rows + jnp.where(connect_f[a : a + 1, :] == id_col, 1.0, 0.0)
        rows = rows.astype(BF16)[: min(LANES, NIF - half * LANES)]
        face[half * LANES : half * LANES + rows.shape[0], :LANES] = rows
        face[half * LANES : half * LANES + rows.shape[0], LANES:] = rows

    copies[2].wait()
    ids[0:1, 0:q] = corner_v[...].astype(F32)
    wanted = column(ids[0:1, :LANES])[:TERM]
    lane = lax.broadcasted_iota(jnp.int32, (TERM, 3 * LANES), 1)
    entry = lax.broadcasted_iota(jnp.int32, (TERM, LANES), 0)
    s, g = lax.axis_index("sub"), lax.axis_index("grp")
    aside = 1 - 2 * (s & 1)
    row = jnp.full((TERM, 3 * LANES), -1, jnp.int32)
    base = 0
    for member in range(members):
        distance, bits, turn = members // 2, member, 0
        while distance:
            turn += (bits & 1) * distance
            distance, bits = distance // 2, bits >> 1
        for owner in (s, s + aside, s - aside):
            first = (owner * members + (g ^ turn)) * block_rows
            row = jnp.where((lane >= base) & (lane < base + block_rows), first - base + lane, row)
            base += block_rows
    for b in range(3):
        cols = slice(b * LANES, (b + 1) * LANES)
        hit = (wanted == row[:, cols].astype(F32)) & (entry < q)
        select[:, cols] = jnp.where(hit, 1.0, 0.0).astype(BF16)

    copies[3].wait()
    copies[4].wait()
    factor = modulus_v[...]
    rows = [strain_v[i].astype(F32) for i in range(COMPS)]
    trace = (rows[0] + rows[1] + rows[2]) * LAME
    for i in range(COMPS):
        value = trace + rows[i] * (2.0 * SHEAR) if i < 3 else rows[i] * SHEAR
        scaled[24 * i : 24 * (i + 1)] = jnp.broadcast_to((value * factor)[:, None, :], (24, 8, LANES))

    copies[5].wait()
    for k in range(nodes // LANES):
        inverse_volume[k * LANES : (k + 1) * LANES, :] = column(1.0 / volume_v[k : k + 1, :])
    copies[6].wait()


def prepare_panels(
    panel_nodes,
    coupling,
    force,
    panel_inv,
    free_t,
    corner_t,
    panel_v,
    coupling_v,
    force_v,
    inverse,
    loads,
    solved,
    sems,
):
    copies = start_copies(
        [
            (panel_nodes, panel_v),
            (coupling, coupling_v),
            (force, force_v),
            (panel_inv, inverse),
        ],
        sems,
    )
    panels, panel_rows, _ = inverse.shape
    panel_size = panel_rows // 3
    nodes = force_v.shape[1]
    q = coupling_v.shape[0]

    copies[0].wait()
    copies[1].wait()
    copies[2].wait()
    for c in range(3):
        loads[pl.ds(c, nodes, stride=3), :] = force_v[c].astype(F32)
    corner_t[len(TERMS) * TERM :, :] = jnp.zeros((corner_t.shape[0] - len(TERMS) * TERM, 3 * nodes), BF16)
    row_of = lax.broadcasted_iota(jnp.int32, (panel_rows, LANES), 0)
    lane = lax.broadcasted_iota(jnp.int32, (panel_rows, LANES), 1)
    copies[3].wait()
    for p in range(panels):
        start = p * panel_rows
        live = row_of < 3 * panel_v[0:1, p : p + 1]
        columns = []
        for k in range(panel_rows // LANES):
            part = coupling_v[:, start + k * LANES : start + (k + 1) * LANES].astype(F32)
            columns.append(jnp.concatenate([part, jnp.zeros((LANES - q, LANES), F32)], axis=0).T)
        sides = [loads[start : start + panel_rows, :], jnp.concatenate(columns, axis=0)]
        sides = jnp.concatenate([jnp.where(live, x, 0.0).astype(BF16) for x in sides], axis=1)
        result = dot(inverse[p], sides)
        for side in range(2):
            solved[side] = jnp.where(live, result[:, side * LANES : (side + 1) * LANES], 0.0)
        for c in range(3):
            cols = slice(c * nodes + p * panel_size, c * nodes + (p + 1) * panel_size)
            free_t[:, cols] = solved[0, pl.ds(c, panel_size, stride=3), :].T
            value = solved[1, pl.ds(c, panel_size, stride=3), :].T[:TERM]
            pieces = split_three(value)
            for k, (piece, _) in enumerate(TERMS):
                corner_t[k * TERM : (k + 1) * TERM, cols] = pieces[piece]


def join_kernel(*refs):
    *parts, out = refs
    start = 0
    for part in parts:
        out[start : start + part.shape[0], :] = part[...]
        start += part.shape[0]


def solve_kernel(
    near,
    across,
    free_t,
    corner_t,
    select,
    onehot,
    face,
    scaled,
    disp_t,
    stress,
    sub_a,
    sub_b,
    grp_a,
    grp_b,
    terms,
    elem_t,
):
    rows = near.shape[0]
    terms[:, 2 * rows :, :] = jnp.zeros((3, terms.shape[1] - 2 * rows, terms.shape[2]), BF16)
    for b, block in enumerate((near, across)):
        for t, value in enumerate(split_three(block[...])):
            terms[t, b * rows : (b + 1) * rows, :] = value
    picked = [dot(select[...], terms[t]) for t in range(3)]
    values = [picked[term] for _, term in TERMS]
    values += [jnp.zeros_like(picked[0])] * (corner_t.shape[0] // TERM - len(values))
    per = LANES // TERM
    values = [jnp.concatenate(values[k : k + per], axis=0).T for k in range(0, len(values), per)]
    values = jnp.concatenate(values, axis=1).astype(BF16)
    nodes = disp_t.shape[1]
    for c in range(3):
        cols = slice(c * nodes, (c + 1) * nodes)
        part = free_t[:, cols] - dot(values, corner_t[:, cols])
        disp_t[c * LANES : (c + 1) * LANES, :] = part.astype(BF16)

    elem_t[...] = dot(disp_t[...], onehot[...])
    step = 32
    for start in range(0, LANES, step):
        sums = [None] * COMPS
        for a in range(CORNERS):
            for c in range(3):
                x = elem_t[c * LANES + start : c * LANES + start + step, a * LANES : (a + 1) * LANES]
                x = x.reshape(step // 8, 8, LANES)
                for i in range(COMPS):
                    term = scaled[24 * i + 3 * a + c] * x
                    sums[i] = term if sums[i] is None else sums[i] + term
        sums = [x.reshape(step, LANES) for x in sums]
        for i in range(COMPS):
            high, low = split_two(sums[i])
            stress[i * LANES + start : i * LANES + start + step, 0:LANES] = high
            stress[i * LANES + start : i * LANES + start + step, LANES : 2 * LANES] = low

    rows = dot_nt(face[...], stress[...])
    for i in range(COMPS):
        part = rows[:, i * LANES : (i + 1) * LANES]
        edge = [part[EDGES + NED * k : EDGES + NED * (k + 1)] for k in range(4)]
        sub_a[i] = part[:NIS]
        sub_b[i] = part[NIS : 2 * NIS]
        grp_a[i] = jnp.concatenate([part[2 * NIS : 2 * NIS + NIG], edge[0], edge[2]], axis=0)
        grp_b[i] = jnp.concatenate([part[2 * NIS + NIG : EDGES], edge[1], edge[3]], axis=0)


def edge_kernel(grp_a, grp_b, from_a, from_b, edge_b, edge_a):
    split = NIG + NED
    edge_a[:, :NED, :] = grp_a[:, NIG:split, :] + from_a[:, NIG:split, :]
    edge_a[:, NED:, :] = grp_b[:, NIG:split, :] + from_b[:, NIG:split, :]
    edge_b[:, :NED, :] = grp_a[:, split:, :] + from_a[:, split:, :]
    edge_b[:, NED:, :] = grp_b[:, split:, :] + from_b[:, split:, :]


def partial_kernel(
    count, stress, disp_t, placing, grp_a, grp_b, partial, disp_out, received
):
    for c in range(3):
        for k in range(0, disp_out.shape[1], LANES):
            part = disp_t[c * LANES : (c + 1) * LANES, k : k + LANES].astype(F32).T
            disp_out[c, k : k + LANES, :] = part.astype(BF16)
    split = NIG + NED
    for i in range(COMPS):
        low, high = grp_a[i], grp_b[i]
        rows = [low[:NIG], high[:NIG], low[NIG:split], high[NIG:split], low[split:], high[split:]]
        rows.append(jnp.zeros((2 * LANES - NIF, LANES), F32))
        first, second = split_two(jnp.concatenate(rows, axis=0))
        received[:LANES, i * LANES : (i + 1) * LANES] = first
        received[LANES:, i * LANES : (i + 1) * LANES] = second
    for i in range(0, COMPS, 2):
        cols = slice(i * LANES, (i + 2) * LANES)
        own = dot_nt(count[...], stress[cols, :])
        total = own + dot(placing[...], received[:, cols])
        partial[i] = total[:, :LANES]
        partial[i + 1] = total[:, LANES:]


def finish_kernel(
    placing, partial, inverse_volume, sub_a, sub_b, edge_b, edge_a, out, received, nodal, sems
):
    gap = jnp.zeros((NIS, LANES), F32)
    for i in range(COMPS):
        cols = slice(i * LANES, (i + 1) * LANES)
        tail = jnp.zeros((2 * LANES - NIF, LANES), F32)
        rows = jnp.concatenate([sub_a[i], sub_b[i], gap, edge_a[i], edge_b[i], tail], axis=0)
        first, second = split_two(rows)
        received[: 2 * LANES, cols] = first
        received[2 * LANES :, cols] = second
    scale = inverse_volume[...]
    copies = []
    for i in range(0, COMPS, 2):
        cols = slice(i * LANES, (i + 2) * LANES)
        added = dot(placing[...], received[: 2 * LANES, cols]) + dot(placing[...], received[2 * LANES :, cols])
        nodal[i] = ((partial[i] + added[:, :LANES]) * scale).astype(BF16)
        nodal[i + 1] = ((partial[i + 1] + added[:, LANES:]) * scale).astype(BF16)
        copy = pltpu.make_async_copy(nodal.at[pl.ds(i, 2)], out.at[pl.ds(i, 2)], sems.at[i // 2])
        copy.start()
        copies.append(copy)
    for copy in copies:
        copy.wait()


def vmem(count):
    return [pl.BlockSpec(memory_space=pltpu.VMEM)] * count


def anywhere(count):
    return [pl.BlockSpec(memory_space=pl.ANY)] * count


def hbm(count):
    return [pl.BlockSpec(memory_space=pltpu.HBM)] * count


def array(shape, dtype=F32):
    return jax.ShapeDtypeStruct(shape, dtype)


def call(kernel, name, out_shape, in_specs, scratch=(), flops=0, moved=0, out_specs=None):
    return pl.pallas_call(
        kernel,
        name=name,
        out_shape=out_shape,
        in_specs=in_specs,
        out_specs=out_specs or vmem(len(out_shape)),
        scratch_shapes=list(scratch),
        compiler_params=pltpu.CompilerParams(vmem_limit_bytes=VMEM_LIMIT),
        cost_estimate=pl.CostEstimate(flops=flops, bytes_accessed=moved, transcendentals=0),
    )


def exchange(block, axis, first):
    count = lax.axis_size(axis)
    pairs = []
    for i in range(first, count - 1, 2):
        pairs += [(i, i + 1), (i + 1, i)]
    return lax.ppermute(block, axis, pairs)


def in_hbm(*arrays):
    return [pltpu.with_memory_space_constraint(x, pltpu.HBM) for x in arrays]


def gather_near(coarse, own, ahead):
    beyond = exchange(coarse, "sub", 1)
    beside = exchange(coarse, "sub", 0)
    parts = [own, beside, beyond]
    distance = lax.axis_size("grp") // 2
    while distance:
        rows = sum(x.shape[0] for x in parts)
        before, ahead = ahead[:1], ahead[1:]

        def join(*refs, skip=len(before)):
            join_kernel(*refs[: len(refs) - 1 - skip], refs[-1])

        (block,) = call(
            join,
            "join_blocks",
            (array((rows, parts[0].shape[1])),),
            vmem(len(parts)) + anywhere(len(before)),
        )(*parts, *before)
        pairs = [(i, i ^ distance) for i in range(lax.axis_size("grp"))]
        parts = [block, lax.ppermute(block, "grp", pairs)]
        distance //= 2
    return parts


def shards(
    coarse,
    corner_idx,
    coupling,
    force,
    panel_inv,
    panel_nodes,
    strain_disp,
    modulus,
    connect,
    interface,
    nodal_volume,
):
    nodes, _, cases = force.shape
    dofs = 3 * nodes
    q = corner_idx.shape[1]

    def lists(*refs):
        prepare_lists(coarse.shape[0], lax.axis_size("grp"), *refs)

    own, select, onehot, face, scaled, count, placing, placing_last, inverse_volume = call(
        lists,
        "prepare_lists",
        (
            array(coarse.shape),
            array((TERM, 3 * LANES), BF16),
            array((nodes, CORNERS * LANES), BF16),
            array((NIF, 2 * LANES), BF16),
            array((COMPS * 24, 8, LANES)),
            array((nodes, 2 * LANES), BF16),
            array((nodes, 2 * LANES), BF16),
            array((nodes, 2 * LANES), BF16),
            array((nodes, LANES)),
        ),
        hbm(7),
        (
            pltpu.VMEM((1, q), jnp.int32),
            pltpu.VMEM(connect.shape, jnp.int32),
            pltpu.VMEM(interface.shape, jnp.int32),
            pltpu.VMEM(strain_disp.shape, BF16),
            pltpu.VMEM((1, LANES), F32),
            pltpu.VMEM((nodes // LANES, LANES), F32),
            pltpu.VMEM((8, 2 * LANES), F32),
            pltpu.SemaphoreType.DMA((7,)),
        ),
        flops=100000000,
        moved=4000000,
    )(
        *in_hbm(
            corner_idx,
            connect,
            interface,
            strain_disp,
            modulus.reshape(1, -1),
            nodal_volume.reshape(-1, LANES),
            coarse,
        )
    )
    panel_rows = panel_inv.shape[1]
    free_t, corner_t = call(
        prepare_panels,
        "prepare_panels",
        (array((cases, dofs)), array((2 * LANES, dofs), BF16)),
        hbm(4),
        (
            pltpu.VMEM(panel_nodes.shape, jnp.int32),
            pltpu.VMEM((q, dofs), BF16),
            pltpu.VMEM((3, nodes, cases), BF16),
            pltpu.VMEM(panel_inv.shape, BF16),
            pltpu.VMEM((dofs, cases), F32),
            pltpu.VMEM((2, panel_rows, LANES), F32),
            pltpu.SemaphoreType.DMA((4,)),
        ),
        flops=400000000,
        moved=4000000,
    )(*in_hbm(panel_nodes, coupling.T, jnp.transpose(force, (1, 0, 2)), panel_inv))

    near = gather_near(coarse, own, [select, corner_t])
    disp_t, stress, sub_a, sub_b, grp_a, grp_b = call(
        solve_kernel,
        "solve_and_stress",
        (
            array((3 * cases, nodes), BF16),
            array((COMPS * cases, 2 * LANES), BF16),
            array((COMPS, NIS, cases)),
            array((COMPS, NIS, cases)),
            array((COMPS, NIG + 2 * NED, cases)),
            array((COMPS, NIG + 2 * NED, cases)),
        ),
        vmem(8),
        (
            pltpu.VMEM((3, 3 * LANES, cases), BF16),
            pltpu.VMEM((3 * cases, CORNERS * LANES), F32),
        ),
        flops=1000000000,
        moved=4000000,
    )(*near, free_t, corner_t, select, onehot, face, scaled)
    from_sub_a = exchange(sub_a, "sub", 0)
    from_grp_a = exchange(grp_a, "grp", 0)
    from_grp_b = exchange(grp_b, "grp", 1)
    edge_b, edge_a = call(
        edge_kernel,
        "sum_edges",
        (array((COMPS, 2 * NED, cases)), array((COMPS, 2 * NED, cases))),
        vmem(4),
    )(grp_a, grp_b, from_grp_a, from_grp_b)
    from_sub_b = exchange(sub_b, "sub", 1)
    from_edge_b = exchange(edge_b, "sub", 1)
    from_edge_a = exchange(edge_a, "sub", 0)
    partial, disp = call(
        partial_kernel,
        "assemble_nodes",
        (array((COMPS, nodes, cases)), array((3, nodes, cases), BF16)),
        vmem(6),
        (pltpu.VMEM((2 * LANES, COMPS * cases), BF16),),
        flops=400000000,
        moved=2000000,
    )(count, stress, disp_t, placing, from_grp_a, from_grp_b)
    (nodal,) = call(
        finish_kernel,
        "add_last",
        (array((COMPS, nodes, cases), BF16),),
        vmem(7),
        (
            pltpu.VMEM((4 * LANES, COMPS * cases), BF16),
            pltpu.VMEM((COMPS, nodes, cases), BF16),
            pltpu.SemaphoreType.DMA((COMPS // 2,)),
        ),
        flops=400000000,
        moved=3000000,
        out_specs=hbm(1),
    )(placing_last, partial, inverse_volume, from_sub_a, from_sub_b, from_edge_b, from_edge_a)
    return jnp.transpose(disp, (1, 0, 2)), jnp.transpose(nodal, (1, 0, 2))


def solution(mesh):
    owner = ("sub", "grp")
    placed = (
        P(owner, None),
        P(owner, None),
        P(owner, None),
        P(owner, None, None),
        P(owner, None, None),
        P(owner, None),
        P(None, None, owner),
        P(owner),
        P(None, owner),
        P(owner, None),
        P(owner),
    )
    return jax.shard_map(
        shards,
        mesh=mesh,
        in_specs=placed,
        out_specs=(P(owner, None, None), P(owner, None, None)),
        check_vma=False,
    )
```

```python
import jax
import jax.numpy as jnp
from jax import lax
from jax.experimental import pallas as pl
from jax.experimental.pallas import tpu as pltpu
from jax.sharding import PartitionSpec as P

NIS = 64
NIG = 32
NED = 8
EDGES = 2 * NIS + 2 * NIG
NIF = EDGES + 4 * NED
LATE = NIS + 4 * NED
CORNERS = 8
COMPS = 6
LANES = 128
TERM = 32
TERMS = ((0, 0), (0, 1), (0, 2), (1, 0), (1, 1), (2, 0))

POISSON = 0.3
LAME = POISSON / ((1.0 + POISSON) * (1.0 - 2.0 * POISSON))
SHEAR = 0.5 / (1.0 + POISSON)

F32 = jnp.float32
BF16 = jnp.bfloat16
VMEM_LIMIT = 24 * 1024 * 1024


def split_two(x):
    high = x.astype(BF16)
    return high, (x - high.astype(F32)).astype(BF16)


def split_three(x):
    high = x.astype(BF16)
    rest = x - high.astype(F32)
    middle = rest.astype(BF16)
    return high, middle, (rest - middle.astype(F32)).astype(BF16)


def dot(a, b):
    return jnp.dot(a, b, preferred_element_type=F32)


def dot_nt(a, b):
    return lax.dot_general(a, b, (((1,), (1,)), ((), ())), preferred_element_type=F32)


def column(row):
    return jnp.broadcast_to(row, (LANES, LANES)).T


def swap_lanes(x, distance):
    lane = lax.broadcasted_iota(jnp.int32, x.shape, 1)
    after = pltpu.roll(x, LANES - distance, 1)
    before = pltpu.roll(x, distance, 1)
    return jnp.where((lane & distance) == 0, after, before)


def order_lists(ids):
    sub_even = (lax.axis_index("sub") & 1) == 0
    grp_even = (lax.axis_index("grp") & 1) == 0
    first, second = ids[:, :LANES], ids[:, LANES:]
    ids[:, :LANES] = jnp.where(sub_even, swap_lanes(first, NIS), first)
    lane = lax.broadcasted_iota(jnp.int32, second.shape, 1)
    groups = jnp.where(grp_even, swap_lanes(second, NIG), second)
    edges = jnp.where(sub_even, swap_lanes(second, 2 * NED), second)
    edges = jnp.where(grp_even, swap_lanes(edges, NED), edges)
    ids[:, LANES:] = jnp.where(lane < 2 * NIG, groups, edges)


def start_copies(pairs, sems):
    copies = [pltpu.make_async_copy(src, dst, sems.at[k]) for k, (src, dst) in enumerate(pairs)]
    for copy in copies:
        copy.start()
    return copies


def prepare_lists(
    block_rows,
    members,
    corner_idx,
    connect,
    interface,
    strain_disp,
    modulus,
    volume,
    coarse,
    own,
    select,
    onehot,
    face,
    scaled,
    count,
    placing,
    placing_last,
    inverse_volume,
    corner_v,
    connect_v,
    interface_v,
    strain_v,
    modulus_v,
    volume_v,
    ids,
    sems,
):
    copies = start_copies(
        [
            (connect, connect_v),
            (interface, interface_v),
            (corner_idx, corner_v),
            (modulus, modulus_v),
            (strain_disp, strain_v),
            (volume, volume_v),
            (coarse, own),
        ],
        sems,
    )
    nodes = onehot.shape[0]
    q = corner_idx.shape[1]

    copies[0].wait()
    node_of = lax.broadcasted_iota(jnp.int32, (nodes, LANES), 0)
    total = jnp.zeros((nodes, LANES), F32)
    for a in range(CORNERS):
        hit = jnp.where(connect_v[a : a + 1, :] == node_of, 1.0, 0.0)
        onehot[:, a * LANES : (a + 1) * LANES] = hit.astype(BF16)
        total = total + hit
    total = total.astype(BF16)
    count[:, :LANES] = total
    count[:, LANES:] = total

    copies[1].wait()
    ids[...] = jnp.full(ids.shape, -1.0, F32)
    ids[0:1, 0:NIF] = interface_v[...].astype(F32)
    order_lists(ids)
    lane = lax.broadcasted_iota(jnp.int32, (8, LANES), 1)
    edges = pltpu.roll(ids[:, LANES:], LANES - NIS, 1)
    again = pltpu.roll(ids[:, :LANES], LANES - NIS + 4 * NED, 1)
    last = jnp.where(lane < 4 * NED, edges, again)
    last = jnp.where(lane < LATE, last, pltpu.roll(edges, LATE, 1))
    for row, target in ((ids[0:1, LANES:], 0), (ids[0:1, :LANES], 1), (last[0:1], 2)):
        hit = jnp.where(row.astype(jnp.int32) == node_of, 1.0, 0.0).astype(BF16)
        if target == 0:
            placing[:, :LANES] = hit
            placing[:, LANES:] = hit
        else:
            placing_last[:, (target - 1) * LANES : target * LANES] = hit
    connect_f = connect_v[...].astype(F32)
    for half in range(2):
        id_col = column(ids[0:1, half * LANES : (half + 1) * LANES])
        rows = jnp.zeros((LANES, LANES), F32)
        for a in range(CORNERS):
            rows = rows + jnp.where(connect_f[a : a + 1, :] == id_col, 1.0, 0.0)
        rows = rows.astype(BF16)[: min(LANES, NIF - half * LANES)]
        face[half * LANES : half * LANES + rows.shape[0], :LANES] = rows
        face[half * LANES : half * LANES + rows.shape[0], LANES:] = rows

    copies[2].wait()
    ids[0:1, 0:q] = corner_v[...].astype(F32)
    wanted = column(ids[0:1, :LANES])[:TERM]
    lane = lax.broadcasted_iota(jnp.int32, (TERM, 3 * LANES), 1)
    entry = lax.broadcasted_iota(jnp.int32, (TERM, LANES), 0)
    s, g = lax.axis_index("sub"), lax.axis_index("grp")
    aside = 1 - 2 * (s & 1)
    row = jnp.full((TERM, 3 * LANES), -1, jnp.int32)
    base = 0
    for member in range(members):
        distance, bits, turn = members // 2, member, 0
        while distance:
            turn += (bits & 1) * distance
            distance, bits = distance // 2, bits >> 1
        for owner in (s, s + aside, s - aside):
            first = (owner * members + (g ^ turn)) * block_rows
            row = jnp.where((lane >= base) & (lane < base + block_rows), first - base + lane, row)
            base += block_rows
    for b in range(3):
        cols = slice(b * LANES, (b + 1) * LANES)
        hit = (wanted == row[:, cols].astype(F32)) & (entry < q)
        select[:, cols] = jnp.where(hit, 1.0, 0.0).astype(BF16)

    copies[3].wait()
    copies[4].wait()
    factor = modulus_v[...]
    rows = [strain_v[i].astype(F32) for i in range(COMPS)]
    trace = (rows[0] + rows[1] + rows[2]) * LAME
    for i in range(COMPS):
        value = trace + rows[i] * (2.0 * SHEAR) if i < 3 else rows[i] * SHEAR
        scaled[24 * i : 24 * (i + 1)] = jnp.broadcast_to((value * factor)[:, None, :], (24, 8, LANES))

    copies[5].wait()
    for k in range(nodes // LANES):
        inverse_volume[k * LANES : (k + 1) * LANES, :] = column(1.0 / volume_v[k : k + 1, :])
    copies[6].wait()


def prepare_panels(
    panel_nodes,
    coupling,
    force,
    panel_inv,
    free_t,
    corner_t,
    panel_v,
    coupling_v,
    force_v,
    inverse,
    loads,
    solved,
    sems,
):
    copies = start_copies(
        [
            (panel_nodes, panel_v),
            (coupling, coupling_v),
            (force, force_v),
            (panel_inv, inverse),
        ],
        sems,
    )
    panels, panel_rows, _ = inverse.shape
    panel_size = panel_rows // 3
    nodes = force_v.shape[1]
    q = coupling_v.shape[0]

    copies[0].wait()
    copies[1].wait()
    copies[2].wait()
    for c in range(3):
        loads[pl.ds(c, nodes, stride=3), :] = force_v[c].astype(F32)
    corner_t[len(TERMS) * TERM :, :] = jnp.zeros((corner_t.shape[0] - len(TERMS) * TERM, 3 * nodes), BF16)
    row_of = lax.broadcasted_iota(jnp.int32, (panel_rows, LANES), 0)
    lane = lax.broadcasted_iota(jnp.int32, (panel_rows, LANES), 1)
    copies[3].wait()
    for p in range(panels):
        start = p * panel_rows
        live = row_of < 3 * panel_v[0:1, p : p + 1]
        columns = []
        for k in range(panel_rows // LANES):
            part = coupling_v[:, start + k * LANES : start + (k + 1) * LANES].astype(F32)
            columns.append(jnp.concatenate([part, jnp.zeros((LANES - q, LANES), F32)], axis=0).T)
        sides = [loads[start : start + panel_rows, :], jnp.concatenate(columns, axis=0)]
        sides = jnp.concatenate([jnp.where(live, x, 0.0).astype(BF16) for x in sides], axis=1)
        result = dot(inverse[p], sides)
        for side in range(2):
            solved[side] = jnp.where(live, result[:, side * LANES : (side + 1) * LANES], 0.0)
        for c in range(3):
            cols = slice(c * nodes + p * panel_size, c * nodes + (p + 1) * panel_size)
            free_t[:, cols] = solved[0, pl.ds(c, panel_size, stride=3), :].T
            value = solved[1, pl.ds(c, panel_size, stride=3), :].T[:TERM]
            pieces = split_three(value)
            for k, (piece, _) in enumerate(TERMS):
                corner_t[k * TERM : (k + 1) * TERM, cols] = pieces[piece]


def join_kernel(*refs):
    *parts, out = refs
    start = 0
    for part in parts:
        out[start : start + part.shape[0], :] = part[...]
        start += part.shape[0]


def solve_kernel(
    near,
    across,
    free_t,
    corner_t,
    select,
    onehot,
    face,
    scaled,
    disp_t,
    stress,
    sub_a,
    sub_b,
    grp_a,
    grp_b,
    terms,
    sofar,
):
    rows = near.shape[0]
    terms[:, 2 * rows :, :] = jnp.zeros((3, terms.shape[1] - 2 * rows, terms.shape[2]), BF16)
    for b, block in enumerate((near, across)):
        for t, value in enumerate(split_three(block[...])):
            terms[t, b * rows : (b + 1) * rows, :] = value
    picked = [dot(select[...], terms[t]) for t in range(3)]
    values = [picked[term] for _, term in TERMS]
    values += [jnp.zeros_like(picked[0])] * (corner_t.shape[0] // TERM - len(values))
    per = LANES // TERM
    values = [jnp.concatenate(values[k : k + per], axis=0).T for k in range(0, len(values), per)]
    values = jnp.concatenate(values, axis=1).astype(BF16)
    nodes = disp_t.shape[1]
    for c in range(3):
        cols = slice(c * nodes, (c + 1) * nodes)
        part = free_t[:, cols] - dot(values, corner_t[:, cols])
        disp_t[c * LANES : (c + 1) * LANES, :] = part.astype(BF16)

    step = 32
    pairs = onehot.shape[1] // (2 * LANES)
    for pair in range(pairs):
        elem_t = dot(disp_t[...], onehot[:, 2 * LANES * pair : 2 * LANES * (pair + 1)])
        for start in range(0, LANES, step):
            sums = [None] * COMPS if pair == 0 else [sofar[i, start : start + step, :] for i in range(COMPS)]
            for half in range(2):
                for c in range(3):
                    x = elem_t[c * LANES + start : c * LANES + start + step, half * LANES : (half + 1) * LANES]
                    x = x.reshape(step // 8, 8, LANES)
                    for i in range(COMPS):
                        term = scaled[24 * i + 3 * (2 * pair + half) + c] * x
                        term = term.reshape(step, LANES)
                        sums[i] = term if sums[i] is None else sums[i] + term
            for i in range(COMPS):
                if pair < pairs - 1:
                    sofar[i, start : start + step, :] = sums[i]
                else:
                    high, low = split_two(sums[i])
                    stress[i * LANES + start : i * LANES + start + step, 0:LANES] = high
                    stress[i * LANES + start : i * LANES + start + step, LANES : 2 * LANES] = low

    rows = dot_nt(face[...], stress[...])
    for i in range(COMPS):
        part = rows[:, i * LANES : (i + 1) * LANES]
        edge = [part[EDGES + NED * k : EDGES + NED * (k + 1)] for k in range(4)]
        sub_a[i] = part[:NIS]
        sub_b[i] = part[NIS : 2 * NIS]
        grp_a[i] = jnp.concatenate([part[2 * NIS : 2 * NIS + NIG], edge[0], edge[2]], axis=0)
        grp_b[i] = jnp.concatenate([part[2 * NIS + NIG : EDGES], edge[1], edge[3]], axis=0)


def edge_kernel(grp_a, grp_b, from_a, from_b, edge_b, edge_a):
    split = NIG + NED
    edge_a[:, :NED, :] = grp_a[:, NIG:split, :] + from_a[:, NIG:split, :]
    edge_a[:, NED:, :] = grp_b[:, NIG:split, :] + from_b[:, NIG:split, :]
    edge_b[:, :NED, :] = grp_a[:, split:, :] + from_a[:, split:, :]
    edge_b[:, NED:, :] = grp_b[:, split:, :] + from_b[:, split:, :]


def partial_kernel(
    count, stress, disp_t, placing, grp_a, grp_b, partial, disp_out, received
):
    for c in range(3):
        for k in range(0, disp_out.shape[1], LANES):
            part = disp_t[c * LANES : (c + 1) * LANES, k : k + LANES].astype(F32).T
            disp_out[c, k : k + LANES, :] = part.astype(BF16)
    split = NIG + NED
    for i in range(COMPS):
        low, high = grp_a[i], grp_b[i]
        rows = [low[:NIG], high[:NIG], low[NIG:split], high[NIG:split], low[split:], high[split:]]
        rows.append(jnp.zeros((2 * LANES - NIF, LANES), F32))
        first, second = split_two(jnp.concatenate(rows, axis=0))
        received[:LANES, i * LANES : (i + 1) * LANES] = first
        received[LANES:, i * LANES : (i + 1) * LANES] = second
    for i in range(0, COMPS, 2):
        cols = slice(i * LANES, (i + 2) * LANES)
        own = dot_nt(count[...], stress[cols, :])
        total = own + dot(placing[...], received[:, cols])
        partial[i] = total[:, :LANES]
        partial[i + 1] = total[:, LANES:]


def finish_kernel(
    placing, partial, inverse_volume, sub_a, sub_b, edge_b, edge_a, out, received, nodal, sems
):
    for i in range(COMPS):
        cols = slice(i * LANES, (i + 1) * LANES)
        late = jnp.concatenate([sub_b[i], edge_a[i], edge_b[i]], axis=0)
        first, second = split_two(late)
        received[:NIS, cols] = sub_a[i].astype(BF16)
        received[NIS : NIS + LATE, cols] = first
        received[NIS + LATE :, cols] = second
    scale = inverse_volume[...]
    copies = []
    for i in range(0, COMPS, 2):
        cols = slice(i * LANES, (i + 2) * LANES)
        added = dot(placing[...], received[:, cols])
        nodal[i] = ((partial[i] + added[:, :LANES]) * scale).astype(BF16)
        nodal[i + 1] = ((partial[i + 1] + added[:, LANES:]) * scale).astype(BF16)
        copy = pltpu.make_async_copy(nodal.at[pl.ds(i, 2)], out.at[pl.ds(i, 2)], sems.at[i // 2])
        copy.start()
        copies.append(copy)
    for copy in copies:
        copy.wait()


def vmem(count):
    return [pl.BlockSpec(memory_space=pltpu.VMEM)] * count


def anywhere(count):
    return [pl.BlockSpec(memory_space=pl.ANY)] * count


def hbm(count):
    return [pl.BlockSpec(memory_space=pltpu.HBM)] * count


def array(shape, dtype=F32):
    return jax.ShapeDtypeStruct(shape, dtype)


def call(kernel, name, out_shape, in_specs, scratch=(), flops=0, moved=0, out_specs=None):
    return pl.pallas_call(
        kernel,
        name=name,
        out_shape=out_shape,
        in_specs=in_specs,
        out_specs=out_specs or vmem(len(out_shape)),
        scratch_shapes=list(scratch),
        compiler_params=pltpu.CompilerParams(vmem_limit_bytes=VMEM_LIMIT),
        cost_estimate=pl.CostEstimate(flops=flops, bytes_accessed=moved, transcendentals=0),
    )


def exchange(block, axis, first):
    count = lax.axis_size(axis)
    pairs = []
    for i in range(first, count - 1, 2):
        pairs += [(i, i + 1), (i + 1, i)]
    return lax.ppermute(block, axis, pairs)


def in_hbm(*arrays):
    return [pltpu.with_memory_space_constraint(x, pltpu.HBM) for x in arrays]


def gather_near(coarse, own, ahead):
    beyond = exchange(coarse, "sub", 1)
    beside = exchange(coarse, "sub", 0)
    parts = [own, beside, beyond]
    distance = lax.axis_size("grp") // 2
    while distance:
        rows = sum(x.shape[0] for x in parts)
        before, ahead = ahead[:1], ahead[1:]

        def join(*refs, skip=len(before)):
            join_kernel(*refs[: len(refs) - 1 - skip], refs[-1])

        (block,) = call(
            join,
            "join_blocks",
            (array((rows, parts[0].shape[1])),),
            vmem(len(parts)) + anywhere(len(before)),
        )(*parts, *before)
        pairs = [(i, i ^ distance) for i in range(lax.axis_size("grp"))]
        parts = [block, lax.ppermute(block, "grp", pairs)]
        distance //= 2
    return parts


def shards(
    coarse,
    corner_idx,
    coupling,
    force,
    panel_inv,
    panel_nodes,
    strain_disp,
    modulus,
    connect,
    interface,
    nodal_volume,
):
    nodes, _, cases = force.shape
    dofs = 3 * nodes
    q = corner_idx.shape[1]

    def lists(*refs):
        prepare_lists(coarse.shape[0], lax.axis_size("grp"), *refs)

    own, select, onehot, face, scaled, count, placing, placing_last, inverse_volume = call(
        lists,
        "prepare_lists",
        (
            array(coarse.shape),
            array((TERM, 3 * LANES), BF16),
            array((nodes, CORNERS * LANES), BF16),
            array((NIF, 2 * LANES), BF16),
            array((COMPS * 24, 8, LANES)),
            array((nodes, 2 * LANES), BF16),
            array((nodes, 2 * LANES), BF16),
            array((nodes, 2 * LANES), BF16),
            array((nodes, LANES)),
        ),
        hbm(7),
        (
            pltpu.VMEM((1, q), jnp.int32),
            pltpu.VMEM(connect.shape, jnp.int32),
            pltpu.VMEM(interface.shape, jnp.int32),
            pltpu.VMEM(strain_disp.shape, BF16),
            pltpu.VMEM((1, LANES), F32),
            pltpu.VMEM((nodes // LANES, LANES), F32),
            pltpu.VMEM((8, 2 * LANES), F32),
            pltpu.SemaphoreType.DMA((7,)),
        ),
        flops=100000000,
        moved=4000000,
    )(
        *in_hbm(
            corner_idx,
            connect,
            interface,
            strain_disp,
            modulus.reshape(1, -1),
            nodal_volume.reshape(-1, LANES),
            coarse,
        )
    )
    panel_rows = panel_inv.shape[1]
    free_t, corner_t = call(
        prepare_panels,
        "prepare_panels",
        (array((cases, dofs)), array((2 * LANES, dofs), BF16)),
        hbm(4),
        (
            pltpu.VMEM(panel_nodes.shape, jnp.int32),
            pltpu.VMEM((q, dofs), BF16),
            pltpu.VMEM((3, nodes, cases), BF16),
            pltpu.VMEM(panel_inv.shape, BF16),
            pltpu.VMEM((dofs, cases), F32),
            pltpu.VMEM((2, panel_rows, LANES), F32),
            pltpu.SemaphoreType.DMA((4,)),
        ),
        flops=400000000,
        moved=4000000,
    )(*in_hbm(panel_nodes, coupling.T, jnp.transpose(force, (1, 0, 2)), panel_inv))

    near = gather_near(coarse, own, [select, corner_t])
    disp_t, stress, sub_a, sub_b, grp_a, grp_b = call(
        solve_kernel,
        "solve_and_stress",
        (
            array((3 * cases, nodes), BF16),
            array((COMPS * cases, 2 * LANES), BF16),
            array((COMPS, NIS, cases)),
            array((COMPS, NIS, cases)),
            array((COMPS, NIG + 2 * NED, cases)),
            array((COMPS, NIG + 2 * NED, cases)),
        ),
        vmem(8),
        (
            pltpu.VMEM((3, 3 * LANES, cases), BF16),
            pltpu.VMEM((COMPS, cases, LANES), F32),
        ),
        flops=1000000000,
        moved=4000000,
    )(*near, free_t, corner_t, select, onehot, face, scaled)
    from_sub_a = exchange(sub_a, "sub", 0)
    from_grp_a = exchange(grp_a, "grp", 0)
    from_grp_b = exchange(grp_b, "grp", 1)
    edge_b, edge_a = call(
        edge_kernel,
        "sum_edges",
        (array((COMPS, 2 * NED, cases)), array((COMPS, 2 * NED, cases))),
        vmem(4),
    )(grp_a, grp_b, from_grp_a, from_grp_b)
    from_sub_b = exchange(sub_b, "sub", 1)
    from_edge_b = exchange(edge_b, "sub", 1)
    from_edge_a = exchange(edge_a, "sub", 0)
    partial, disp = call(
        partial_kernel,
        "assemble_nodes",
        (array((COMPS, nodes, cases)), array((3, nodes, cases), BF16)),
        vmem(6),
        (pltpu.VMEM((2 * LANES, COMPS * cases), BF16),),
        flops=400000000,
        moved=2000000,
    )(count, stress, disp_t, placing, from_grp_a, from_grp_b)
    (nodal,) = call(
        finish_kernel,
        "add_last",
        (array((COMPS, nodes, cases), BF16),),
        vmem(7),
        (
            pltpu.VMEM((NIS + 2 * LATE, COMPS * cases), BF16),
            pltpu.VMEM((COMPS, nodes, cases), BF16),
            pltpu.SemaphoreType.DMA((COMPS // 2,)),
        ),
        flops=400000000,
        moved=3000000,
        out_specs=hbm(1),
    )(placing_last, partial, inverse_volume, from_sub_a, from_sub_b, from_edge_b, from_edge_a)
    return jnp.transpose(disp, (1, 0, 2)), jnp.transpose(nodal, (1, 0, 2))


def solution(mesh):
    owner = ("sub", "grp")
    placed = (
        P(owner, None),
        P(owner, None),
        P(owner, None),
        P(owner, None, None),
        P(owner, None, None),
        P(owner, None),
        P(None, None, owner),
        P(owner),
        P(None, owner),
        P(owner, None),
        P(owner),
    )
    return jax.shard_map(
        shards,
        mesh=mesh,
        in_specs=placed,
        out_specs=(P(owner, None, None), P(owner, None, None)),
        check_vma=False,
    )
```

```python
import jax
import jax.numpy as jnp
from jax import lax
from jax.experimental import pallas as pl
from jax.experimental.pallas import tpu as pltpu
from jax.sharding import PartitionSpec as P

NIS = 64
NIG = 32
NED = 8
EDGES = 2 * NIS + 2 * NIG
NIF = EDGES + 4 * NED
LATE = NIS + 4 * NED
CORNERS = 8
COMPS = 6
LANES = 128
TERM = 32
TERMS = ((0, 0), (0, 1), (0, 2), (1, 0), (1, 1), (2, 0))

POISSON = 0.3
LAME = POISSON / ((1.0 + POISSON) * (1.0 - 2.0 * POISSON))
SHEAR = 0.5 / (1.0 + POISSON)

F32 = jnp.float32
BF16 = jnp.bfloat16
VMEM_LIMIT = 24 * 1024 * 1024


def split_two(x):
    high = x.astype(BF16)
    return high, (x - high.astype(F32)).astype(BF16)


def split_three(x):
    high = x.astype(BF16)
    rest = x - high.astype(F32)
    middle = rest.astype(BF16)
    return high, middle, (rest - middle.astype(F32)).astype(BF16)


def dot(a, b):
    return jnp.dot(a, b, preferred_element_type=F32)


def dot_nt(a, b):
    return lax.dot_general(a, b, (((1,), (1,)), ((), ())), preferred_element_type=F32)


def column(row):
    return jnp.broadcast_to(row, (LANES, LANES)).T


def swap_lanes(x, distance):
    lane = lax.broadcasted_iota(jnp.int32, x.shape, 1)
    after = pltpu.roll(x, LANES - distance, 1)
    before = pltpu.roll(x, distance, 1)
    return jnp.where((lane & distance) == 0, after, before)


def order_lists(ids):
    sub_even = (lax.axis_index("sub") & 1) == 0
    grp_even = (lax.axis_index("grp") & 1) == 0
    first, second = ids[:, :LANES], ids[:, LANES:]
    ids[:, :LANES] = jnp.where(sub_even, swap_lanes(first, NIS), first)
    lane = lax.broadcasted_iota(jnp.int32, second.shape, 1)
    groups = jnp.where(grp_even, swap_lanes(second, NIG), second)
    edges = jnp.where(sub_even, swap_lanes(second, 2 * NED), second)
    edges = jnp.where(grp_even, swap_lanes(edges, NED), edges)
    ids[:, LANES:] = jnp.where(lane < 2 * NIG, groups, edges)


def start_copies(pairs, sems):
    copies = [pltpu.make_async_copy(src, dst, sems.at[k]) for k, (src, dst) in enumerate(pairs)]
    for copy in copies:
        copy.start()
    return copies


def prepare_lists(
    block_rows,
    members,
    corner_idx,
    connect,
    interface,
    strain_disp,
    modulus,
    volume,
    coarse,
    own,
    select,
    onehot,
    face,
    scaled,
    count,
    placing,
    placing_last,
    inverse_volume,
    corner_v,
    connect_v,
    interface_v,
    strain_v,
    modulus_v,
    volume_v,
    ids,
    sems,
):
    copies = start_copies(
        [
            (connect, connect_v),
            (interface, interface_v),
            (corner_idx, corner_v),
            (modulus, modulus_v),
            (strain_disp, strain_v),
            (volume, volume_v),
            (coarse, own),
        ],
        sems,
    )
    nodes = onehot.shape[0]
    q = corner_idx.shape[1]

    copies[0].wait()
    node_of = lax.broadcasted_iota(jnp.int32, (nodes, LANES), 0)
    total = jnp.zeros((nodes, LANES), F32)
    for a in range(CORNERS):
        hit = jnp.where(connect_v[a : a + 1, :] == node_of, 1.0, 0.0)
        onehot[:, a * LANES : (a + 1) * LANES] = hit.astype(BF16)
        total = total + hit
    total = total.astype(BF16)
    count[:, :LANES] = total
    count[:, LANES:] = total

    copies[1].wait()
    ids[...] = jnp.full(ids.shape, -1.0, F32)
    ids[0:1, 0:NIF] = interface_v[...].astype(F32)
    order_lists(ids)
    lane = lax.broadcasted_iota(jnp.int32, (8, LANES), 1)
    edges = pltpu.roll(ids[:, LANES:], LANES - NIS, 1)
    again = pltpu.roll(ids[:, :LANES], LANES - NIS + 4 * NED, 1)
    last = jnp.where(lane < 4 * NED, edges, again)
    last = jnp.where(lane < LATE, last, pltpu.roll(edges, LATE, 1))
    for row, target in ((ids[0:1, LANES:], 0), (ids[0:1, :LANES], 1), (last[0:1], 2)):
        hit = jnp.where(row.astype(jnp.int32) == node_of, 1.0, 0.0).astype(BF16)
        if target == 0:
            placing[:, :LANES] = hit
            placing[:, LANES:] = hit
        else:
            placing_last[:, (target - 1) * LANES : target * LANES] = hit
    connect_f = connect_v[...].astype(F32)
    for half in range(2):
        id_col = column(ids[0:1, half * LANES : (half + 1) * LANES])
        rows = jnp.zeros((LANES, LANES), F32)
        for a in range(CORNERS):
            rows = rows + jnp.where(connect_f[a : a + 1, :] == id_col, 1.0, 0.0)
        rows = rows.astype(BF16)[: min(LANES, NIF - half * LANES)]
        face[half * LANES : half * LANES + rows.shape[0], :LANES] = rows
        face[half * LANES : half * LANES + rows.shape[0], LANES:] = rows

    copies[2].wait()
    ids[0:1, 0:q] = corner_v[...].astype(F32)
    wanted = column(ids[0:1, :LANES])[:TERM]
    lane = lax.broadcasted_iota(jnp.int32, (TERM, 3 * LANES), 1)
    entry = lax.broadcasted_iota(jnp.int32, (TERM, LANES), 0)
    s, g = lax.axis_index("sub"), lax.axis_index("grp")
    aside = 1 - 2 * (s & 1)
    row = jnp.full((TERM, 3 * LANES), -1, jnp.int32)
    base = 0
    for member in range(members):
        distance, bits, turn = members // 2, member, 0
        while distance:
            turn += (bits & 1) * distance
            distance, bits = distance // 2, bits >> 1
        for owner in (s, s + aside, s - aside):
            first = (owner * members + (g ^ turn)) * block_rows
            row = jnp.where((lane >= base) & (lane < base + block_rows), first - base + lane, row)
            base += block_rows
    for b in range(3):
        cols = slice(b * LANES, (b + 1) * LANES)
        hit = (wanted == row[:, cols].astype(F32)) & (entry < q)
        select[:, cols] = jnp.where(hit, 1.0, 0.0).astype(BF16)

    copies[3].wait()
    copies[4].wait()
    factor = modulus_v[...]
    rows = [strain_v[i].astype(F32) for i in range(COMPS)]
    trace = (rows[0] + rows[1] + rows[2]) * LAME
    for i in range(COMPS):
        value = trace + rows[i] * (2.0 * SHEAR) if i < 3 else rows[i] * SHEAR
        scaled[24 * i : 24 * (i + 1)] = jnp.broadcast_to((value * factor)[:, None, :], (24, 8, LANES))

    copies[5].wait()
    for k in range(nodes // LANES):
        inverse_volume[k * LANES : (k + 1) * LANES, :] = column(1.0 / volume_v[k : k + 1, :])
    copies[6].wait()


def prepare_panels(
    panel_nodes,
    coupling,
    force,
    panel_inv,
    free_t,
    corner_t,
    panel_v,
    coupling_v,
    force_v,
    inverse,
    loads,
    solved,
    sems,
):
    copies = start_copies(
        [
            (panel_nodes, panel_v),
            (coupling, coupling_v),
            (force, force_v),
            (panel_inv, inverse),
        ],
        sems,
    )
    panels, panel_rows, _ = inverse.shape
    panel_size = panel_rows // 3
    nodes = force_v.shape[1]
    q = coupling_v.shape[0]

    copies[0].wait()
    copies[1].wait()
    copies[2].wait()
    for c in range(3):
        loads[pl.ds(c, nodes, stride=3), :] = force_v[c].astype(F32)
    corner_t[len(TERMS) * TERM :, :] = jnp.zeros((corner_t.shape[0] - len(TERMS) * TERM, 3 * nodes), BF16)
    row_of = lax.broadcasted_iota(jnp.int32, (panel_rows, LANES), 0)
    lane = lax.broadcasted_iota(jnp.int32, (panel_rows, LANES), 1)
    copies[3].wait()
    for p in range(panels):
        start = p * panel_rows
        live = row_of < 3 * panel_v[0:1, p : p + 1]
        columns = []
        for k in range(panel_rows // LANES):
            part = coupling_v[:, start + k * LANES : start + (k + 1) * LANES].astype(F32)
            columns.append(jnp.concatenate([part, jnp.zeros((LANES - q, LANES), F32)], axis=0).T)
        sides = [loads[start : start + panel_rows, :], jnp.concatenate(columns, axis=0)]
        sides = jnp.concatenate([jnp.where(live, x, 0.0).astype(BF16) for x in sides], axis=1)
        result = dot(inverse[p], sides)
        for side in range(2):
            solved[side] = jnp.where(live, result[:, side * LANES : (side + 1) * LANES], 0.0)
        for c in range(3):
            cols = slice(c * nodes + p * panel_size, c * nodes + (p + 1) * panel_size)
            free_t[:, cols] = solved[0, pl.ds(c, panel_size, stride=3), :].T
            value = solved[1, pl.ds(c, panel_size, stride=3), :].T[:TERM]
            pieces = split_three(value)
            for k, (piece, _) in enumerate(TERMS):
                corner_t[k * TERM : (k + 1) * TERM, cols] = pieces[piece]


def join_kernel(*refs):
    *parts, out = refs
    start = 0
    for part in parts:
        out[start : start + part.shape[0], :] = part[...]
        start += part.shape[0]


def solve_kernel(
    near,
    across,
    free_t,
    corner_t,
    select,
    onehot,
    face,
    scaled,
    disp_t,
    stress,
    sub_a,
    sub_b,
    grp_a,
    grp_b,
    terms,
    sofar,
):
    rows = near.shape[0]
    terms[:, 2 * rows :, :] = jnp.zeros((3, terms.shape[1] - 2 * rows, terms.shape[2]), BF16)
    for b, block in enumerate((near, across)):
        for t, value in enumerate(split_three(block[...])):
            terms[t, b * rows : (b + 1) * rows, :] = value
    picked = [dot(select[...], terms[t]) for t in range(3)]
    values = [picked[term] for _, term in TERMS]
    values += [jnp.zeros_like(picked[0])] * (corner_t.shape[0] // TERM - len(values))
    per = LANES // TERM
    values = [jnp.concatenate(values[k : k + per], axis=0).T for k in range(0, len(values), per)]
    values = jnp.concatenate(values, axis=1).astype(BF16)
    nodes = disp_t.shape[1]
    for c in range(3):
        cols = slice(c * nodes, (c + 1) * nodes)
        part = free_t[:, cols] - dot(values, corner_t[:, cols])
        disp_t[c * LANES : (c + 1) * LANES, :] = part.astype(BF16)

    step = 32
    pairs = onehot.shape[1] // (2 * LANES)
    for pair in range(pairs):
        elem_t = dot(disp_t[...], onehot[:, 2 * LANES * pair : 2 * LANES * (pair + 1)])
        for start in range(0, LANES, step):
            sums = [None] * COMPS if pair == 0 else [sofar[i, start : start + step, :] for i in range(COMPS)]
            for half in range(2):
                for c in range(3):
                    x = elem_t[c * LANES + start : c * LANES + start + step, half * LANES : (half + 1) * LANES]
                    x = x.reshape(step // 8, 8, LANES)
                    for i in range(COMPS):
                        term = scaled[24 * i + 3 * (2 * pair + half) + c] * x
                        term = term.reshape(step, LANES)
                        sums[i] = term if sums[i] is None else sums[i] + term
            for i in range(COMPS):
                if pair < pairs - 1:
                    sofar[i, start : start + step, :] = sums[i]
                else:
                    high, low = split_two(sums[i])
                    stress[i * LANES + start : i * LANES + start + step, 0:LANES] = high
                    stress[i * LANES + start : i * LANES + start + step, LANES : 2 * LANES] = low

    rows = dot_nt(face[...], stress[...])
    for i in range(COMPS):
        part = rows[:, i * LANES : (i + 1) * LANES]
        edge = [part[EDGES + NED * k : EDGES + NED * (k + 1)] for k in range(4)]
        sub_a[i] = part[:NIS]
        sub_b[i] = part[NIS : 2 * NIS]
        grp_a[i] = jnp.concatenate([part[2 * NIS : 2 * NIS + NIG], edge[0], edge[2]], axis=0)
        grp_b[i] = jnp.concatenate([part[2 * NIS + NIG : EDGES], edge[1], edge[3]], axis=0)


def edge_kernel(grp_b, grp_a, from_b, from_a, edge_b, edge_a):
    split = NIG + NED
    edge_a[:, :NED, :] = grp_a[:, NIG:split, :] + from_a[:, NIG:split, :]
    edge_a[:, NED:, :] = grp_b[:, NIG:split, :] + from_b[:, NIG:split, :]
    edge_b[:, :NED, :] = grp_a[:, split:, :] + from_a[:, split:, :]
    edge_b[:, NED:, :] = grp_b[:, split:, :] + from_b[:, split:, :]


def partial_kernel(
    count, stress, disp_t, placing, grp_b, grp_a, partial, disp_out, received
):
    for c in range(3):
        for k in range(0, disp_out.shape[1], LANES):
            part = disp_t[c * LANES : (c + 1) * LANES, k : k + LANES].astype(F32).T
            disp_out[c, k : k + LANES, :] = part.astype(BF16)
    split = NIG + NED
    for i in range(COMPS):
        low, high = grp_a[i], grp_b[i]
        rows = [low[:NIG], high[:NIG], low[NIG:split], high[NIG:split], low[split:], high[split:]]
        rows.append(jnp.zeros((2 * LANES - NIF, LANES), F32))
        first, second = split_two(jnp.concatenate(rows, axis=0))
        received[:LANES, i * LANES : (i + 1) * LANES] = first
        received[LANES:, i * LANES : (i + 1) * LANES] = second
    for i in range(0, COMPS, 2):
        cols = slice(i * LANES, (i + 2) * LANES)
        own = dot_nt(count[...], stress[cols, :])
        total = own + dot(placing[...], received[:, cols])
        partial[i] = total[:, :LANES]
        partial[i + 1] = total[:, LANES:]


def finish_kernel(
    placing, partial, inverse_volume, sub_a, sub_b, edge_b, edge_a, out, received, nodal, sems
):
    for i in range(COMPS):
        cols = slice(i * LANES, (i + 1) * LANES)
        late = jnp.concatenate([sub_b[i], edge_a[i], edge_b[i]], axis=0)
        first, second = split_two(late)
        received[:NIS, cols] = sub_a[i].astype(BF16)
        received[NIS : NIS + LATE, cols] = first
        received[NIS + LATE :, cols] = second
    scale = inverse_volume[...]
    copies = []
    for i in range(0, COMPS, 2):
        cols = slice(i * LANES, (i + 2) * LANES)
        added = dot(placing[...], received[:, cols])
        nodal[i] = ((partial[i] + added[:, :LANES]) * scale).astype(BF16)
        nodal[i + 1] = ((partial[i + 1] + added[:, LANES:]) * scale).astype(BF16)
        copy = pltpu.make_async_copy(nodal.at[pl.ds(i, 2)], out.at[pl.ds(i, 2)], sems.at[i // 2])
        copy.start()
        copies.append(copy)
    for copy in copies:
        copy.wait()


def vmem(count):
    return [pl.BlockSpec(memory_space=pltpu.VMEM)] * count


def anywhere(count):
    return [pl.BlockSpec(memory_space=pl.ANY)] * count


def hbm(count):
    return [pl.BlockSpec(memory_space=pltpu.HBM)] * count


def array(shape, dtype=F32):
    return jax.ShapeDtypeStruct(shape, dtype)


def call(kernel, name, out_shape, in_specs, scratch=(), flops=0, moved=0, out_specs=None):
    return pl.pallas_call(
        kernel,
        name=name,
        out_shape=out_shape,
        in_specs=in_specs,
        out_specs=out_specs or vmem(len(out_shape)),
        scratch_shapes=list(scratch),
        compiler_params=pltpu.CompilerParams(vmem_limit_bytes=VMEM_LIMIT),
        cost_estimate=pl.CostEstimate(flops=flops, bytes_accessed=moved, transcendentals=0),
    )


def exchange(block, axis, first):
    count = lax.axis_size(axis)
    pairs = []
    for i in range(first, count - 1, 2):
        pairs += [(i, i + 1), (i + 1, i)]
    return lax.ppermute(block, axis, pairs)


def in_hbm(*arrays):
    return [pltpu.with_memory_space_constraint(x, pltpu.HBM) for x in arrays]


def gather_near(coarse, own, ahead):
    beyond = exchange(coarse, "sub", 1)
    beside = exchange(coarse, "sub", 0)
    parts = [own, beside, beyond]
    distance = lax.axis_size("grp") // 2
    while distance:
        rows = sum(x.shape[0] for x in parts)
        before, ahead = ahead[:1], ahead[1:]

        def join(*refs, skip=len(before)):
            join_kernel(*refs[: len(refs) - 1 - skip], refs[-1])

        (block,) = call(
            join,
            "join_blocks",
            (array((rows, parts[0].shape[1])),),
            vmem(len(parts)) + anywhere(len(before)),
        )(*parts, *before)
        pairs = [(i, i ^ distance) for i in range(lax.axis_size("grp"))]
        parts = [block, lax.ppermute(block, "grp", pairs)]
        distance //= 2
    return parts


def shards(
    coarse,
    corner_idx,
    coupling,
    force,
    panel_inv,
    panel_nodes,
    strain_disp,
    modulus,
    connect,
    interface,
    nodal_volume,
):
    nodes, _, cases = force.shape
    dofs = 3 * nodes
    q = corner_idx.shape[1]

    def lists(*refs):
        prepare_lists(coarse.shape[0], lax.axis_size("grp"), *refs)

    own, select, onehot, face, scaled, count, placing, placing_last, inverse_volume = call(
        lists,
        "prepare_lists",
        (
            array(coarse.shape),
            array((TERM, 3 * LANES), BF16),
            array((nodes, CORNERS * LANES), BF16),
            array((NIF, 2 * LANES), BF16),
            array((COMPS * 24, 8, LANES)),
            array((nodes, 2 * LANES), BF16),
            array((nodes, 2 * LANES), BF16),
            array((nodes, 2 * LANES), BF16),
            array((nodes, LANES)),
        ),
        hbm(7),
        (
            pltpu.VMEM((1, q), jnp.int32),
            pltpu.VMEM(connect.shape, jnp.int32),
            pltpu.VMEM(interface.shape, jnp.int32),
            pltpu.VMEM(strain_disp.shape, BF16),
            pltpu.VMEM((1, LANES), F32),
            pltpu.VMEM((nodes // LANES, LANES), F32),
            pltpu.VMEM((8, 2 * LANES), F32),
            pltpu.SemaphoreType.DMA((7,)),
        ),
        flops=100000000,
        moved=4000000,
    )(
        *in_hbm(
            corner_idx,
            connect,
            interface,
            strain_disp,
            modulus.reshape(1, -1),
            nodal_volume.reshape(-1, LANES),
            coarse,
        )
    )
    panel_rows = panel_inv.shape[1]
    free_t, corner_t = call(
        prepare_panels,
        "prepare_panels",
        (array((cases, dofs)), array((2 * LANES, dofs), BF16)),
        hbm(4),
        (
            pltpu.VMEM(panel_nodes.shape, jnp.int32),
            pltpu.VMEM((q, dofs), BF16),
            pltpu.VMEM((3, nodes, cases), BF16),
            pltpu.VMEM(panel_inv.shape, BF16),
            pltpu.VMEM((dofs, cases), F32),
            pltpu.VMEM((2, panel_rows, LANES), F32),
            pltpu.SemaphoreType.DMA((4,)),
        ),
        flops=400000000,
        moved=4000000,
    )(*in_hbm(panel_nodes, coupling.T, jnp.transpose(force, (1, 0, 2)), panel_inv))

    near = gather_near(coarse, own, [select, corner_t])
    disp_t, stress, sub_a, sub_b, grp_a, grp_b = call(
        solve_kernel,
        "solve_and_stress",
        (
            array((3 * cases, nodes), BF16),
            array((COMPS * cases, 2 * LANES), BF16),
            array((COMPS, NIS, cases)),
            array((COMPS, NIS, cases)),
            array((COMPS, NIG + 2 * NED, cases)),
            array((COMPS, NIG + 2 * NED, cases)),
        ),
        vmem(8),
        (
            pltpu.VMEM((3, 3 * LANES, cases), BF16),
            pltpu.VMEM((COMPS, cases, LANES), F32),
        ),
        flops=1000000000,
        moved=4000000,
    )(*near, free_t, corner_t, select, onehot, face, scaled)
    from_sub_a = exchange(sub_a, "sub", 0)
    from_grp_b = exchange(grp_b, "grp", 1)
    from_grp_a = exchange(grp_a, "grp", 0)
    edge_b, edge_a = call(
        edge_kernel,
        "sum_edges",
        (array((COMPS, 2 * NED, cases)), array((COMPS, 2 * NED, cases))),
        vmem(4),
    )(grp_b, grp_a, from_grp_b, from_grp_a)
    from_sub_b = exchange(sub_b, "sub", 1)
    from_edge_b = exchange(edge_b, "sub", 1)
    from_edge_a = exchange(edge_a, "sub", 0)
    partial, disp = call(
        partial_kernel,
        "assemble_nodes",
        (array((COMPS, nodes, cases)), array((3, nodes, cases), BF16)),
        vmem(6),
        (pltpu.VMEM((2 * LANES, COMPS * cases), BF16),),
        flops=400000000,
        moved=2000000,
    )(count, stress, disp_t, placing, from_grp_b, from_grp_a)
    (nodal,) = call(
        finish_kernel,
        "add_last",
        (array((COMPS, nodes, cases), BF16),),
        vmem(7),
        (
            pltpu.VMEM((NIS + 2 * LATE, COMPS * cases), BF16),
            pltpu.VMEM((COMPS, nodes, cases), BF16),
            pltpu.SemaphoreType.DMA((COMPS // 2,)),
        ),
        flops=400000000,
        moved=3000000,
        out_specs=hbm(1),
    )(placing_last, partial, inverse_volume, from_sub_a, from_sub_b, from_edge_b, from_edge_a)
    return jnp.transpose(disp, (1, 0, 2)), jnp.transpose(nodal, (1, 0, 2))


def solution(mesh):
    owner = ("sub", "grp")
    placed = (
        P(owner, None),
        P(owner, None),
        P(owner, None),
        P(owner, None, None),
        P(owner, None, None),
        P(owner, None),
        P(None, None, owner),
        P(owner),
        P(None, owner),
        P(owner, None),
        P(owner),
    )
    return jax.shard_map(
        shards,
        mesh=mesh,
        in_specs=placed,
        out_specs=(P(owner, None, None), P(owner, None, None)),
        check_vma=False,
    )
```

```python
import jax
import jax.numpy as jnp
from jax import lax
from jax.experimental import pallas as pl
from jax.experimental.pallas import tpu as pltpu
from jax.sharding import PartitionSpec as P

NIS = 64
NIG = 32
NED = 8
EDGES = 2 * NIS + 2 * NIG
NIF = EDGES + 4 * NED
LATE = NIS + 4 * NED
CORNERS = 8
COMPS = 6
LANES = 128
TERM = 32
TERMS = ((0, 0), (0, 1), (0, 2), (1, 0), (1, 1), (2, 0))

POISSON = 0.3
LAME = POISSON / ((1.0 + POISSON) * (1.0 - 2.0 * POISSON))
SHEAR = 0.5 / (1.0 + POISSON)

F32 = jnp.float32
BF16 = jnp.bfloat16
VMEM_LIMIT = 24 * 1024 * 1024


def split_two(x):
    high = x.astype(BF16)
    return high, (x - high.astype(F32)).astype(BF16)


def split_three(x):
    high = x.astype(BF16)
    rest = x - high.astype(F32)
    middle = rest.astype(BF16)
    return high, middle, (rest - middle.astype(F32)).astype(BF16)


def dot(a, b):
    return jnp.dot(a, b, preferred_element_type=F32)


def dot_nt(a, b):
    return lax.dot_general(a, b, (((1,), (1,)), ((), ())), preferred_element_type=F32)


def column(row):
    return jnp.broadcast_to(row, (LANES, LANES)).T


def swap_lanes(x, distance):
    lane = lax.broadcasted_iota(jnp.int32, x.shape, 1)
    after = pltpu.roll(x, LANES - distance, 1)
    before = pltpu.roll(x, distance, 1)
    return jnp.where((lane & distance) == 0, after, before)


def order_lists(ids):
    sub_even = (lax.axis_index("sub") & 1) == 0
    grp_even = (lax.axis_index("grp") & 1) == 0
    first, second = ids[:, :LANES], ids[:, LANES:]
    ids[:, :LANES] = jnp.where(sub_even, swap_lanes(first, NIS), first)
    lane = lax.broadcasted_iota(jnp.int32, second.shape, 1)
    groups = jnp.where(grp_even, swap_lanes(second, NIG), second)
    edges = jnp.where(sub_even, swap_lanes(second, 2 * NED), second)
    edges = jnp.where(grp_even, swap_lanes(edges, NED), edges)
    ids[:, LANES:] = jnp.where(lane < 2 * NIG, groups, edges)


def element_stress(terms, rows, onehot, scaled, sofar, store):
    step = 32
    pairs = onehot.shape[1] // (2 * LANES)
    for pair in range(pairs):
        operand = onehot[:, 2 * LANES * pair : 2 * LANES * (pair + 1)]
        elem = dot(terms[0], operand)
        for term in terms[1:]:
            elem = elem + dot(term, operand)
        for start in range(0, rows, step):
            sums = [None] * COMPS if pair == 0 else [sofar[i, start : start + step, :] for i in range(COMPS)]
            for half in range(2):
                for c in range(3):
                    x = elem[c * rows + start : c * rows + start + step, half * LANES : (half + 1) * LANES]
                    x = x.reshape(step // 8, 8, LANES)
                    for i in range(COMPS):
                        term = scaled[24 * i + 3 * (2 * pair + half) + c] * x
                        term = term.reshape(step, LANES)
                        sums[i] = term if sums[i] is None else sums[i] + term
            for i in range(COMPS):
                if pair < pairs - 1:
                    sofar[i, start : start + step, :] = sums[i]
                else:
                    store(i, start, sums[i])


def free_stress(free_t, first, rows, onehot, scaled, sofar, out):
    nodes = onehot.shape[0]
    parts = [free_t[first : first + rows, c * nodes : (c + 1) * nodes] for c in range(3)]

    def store(i, start, value):
        out[i, start : start + value.shape[0], :] = value

    element_stress(split_two(jnp.concatenate(parts, axis=0)), rows, onehot, scaled, sofar, store)


def start_copies(pairs, sems):
    copies = [pltpu.make_async_copy(src, dst, sems.at[k]) for k, (src, dst) in enumerate(pairs)]
    for copy in copies:
        copy.start()
    return copies


def prepare_lists(
    block_rows,
    members,
    corner_idx,
    connect,
    interface,
    strain_disp,
    modulus,
    volume,
    coarse,
    panel_nodes,
    coupling,
    force,
    panel_inv,
    own,
    panel_v,
    coupling_v,
    force_v,
    inverse,
    select,
    onehot,
    face,
    scaled,
    count,
    placing,
    placing_last,
    inverse_volume,
    corner_v,
    connect_v,
    interface_v,
    strain_v,
    modulus_v,
    volume_v,
    ids,
    sems,
):
    copies = start_copies(
        [
            (connect, connect_v),
            (interface, interface_v),
            (corner_idx, corner_v),
            (modulus, modulus_v),
            (strain_disp, strain_v),
            (volume, volume_v),
            (coarse, own),
            (panel_nodes, panel_v),
            (coupling, coupling_v),
            (force, force_v),
            (panel_inv, inverse),
        ],
        sems,
    )
    nodes = onehot.shape[0]
    q = corner_idx.shape[1]

    copies[0].wait()
    node_of = lax.broadcasted_iota(jnp.int32, (nodes, LANES), 0)
    total = jnp.zeros((nodes, LANES), F32)
    for a in range(CORNERS):
        hit = jnp.where(connect_v[a : a + 1, :] == node_of, 1.0, 0.0)
        onehot[:, a * LANES : (a + 1) * LANES] = hit.astype(BF16)
        total = total + hit
    total = total.astype(BF16)
    count[:, :LANES] = total
    count[:, LANES:] = total

    copies[1].wait()
    ids[...] = jnp.full(ids.shape, -1.0, F32)
    ids[0:1, 0:NIF] = interface_v[...].astype(F32)
    order_lists(ids)
    lane = lax.broadcasted_iota(jnp.int32, (8, LANES), 1)
    edges = pltpu.roll(ids[:, LANES:], LANES - NIS, 1)
    again = pltpu.roll(ids[:, :LANES], LANES - NIS + 4 * NED, 1)
    last = jnp.where(lane < 4 * NED, edges, again)
    last = jnp.where(lane < LATE, last, pltpu.roll(edges, LATE, 1))
    for row, target in ((ids[0:1, LANES:], 0), (ids[0:1, :LANES], 1), (last[0:1], 2)):
        hit = jnp.where(row.astype(jnp.int32) == node_of, 1.0, 0.0).astype(BF16)
        if target == 0:
            placing[:, :LANES] = hit
            placing[:, LANES:] = hit
        else:
            placing_last[:, (target - 1) * LANES : target * LANES] = hit
    connect_f = connect_v[...].astype(F32)
    for half in range(2):
        id_col = column(ids[0:1, half * LANES : (half + 1) * LANES])
        rows = jnp.zeros((LANES, LANES), F32)
        for a in range(CORNERS):
            rows = rows + jnp.where(connect_f[a : a + 1, :] == id_col, 1.0, 0.0)
        rows = rows.astype(BF16)[: min(LANES, NIF - half * LANES)]
        face[half * LANES : half * LANES + rows.shape[0], :LANES] = rows
        face[half * LANES : half * LANES + rows.shape[0], LANES:] = rows

    copies[2].wait()
    ids[0:1, 0:q] = corner_v[...].astype(F32)
    wanted = column(ids[0:1, :LANES])[:TERM]
    lane = lax.broadcasted_iota(jnp.int32, (TERM, 3 * LANES), 1)
    entry = lax.broadcasted_iota(jnp.int32, (TERM, LANES), 0)
    s, g = lax.axis_index("sub"), lax.axis_index("grp")
    aside = 1 - 2 * (s & 1)
    row = jnp.full((TERM, 3 * LANES), -1, jnp.int32)
    base = 0
    for member in range(members):
        distance, bits, turn = members // 2, member, 0
        while distance:
            turn += (bits & 1) * distance
            distance, bits = distance // 2, bits >> 1
        for owner in (s, s - aside, s + aside):
            first = (owner * members + (g ^ turn)) * block_rows
            row = jnp.where((lane >= base) & (lane < base + block_rows), first - base + lane, row)
            base += block_rows
    for b in range(3):
        cols = slice(b * LANES, (b + 1) * LANES)
        hit = (wanted == row[:, cols].astype(F32)) & (entry < q)
        select[:, cols] = jnp.where(hit, 1.0, 0.0).astype(BF16)

    copies[3].wait()
    copies[4].wait()
    factor = modulus_v[...]
    rows = [strain_v[i].astype(F32) for i in range(COMPS)]
    trace = (rows[0] + rows[1] + rows[2]) * LAME
    for i in range(COMPS):
        value = trace + rows[i] * (2.0 * SHEAR) if i < 3 else rows[i] * SHEAR
        scaled[24 * i : 24 * (i + 1)] = jnp.broadcast_to((value * factor)[:, None, :], (24, 8, LANES))

    copies[5].wait()
    for k in range(nodes // LANES):
        inverse_volume[k * LANES : (k + 1) * LANES, :] = column(1.0 / volume_v[k : k + 1, :])
    for copy in copies[6:]:
        copy.wait()


def prepare_panels(
    panel_v,
    coupling_v,
    force_v,
    inverse,
    onehot,
    scaled,
    free_t,
    corner_t,
    stress_first,
    stress_corner,
    loads,
    solved,
    whole,
    sofar,
):
    panels, panel_rows, _ = inverse.shape
    panel_size = panel_rows // 3
    nodes = force_v.shape[1]
    q = coupling_v.shape[0]
    for c in range(3):
        loads[pl.ds(c, nodes, stride=3), :] = force_v[c].astype(F32)
    spare = corner_t.shape[0] - len(TERMS) * TERM
    stress_corner[len(TERMS) * TERM :, :] = jnp.zeros((spare, stress_corner.shape[1]), BF16)
    corner_t[len(TERMS) * TERM :, :] = jnp.zeros((spare, 3 * nodes), BF16)
    row_of = lax.broadcasted_iota(jnp.int32, (panel_rows, LANES), 0)
    for p in range(panels):
        start = p * panel_rows
        live = row_of < 3 * panel_v[0:1, p : p + 1]
        columns = []
        for k in range(panel_rows // LANES):
            part = coupling_v[:, start + k * LANES : start + (k + 1) * LANES].astype(F32)
            columns.append(jnp.concatenate([part, jnp.zeros((LANES - q, LANES), F32)], axis=0).T)
        sides = [loads[start : start + panel_rows, :], jnp.concatenate(columns, axis=0)]
        sides = jnp.concatenate([jnp.where(live, x, 0.0).astype(BF16) for x in sides], axis=1)
        result = dot(inverse[p], sides)
        for side in range(2):
            solved[side] = jnp.where(live, result[:, side * LANES : (side + 1) * LANES], 0.0)
        for c in range(3):
            cols = slice(c * nodes + p * panel_size, c * nodes + (p + 1) * panel_size)
            free_t[:, cols] = solved[0, pl.ds(c, panel_size, stride=3), :].T
            value = solved[1, pl.ds(c, panel_size, stride=3), :].T[:TERM]
            whole[:, cols] = value
            pieces = split_three(value)
            for k, (piece, _) in enumerate(TERMS):
                corner_t[k * TERM : (k + 1) * TERM, cols] = pieces[piece]

    def store(i, start, value):
        pieces = split_three(value)
        for k, (piece, _) in enumerate(TERMS):
            stress_corner[k * TERM : (k + 1) * TERM, i * LANES : (i + 1) * LANES] = pieces[piece]

    parts = jnp.concatenate([whole[:, c * nodes : (c + 1) * nodes] for c in range(3)], axis=0)
    element_stress(split_two(parts), TERM, onehot, scaled, sofar, store)
    free_stress(free_t, 0, stress_first.shape[1], onehot, scaled, sofar, stress_first)


def stress_kernel(free_t, onehot, scaled, out, sofar):
    rows = out.shape[1]
    free_stress(free_t, free_t.shape[0] - rows, rows, onehot, scaled, sofar, out)


def join_kernel(*refs):
    *parts, out = refs
    start = 0
    for part in parts:
        out[start : start + part.shape[0], :] = part[...]
        start += part.shape[0]


def solve_kernel(
    near,
    across,
    select,
    stress_first,
    stress_rest,
    stress_corner,
    face,
    values,
    stress,
    sub_a,
    sub_b,
    grp_a,
    grp_b,
    terms,
):
    rows = near.shape[0]
    terms[:, 2 * rows :, :] = jnp.zeros((3, terms.shape[1] - 2 * rows, terms.shape[2]), BF16)
    for b, block in enumerate((near, across)):
        for t, value in enumerate(split_three(block[...])):
            terms[t, b * rows : (b + 1) * rows, :] = value
    picked = [dot(select[...], terms[t]) for t in range(3)]
    ordered = [picked[term] for _, term in TERMS]
    ordered += [jnp.zeros_like(picked[0])] * (stress_corner.shape[0] // TERM - len(ordered))
    per = LANES // TERM
    for k in range(0, len(ordered), per):
        block = jnp.concatenate(ordered[k : k + per], axis=0).T.astype(BF16)
        values[:, k * TERM : (k + per) * TERM] = block
    moved = dot(values[...], stress_corner[...])
    for i in range(COMPS):
        cols = slice(i * LANES, (i + 1) * LANES)
        free = jnp.concatenate([stress_first[i], stress_rest[i]], axis=0)
        high, low = split_two(free - moved[:, cols])
        stress[cols, 0:LANES] = high
        stress[cols, LANES : 2 * LANES] = low

    rows = dot_nt(face[...], stress[...])
    for i in range(COMPS):
        part = rows[:, i * LANES : (i + 1) * LANES]
        edge = [part[EDGES + NED * k : EDGES + NED * (k + 1)] for k in range(4)]
        sub_a[i] = part[:NIS]
        sub_b[i] = part[NIS : 2 * NIS]
        grp_a[i] = jnp.concatenate([part[2 * NIS : 2 * NIS + NIG], edge[0], edge[2]], axis=0)
        grp_b[i] = jnp.concatenate([part[2 * NIS + NIG : EDGES], edge[1], edge[3]], axis=0)


def edge_kernel(grp_a, grp_b, from_a, from_b, edge_b, edge_a):
    split = NIG + NED
    edge_a[:, :NED, :] = grp_a[:, NIG:split, :] + from_a[:, NIG:split, :]
    edge_a[:, NED:, :] = grp_b[:, NIG:split, :] + from_b[:, NIG:split, :]
    edge_b[:, :NED, :] = grp_a[:, split:, :] + from_a[:, split:, :]
    edge_b[:, NED:, :] = grp_b[:, split:, :] + from_b[:, split:, :]


def partial_kernel(
    count, stress, free_t, corner_t, values, placing, grp_a, grp_b, partial, disp_out, received
):
    nodes = disp_out.shape[1]
    for c in range(3):
        cols = slice(c * nodes, (c + 1) * nodes)
        part = free_t[:, cols] - dot(values[...], corner_t[:, cols])
        for k in range(0, nodes, LANES):
            disp_out[c, k : k + LANES, :] = part[:, k : k + LANES].T.astype(BF16)
    split = NIG + NED
    for i in range(COMPS):
        low, high = grp_a[i], grp_b[i]
        rows = [low[:NIG], high[:NIG], low[NIG:split], high[NIG:split], low[split:], high[split:]]
        rows.append(jnp.zeros((2 * LANES - NIF, LANES), F32))
        first, second = split_two(jnp.concatenate(rows, axis=0))
        received[:LANES, i * LANES : (i + 1) * LANES] = first
        received[LANES:, i * LANES : (i + 1) * LANES] = second
    for i in range(0, COMPS, 2):
        cols = slice(i * LANES, (i + 2) * LANES)
        own = dot_nt(count[...], stress[cols, :])
        total = own + dot(placing[...], received[:, cols])
        partial[i] = total[:, :LANES]
        partial[i + 1] = total[:, LANES:]


def finish_kernel(
    placing, partial, inverse_volume, sub_a, sub_b, edge_b, edge_a, out, received, nodal, sems
):
    for i in range(COMPS):
        cols = slice(i * LANES, (i + 1) * LANES)
        late = jnp.concatenate([sub_b[i], edge_a[i], edge_b[i]], axis=0)
        first, second = split_two(late)
        received[:NIS, cols] = sub_a[i].astype(BF16)
        received[NIS : NIS + LATE, cols] = first
        received[NIS + LATE :, cols] = second
    scale = inverse_volume[...]
    copies = []
    for i in range(0, COMPS, 2):
        cols = slice(i * LANES, (i + 2) * LANES)
        added = dot(placing[...], received[:, cols])
        nodal[i] = ((partial[i] + added[:, :LANES]) * scale).astype(BF16)
        nodal[i + 1] = ((partial[i + 1] + added[:, LANES:]) * scale).astype(BF16)
        copy = pltpu.make_async_copy(nodal.at[pl.ds(i, 2)], out.at[pl.ds(i, 2)], sems.at[i // 2])
        copy.start()
        copies.append(copy)
    for copy in copies:
        copy.wait()


def vmem(count):
    return [pl.BlockSpec(memory_space=pltpu.VMEM)] * count


def anywhere(count):
    return [pl.BlockSpec(memory_space=pl.ANY)] * count


def hbm(count):
    return [pl.BlockSpec(memory_space=pltpu.HBM)] * count


def array(shape, dtype=F32):
    return jax.ShapeDtypeStruct(shape, dtype)


def call(kernel, name, out_shape, in_specs, scratch=(), flops=0, moved=0, out_specs=None):
    return pl.pallas_call(
        kernel,
        name=name,
        out_shape=out_shape,
        in_specs=in_specs,
        out_specs=out_specs or vmem(len(out_shape)),
        scratch_shapes=list(scratch),
        compiler_params=pltpu.CompilerParams(vmem_limit_bytes=VMEM_LIMIT),
        cost_estimate=pl.CostEstimate(flops=flops, bytes_accessed=moved, transcendentals=0),
    )


def exchange(block, axis, first):
    count = lax.axis_size(axis)
    pairs = []
    for i in range(first, count - 1, 2):
        pairs += [(i, i + 1), (i + 1, i)]
    return lax.ppermute(block, axis, pairs)


def in_hbm(*arrays):
    return [pltpu.with_memory_space_constraint(x, pltpu.HBM) for x in arrays]


def gather_near(coarse, own, ahead):
    beyond = exchange(coarse, "sub", 1)
    beside = exchange(coarse, "sub", 0)
    parts = [own, beyond, beside]
    distance = lax.axis_size("grp") // 2
    while distance:
        rows = sum(x.shape[0] for x in parts)
        before, ahead = ahead[:1], ahead[1:]

        def join(*refs, skip=len(before)):
            join_kernel(*refs[: len(refs) - 1 - skip], refs[-1])

        (block,) = call(
            join,
            "join_blocks",
            (array((rows, parts[0].shape[1])),),
            vmem(len(parts)) + anywhere(len(before)),
        )(*parts, *before)
        pairs = [(i, i ^ distance) for i in range(lax.axis_size("grp"))]
        parts = [block, lax.ppermute(block, "grp", pairs)]
        distance //= 2
    return parts


def shards(
    coarse,
    corner_idx,
    coupling,
    force,
    panel_inv,
    panel_nodes,
    strain_disp,
    modulus,
    connect,
    interface,
    nodal_volume,
):
    nodes, _, cases = force.shape
    dofs = 3 * nodes
    q = corner_idx.shape[1]

    def lists(*refs):
        prepare_lists(coarse.shape[0], lax.axis_size("grp"), *refs)

    own, *panels, select, onehot, face, scaled, count, placing, placing_last, inverse_volume = call(
        lists,
        "prepare_lists",
        (
            array(coarse.shape),
            array(panel_nodes.shape, jnp.int32),
            array((q, dofs), BF16),
            array((3, nodes, cases), BF16),
            array(panel_inv.shape, BF16),
            array((TERM, 3 * LANES), BF16),
            array((nodes, CORNERS * LANES), BF16),
            array((NIF, 2 * LANES), BF16),
            array((COMPS * 24, 8, LANES)),
            array((nodes, 2 * LANES), BF16),
            array((nodes, 2 * LANES), BF16),
            array((nodes, 2 * LANES), BF16),
            array((nodes, LANES)),
        ),
        hbm(11),
        (
            pltpu.VMEM((1, q), jnp.int32),
            pltpu.VMEM(connect.shape, jnp.int32),
            pltpu.VMEM(interface.shape, jnp.int32),
            pltpu.VMEM(strain_disp.shape, BF16),
            pltpu.VMEM((1, LANES), F32),
            pltpu.VMEM((nodes // LANES, LANES), F32),
            pltpu.VMEM((8, 2 * LANES), F32),
            pltpu.SemaphoreType.DMA((11,)),
        ),
        flops=100000000,
        moved=4000000,
    )(
        *in_hbm(
            corner_idx,
            connect,
            interface,
            strain_disp,
            modulus.reshape(1, -1),
            nodal_volume.reshape(-1, LANES),
            coarse,
            panel_nodes,
            coupling.T,
            jnp.transpose(force, (1, 0, 2)),
            panel_inv,
        )
    )
    first = 32
    free_t, corner_t, stress_first, stress_corner = call(
        prepare_panels,
        "prepare_panels",
        (
            array((cases, dofs)),
            array((2 * LANES, dofs), BF16),
            array((COMPS, first, LANES)),
            array((2 * LANES, COMPS * LANES), BF16),
        ),
        vmem(6),
        (
            pltpu.VMEM((dofs, cases), F32),
            pltpu.VMEM((2, panel_inv.shape[1], LANES), F32),
            pltpu.VMEM((TERM, dofs), F32),
            pltpu.VMEM((COMPS, max(first, TERM), LANES), F32),
        ),
        flops=400000000,
        moved=4000000,
    )(*panels, onehot, scaled)
    (stress_rest,) = call(
        stress_kernel,
        "stress_of_loads",
        (array((COMPS, cases - first, LANES)),),
        vmem(3),
        (pltpu.VMEM((COMPS, cases - first, LANES), F32),),
        flops=400000000,
        moved=4000000,
    )(free_t, onehot, scaled)

    near = gather_near(coarse, own, [select, corner_t])
    values, stress, sub_a, sub_b, grp_a, grp_b = call(
        solve_kernel,
        "stress_and_rows",
        (
            array((cases, 2 * LANES), BF16),
            array((COMPS * cases, 2 * LANES), BF16),
            array((COMPS, NIS, cases)),
            array((COMPS, NIS, cases)),
            array((COMPS, NIG + 2 * NED, cases)),
            array((COMPS, NIG + 2 * NED, cases)),
        ),
        vmem(7),
        (pltpu.VMEM((3, 3 * LANES, cases), BF16),),
        flops=300000000,
        moved=3000000,
    )(*near, select, stress_first, stress_rest, stress_corner, face)
    from_sub_a = exchange(sub_a, "sub", 0)
    from_grp_a = exchange(grp_a, "grp", 0)
    from_grp_b = exchange(grp_b, "grp", 1)
    edge_b, edge_a = call(
        edge_kernel,
        "sum_edges",
        (array((COMPS, 2 * NED, cases)), array((COMPS, 2 * NED, cases))),
        vmem(4),
    )(grp_a, grp_b, from_grp_a, from_grp_b)
    from_sub_b = exchange(sub_b, "sub", 1)
    from_edge_b = exchange(edge_b, "sub", 1)
    from_edge_a = exchange(edge_a, "sub", 0)
    partial, disp = call(
        partial_kernel,
        "assemble_nodes",
        (array((COMPS, nodes, cases)), array((3, nodes, cases), BF16)),
        vmem(8),
        (pltpu.VMEM((2 * LANES, COMPS * cases), BF16),),
        flops=400000000,
        moved=2000000,
    )(count, stress, free_t, corner_t, values, placing, from_grp_a, from_grp_b)
    (nodal,) = call(
        finish_kernel,
        "add_last",
        (array((COMPS, nodes, cases), BF16),),
        vmem(7),
        (
            pltpu.VMEM((NIS + 2 * LATE, COMPS * cases), BF16),
            pltpu.VMEM((COMPS, nodes, cases), BF16),
            pltpu.SemaphoreType.DMA((COMPS // 2,)),
        ),
        flops=400000000,
        moved=3000000,
        out_specs=hbm(1),
    )(placing_last, partial, inverse_volume, from_sub_a, from_sub_b, from_edge_b, from_edge_a)
    return jnp.transpose(disp, (1, 0, 2)), jnp.transpose(nodal, (1, 0, 2))


def solution(mesh):
    owner = ("sub", "grp")
    placed = (
        P(owner, None),
        P(owner, None),
        P(owner, None),
        P(owner, None, None),
        P(owner, None, None),
        P(owner, None),
        P(None, None, owner),
        P(owner),
        P(None, owner),
        P(owner, None),
        P(owner),
    )
    return jax.shard_map(
        shards,
        mesh=mesh,
        in_specs=placed,
        out_specs=(P(owner, None, None), P(owner, None, None)),
        check_vma=False,
    )
```

```python
import jax
import jax.numpy as jnp
from jax import lax
from jax.experimental import pallas as pl
from jax.experimental.pallas import tpu as pltpu
from jax.sharding import PartitionSpec as P

NIS = 64
NIG = 32
NED = 8
EDGES = 2 * NIS + 2 * NIG
NIF = EDGES + 4 * NED
LATE = NIS + 4 * NED
CORNERS = 8
COMPS = 6
LANES = 128
TERM = 32
TERMS = ((0, 0), (0, 1), (0, 2), (1, 0), (1, 1), (2, 0))

POISSON = 0.3
LAME = POISSON / ((1.0 + POISSON) * (1.0 - 2.0 * POISSON))
SHEAR = 0.5 / (1.0 + POISSON)

F32 = jnp.float32
BF16 = jnp.bfloat16
VMEM_LIMIT = 24 * 1024 * 1024


def split_two(x):
    high = x.astype(BF16)
    return high, (x - high.astype(F32)).astype(BF16)


def split_three(x):
    high = x.astype(BF16)
    rest = x - high.astype(F32)
    middle = rest.astype(BF16)
    return high, middle, (rest - middle.astype(F32)).astype(BF16)


def dot(a, b):
    return jnp.dot(a, b, preferred_element_type=F32)


def dot_nt(a, b):
    return lax.dot_general(a, b, (((1,), (1,)), ((), ())), preferred_element_type=F32)


def column(row):
    return jnp.broadcast_to(row, (LANES, LANES)).T


def swap_lanes(x, distance):
    lane = lax.broadcasted_iota(jnp.int32, x.shape, 1)
    after = pltpu.roll(x, LANES - distance, 1)
    before = pltpu.roll(x, distance, 1)
    return jnp.where((lane & distance) == 0, after, before)


def order_lists(ids):
    sub_even = (lax.axis_index("sub") & 1) == 0
    grp_even = (lax.axis_index("grp") & 1) == 0
    first, second = ids[:, :LANES], ids[:, LANES:]
    ids[:, :LANES] = jnp.where(sub_even, swap_lanes(first, NIS), first)
    lane = lax.broadcasted_iota(jnp.int32, second.shape, 1)
    groups = jnp.where(grp_even, swap_lanes(second, NIG), second)
    edges = jnp.where(sub_even, swap_lanes(second, 2 * NED), second)
    edges = jnp.where(grp_even, swap_lanes(edges, NED), edges)
    ids[:, LANES:] = jnp.where(lane < 2 * NIG, groups, edges)


def element_stress(terms, rows, onehot, scaled, sofar, store):
    step = 32
    pairs = onehot.shape[1] // (2 * LANES)
    for pair in range(pairs):
        operand = onehot[:, 2 * LANES * pair : 2 * LANES * (pair + 1)]
        elem = dot(terms[0], operand)
        for term in terms[1:]:
            elem = elem + dot(term, operand)
        for start in range(0, rows, step):
            sums = [None] * COMPS if pair == 0 else [sofar[i, start : start + step, :] for i in range(COMPS)]
            for half in range(2):
                for c in range(3):
                    x = elem[c * rows + start : c * rows + start + step, half * LANES : (half + 1) * LANES]
                    x = x.reshape(step // 8, 8, LANES)
                    for i in range(COMPS):
                        term = scaled[24 * i + 3 * (2 * pair + half) + c] * x
                        term = term.reshape(step, LANES)
                        sums[i] = term if sums[i] is None else sums[i] + term
            for i in range(COMPS):
                if pair < pairs - 1:
                    sofar[i, start : start + step, :] = sums[i]
                else:
                    store(i, start, sums[i])


def free_stress(free_t, first, rows, onehot, scaled, sofar, out):
    nodes = onehot.shape[0]
    parts = [free_t[first : first + rows, c * nodes : (c + 1) * nodes] for c in range(3)]

    def store(i, start, value):
        out[i, start : start + value.shape[0], :] = value

    element_stress(split_two(jnp.concatenate(parts, axis=0)), rows, onehot, scaled, sofar, store)


def start_copies(pairs, sems):
    copies = [pltpu.make_async_copy(src, dst, sems.at[k]) for k, (src, dst) in enumerate(pairs)]
    for copy in copies:
        copy.start()
    return copies


def prepare_lists(
    block_rows,
    members,
    corner_idx,
    connect,
    interface,
    strain_disp,
    modulus,
    volume,
    coarse,
    panel_nodes,
    coupling,
    force,
    panel_inv,
    own,
    panel_v,
    coupling_v,
    force_v,
    inverse,
    select,
    onehot,
    face,
    scaled,
    count,
    placing,
    placing_last,
    inverse_volume,
    corner_v,
    connect_v,
    interface_v,
    strain_v,
    modulus_v,
    volume_v,
    ids,
    sems,
):
    copies = start_copies(
        [
            (connect, connect_v),
            (interface, interface_v),
            (corner_idx, corner_v),
            (modulus, modulus_v),
            (strain_disp, strain_v),
            (volume, volume_v),
            (coarse, own),
            (panel_nodes, panel_v),
            (coupling, coupling_v),
            (force, force_v),
            (panel_inv, inverse),
        ],
        sems,
    )
    nodes = onehot.shape[0]
    q = corner_idx.shape[1]

    copies[0].wait()
    node_of = lax.broadcasted_iota(jnp.int32, (nodes, LANES), 0)
    total = jnp.zeros((nodes, LANES), F32)
    for a in range(CORNERS):
        hit = jnp.where(connect_v[a : a + 1, :] == node_of, 1.0, 0.0)
        onehot[:, a * LANES : (a + 1) * LANES] = hit.astype(BF16)
        total = total + hit
    total = total.astype(BF16)
    count[:, :LANES] = total
    count[:, LANES:] = total

    copies[1].wait()
    ids[...] = jnp.full(ids.shape, -1.0, F32)
    ids[0:1, 0:NIF] = interface_v[...].astype(F32)
    order_lists(ids)
    lane = lax.broadcasted_iota(jnp.int32, (8, LANES), 1)
    faces, others = ids[:, :LANES], ids[:, LANES:]
    turned = pltpu.roll(others, NIS, 1)
    lists = (
        (placing, 0, jnp.where(lane < NIS, faces, turned)),
        (placing, 1, jnp.where(lane < 4 * NED, turned, pltpu.roll(others, 4 * NED, 1))),
        (
            placing_last,
            0,
            jnp.where(
                lane < NIS,
                pltpu.roll(faces, NIS, 1),
                jnp.where(lane < LATE, others, pltpu.roll(faces, 4 * NED, 1)),
            ),
        ),
        (
            placing_last,
            1,
            jnp.where(
                lane < 4 * NED,
                pltpu.roll(faces, 4 * NED, 1),
                jnp.where(lane < 8 * NED, pltpu.roll(others, LATE, 1), -1.0),
            ),
        ),
    )
    for target, half, row in lists:
        hit = jnp.where(row[0:1].astype(jnp.int32) == node_of, 1.0, 0.0).astype(BF16)
        target[:, half * LANES : (half + 1) * LANES] = hit
    connect_f = connect_v[...].astype(F32)
    for half in range(2):
        id_col = column(ids[0:1, half * LANES : (half + 1) * LANES])
        rows = jnp.zeros((LANES, LANES), F32)
        for a in range(CORNERS):
            rows = rows + jnp.where(connect_f[a : a + 1, :] == id_col, 1.0, 0.0)
        rows = rows.astype(BF16)[: min(LANES, NIF - half * LANES)]
        face[half * LANES : half * LANES + rows.shape[0], :LANES] = rows
        face[half * LANES : half * LANES + rows.shape[0], LANES:] = rows

    copies[2].wait()
    ids[0:1, 0:q] = corner_v[...].astype(F32)
    wanted = column(ids[0:1, :LANES])[:TERM]
    lane = lax.broadcasted_iota(jnp.int32, (TERM, 3 * LANES), 1)
    entry = lax.broadcasted_iota(jnp.int32, (TERM, LANES), 0)
    s, g = lax.axis_index("sub"), lax.axis_index("grp")
    aside = 1 - 2 * (s & 1)
    row = jnp.full((TERM, 3 * LANES), -1, jnp.int32)
    base = 0
    for member in range(members):
        distance, bits, turn = members // 2, member, 0
        while distance:
            turn += (bits & 1) * distance
            distance, bits = distance // 2, bits >> 1
        for owner in (s, s - aside, s + aside):
            first = (owner * members + (g ^ turn)) * block_rows
            row = jnp.where((lane >= base) & (lane < base + block_rows), first - base + lane, row)
            base += block_rows
    for b in range(3):
        cols = slice(b * LANES, (b + 1) * LANES)
        hit = (wanted == row[:, cols].astype(F32)) & (entry < q)
        select[:, cols] = jnp.where(hit, 1.0, 0.0).astype(BF16)

    copies[3].wait()
    copies[4].wait()
    factor = modulus_v[...]
    rows = [strain_v[i].astype(F32) for i in range(COMPS)]
    trace = (rows[0] + rows[1] + rows[2]) * LAME
    for i in range(COMPS):
        value = trace + rows[i] * (2.0 * SHEAR) if i < 3 else rows[i] * SHEAR
        scaled[24 * i : 24 * (i + 1)] = jnp.broadcast_to((value * factor)[:, None, :], (24, 8, LANES))

    copies[5].wait()
    for k in range(nodes // LANES):
        inverse_volume[k * LANES : (k + 1) * LANES, :] = column(1.0 / volume_v[k : k + 1, :])
    for copy in copies[6:]:
        copy.wait()


def prepare_panels(
    panel_v,
    coupling_v,
    force_v,
    inverse,
    onehot,
    scaled,
    free_t,
    corner_t,
    stress_first,
    stress_corner,
    loads,
    solved,
    whole,
    sofar,
):
    panels, panel_rows, _ = inverse.shape
    panel_size = panel_rows // 3
    nodes = force_v.shape[1]
    q = coupling_v.shape[0]
    for c in range(3):
        loads[pl.ds(c, nodes, stride=3), :] = force_v[c].astype(F32)
    spare = corner_t.shape[0] - len(TERMS) * TERM
    stress_corner[len(TERMS) * TERM :, :] = jnp.zeros((spare, stress_corner.shape[1]), BF16)
    corner_t[len(TERMS) * TERM :, :] = jnp.zeros((spare, 3 * nodes), BF16)
    row_of = lax.broadcasted_iota(jnp.int32, (panel_rows, LANES), 0)
    for p in range(panels):
        start = p * panel_rows
        live = row_of < 3 * panel_v[0:1, p : p + 1]
        columns = []
        for k in range(panel_rows // LANES):
            part = coupling_v[:, start + k * LANES : start + (k + 1) * LANES].astype(F32)
            columns.append(jnp.concatenate([part, jnp.zeros((LANES - q, LANES), F32)], axis=0).T)
        sides = [loads[start : start + panel_rows, :], jnp.concatenate(columns, axis=0)]
        sides = jnp.concatenate([jnp.where(live, x, 0.0).astype(BF16) for x in sides], axis=1)
        result = dot(inverse[p], sides)
        for side in range(2):
            solved[side] = jnp.where(live, result[:, side * LANES : (side + 1) * LANES], 0.0)
        for c in range(3):
            cols = slice(c * nodes + p * panel_size, c * nodes + (p + 1) * panel_size)
            free_t[:, cols] = solved[0, pl.ds(c, panel_size, stride=3), :].T
            value = solved[1, pl.ds(c, panel_size, stride=3), :].T[:TERM]
            whole[:, cols] = value
            pieces = split_three(value)
            for k, (piece, _) in enumerate(TERMS):
                corner_t[k * TERM : (k + 1) * TERM, cols] = pieces[piece]

    def store(i, start, value):
        pieces = split_three(value)
        for k, (piece, _) in enumerate(TERMS):
            stress_corner[k * TERM : (k + 1) * TERM, i * LANES : (i + 1) * LANES] = pieces[piece]

    parts = jnp.concatenate([whole[:, c * nodes : (c + 1) * nodes] for c in range(3)], axis=0)
    element_stress(split_two(parts), TERM, onehot, scaled, sofar, store)
    free_stress(free_t, 0, stress_first.shape[1], onehot, scaled, sofar, stress_first)


def stress_kernel(free_t, onehot, scaled, out, sofar):
    rows = out.shape[1]
    free_stress(free_t, free_t.shape[0] - rows, rows, onehot, scaled, sofar, out)


def join_kernel(*refs):
    *parts, out = refs
    start = 0
    for part in parts:
        out[start : start + part.shape[0], :] = part[...]
        start += part.shape[0]


def solve_kernel(
    near,
    across,
    select,
    stress_first,
    stress_rest,
    stress_corner,
    face,
    values,
    stress,
    sub_a,
    sub_b,
    grp_a,
    grp_b,
    terms,
):
    rows = near.shape[0]
    terms[:, 2 * rows :, :] = jnp.zeros((3, terms.shape[1] - 2 * rows, terms.shape[2]), BF16)
    for b, block in enumerate((near, across)):
        for t, value in enumerate(split_three(block[...])):
            terms[t, b * rows : (b + 1) * rows, :] = value
    picked = [dot(select[...], terms[t]) for t in range(3)]
    ordered = [picked[term] for _, term in TERMS]
    ordered += [jnp.zeros_like(picked[0])] * (stress_corner.shape[0] // TERM - len(ordered))
    per = LANES // TERM
    for k in range(0, len(ordered), per):
        block = jnp.concatenate(ordered[k : k + per], axis=0).T.astype(BF16)
        values[:, k * TERM : (k + per) * TERM] = block
    moved = dot(values[...], stress_corner[...])
    for i in range(COMPS):
        cols = slice(i * LANES, (i + 1) * LANES)
        free = jnp.concatenate([stress_first[i], stress_rest[i]], axis=0)
        high, low = split_two(free - moved[:, cols])
        stress[cols, 0:LANES] = high
        stress[cols, LANES : 2 * LANES] = low

    rows = dot_nt(face[...], stress[...])
    for i in range(COMPS):
        part = rows[:, i * LANES : (i + 1) * LANES]
        edge = [part[EDGES + NED * k : EDGES + NED * (k + 1)] for k in range(4)]
        sub_a[i] = part[:NIS]
        sub_b[i] = part[NIS : 2 * NIS]
        grp_a[i] = jnp.concatenate([part[2 * NIS : 2 * NIS + NIG], edge[0], edge[2]], axis=0)
        grp_b[i] = jnp.concatenate([part[2 * NIS + NIG : EDGES], edge[1], edge[3]], axis=0)


def edge_kernel(grp_a, grp_b, from_a, from_b, edge_b, edge_a):
    split = NIG + NED
    edge_a[:, :NED, :] = grp_a[:, NIG:split, :] + from_a[:, NIG:split, :]
    edge_a[:, NED:, :] = grp_b[:, NIG:split, :] + from_b[:, NIG:split, :]
    edge_b[:, :NED, :] = grp_a[:, split:, :] + from_a[:, split:, :]
    edge_b[:, NED:, :] = grp_b[:, split:, :] + from_b[:, split:, :]


def partial_kernel(
    count, stress, free_t, corner_t, values, placing, sub_a, grp_a, grp_b, partial, disp_out, received
):
    nodes = disp_out.shape[1]
    for c in range(3):
        cols = slice(c * nodes, (c + 1) * nodes)
        part = free_t[:, cols] - dot(values[...], corner_t[:, cols])
        for k in range(0, nodes, LANES):
            disp_out[c, k : k + LANES, :] = part[:, k : k + LANES].T.astype(BF16)
    split = NIG + NED
    for i in range(COMPS):
        low, high = grp_a[i], grp_b[i]
        rows = [low[:NIG], high[:NIG], low[NIG:split], high[NIG:split], low[split:], high[split:]]
        first, second = split_two(jnp.concatenate(rows, axis=0))
        cols = slice(i * LANES, (i + 1) * LANES)
        received[:NIS, cols] = sub_a[i].astype(BF16)
        received[NIS : NIS + LATE, cols] = first
        received[NIS + LATE :, cols] = second
    for i in range(0, COMPS, 2):
        cols = slice(i * LANES, (i + 2) * LANES)
        own = dot_nt(count[...], stress[cols, :])
        total = own + dot(placing[...], received[:, cols])
        partial[i] = total[:, :LANES]
        partial[i + 1] = total[:, LANES:]


def finish_kernel(
    placing, partial, inverse_volume, sub_b, edge_b, edge_a, out, received, nodal, sems
):
    received[2 * LATE :, :] = jnp.zeros((received.shape[0] - 2 * LATE, received.shape[1]), BF16)
    for i in range(COMPS):
        cols = slice(i * LANES, (i + 1) * LANES)
        late = jnp.concatenate([sub_b[i], edge_a[i], edge_b[i]], axis=0)
        first, second = split_two(late)
        received[:LATE, cols] = first
        received[LATE : 2 * LATE, cols] = second
    scale = inverse_volume[...]
    copies = []
    for i in range(0, COMPS, 2):
        cols = slice(i * LANES, (i + 2) * LANES)
        added = dot(placing[...], received[:, cols])
        nodal[i] = ((partial[i] + added[:, :LANES]) * scale).astype(BF16)
        nodal[i + 1] = ((partial[i + 1] + added[:, LANES:]) * scale).astype(BF16)
        copy = pltpu.make_async_copy(nodal.at[pl.ds(i, 2)], out.at[pl.ds(i, 2)], sems.at[i // 2])
        copy.start()
        copies.append(copy)
    for copy in copies:
        copy.wait()


def vmem(count):
    return [pl.BlockSpec(memory_space=pltpu.VMEM)] * count


def anywhere(count):
    return [pl.BlockSpec(memory_space=pl.ANY)] * count


def hbm(count):
    return [pl.BlockSpec(memory_space=pltpu.HBM)] * count


def array(shape, dtype=F32):
    return jax.ShapeDtypeStruct(shape, dtype)


def call(kernel, name, out_shape, in_specs, scratch=(), flops=0, moved=0, out_specs=None):
    return pl.pallas_call(
        kernel,
        name=name,
        out_shape=out_shape,
        in_specs=in_specs,
        out_specs=out_specs or vmem(len(out_shape)),
        scratch_shapes=list(scratch),
        compiler_params=pltpu.CompilerParams(vmem_limit_bytes=VMEM_LIMIT),
        cost_estimate=pl.CostEstimate(flops=flops, bytes_accessed=moved, transcendentals=0),
    )


def exchange(block, axis, first):
    count = lax.axis_size(axis)
    pairs = []
    for i in range(first, count - 1, 2):
        pairs += [(i, i + 1), (i + 1, i)]
    return lax.ppermute(block, axis, pairs)


def in_hbm(*arrays):
    return [pltpu.with_memory_space_constraint(x, pltpu.HBM) for x in arrays]


def gather_near(coarse, own, ahead):
    beyond = exchange(coarse, "sub", 1)
    beside = exchange(coarse, "sub", 0)
    parts = [own, beyond, beside]
    distance = lax.axis_size("grp") // 2
    while distance:
        rows = sum(x.shape[0] for x in parts)
        before, ahead = ahead[:1], ahead[1:]

        def join(*refs, skip=len(before)):
            join_kernel(*refs[: len(refs) - 1 - skip], refs[-1])

        (block,) = call(
            join,
            "join_blocks",
            (array((rows, parts[0].shape[1])),),
            vmem(len(parts)) + anywhere(len(before)),
        )(*parts, *before)
        pairs = [(i, i ^ distance) for i in range(lax.axis_size("grp"))]
        parts = [block, lax.ppermute(block, "grp", pairs)]
        distance //= 2
    return parts


def shards(
    coarse,
    corner_idx,
    coupling,
    force,
    panel_inv,
    panel_nodes,
    strain_disp,
    modulus,
    connect,
    interface,
    nodal_volume,
):
    nodes, _, cases = force.shape
    dofs = 3 * nodes
    q = corner_idx.shape[1]

    def lists(*refs):
        prepare_lists(coarse.shape[0], lax.axis_size("grp"), *refs)

    own, *panels, select, onehot, face, scaled, count, placing, placing_last, inverse_volume = call(
        lists,
        "prepare_lists",
        (
            array(coarse.shape),
            array(panel_nodes.shape, jnp.int32),
            array((q, dofs), BF16),
            array((3, nodes, cases), BF16),
            array(panel_inv.shape, BF16),
            array((TERM, 3 * LANES), BF16),
            array((nodes, CORNERS * LANES), BF16),
            array((NIF, 2 * LANES), BF16),
            array((COMPS * 24, 8, LANES)),
            array((nodes, 2 * LANES), BF16),
            array((nodes, 2 * LANES), BF16),
            array((nodes, 2 * LANES), BF16),
            array((nodes, LANES)),
        ),
        hbm(11),
        (
            pltpu.VMEM((1, q), jnp.int32),
            pltpu.VMEM(connect.shape, jnp.int32),
            pltpu.VMEM(interface.shape, jnp.int32),
            pltpu.VMEM(strain_disp.shape, BF16),
            pltpu.VMEM((1, LANES), F32),
            pltpu.VMEM((nodes // LANES, LANES), F32),
            pltpu.VMEM((8, 2 * LANES), F32),
            pltpu.SemaphoreType.DMA((11,)),
        ),
        flops=100000000,
        moved=4000000,
    )(
        *in_hbm(
            corner_idx,
            connect,
            interface,
            strain_disp,
            modulus.reshape(1, -1),
            nodal_volume.reshape(-1, LANES),
            coarse,
            panel_nodes,
            coupling.T,
            jnp.transpose(force, (1, 0, 2)),
            panel_inv,
        )
    )
    first = 64
    free_t, corner_t, stress_first, stress_corner = call(
        prepare_panels,
        "prepare_panels",
        (
            array((cases, dofs)),
            array((2 * LANES, dofs), BF16),
            array((COMPS, first, LANES)),
            array((2 * LANES, COMPS * LANES), BF16),
        ),
        vmem(6),
        (
            pltpu.VMEM((dofs, cases), F32),
            pltpu.VMEM((2, panel_inv.shape[1], LANES), F32),
            pltpu.VMEM((TERM, dofs), F32),
            pltpu.VMEM((COMPS, max(first, TERM), LANES), F32),
        ),
        flops=400000000,
        moved=4000000,
    )(*panels, onehot, scaled)
    (stress_rest,) = call(
        stress_kernel,
        "stress_of_loads",
        (array((COMPS, cases - first, LANES)),),
        vmem(3),
        (pltpu.VMEM((COMPS, cases - first, LANES), F32),),
        flops=400000000,
        moved=4000000,
    )(free_t, onehot, scaled)

    near = gather_near(coarse, own, [select, corner_t])
    values, stress, sub_a, sub_b, grp_a, grp_b = call(
        solve_kernel,
        "stress_and_rows",
        (
            array((cases, 2 * LANES), BF16),
            array((COMPS * cases, 2 * LANES), BF16),
            array((COMPS, NIS, cases)),
            array((COMPS, NIS, cases)),
            array((COMPS, NIG + 2 * NED, cases)),
            array((COMPS, NIG + 2 * NED, cases)),
        ),
        vmem(7),
        (pltpu.VMEM((3, 3 * LANES, cases), BF16),),
        flops=300000000,
        moved=3000000,
    )(*near, select, stress_first, stress_rest, stress_corner, face)
    from_sub_a = exchange(sub_a, "sub", 0)
    from_grp_a = exchange(grp_a, "grp", 0)
    from_grp_b = exchange(grp_b, "grp", 1)
    edge_b, edge_a = call(
        edge_kernel,
        "sum_edges",
        (array((COMPS, 2 * NED, cases)), array((COMPS, 2 * NED, cases))),
        vmem(4),
    )(grp_a, grp_b, from_grp_a, from_grp_b)
    from_sub_b = exchange(sub_b, "sub", 1)
    from_edge_b = exchange(edge_b, "sub", 1)
    from_edge_a = exchange(edge_a, "sub", 0)
    partial, disp = call(
        partial_kernel,
        "assemble_nodes",
        (array((COMPS, nodes, cases)), array((3, nodes, cases), BF16)),
        vmem(9),
        (pltpu.VMEM((NIS + 2 * LATE, COMPS * cases), BF16),),
        flops=400000000,
        moved=2000000,
    )(count, stress, free_t, corner_t, values, placing, from_sub_a, from_grp_a, from_grp_b)
    (nodal,) = call(
        finish_kernel,
        "add_last",
        (array((COMPS, nodes, cases), BF16),),
        vmem(6),
        (
            pltpu.VMEM((2 * LANES, COMPS * cases), BF16),
            pltpu.VMEM((COMPS, nodes, cases), BF16),
            pltpu.SemaphoreType.DMA((COMPS // 2,)),
        ),
        flops=400000000,
        moved=3000000,
        out_specs=hbm(1),
    )(placing_last, partial, inverse_volume, from_sub_b, from_edge_b, from_edge_a)
    return jnp.transpose(disp, (1, 0, 2)), jnp.transpose(nodal, (1, 0, 2))


def solution(mesh):
    owner = ("sub", "grp")
    placed = (
        P(owner, None),
        P(owner, None),
        P(owner, None),
        P(owner, None, None),
        P(owner, None, None),
        P(owner, None),
        P(None, None, owner),
        P(owner),
        P(None, owner),
        P(owner, None),
        P(owner),
    )
    return jax.shard_map(
        shards,
        mesh=mesh,
        in_specs=placed,
        out_specs=(P(owner, None, None), P(owner, None, None)),
        check_vma=False,
    )
```

```python
import functools

import jax
import jax.numpy as jnp
from jax import lax
from jax.experimental import pallas as pl
from jax.experimental.pallas import tpu as pltpu
from jax.sharding import PartitionSpec as P

NIS = 64
NIG = 32
NED = 8
EDGES = 2 * NIS + 2 * NIG
NIF = EDGES + 4 * NED
LATE = NIS + 4 * NED
CORNERS = 8
COMPS = 6
LANES = 128
TERM = 32
TERMS = ((0, 0), (0, 1), (0, 2), (1, 0), (1, 1), (2, 0))

POISSON = 0.3
LAME = POISSON / ((1.0 + POISSON) * (1.0 - 2.0 * POISSON))
SHEAR = 0.5 / (1.0 + POISSON)

F32 = jnp.float32
BF16 = jnp.bfloat16
VMEM_LIMIT = 24 * 1024 * 1024


def split_two(x):
    high = x.astype(BF16)
    return high, (x - high.astype(F32)).astype(BF16)


def split_three(x):
    high = x.astype(BF16)
    rest = x - high.astype(F32)
    middle = rest.astype(BF16)
    return high, middle, (rest - middle.astype(F32)).astype(BF16)


def dot(a, b):
    return jnp.dot(a, b, preferred_element_type=F32)


def dot_nt(a, b):
    return lax.dot_general(a, b, (((1,), (1,)), ((), ())), preferred_element_type=F32)


def column(row):
    return jnp.broadcast_to(row, (LANES, LANES)).T


def swap_lanes(x, distance):
    lane = lax.broadcasted_iota(jnp.int32, x.shape, 1)
    after = pltpu.roll(x, LANES - distance, 1)
    before = pltpu.roll(x, distance, 1)
    return jnp.where((lane & distance) == 0, after, before)


def order_lists(ids):
    sub_even = (lax.axis_index("sub") & 1) == 0
    grp_even = (lax.axis_index("grp") & 1) == 0
    first, second = ids[:, :LANES], ids[:, LANES:]
    ids[:, :LANES] = jnp.where(sub_even, swap_lanes(first, NIS), first)
    lane = lax.broadcasted_iota(jnp.int32, second.shape, 1)
    groups = jnp.where(grp_even, swap_lanes(second, NIG), second)
    edges = jnp.where(sub_even, swap_lanes(second, 2 * NED), second)
    edges = jnp.where(grp_even, swap_lanes(edges, NED), edges)
    ids[:, LANES:] = jnp.where(lane < 2 * NIG, groups, edges)


def element_stress(terms, rows, onehot, scaled, sofar, store):
    step = 32
    pairs = onehot.shape[1] // (2 * LANES)
    for pair in range(pairs):
        operand = onehot[:, 2 * LANES * pair : 2 * LANES * (pair + 1)]
        elem = dot(terms[0], operand)
        for term in terms[1:]:
            elem = elem + dot(term, operand)
        for start in range(0, rows, step):
            sums = [None] * COMPS if pair == 0 else [sofar[i, start : start + step, :] for i in range(COMPS)]
            for half in range(2):
                for c in range(3):
                    x = elem[c * rows + start : c * rows + start + step, half * LANES : (half + 1) * LANES]
                    x = x.reshape(step // 8, 8, LANES)
                    for i in range(COMPS):
                        term = scaled[24 * i + 3 * (2 * pair + half) + c] * x
                        term = term.reshape(step, LANES)
                        sums[i] = term if sums[i] is None else sums[i] + term
            for i in range(COMPS):
                if pair < pairs - 1:
                    sofar[i, start : start + step, :] = sums[i]
                else:
                    store(i, start, sums[i])


def free_stress(free_t, first, rows, onehot, scaled, sofar, out):
    nodes = onehot.shape[0]
    parts = [free_t[first : first + rows, c * nodes : (c + 1) * nodes] for c in range(3)]

    def store(i, start, value):
        out[i, start : start + value.shape[0], :] = value

    element_stress(split_two(jnp.concatenate(parts, axis=0)), rows, onehot, scaled, sofar, store)


def start_copies(pairs, sems):
    copies = [pltpu.make_async_copy(src, dst, sems.at[k]) for k, (src, dst) in enumerate(pairs)]
    for copy in copies:
        copy.start()
    return copies


def prepare_lists(
    block_rows,
    members,
    corner_idx,
    connect,
    interface,
    strain_disp,
    modulus,
    volume,
    coarse,
    panel_nodes,
    coupling,
    force,
    panel_inv,
    own,
    panel_v,
    coupling_v,
    force_v,
    inverse,
    select,
    onehot,
    face,
    scaled,
    count,
    placing,
    placing_last,
    inverse_volume,
    corner_v,
    connect_v,
    interface_v,
    strain_v,
    modulus_v,
    volume_v,
    ids,
    sems,
):
    copies = start_copies(
        [
            (connect, connect_v),
            (interface, interface_v),
            (corner_idx, corner_v),
            (modulus, modulus_v),
            (strain_disp, strain_v),
            (volume, volume_v),
            (coarse, own),
            (panel_nodes, panel_v),
            (coupling, coupling_v),
            (force, force_v),
            (panel_inv, inverse),
        ],
        sems,
    )
    nodes = onehot.shape[0]
    q = corner_idx.shape[1]

    copies[0].wait()
    node_of = lax.broadcasted_iota(jnp.int32, (nodes, LANES), 0)
    total = jnp.zeros((nodes, LANES), F32)
    for a in range(CORNERS):
        hit = jnp.where(connect_v[a : a + 1, :] == node_of, 1.0, 0.0)
        onehot[:, a * LANES : (a + 1) * LANES] = hit.astype(BF16)
        total = total + hit
    total = total.astype(BF16)
    count[:, :LANES] = total
    count[:, LANES:] = total

    copies[1].wait()
    ids[...] = jnp.full(ids.shape, -1.0, F32)
    ids[0:1, 0:NIF] = interface_v[...].astype(F32)
    order_lists(ids)
    lane = lax.broadcasted_iota(jnp.int32, (8, LANES), 1)
    edges = pltpu.roll(ids[:, LANES:], LANES - NIS, 1)
    again = pltpu.roll(ids[:, :LANES], LANES - NIS + 4 * NED, 1)
    last = jnp.where(lane < 4 * NED, edges, again)
    last = jnp.where(lane < LATE, last, pltpu.roll(edges, LATE, 1))
    for row, target in ((ids[0:1, LANES:], 0), (ids[0:1, :LANES], 1), (last[0:1], 2)):
        hit = jnp.where(row.astype(jnp.int32) == node_of, 1.0, 0.0).astype(BF16)
        if target == 0:
            placing[:, :LANES] = hit
            placing[:, LANES:] = hit
        else:
            placing_last[:, (target - 1) * LANES : target * LANES] = hit
    connect_f = connect_v[...].astype(F32)
    for half in range(2):
        id_col = column(ids[0:1, half * LANES : (half + 1) * LANES])
        rows = jnp.zeros((LANES, LANES), F32)
        for a in range(CORNERS):
            rows = rows + jnp.where(connect_f[a : a + 1, :] == id_col, 1.0, 0.0)
        rows = rows.astype(BF16)[: min(LANES, NIF - half * LANES)]
        face[half * LANES : half * LANES + rows.shape[0], :LANES] = rows
        face[half * LANES : half * LANES + rows.shape[0], LANES:] = rows

    copies[2].wait()
    ids[0:1, 0:q] = corner_v[...].astype(F32)
    wanted = column(ids[0:1, :LANES])[:TERM]
    lane = lax.broadcasted_iota(jnp.int32, (TERM, 3 * LANES), 1)
    entry = lax.broadcasted_iota(jnp.int32, (TERM, LANES), 0)
    s, g = lax.axis_index("sub"), lax.axis_index("grp")
    aside = 1 - 2 * (s & 1)
    row = jnp.full((TERM, 3 * LANES), -1, jnp.int32)
    base = 0
    for member in range(members):
        distance, bits, turn = members // 2, member, 0
        while distance:
            turn += (bits & 1) * distance
            distance, bits = distance // 2, bits >> 1
        for owner in (s, s - aside, s + aside):
            first = (owner * members + (g ^ turn)) * block_rows
            row = jnp.where((lane >= base) & (lane < base + block_rows), first - base + lane, row)
            base += block_rows
    for b in range(3):
        cols = slice(b * LANES, (b + 1) * LANES)
        hit = (wanted == row[:, cols].astype(F32)) & (entry < q)
        select[:, cols] = jnp.where(hit, 1.0, 0.0).astype(BF16)

    copies[3].wait()
    copies[4].wait()
    factor = modulus_v[...]
    rows = [strain_v[i].astype(F32) for i in range(COMPS)]
    trace = (rows[0] + rows[1] + rows[2]) * LAME
    for i in range(COMPS):
        value = trace + rows[i] * (2.0 * SHEAR) if i < 3 else rows[i] * SHEAR
        scaled[24 * i : 24 * (i + 1)] = jnp.broadcast_to((value * factor)[:, None, :], (24, 8, LANES))

    copies[5].wait()
    for k in range(nodes // LANES):
        inverse_volume[k * LANES : (k + 1) * LANES, :] = column(1.0 / volume_v[k : k + 1, :])
    for copy in copies[6:]:
        copy.wait()


def prepare_panels(
    panel_v,
    coupling_v,
    force_v,
    inverse,
    onehot,
    scaled,
    free_t,
    corner_t,
    stress_first,
    stress_corner,
    loads,
    solved,
    whole,
    sofar,
):
    panels, panel_rows, _ = inverse.shape
    panel_size = panel_rows // 3
    nodes = force_v.shape[1]
    q = coupling_v.shape[0]
    for c in range(3):
        loads[pl.ds(c, nodes, stride=3), :] = force_v[c].astype(F32)
    spare = corner_t.shape[0] - len(TERMS) * TERM
    stress_corner[len(TERMS) * TERM :, :] = jnp.zeros((spare, stress_corner.shape[1]), BF16)
    corner_t[len(TERMS) * TERM :, :] = jnp.zeros((spare, 3 * nodes), BF16)
    row_of = lax.broadcasted_iota(jnp.int32, (panel_rows, LANES), 0)
    for p in range(panels):
        start = p * panel_rows
        live = row_of < 3 * panel_v[0:1, p : p + 1]
        columns = []
        for k in range(panel_rows // LANES):
            part = coupling_v[:, start + k * LANES : start + (k + 1) * LANES].astype(F32)
            columns.append(jnp.concatenate([part, jnp.zeros((LANES - q, LANES), F32)], axis=0).T)
        sides = [loads[start : start + panel_rows, :], jnp.concatenate(columns, axis=0)]
        sides = jnp.concatenate([jnp.where(live, x, 0.0).astype(BF16) for x in sides], axis=1)
        result = dot(inverse[p], sides)
        for side in range(2):
            solved[side] = jnp.where(live, result[:, side * LANES : (side + 1) * LANES], 0.0)
        for c in range(3):
            cols = slice(c * nodes + p * panel_size, c * nodes + (p + 1) * panel_size)
            free_t[:, cols] = solved[0, pl.ds(c, panel_size, stride=3), :].T
            value = solved[1, pl.ds(c, panel_size, stride=3), :].T[:TERM]
            whole[:, cols] = value
            pieces = split_three(value)
            for k, (piece, _) in enumerate(TERMS):
                corner_t[k * TERM : (k + 1) * TERM, cols] = pieces[piece]

    def store(i, start, value):
        pieces = split_three(value)
        for k, (piece, _) in enumerate(TERMS):
            stress_corner[k * TERM : (k + 1) * TERM, i * LANES : (i + 1) * LANES] = pieces[piece]

    parts = jnp.concatenate([whole[:, c * nodes : (c + 1) * nodes] for c in range(3)], axis=0)
    element_stress(split_two(parts), TERM, onehot, scaled, sofar, store)
    free_stress(free_t, 0, stress_first.shape[1], onehot, scaled, sofar, stress_first)


def stress_kernel(free_t, onehot, scaled, out, sofar):
    rows = out.shape[1]
    free_stress(free_t, free_t.shape[0] - rows, rows, onehot, scaled, sofar, out)


def join_kernel(*refs):
    *parts, out = refs
    start = 0
    for part in parts:
        out[start : start + part.shape[0], :] = part[...]
        start += part.shape[0]


def solve_kernel(
    near,
    across,
    select,
    stress_first,
    stress_rest,
    stress_corner,
    face,
    values,
    stress,
    sub_a,
    sub_b,
    grp_a,
    grp_b,
    terms,
):
    rows = near.shape[0]
    terms[:, 2 * rows :, :] = jnp.zeros((3, terms.shape[1] - 2 * rows, terms.shape[2]), BF16)
    for b, block in enumerate((near, across)):
        for t, value in enumerate(split_three(block[...])):
            terms[t, b * rows : (b + 1) * rows, :] = value
    picked = [dot(select[...], terms[t]) for t in range(3)]
    ordered = [picked[term] for _, term in TERMS]
    ordered += [jnp.zeros_like(picked[0])] * (stress_corner.shape[0] // TERM - len(ordered))
    per = LANES // TERM
    for k in range(0, len(ordered), per):
        block = jnp.concatenate(ordered[k : k + per], axis=0).T.astype(BF16)
        values[:, k * TERM : (k + per) * TERM] = block
    moved = dot(values[...], stress_corner[...])
    for i in range(COMPS):
        cols = slice(i * LANES, (i + 1) * LANES)
        free = jnp.concatenate([stress_first[i], stress_rest[i]], axis=0)
        high, low = split_two(free - moved[:, cols])
        stress[cols, 0:LANES] = high
        stress[cols, LANES : 2 * LANES] = low

    rows = dot_nt(face[...], stress[...])
    for i in range(COMPS):
        part = rows[:, i * LANES : (i + 1) * LANES]
        edge = [part[EDGES + NED * k : EDGES + NED * (k + 1)] for k in range(4)]
        sub_a[i] = part[:NIS]
        sub_b[i] = part[NIS : 2 * NIS]
        grp_a[i] = jnp.concatenate([part[2 * NIS : 2 * NIS + NIG], edge[0], edge[2]], axis=0)
        grp_b[i] = jnp.concatenate([part[2 * NIS + NIG : EDGES], edge[1], edge[3]], axis=0)


def grp_b_rows(members, rows):
    g = lax.axis_index("grp")
    partner = g - 1 + 2 * (g & 1)
    return jnp.where((partner >= 0) & (partner < members), rows, 0.0)


def edge_kernel(members, grp_a, grp_b, from_a, from_b, edge_b, edge_a):
    split = NIG + NED
    edge_a[:, :NED, :] = grp_a[:, NIG:split, :] + from_a[:, NIG:split, :]
    edge_a[:, NED:, :] = grp_b[:, NIG:split, :] + grp_b_rows(members, from_b[:, NIG:split, :])
    edge_b[:, :NED, :] = grp_a[:, split:, :] + from_a[:, split:, :]
    edge_b[:, NED:, :] = grp_b[:, split:, :] + grp_b_rows(members, from_b[:, split:, :])


def partial_kernel(
    members, count, stress, free_t, corner_t, values, placing, grp_a, grp_b, partial, disp_out, received
):
    nodes = disp_out.shape[1]
    for c in range(3):
        cols = slice(c * nodes, (c + 1) * nodes)
        part = free_t[:, cols] - dot(values[...], corner_t[:, cols])
        for k in range(0, nodes, LANES):
            disp_out[c, k : k + LANES, :] = part[:, k : k + LANES].T.astype(BF16)
    split = NIG + NED
    for i in range(COMPS):
        low, high = grp_a[i], grp_b_rows(members, grp_b[i])
        rows = [low[:NIG], high[:NIG], low[NIG:split], high[NIG:split], low[split:], high[split:]]
        rows.append(jnp.zeros((2 * LANES - NIF, LANES), F32))
        first, second = split_two(jnp.concatenate(rows, axis=0))
        received[:LANES, i * LANES : (i + 1) * LANES] = first
        received[LANES:, i * LANES : (i + 1) * LANES] = second
    for i in range(0, COMPS, 2):
        cols = slice(i * LANES, (i + 2) * LANES)
        own = dot_nt(count[...], stress[cols, :])
        total = own + dot(placing[...], received[:, cols])
        partial[i] = total[:, :LANES]
        partial[i + 1] = total[:, LANES:]


def finish_kernel(
    placing, partial, inverse_volume, sub_a, sub_b, edge_b, edge_a, out, received, nodal, sems
):
    for i in range(COMPS):
        cols = slice(i * LANES, (i + 1) * LANES)
        late = jnp.concatenate([sub_b[i], edge_a[i], edge_b[i]], axis=0)
        first, second = split_two(late)
        received[:NIS, cols] = sub_a[i].astype(BF16)
        received[NIS : NIS + LATE, cols] = first
        received[NIS + LATE :, cols] = second
    scale = inverse_volume[...]
    copies = []
    for i in range(0, COMPS, 2):
        cols = slice(i * LANES, (i + 2) * LANES)
        added = dot(placing[...], received[:, cols])
        nodal[i] = ((partial[i] + added[:, :LANES]) * scale).astype(BF16)
        nodal[i + 1] = ((partial[i + 1] + added[:, LANES:]) * scale).astype(BF16)
        copy = pltpu.make_async_copy(nodal.at[pl.ds(i, 2)], out.at[pl.ds(i, 2)], sems.at[i // 2])
        copy.start()
        copies.append(copy)
    for copy in copies:
        copy.wait()


def vmem(count):
    return [pl.BlockSpec(memory_space=pltpu.VMEM)] * count


def anywhere(count):
    return [pl.BlockSpec(memory_space=pl.ANY)] * count


def hbm(count):
    return [pl.BlockSpec(memory_space=pltpu.HBM)] * count


def array(shape, dtype=F32):
    return jax.ShapeDtypeStruct(shape, dtype)


def call(kernel, name, out_shape, in_specs, scratch=(), flops=0, moved=0, out_specs=None):
    return pl.pallas_call(
        kernel,
        name=name,
        out_shape=out_shape,
        in_specs=in_specs,
        out_specs=out_specs or vmem(len(out_shape)),
        scratch_shapes=list(scratch),
        compiler_params=pltpu.CompilerParams(vmem_limit_bytes=VMEM_LIMIT),
        cost_estimate=pl.CostEstimate(flops=flops, bytes_accessed=moved, transcendentals=0),
    )


def exchange(block, axis, first, keep=False):
    count = lax.axis_size(axis)
    pairs = []
    for i in range(first, count - 1, 2):
        pairs += [(i, i + 1), (i + 1, i)]
    if keep:
        alone = set(range(count)) - {i for i, _ in pairs}
        pairs += [(i, i) for i in sorted(alone)]
    return lax.ppermute(block, axis, pairs)


def in_hbm(*arrays):
    return [pltpu.with_memory_space_constraint(x, pltpu.HBM) for x in arrays]


def gather_near(coarse, own, ahead):
    beyond = exchange(coarse, "sub", 1)
    beside = exchange(coarse, "sub", 0)
    parts = [own, beyond, beside]
    distance = lax.axis_size("grp") // 2
    while distance:
        rows = sum(x.shape[0] for x in parts)
        before, ahead = ahead[:1], ahead[1:]

        def join(*refs, skip=len(before)):
            join_kernel(*refs[: len(refs) - 1 - skip], refs[-1])

        (block,) = call(
            join,
            "join_blocks",
            (array((rows, parts[0].shape[1])),),
            vmem(len(parts)) + anywhere(len(before)),
        )(*parts, *before)
        pairs = [(i, i ^ distance) for i in range(lax.axis_size("grp"))]
        parts = [block, lax.ppermute(block, "grp", pairs)]
        distance //= 2
    return parts


def shards(
    coarse,
    corner_idx,
    coupling,
    force,
    panel_inv,
    panel_nodes,
    strain_disp,
    modulus,
    connect,
    interface,
    nodal_volume,
):
    nodes, _, cases = force.shape
    dofs = 3 * nodes
    q = corner_idx.shape[1]

    def lists(*refs):
        prepare_lists(coarse.shape[0], lax.axis_size("grp"), *refs)

    own, *panels, select, onehot, face, scaled, count, placing, placing_last, inverse_volume = call(
        lists,
        "prepare_lists",
        (
            array(coarse.shape),
            array(panel_nodes.shape, jnp.int32),
            array((q, dofs), BF16),
            array((3, nodes, cases), BF16),
            array(panel_inv.shape, BF16),
            array((TERM, 3 * LANES), BF16),
            array((nodes, CORNERS * LANES), BF16),
            array((NIF, 2 * LANES), BF16),
            array((COMPS * 24, 8, LANES)),
            array((nodes, 2 * LANES), BF16),
            array((nodes, 2 * LANES), BF16),
            array((nodes, 2 * LANES), BF16),
            array((nodes, LANES)),
        ),
        hbm(11),
        (
            pltpu.VMEM((1, q), jnp.int32),
            pltpu.VMEM(connect.shape, jnp.int32),
            pltpu.VMEM(interface.shape, jnp.int32),
            pltpu.VMEM(strain_disp.shape, BF16),
            pltpu.VMEM((1, LANES), F32),
            pltpu.VMEM((nodes // LANES, LANES), F32),
            pltpu.VMEM((8, 2 * LANES), F32),
            pltpu.SemaphoreType.DMA((11,)),
        ),
        flops=100000000,
        moved=4000000,
    )(
        *in_hbm(
            corner_idx,
            connect,
            interface,
            strain_disp,
            modulus.reshape(1, -1),
            nodal_volume.reshape(-1, LANES),
            coarse,
            panel_nodes,
            coupling.T,
            jnp.transpose(force, (1, 0, 2)),
            panel_inv,
        )
    )
    first = 32
    free_t, corner_t, stress_first, stress_corner = call(
        prepare_panels,
        "prepare_panels",
        (
            array((cases, dofs)),
            array((2 * LANES, dofs), BF16),
            array((COMPS, first, LANES)),
            array((2 * LANES, COMPS * LANES), BF16),
        ),
        vmem(6),
        (
            pltpu.VMEM((dofs, cases), F32),
            pltpu.VMEM((2, panel_inv.shape[1], LANES), F32),
            pltpu.VMEM((TERM, dofs), F32),
            pltpu.VMEM((COMPS, max(first, TERM), LANES), F32),
        ),
        flops=400000000,
        moved=4000000,
    )(*panels, onehot, scaled)
    (stress_rest,) = call(
        stress_kernel,
        "stress_of_loads",
        (array((COMPS, cases - first, LANES)),),
        vmem(3),
        (pltpu.VMEM((COMPS, cases - first, LANES), F32),),
        flops=400000000,
        moved=4000000,
    )(free_t, onehot, scaled)

    near = gather_near(coarse, own, [select, corner_t])
    values, stress, sub_a, sub_b, grp_a, grp_b = call(
        solve_kernel,
        "stress_and_rows",
        (
            array((cases, 2 * LANES), BF16),
            array((COMPS * cases, 2 * LANES), BF16),
            array((COMPS, NIS, cases)),
            array((COMPS, NIS, cases)),
            array((COMPS, NIG + 2 * NED, cases)),
            array((COMPS, NIG + 2 * NED, cases)),
        ),
        vmem(7),
        (pltpu.VMEM((3, 3 * LANES, cases), BF16),),
        flops=300000000,
        moved=3000000,
    )(*near, select, stress_first, stress_rest, stress_corner, face)
    from_sub_a = exchange(sub_a, "sub", 0)
    from_grp_a = exchange(grp_a, "grp", 0)
    from_grp_b = exchange(grp_b, "grp", 1, keep=True)
    members = lax.axis_size("grp")
    edge_b, edge_a = call(
        functools.partial(edge_kernel, members),
        "sum_edges",
        (array((COMPS, 2 * NED, cases)), array((COMPS, 2 * NED, cases))),
        vmem(4),
    )(grp_a, grp_b, from_grp_a, from_grp_b)
    from_sub_b = exchange(sub_b, "sub", 1)
    from_edge_b = exchange(edge_b, "sub", 1)
    from_edge_a = exchange(edge_a, "sub", 0)
    partial, disp = call(
        functools.partial(partial_kernel, members),
        "assemble_nodes",
        (array((COMPS, nodes, cases)), array((3, nodes, cases), BF16)),
        vmem(8),
        (pltpu.VMEM((2 * LANES, COMPS * cases), BF16),),
        flops=400000000,
        moved=2000000,
    )(count, stress, free_t, corner_t, values, placing, from_grp_a, from_grp_b)
    (nodal,) = call(
        finish_kernel,
        "add_last",
        (array((COMPS, nodes, cases), BF16),),
        vmem(7),
        (
            pltpu.VMEM((NIS + 2 * LATE, COMPS * cases), BF16),
            pltpu.VMEM((COMPS, nodes, cases), BF16),
            pltpu.SemaphoreType.DMA((COMPS // 2,)),
        ),
        flops=400000000,
        moved=3000000,
        out_specs=hbm(1),
    )(placing_last, partial, inverse_volume, from_sub_a, from_sub_b, from_edge_b, from_edge_a)
    return jnp.transpose(disp, (1, 0, 2)), jnp.transpose(nodal, (1, 0, 2))


def solution(mesh):
    owner = ("sub", "grp")
    placed = (
        P(owner, None),
        P(owner, None),
        P(owner, None),
        P(owner, None, None),
        P(owner, None, None),
        P(owner, None),
        P(None, None, owner),
        P(owner),
        P(None, owner),
        P(owner, None),
        P(owner),
    )
    return jax.shard_map(
        shards,
        mesh=mesh,
        in_specs=placed,
        out_specs=(P(owner, None, None), P(owner, None, None)),
        check_vma=False,
    )
```

```python
import jax
import jax.numpy as jnp
from jax import lax
from jax.experimental import pallas as pl
from jax.experimental.pallas import tpu as pltpu
from jax.sharding import PartitionSpec as P

NIS = 64
NIG = 32
NED = 8
EDGES = 2 * NIS + 2 * NIG
NIF = EDGES + 4 * NED
LATE = NIS + 4 * NED
CORNERS = 8
COMPS = 6
LANES = 128
TERM = 32
TERMS = ((0, 0), (0, 1), (0, 2), (1, 0), (1, 1), (2, 0))

POISSON = 0.3
LAME = POISSON / ((1.0 + POISSON) * (1.0 - 2.0 * POISSON))
SHEAR = 0.5 / (1.0 + POISSON)

F32 = jnp.float32
BF16 = jnp.bfloat16
VMEM_LIMIT = 24 * 1024 * 1024


def split_two(x):
    high = x.astype(BF16)
    return high, (x - high.astype(F32)).astype(BF16)


def split_three(x):
    high = x.astype(BF16)
    rest = x - high.astype(F32)
    middle = rest.astype(BF16)
    return high, middle, (rest - middle.astype(F32)).astype(BF16)


def dot(a, b):
    return jnp.dot(a, b, preferred_element_type=F32)


def dot_nt(a, b):
    return lax.dot_general(a, b, (((1,), (1,)), ((), ())), preferred_element_type=F32)


def column(row):
    return jnp.broadcast_to(row, (LANES, LANES)).T


def swap_lanes(x, distance):
    lane = lax.broadcasted_iota(jnp.int32, x.shape, 1)
    after = pltpu.roll(x, LANES - distance, 1)
    before = pltpu.roll(x, distance, 1)
    return jnp.where((lane & distance) == 0, after, before)


def order_lists(ids):
    sub_even = (lax.axis_index("sub") & 1) == 0
    grp_even = (lax.axis_index("grp") & 1) == 0
    first, second = ids[:, :LANES], ids[:, LANES:]
    ids[:, :LANES] = jnp.where(sub_even, swap_lanes(first, NIS), first)
    lane = lax.broadcasted_iota(jnp.int32, second.shape, 1)
    groups = jnp.where(grp_even, swap_lanes(second, NIG), second)
    edges = jnp.where(sub_even, swap_lanes(second, 2 * NED), second)
    edges = jnp.where(grp_even, swap_lanes(edges, NED), edges)
    ids[:, LANES:] = jnp.where(lane < 2 * NIG, groups, edges)


def element_stress(terms, rows, onehot, scaled, sofar, store):
    step = 32
    pairs = onehot.shape[1] // (2 * LANES)
    for pair in range(pairs):
        operand = onehot[:, 2 * LANES * pair : 2 * LANES * (pair + 1)]
        elem = dot(terms[0], operand)
        for term in terms[1:]:
            elem = elem + dot(term, operand)
        for start in range(0, rows, step):
            sums = [None] * COMPS if pair == 0 else [sofar[i, start : start + step, :] for i in range(COMPS)]
            for half in range(2):
                for c in range(3):
                    x = elem[c * rows + start : c * rows + start + step, half * LANES : (half + 1) * LANES]
                    x = x.reshape(step // 8, 8, LANES)
                    for i in range(COMPS):
                        term = scaled[24 * i + 3 * (2 * pair + half) + c] * x
                        term = term.reshape(step, LANES)
                        sums[i] = term if sums[i] is None else sums[i] + term
            for i in range(COMPS):
                if pair < pairs - 1:
                    sofar[i, start : start + step, :] = sums[i]
                else:
                    store(i, start, sums[i])


def free_stress(free_t, first, rows, onehot, scaled, sofar, out):
    nodes = onehot.shape[0]
    parts = [free_t[first : first + rows, c * nodes : (c + 1) * nodes] for c in range(3)]

    def store(i, start, value):
        out[i, start : start + value.shape[0], :] = value

    element_stress(split_two(jnp.concatenate(parts, axis=0)), rows, onehot, scaled, sofar, store)


def start_copies(pairs, sems):
    copies = [pltpu.make_async_copy(src, dst, sems.at[k]) for k, (src, dst) in enumerate(pairs)]
    for copy in copies:
        copy.start()
    return copies


def prepare_lists(
    block_rows,
    members,
    corner_idx,
    connect,
    interface,
    strain_disp,
    modulus,
    volume,
    coarse,
    panel_nodes,
    coupling,
    force,
    panel_inv,
    own,
    panel_v,
    coupling_v,
    force_v,
    inverse,
    select,
    onehot,
    face,
    scaled,
    count,
    placing,
    placing_last,
    inverse_volume,
    corner_v,
    connect_v,
    interface_v,
    strain_v,
    modulus_v,
    volume_v,
    ids,
    sems,
):
    copies = start_copies(
        [
            (connect, connect_v),
            (interface, interface_v),
            (corner_idx, corner_v),
            (modulus, modulus_v),
            (strain_disp, strain_v),
            (volume, volume_v),
            (coarse, own),
            (panel_nodes, panel_v),
            (coupling, coupling_v),
            (force, force_v),
            (panel_inv, inverse),
        ],
        sems,
    )
    nodes = onehot.shape[0]
    q = corner_idx.shape[1]

    copies[0].wait()
    node_of = lax.broadcasted_iota(jnp.int32, (nodes, LANES), 0)
    total = jnp.zeros((nodes, LANES), F32)
    for a in range(CORNERS):
        hit = jnp.where(connect_v[a : a + 1, :] == node_of, 1.0, 0.0)
        onehot[:, a * LANES : (a + 1) * LANES] = hit.astype(BF16)
        total = total + hit
    total = total.astype(BF16)
    count[:, :LANES] = total
    count[:, LANES:] = total

    copies[1].wait()
    ids[...] = jnp.full(ids.shape, -1.0, F32)
    ids[0:1, 0:NIF] = interface_v[...].astype(F32)
    order_lists(ids)
    lane = lax.broadcasted_iota(jnp.int32, (8, LANES), 1)
    edges = pltpu.roll(ids[:, LANES:], LANES - NIS, 1)
    again = pltpu.roll(ids[:, :LANES], LANES - NIS + 4 * NED, 1)
    last = jnp.where(lane < 4 * NED, edges, again)
    last = jnp.where(lane < LATE, last, pltpu.roll(edges, LATE, 1))
    for row, target in ((ids[0:1, LANES:], 0), (ids[0:1, :LANES], 1), (last[0:1], 2)):
        hit = jnp.where(row.astype(jnp.int32) == node_of, 1.0, 0.0).astype(BF16)
        if target == 0:
            placing[:, :LANES] = hit
            placing[:, LANES:] = hit
        else:
            placing_last[:, (target - 1) * LANES : target * LANES] = hit
    connect_f = connect_v[...].astype(F32)
    for half in range(2):
        id_col = column(ids[0:1, half * LANES : (half + 1) * LANES])
        rows = jnp.zeros((LANES, LANES), F32)
        for a in range(CORNERS):
            rows = rows + jnp.where(connect_f[a : a + 1, :] == id_col, 1.0, 0.0)
        rows = rows.astype(BF16)[: min(LANES, NIF - half * LANES)]
        face[half * LANES : half * LANES + rows.shape[0], :LANES] = rows
        face[half * LANES : half * LANES + rows.shape[0], LANES:] = rows

    copies[2].wait()
    ids[0:1, 0:q] = corner_v[...].astype(F32)
    wanted = column(ids[0:1, :LANES])[:TERM]
    lane = lax.broadcasted_iota(jnp.int32, (TERM, 3 * LANES), 1)
    entry = lax.broadcasted_iota(jnp.int32, (TERM, LANES), 0)
    s, g = lax.axis_index("sub"), lax.axis_index("grp")
    aside = 1 - 2 * (s & 1)
    row = jnp.full((TERM, 3 * LANES), -1, jnp.int32)
    base = 0
    for member in range(members):
        distance, bits, turn = members // 2, member, 0
        while distance:
            turn += (bits & 1) * distance
            distance, bits = distance // 2, bits >> 1
        for owner in (s, s - aside, s + aside):
            first = (owner * members + (g ^ turn)) * block_rows
            row = jnp.where((lane >= base) & (lane < base + block_rows), first - base + lane, row)
            base += block_rows
    for b in range(3):
        cols = slice(b * LANES, (b + 1) * LANES)
        hit = (wanted == row[:, cols].astype(F32)) & (entry < q)
        select[:, cols] = jnp.where(hit, 1.0, 0.0).astype(BF16)

    copies[3].wait()
    copies[4].wait()
    factor = modulus_v[...]
    whole = strain_v[...].astype(F32)
    rows = [whole[24 * i : 24 * (i + 1)] for i in range(COMPS)]
    trace = (rows[0] + rows[1] + rows[2]) * LAME
    for i in range(COMPS):
        value = trace + rows[i] * (2.0 * SHEAR) if i < 3 else rows[i] * SHEAR
        scaled[24 * i : 24 * (i + 1)] = jnp.broadcast_to((value * factor)[:, None, :], (24, 8, LANES))

    copies[5].wait()
    for k in range(nodes // LANES):
        inverse_volume[k * LANES : (k + 1) * LANES, :] = column(1.0 / volume_v[k : k + 1, :])
    for copy in copies[6:]:
        copy.wait()


def prepare_panels(
    panel_v,
    coupling_v,
    force_v,
    inverse,
    onehot,
    scaled,
    free_t,
    corner_t,
    stress_first,
    stress_corner,
    loads,
    solved,
    whole,
    sofar,
):
    panels, panel_rows, _ = inverse.shape
    panel_size = panel_rows // 3
    nodes = force_v.shape[1]
    q = coupling_v.shape[0]
    for c in range(3):
        loads[pl.ds(c, nodes, stride=3), :] = force_v[c].astype(F32)
    spare = corner_t.shape[0] - len(TERMS) * TERM
    stress_corner[len(TERMS) * TERM :, :] = jnp.zeros((spare, stress_corner.shape[1]), BF16)
    corner_t[len(TERMS) * TERM :, :] = jnp.zeros((spare, 3 * nodes), BF16)
    row_of = lax.broadcasted_iota(jnp.int32, (panel_rows, LANES), 0)
    for p in range(panels):
        start = p * panel_rows
        live = row_of < 3 * panel_v[0:1, p : p + 1]
        columns = []
        for k in range(panel_rows // LANES):
            part = coupling_v[:, start + k * LANES : start + (k + 1) * LANES].astype(F32)
            columns.append(jnp.concatenate([part, jnp.zeros((LANES - q, LANES), F32)], axis=0).T)
        sides = [loads[start : start + panel_rows, :], jnp.concatenate(columns, axis=0)]
        sides = jnp.concatenate([jnp.where(live, x, 0.0).astype(BF16) for x in sides], axis=1)
        result = dot(inverse[p], sides)
        for side in range(2):
            solved[side] = jnp.where(live, result[:, side * LANES : (side + 1) * LANES], 0.0)
        for c in range(3):
            cols = slice(c * nodes + p * panel_size, c * nodes + (p + 1) * panel_size)
            free_t[:, cols] = solved[0, pl.ds(c, panel_size, stride=3), :].T
            value = solved[1, pl.ds(c, panel_size, stride=3), :].T[:TERM]
            whole[:, cols] = value
            pieces = split_three(value)
            for k, (piece, _) in enumerate(TERMS):
                corner_t[k * TERM : (k + 1) * TERM, cols] = pieces[piece]

    def store(i, start, value):
        pieces = split_three(value)
        for k, (piece, _) in enumerate(TERMS):
            stress_corner[k * TERM : (k + 1) * TERM, i * LANES : (i + 1) * LANES] = pieces[piece]

    parts = jnp.concatenate([whole[:, c * nodes : (c + 1) * nodes] for c in range(3)], axis=0)
    element_stress(split_two(parts), TERM, onehot, scaled, sofar, store)
    free_stress(free_t, 0, stress_first.shape[1], onehot, scaled, sofar, stress_first)


def stress_kernel(free_t, onehot, scaled, out, sofar):
    rows = out.shape[1]
    free_stress(free_t, free_t.shape[0] - rows, rows, onehot, scaled, sofar, out)


def join_kernel(*refs):
    *parts, out = refs
    start = 0
    for part in parts:
        out[start : start + part.shape[0], :] = part[...]
        start += part.shape[0]


def solve_kernel(
    near,
    across,
    select,
    stress_first,
    stress_rest,
    stress_corner,
    face,
    values,
    stress,
    sub_a,
    sub_b,
    grp_a,
    grp_b,
    terms,
):
    rows = near.shape[0]
    terms[:, 2 * rows :, :] = jnp.zeros((3, terms.shape[1] - 2 * rows, terms.shape[2]), BF16)
    for b, block in enumerate((near, across)):
        for t, value in enumerate(split_three(block[...])):
            terms[t, b * rows : (b + 1) * rows, :] = value
    picked = [dot(select[...], terms[t]) for t in range(3)]
    ordered = [picked[term] for _, term in TERMS]
    ordered += [jnp.zeros_like(picked[0])] * (stress_corner.shape[0] // TERM - len(ordered))
    per = LANES // TERM
    for k in range(0, len(ordered), per):
        block = jnp.concatenate(ordered[k : k + per], axis=0).T.astype(BF16)
        values[:, k * TERM : (k + per) * TERM] = block
    moved = dot(values[...], stress_corner[...])
    for i in range(COMPS):
        cols = slice(i * LANES, (i + 1) * LANES)
        free = jnp.concatenate([stress_first[i], stress_rest[i]], axis=0)
        high, low = split_two(free - moved[:, cols])
        stress[cols, 0:LANES] = high
        stress[cols, LANES : 2 * LANES] = low

    rows = dot_nt(face[...], stress[...])
    for i in range(COMPS):
        part = rows[:, i * LANES : (i + 1) * LANES]
        edge = [part[EDGES + NED * k : EDGES + NED * (k + 1)] for k in range(4)]
        sub_a[i] = part[:NIS]
        sub_b[i] = part[NIS : 2 * NIS]
        grp_a[i] = jnp.concatenate([part[2 * NIS : 2 * NIS + NIG], edge[0], edge[2]], axis=0)
        grp_b[i] = jnp.concatenate([part[2 * NIS + NIG : EDGES], edge[1], edge[3]], axis=0)


def edge_kernel(grp_a, grp_b, from_a, from_b, edge_b, edge_a):
    split = NIG + NED
    edge_a[:, :NED, :] = grp_a[:, NIG:split, :] + from_a[:, NIG:split, :]
    edge_a[:, NED:, :] = grp_b[:, NIG:split, :] + from_b[:, NIG:split, :]
    edge_b[:, :NED, :] = grp_a[:, split:, :] + from_a[:, split:, :]
    edge_b[:, NED:, :] = grp_b[:, split:, :] + from_b[:, split:, :]


def partial_kernel(
    count, stress, free_t, corner_t, values, placing, grp_a, grp_b, partial, disp_out, received
):
    nodes = disp_out.shape[1]
    for c in range(3):
        cols = slice(c * nodes, (c + 1) * nodes)
        part = free_t[:, cols] - dot(values[...], corner_t[:, cols])
        for k in range(0, nodes, LANES):
            disp_out[c, k : k + LANES, :] = part[:, k : k + LANES].T.astype(BF16)
    split = NIG + NED
    for i in range(COMPS):
        low, high = grp_a[i], grp_b[i]
        rows = [low[:NIG], high[:NIG], low[NIG:split], high[NIG:split], low[split:], high[split:]]
        rows.append(jnp.zeros((2 * LANES - NIF, LANES), F32))
        first, second = split_two(jnp.concatenate(rows, axis=0))
        received[:LANES, i * LANES : (i + 1) * LANES] = first
        received[LANES:, i * LANES : (i + 1) * LANES] = second
    for i in range(0, COMPS, 2):
        cols = slice(i * LANES, (i + 2) * LANES)
        own = dot_nt(count[...], stress[cols, :])
        total = own + dot(placing[...], received[:, cols])
        partial[i] = total[:, :LANES]
        partial[i + 1] = total[:, LANES:]


def finish_kernel(
    placing, partial, inverse_volume, sub_a, sub_b, edge_b, edge_a, out, received, nodal, sems
):
    for i in range(COMPS):
        cols = slice(i * LANES, (i + 1) * LANES)
        late = jnp.concatenate([sub_b[i], edge_a[i], edge_b[i]], axis=0)
        first, second = split_two(late)
        received[:NIS, cols] = sub_a[i].astype(BF16)
        received[NIS : NIS + LATE, cols] = first
        received[NIS + LATE :, cols] = second
    scale = inverse_volume[...]
    copies = []
    for i in range(0, COMPS, 2):
        cols = slice(i * LANES, (i + 2) * LANES)
        added = dot(placing[...], received[:, cols])
        nodal[i] = ((partial[i] + added[:, :LANES]) * scale).astype(BF16)
        nodal[i + 1] = ((partial[i + 1] + added[:, LANES:]) * scale).astype(BF16)
        copy = pltpu.make_async_copy(nodal.at[pl.ds(i, 2)], out.at[pl.ds(i, 2)], sems.at[i // 2])
        copy.start()
        copies.append(copy)
    for copy in copies:
        copy.wait()


def vmem(count):
    return [pl.BlockSpec(memory_space=pltpu.VMEM)] * count


def anywhere(count):
    return [pl.BlockSpec(memory_space=pl.ANY)] * count


def hbm(count):
    return [pl.BlockSpec(memory_space=pltpu.HBM)] * count


def array(shape, dtype=F32):
    return jax.ShapeDtypeStruct(shape, dtype)


def call(kernel, name, out_shape, in_specs, scratch=(), flops=0, moved=0, out_specs=None):
    return pl.pallas_call(
        kernel,
        name=name,
        out_shape=out_shape,
        in_specs=in_specs,
        out_specs=out_specs or vmem(len(out_shape)),
        scratch_shapes=list(scratch),
        compiler_params=pltpu.CompilerParams(vmem_limit_bytes=VMEM_LIMIT),
        cost_estimate=pl.CostEstimate(flops=flops, bytes_accessed=moved, transcendentals=0),
    )


def exchange(block, axis, first):
    count = lax.axis_size(axis)
    pairs = []
    for i in range(first, count - 1, 2):
        pairs += [(i, i + 1), (i + 1, i)]
    return lax.ppermute(block, axis, pairs)


def in_hbm(*arrays):
    return [pltpu.with_memory_space_constraint(x, pltpu.HBM) for x in arrays]


def gather_near(coarse, own, ahead):
    beyond = exchange(coarse, "sub", 1)
    beside = exchange(coarse, "sub", 0)
    parts = [own, beyond, beside]
    distance = lax.axis_size("grp") // 2
    while distance:
        rows = sum(x.shape[0] for x in parts)
        before, ahead = ahead[:1], ahead[1:]

        def join(*refs, skip=len(before)):
            join_kernel(*refs[: len(refs) - 1 - skip], refs[-1])

        (block,) = call(
            join,
            "join_blocks",
            (array((rows, parts[0].shape[1])),),
            vmem(len(parts)) + anywhere(len(before)),
        )(*parts, *before)
        pairs = [(i, i ^ distance) for i in range(lax.axis_size("grp"))]
        parts = [block, lax.ppermute(block, "grp", pairs)]
        distance //= 2
    return parts


def shards(
    coarse,
    corner_idx,
    coupling,
    force,
    panel_inv,
    panel_nodes,
    strain_disp,
    modulus,
    connect,
    interface,
    nodal_volume,
):
    nodes, _, cases = force.shape
    dofs = 3 * nodes
    q = corner_idx.shape[1]

    def lists(*refs):
        prepare_lists(coarse.shape[0], lax.axis_size("grp"), *refs)

    own, *panels, select, onehot, face, scaled, count, placing, placing_last, inverse_volume = call(
        lists,
        "prepare_lists",
        (
            array(coarse.shape),
            array(panel_nodes.shape, jnp.int32),
            array((q, dofs), BF16),
            array((3, nodes, cases), BF16),
            array(panel_inv.shape, BF16),
            array((TERM, 3 * LANES), BF16),
            array((nodes, CORNERS * LANES), BF16),
            array((NIF, 2 * LANES), BF16),
            array((COMPS * 24, 8, LANES)),
            array((nodes, 2 * LANES), BF16),
            array((nodes, 2 * LANES), BF16),
            array((nodes, 2 * LANES), BF16),
            array((nodes, LANES)),
        ),
        hbm(11),
        (
            pltpu.VMEM((1, q), jnp.int32),
            pltpu.VMEM(connect.shape, jnp.int32),
            pltpu.VMEM(interface.shape, jnp.int32),
            pltpu.VMEM((COMPS * 24, LANES), BF16),
            pltpu.VMEM((1, LANES), F32),
            pltpu.VMEM((nodes // LANES, LANES), F32),
            pltpu.VMEM((8, 2 * LANES), F32),
            pltpu.SemaphoreType.DMA((11,)),
        ),
        flops=100000000,
        moved=4000000,
    )(
        *in_hbm(
            corner_idx,
            connect,
            interface,
            strain_disp.reshape(COMPS * 24, LANES),
            modulus.reshape(1, -1),
            nodal_volume.reshape(-1, LANES),
            coarse,
            panel_nodes,
            coupling.T,
            jnp.transpose(force, (1, 0, 2)),
            panel_inv,
        )
    )
    first = 64
    free_t, corner_t, stress_first, stress_corner = call(
        prepare_panels,
        "prepare_panels",
        (
            array((cases, dofs)),
            array((2 * LANES, dofs), BF16),
            array((COMPS, first, LANES)),
            array((2 * LANES, COMPS * LANES), BF16),
        ),
        vmem(6),
        (
            pltpu.VMEM((dofs, cases), F32),
            pltpu.VMEM((2, panel_inv.shape[1], LANES), F32),
            pltpu.VMEM((TERM, dofs), F32),
            pltpu.VMEM((COMPS, max(first, TERM), LANES), F32),
        ),
        flops=400000000,
        moved=4000000,
    )(*panels, onehot, scaled)
    (stress_rest,) = call(
        stress_kernel,
        "stress_of_loads",
        (array((COMPS, cases - first, LANES)),),
        vmem(3),
        (pltpu.VMEM((COMPS, cases - first, LANES), F32),),
        flops=400000000,
        moved=4000000,
    )(free_t, onehot, scaled)

    near = gather_near(coarse, own, [select, corner_t])
    values, stress, sub_a, sub_b, grp_a, grp_b = call(
        solve_kernel,
        "stress_and_rows",
        (
            array((cases, 2 * LANES), BF16),
            array((COMPS * cases, 2 * LANES), BF16),
            array((COMPS, NIS, cases)),
            array((COMPS, NIS, cases)),
            array((COMPS, NIG + 2 * NED, cases)),
            array((COMPS, NIG + 2 * NED, cases)),
        ),
        vmem(7),
        (pltpu.VMEM((3, 3 * LANES, cases), BF16),),
        flops=300000000,
        moved=3000000,
    )(*near, select, stress_first, stress_rest, stress_corner, face)
    from_sub_a = exchange(sub_a, "sub", 0)
    from_grp_a = exchange(grp_a, "grp", 0)
    from_grp_b = exchange(grp_b, "grp", 1)
    edge_b, edge_a = call(
        edge_kernel,
        "sum_edges",
        (array((COMPS, 2 * NED, cases)), array((COMPS, 2 * NED, cases))),
        vmem(4),
    )(grp_a, grp_b, from_grp_a, from_grp_b)
    from_sub_b = exchange(sub_b, "sub", 1)
    from_edge_b = exchange(edge_b, "sub", 1)
    from_edge_a = exchange(edge_a, "sub", 0)
    partial, disp = call(
        partial_kernel,
        "assemble_nodes",
        (array((COMPS, nodes, cases)), array((3, nodes, cases), BF16)),
        vmem(8),
        (pltpu.VMEM((2 * LANES, COMPS * cases), BF16),),
        flops=400000000,
        moved=2000000,
    )(count, stress, free_t, corner_t, values, placing, from_grp_a, from_grp_b)
    (nodal,) = call(
        finish_kernel,
        "add_last",
        (array((COMPS, nodes, cases), BF16),),
        vmem(7),
        (
            pltpu.VMEM((NIS + 2 * LATE, COMPS * cases), BF16),
            pltpu.VMEM((COMPS, nodes, cases), BF16),
            pltpu.SemaphoreType.DMA((COMPS // 2,)),
        ),
        flops=400000000,
        moved=3000000,
        out_specs=hbm(1),
    )(placing_last, partial, inverse_volume, from_sub_a, from_sub_b, from_edge_b, from_edge_a)
    return jnp.transpose(disp, (1, 0, 2)), jnp.transpose(nodal, (1, 0, 2))


def solution(mesh):
    owner = ("sub", "grp")
    placed = (
        P(owner, None),
        P(owner, None),
        P(owner, None),
        P(owner, None, None),
        P(owner, None, None),
        P(owner, None),
        P(None, None, owner),
        P(owner),
        P(None, owner),
        P(owner, None),
        P(owner),
    )
    return jax.shard_map(
        shards,
        mesh=mesh,
        in_specs=placed,
        out_specs=(P(owner, None, None), P(owner, None, None)),
        check_vma=False,
    )
```

```python
import jax
import jax.numpy as jnp
from jax import lax
from jax.experimental import pallas as pl
from jax.experimental.pallas import tpu as pltpu
from jax.sharding import PartitionSpec as P

NIS = 64
NIG = 32
NED = 8
EDGES = 2 * NIS + 2 * NIG
NIF = EDGES + 4 * NED
LATE = NIS + 4 * NED
CORNERS = 8
COMPS = 6
LANES = 128
TERM = 32
SPARE = 8
TERMS = ((0, 0), (0, 1), (0, 2), (1, 0), (1, 1), (2, 0))

POISSON = 0.3
LAME = POISSON / ((1.0 + POISSON) * (1.0 - 2.0 * POISSON))
SHEAR = 0.5 / (1.0 + POISSON)

F32 = jnp.float32
BF16 = jnp.bfloat16
VMEM_LIMIT = 24 * 1024 * 1024


def split_two(x):
    high = x.astype(BF16)
    return high, (x - high.astype(F32)).astype(BF16)


def split_three(x):
    high = x.astype(BF16)
    rest = x - high.astype(F32)
    middle = rest.astype(BF16)
    return high, middle, (rest - middle.astype(F32)).astype(BF16)


def dot(a, b):
    return jnp.dot(a, b, preferred_element_type=F32)


def dot_nt(a, b):
    return lax.dot_general(a, b, (((1,), (1,)), ((), ())), preferred_element_type=F32)


def column(row):
    return jnp.broadcast_to(row, (LANES, LANES)).T


def swap_lanes(x, distance):
    lane = lax.broadcasted_iota(jnp.int32, x.shape, 1)
    after = pltpu.roll(x, LANES - distance, 1)
    before = pltpu.roll(x, distance, 1)
    return jnp.where((lane & distance) == 0, after, before)


def order_lists(ids):
    sub_even = (lax.axis_index("sub") & 1) == 0
    grp_even = (lax.axis_index("grp") & 1) == 0
    first, second = ids[:, :LANES], ids[:, LANES:]
    ids[:, :LANES] = jnp.where(sub_even, swap_lanes(first, NIS), first)
    lane = lax.broadcasted_iota(jnp.int32, second.shape, 1)
    groups = jnp.where(grp_even, swap_lanes(second, NIG), second)
    edges = jnp.where(sub_even, swap_lanes(second, 2 * NED), second)
    edges = jnp.where(grp_even, swap_lanes(edges, NED), edges)
    ids[:, LANES:] = jnp.where(lane < 2 * NIG, groups, edges)


def element_stress(terms, rows, onehot, scaled, sofar, store):
    step = 32
    pairs = onehot.shape[1] // (2 * LANES)
    for pair in range(pairs):
        operand = onehot[:, 2 * LANES * pair : 2 * LANES * (pair + 1)]
        elem = dot(terms[0], operand)
        for term in terms[1:]:
            elem = elem + dot(term, operand)
        for start in range(0, rows, step):
            sums = [None] * COMPS if pair == 0 else [sofar[i, start : start + step, :] for i in range(COMPS)]
            for half in range(2):
                for c in range(3):
                    x = elem[c * rows + start : c * rows + start + step, half * LANES : (half + 1) * LANES]
                    x = x.reshape(step // 8, 8, LANES)
                    for i in range(COMPS):
                        term = scaled[24 * i + 3 * (2 * pair + half) + c] * x
                        term = term.reshape(step, LANES)
                        sums[i] = term if sums[i] is None else sums[i] + term
            for i in range(COMPS):
                if pair < pairs - 1:
                    sofar[i, start : start + step, :] = sums[i]
                else:
                    store(i, start, sums[i])


def free_stress(free_t, first, rows, onehot, scaled, sofar, out):
    nodes = onehot.shape[0]
    parts = [free_t[first : first + rows, c * nodes : (c + 1) * nodes] for c in range(3)]

    def store(i, start, value):
        out[i, start : start + value.shape[0], :] = value

    element_stress(split_two(jnp.concatenate(parts, axis=0)), rows, onehot, scaled, sofar, store)


def start_copies(pairs, sems):
    copies = [pltpu.make_async_copy(src, dst, sems.at[k]) for k, (src, dst) in enumerate(pairs)]
    for copy in copies:
        copy.start()
    return copies


def prepare_lists(
    block_rows,
    members,
    corner_idx,
    connect,
    interface,
    strain_disp,
    modulus,
    volume,
    coarse,
    panel_nodes,
    coupling,
    force,
    panel_inv,
    own,
    panel_v,
    coupling_v,
    force_v,
    inverse,
    select,
    onehot,
    face,
    scaled,
    count,
    placing,
    placing_last,
    inverse_volume,
    corner_v,
    connect_v,
    interface_v,
    strain_v,
    modulus_v,
    volume_v,
    ids,
    sems,
):
    copies = start_copies(
        [
            (connect, connect_v),
            (interface, interface_v),
            (corner_idx, corner_v),
            (modulus, modulus_v),
            (strain_disp, strain_v),
            (volume, volume_v),
            (coarse, own),
            (panel_nodes, panel_v),
            (coupling, coupling_v),
            (force, force_v),
            (panel_inv, inverse),
        ],
        sems,
    )
    nodes = onehot.shape[0]
    q = corner_idx.shape[1]

    copies[0].wait()
    node_of = lax.broadcasted_iota(jnp.int32, (nodes, LANES), 0)
    total = jnp.zeros((nodes, LANES), F32)
    for a in range(CORNERS):
        hit = jnp.where(connect_v[a : a + 1, :] == node_of, 1.0, 0.0)
        onehot[:, a * LANES : (a + 1) * LANES] = hit.astype(BF16)
        total = total + hit
    total = total.astype(BF16)
    count[:, :LANES] = total
    count[:, LANES:] = total

    copies[1].wait()
    ids[...] = jnp.full(ids.shape, -1.0, F32)
    ids[0:1, 0:NIF] = interface_v[...].astype(F32)
    order_lists(ids)
    lane = lax.broadcasted_iota(jnp.int32, (8, LANES), 1)
    edges = pltpu.roll(ids[:, LANES:], LANES - NIS, 1)
    again = pltpu.roll(ids[:, :LANES], LANES - NIS + 4 * NED, 1)
    last = jnp.where(lane < 4 * NED, edges, again)
    last = jnp.where(lane < LATE, last, pltpu.roll(edges, LATE, 1))
    for row, target in ((ids[0:1, LANES:], 0), (ids[0:1, :LANES], 1), (last[0:1], 2)):
        hit = jnp.where(row.astype(jnp.int32) == node_of, 1.0, 0.0).astype(BF16)
        if target == 0:
            placing[:, :LANES] = hit
            placing[:, LANES:] = hit
        else:
            placing_last[:, (target - 1) * LANES : target * LANES] = hit
    connect_f = connect_v[...].astype(F32)
    for half in range(2):
        id_col = column(ids[0:1, half * LANES : (half + 1) * LANES])
        rows = jnp.zeros((LANES, LANES), F32)
        for a in range(CORNERS):
            rows = rows + jnp.where(connect_f[a : a + 1, :] == id_col, 1.0, 0.0)
        rows = rows.astype(BF16)[: min(LANES, NIF - half * LANES)]
        face[half * LANES : half * LANES + rows.shape[0], :LANES] = rows
        face[half * LANES : half * LANES + rows.shape[0], LANES:] = rows

    copies[2].wait()
    ids[0:1, 0:q] = corner_v[...].astype(F32)
    wanted = column(ids[0:1, :LANES])[:TERM]
    lane = lax.broadcasted_iota(jnp.int32, (TERM, 3 * LANES), 1)
    entry = lax.broadcasted_iota(jnp.int32, (TERM, LANES), 0)
    s, g = lax.axis_index("sub"), lax.axis_index("grp")
    aside = 1 - 2 * (s & 1)
    row = jnp.full((TERM, 3 * LANES), -1, jnp.int32)
    base = 0
    for member in range(members):
        distance, bits, turn = members // 2, member, 0
        while distance:
            turn += (bits & 1) * distance
            distance, bits = distance // 2, bits >> 1
        for owner in (s, s - aside, s + aside):
            first = (owner * members + (g ^ turn)) * block_rows
            row = jnp.where((lane >= base) & (lane < base + block_rows), first - base + lane, row)
            base += block_rows
    for b in range(3):
        cols = slice(b * LANES, (b + 1) * LANES)
        hit = (wanted == row[:, cols].astype(F32)) & (entry < q)
        select[:, cols] = jnp.where(hit, 1.0, 0.0).astype(BF16)

    copies[3].wait()
    copies[4].wait()
    factor = modulus_v[...]
    whole = strain_v[...].astype(F32)
    rows = [whole[24 * i : 24 * (i + 1)] for i in range(COMPS)]
    trace = (rows[0] + rows[1] + rows[2]) * LAME
    for i in range(COMPS):
        value = trace + rows[i] * (2.0 * SHEAR) if i < 3 else rows[i] * SHEAR
        scaled[24 * i : 24 * (i + 1)] = jnp.broadcast_to((value * factor)[:, None, :], (24, 8, LANES))

    copies[5].wait()
    for k in range(nodes // LANES):
        inverse_volume[k * LANES : (k + 1) * LANES, :] = column(1.0 / volume_v[k : k + 1, :])
    for copy in copies[6:]:
        copy.wait()


def prepare_panels(
    panel_v,
    coupling_v,
    force_v,
    inverse,
    onehot,
    scaled,
    free_t,
    corner_t,
    stress_first,
    stress_corner,
    loads,
    solved,
    whole,
    sofar,
):
    panels, panel_rows, _ = inverse.shape
    panel_size = panel_rows // 3
    nodes = force_v.shape[1]
    q = coupling_v.shape[0]
    for c in range(3):
        loads[pl.ds(c, nodes, stride=3), :] = force_v[c].astype(F32)
    spare = corner_t.shape[0] - len(TERMS) * TERM
    stress_corner[len(TERMS) * TERM :, :] = jnp.zeros((spare, stress_corner.shape[1]), BF16)
    corner_t[len(TERMS) * TERM :, :] = jnp.zeros((spare, 3 * nodes), BF16)
    row_of = lax.broadcasted_iota(jnp.int32, (panel_rows, LANES), 0)
    for p in range(panels):
        start = p * panel_rows
        live = row_of < 3 * panel_v[0:1, p : p + 1]
        columns = []
        for k in range(panel_rows // LANES):
            part = coupling_v[:, start + k * LANES : start + (k + 1) * LANES].astype(F32)
            columns.append(jnp.concatenate([part, jnp.zeros((LANES - q, LANES), F32)], axis=0).T)
        sides = [loads[start : start + panel_rows, :], jnp.concatenate(columns, axis=0)]
        sides = jnp.concatenate([jnp.where(live, x, 0.0).astype(BF16) for x in sides], axis=1)
        result = dot(inverse[p], sides)
        for side in range(2):
            solved[side, :panel_rows, :] = jnp.where(live, result[:, side * LANES : (side + 1) * LANES], 0.0)
        for c in range(3):
            cols = slice(c * nodes + p * panel_size, c * nodes + (p + 1) * panel_size)
            free_t[:, cols] = solved[0, pl.ds(c, panel_size, stride=3), :].T
            value = solved[1, pl.ds(c, panel_size, stride=3), :].T[:TERM]
            whole[:, cols] = value
            pieces = split_three(value)
            for k, (piece, _) in enumerate(TERMS):
                corner_t[k * TERM : (k + 1) * TERM, cols] = pieces[piece]

    def store(i, start, value):
        pieces = split_three(value)
        for k, (piece, _) in enumerate(TERMS):
            stress_corner[k * TERM : (k + 1) * TERM, i * LANES : (i + 1) * LANES] = pieces[piece]

    parts = jnp.concatenate([whole[:, c * nodes : (c + 1) * nodes] for c in range(3)], axis=0)
    element_stress(split_two(parts), TERM, onehot, scaled, sofar, store)
    free_stress(free_t, 0, stress_first.shape[1], onehot, scaled, sofar, stress_first)


def stress_kernel(free_t, onehot, scaled, out, sofar):
    rows = out.shape[1]
    free_stress(free_t, free_t.shape[0] - rows, rows, onehot, scaled, sofar, out)


def join_kernel(*refs):
    *parts, out = refs
    start = 0
    for part in parts:
        out[start : start + part.shape[0], :] = part[...]
        start += part.shape[0]


def solve_kernel(
    near,
    across,
    select,
    stress_first,
    stress_rest,
    stress_corner,
    face,
    values,
    stress,
    sub_a,
    sub_b,
    grp_a,
    grp_b,
    terms,
):
    rows = near.shape[0]
    terms[:, 2 * rows :, :] = jnp.zeros((3, terms.shape[1] - 2 * rows, terms.shape[2]), BF16)
    for b, block in enumerate((near, across)):
        for t, value in enumerate(split_three(block[...])):
            terms[t, b * rows : (b + 1) * rows, :] = value
    picked = [dot(select[...], terms[t]) for t in range(3)]
    ordered = [picked[term] for _, term in TERMS]
    ordered += [jnp.zeros_like(picked[0])] * (stress_corner.shape[0] // TERM - len(ordered))
    per = LANES // TERM
    for k in range(0, len(ordered), per):
        block = jnp.concatenate(ordered[k : k + per], axis=0).T.astype(BF16)
        values[:, k * TERM : (k + per) * TERM] = block
    moved = dot(values[...], stress_corner[...])
    for i in range(COMPS):
        cols = slice(i * LANES, (i + 1) * LANES)
        free = jnp.concatenate([stress_first[i], stress_rest[i]], axis=0)
        high, low = split_two(free - moved[:, cols])
        stress[cols, 0:LANES] = high
        stress[cols, LANES : 2 * LANES] = low

    rows = dot_nt(face[...], stress[...])
    for i in range(COMPS):
        part = rows[:, i * LANES : (i + 1) * LANES]
        edge = [part[EDGES + NED * k : EDGES + NED * (k + 1)] for k in range(4)]
        sub_a[i] = part[:NIS]
        sub_b[i] = part[NIS : 2 * NIS]
        grp_a[i] = jnp.concatenate([part[2 * NIS : 2 * NIS + NIG], edge[0], edge[2]], axis=0)
        grp_b[i] = jnp.concatenate([part[2 * NIS + NIG : EDGES], edge[1], edge[3]], axis=0)


def edge_kernel(grp_a, grp_b, from_a, from_b, edge_b, edge_a):
    split = NIG + NED
    edge_a[:, :NED, :] = grp_a[:, NIG:split, :] + from_a[:, NIG:split, :]
    edge_a[:, NED:, :] = grp_b[:, NIG:split, :] + from_b[:, NIG:split, :]
    edge_b[:, :NED, :] = grp_a[:, split:, :] + from_a[:, split:, :]
    edge_b[:, NED:, :] = grp_b[:, split:, :] + from_b[:, split:, :]


def partial_kernel(
    count, stress, free_t, corner_t, values, placing, grp_a, grp_b, partial, disp_out, received
):
    nodes = disp_out.shape[1]
    for c in range(3):
        cols = slice(c * nodes, (c + 1) * nodes)
        part = free_t[:, cols] - dot(values[...], corner_t[:, cols])
        for k in range(0, nodes, LANES):
            disp_out[c, k : k + LANES, :] = part[:, k : k + LANES].T.astype(BF16)
    split = NIG + NED
    for i in range(COMPS):
        low, high = grp_a[i], grp_b[i]
        rows = [low[:NIG], high[:NIG], low[NIG:split], high[NIG:split], low[split:], high[split:]]
        rows.append(jnp.zeros((2 * LANES - NIF, LANES), F32))
        first, second = split_two(jnp.concatenate(rows, axis=0))
        received[:LANES, i * LANES : (i + 1) * LANES] = first
        received[LANES:, i * LANES : (i + 1) * LANES] = second
    for i in range(0, COMPS, 2):
        cols = slice(i * LANES, (i + 2) * LANES)
        own = dot_nt(count[...], stress[cols, :])
        total = own + dot(placing[...], received[:, cols])
        partial[i] = total[:, :LANES]
        partial[i + 1] = total[:, LANES:]


def finish_kernel(
    placing, partial, inverse_volume, sub_a, sub_b, edge_b, edge_a, out, received, nodal, sems
):
    scale = inverse_volume[...]
    copies = []
    for i in range(0, COMPS, 2):
        for k in (i, i + 1):
            cols = slice(k * LANES, (k + 1) * LANES)
            late = jnp.concatenate([sub_b[k], edge_a[k], edge_b[k]], axis=0)
            first, second = split_two(late)
            received[:NIS, cols] = sub_a[k].astype(BF16)
            received[NIS : NIS + LATE, cols] = first
            received[NIS + LATE :, cols] = second
        added = dot(placing[...], received[:, i * LANES : (i + 2) * LANES])
        nodal[i] = ((partial[i] + added[:, :LANES]) * scale).astype(BF16)
        nodal[i + 1] = ((partial[i + 1] + added[:, LANES:]) * scale).astype(BF16)
        copy = pltpu.make_async_copy(nodal.at[pl.ds(i, 2)], out.at[pl.ds(i, 2)], sems.at[i // 2])
        copy.start()
        copies.append(copy)
    for copy in copies:
        copy.wait()


def vmem(count):
    return [pl.BlockSpec(memory_space=pltpu.VMEM)] * count


def anywhere(count):
    return [pl.BlockSpec(memory_space=pl.ANY)] * count


def hbm(count):
    return [pl.BlockSpec(memory_space=pltpu.HBM)] * count


def array(shape, dtype=F32):
    return jax.ShapeDtypeStruct(shape, dtype)


def call(kernel, name, out_shape, in_specs, scratch=(), flops=0, moved=0, out_specs=None):
    return pl.pallas_call(
        kernel,
        name=name,
        out_shape=out_shape,
        in_specs=in_specs,
        out_specs=out_specs or vmem(len(out_shape)),
        scratch_shapes=list(scratch),
        compiler_params=pltpu.CompilerParams(vmem_limit_bytes=VMEM_LIMIT),
        cost_estimate=pl.CostEstimate(flops=flops, bytes_accessed=moved, transcendentals=0),
    )


def exchange(block, axis, first):
    count = lax.axis_size(axis)
    pairs = []
    for i in range(first, count - 1, 2):
        pairs += [(i, i + 1), (i + 1, i)]
    return lax.ppermute(block, axis, pairs)


def in_hbm(*arrays):
    return [pltpu.with_memory_space_constraint(x, pltpu.HBM) for x in arrays]


def gather_near(coarse, own, ahead):
    beyond = exchange(coarse, "sub", 1)
    beside = exchange(coarse, "sub", 0)
    parts = [own, beyond, beside]
    distance = lax.axis_size("grp") // 2
    while distance:
        rows = sum(x.shape[0] for x in parts)
        before, ahead = ahead[:1], ahead[1:]

        def join(*refs, skip=len(before)):
            join_kernel(*refs[: len(refs) - 1 - skip], refs[-1])

        (block,) = call(
            join,
            "join_blocks",
            (array((rows, parts[0].shape[1])),),
            vmem(len(parts)) + anywhere(len(before)),
        )(*parts, *before)
        pairs = [(i, i ^ distance) for i in range(lax.axis_size("grp"))]
        parts = [block, lax.ppermute(block, "grp", pairs)]
        distance //= 2
    return parts


def shards(
    coarse,
    corner_idx,
    coupling,
    force,
    panel_inv,
    panel_nodes,
    strain_disp,
    modulus,
    connect,
    interface,
    nodal_volume,
):
    nodes, _, cases = force.shape
    dofs = 3 * nodes
    q = corner_idx.shape[1]

    def lists(*refs):
        prepare_lists(coarse.shape[0], lax.axis_size("grp"), *refs)

    own, *panels, select, onehot, face, scaled, count, placing, placing_last, inverse_volume = call(
        lists,
        "prepare_lists",
        (
            array(coarse.shape),
            array(panel_nodes.shape, jnp.int32),
            array((q, dofs), BF16),
            array((3, nodes, cases), BF16),
            array(panel_inv.shape, BF16),
            array((TERM, 3 * LANES), BF16),
            array((nodes, CORNERS * LANES), BF16),
            array((NIF, 2 * LANES), BF16),
            array((COMPS * 24, 8, LANES)),
            array((nodes, 2 * LANES), BF16),
            array((nodes, 2 * LANES), BF16),
            array((nodes, 2 * LANES), BF16),
            array((nodes, LANES)),
        ),
        hbm(11),
        (
            pltpu.VMEM((1, q), jnp.int32),
            pltpu.VMEM(connect.shape, jnp.int32),
            pltpu.VMEM(interface.shape, jnp.int32),
            pltpu.VMEM((COMPS * 24, LANES), BF16),
            pltpu.VMEM((1, LANES), F32),
            pltpu.VMEM((nodes // LANES, LANES), F32),
            pltpu.VMEM((8, 2 * LANES), F32),
            pltpu.SemaphoreType.DMA((11,)),
        ),
        flops=100000000,
        moved=4000000,
    )(
        *in_hbm(
            corner_idx,
            connect,
            interface,
            strain_disp.reshape(COMPS * 24, LANES),
            modulus.reshape(1, -1),
            nodal_volume.reshape(-1, LANES),
            coarse,
            panel_nodes,
            coupling.T,
            jnp.transpose(force, (1, 0, 2)),
            panel_inv,
        )
    )
    first = 64
    free_t, corner_t, stress_first, stress_corner = call(
        prepare_panels,
        "prepare_panels",
        (
            array((cases, dofs)),
            array((2 * LANES, dofs), BF16),
            array((COMPS, first, LANES)),
            array((2 * LANES, COMPS * LANES), BF16),
        ),
        vmem(6),
        (
            pltpu.VMEM((dofs + SPARE, cases), F32),
            pltpu.VMEM((2, panel_inv.shape[1] + SPARE, LANES), F32),
            pltpu.VMEM((TERM, dofs), F32),
            pltpu.VMEM((COMPS, max(first, TERM), LANES), F32),
        ),
        flops=400000000,
        moved=4000000,
    )(*panels, onehot, scaled)
    (stress_rest,) = call(
        stress_kernel,
        "stress_of_loads",
        (array((COMPS, cases - first, LANES)),),
        vmem(3),
        (pltpu.VMEM((COMPS, cases - first, LANES), F32),),
        flops=400000000,
        moved=4000000,
    )(free_t, onehot, scaled)

    near = gather_near(coarse, own, [select, corner_t])
    values, stress, sub_a, sub_b, grp_a, grp_b = call(
        solve_kernel,
        "stress_and_rows",
        (
            array((cases, 2 * LANES), BF16),
            array((COMPS * cases, 2 * LANES), BF16),
            array((COMPS, NIS, cases)),
            array((COMPS, NIS, cases)),
            array((COMPS, NIG + 2 * NED, cases)),
            array((COMPS, NIG + 2 * NED, cases)),
        ),
        vmem(7),
        (pltpu.VMEM((3, 3 * LANES, cases), BF16),),
        flops=300000000,
        moved=3000000,
    )(*near, select, stress_first, stress_rest, stress_corner, face)
    from_sub_a = exchange(sub_a, "sub", 0)
    from_grp_a = exchange(grp_a, "grp", 0)
    from_grp_b = exchange(grp_b, "grp", 1)
    edge_b, edge_a = call(
        edge_kernel,
        "sum_edges",
        (array((COMPS, 2 * NED, cases)), array((COMPS, 2 * NED, cases))),
        vmem(4),
    )(grp_a, grp_b, from_grp_a, from_grp_b)
    from_sub_b = exchange(sub_b, "sub", 1)
    from_edge_b = exchange(edge_b, "sub", 1)
    from_edge_a = exchange(edge_a, "sub", 0)
    partial, disp = call(
        partial_kernel,
        "assemble_nodes",
        (array((COMPS, nodes, cases)), array((3, nodes, cases), BF16)),
        vmem(8),
        (pltpu.VMEM((2 * LANES, COMPS * cases), BF16),),
        flops=400000000,
        moved=2000000,
    )(count, stress, free_t, corner_t, values, placing, from_grp_a, from_grp_b)
    (nodal,) = call(
        finish_kernel,
        "add_last",
        (array((COMPS, nodes, cases), BF16),),
        vmem(7),
        (
            pltpu.VMEM((NIS + 2 * LATE, COMPS * cases), BF16),
            pltpu.VMEM((COMPS, nodes, cases), BF16),
            pltpu.SemaphoreType.DMA((COMPS // 2,)),
        ),
        flops=400000000,
        moved=3000000,
        out_specs=hbm(1),
    )(placing_last, partial, inverse_volume, from_sub_a, from_sub_b, from_edge_b, from_edge_a)
    return jnp.transpose(disp, (1, 0, 2)), jnp.transpose(nodal, (1, 0, 2))


def solution(mesh):
    owner = ("sub", "grp")
    placed = (
        P(owner, None),
        P(owner, None),
        P(owner, None),
        P(owner, None, None),
        P(owner, None, None),
        P(owner, None),
        P(None, None, owner),
        P(owner),
        P(None, owner),
        P(owner, None),
        P(owner),
    )
    return jax.shard_map(
        shards,
        mesh=mesh,
        in_specs=placed,
        out_specs=(P(owner, None, None), P(owner, None, None)),
        check_vma=False,
    )
```

```python
import jax
import jax.numpy as jnp
from jax import lax
from jax.experimental import pallas as pl
from jax.experimental.pallas import tpu as pltpu
from jax.sharding import PartitionSpec as P

NIS = 64
NIG = 32
NED = 8
EDGES = 2 * NIS + 2 * NIG
NIF = EDGES + 4 * NED
LATE = NIS + 4 * NED
CORNERS = 8
COMPS = 6
LANES = 128
TERM = 32
SPARE = 8
TERMS = ((0, 0), (0, 1), (0, 2), (1, 0), (1, 1), (2, 0))

POISSON = 0.3
LAME = POISSON / ((1.0 + POISSON) * (1.0 - 2.0 * POISSON))
SHEAR = 0.5 / (1.0 + POISSON)

F32 = jnp.float32
BF16 = jnp.bfloat16
VMEM_LIMIT = 24 * 1024 * 1024


def split_two(x):
    high = x.astype(BF16)
    return high, (x - high.astype(F32)).astype(BF16)


def split_three(x):
    high = x.astype(BF16)
    rest = x - high.astype(F32)
    middle = rest.astype(BF16)
    return high, middle, (rest - middle.astype(F32)).astype(BF16)


def dot(a, b):
    return jnp.dot(a, b, preferred_element_type=F32)


def dot_nt(a, b):
    return lax.dot_general(a, b, (((1,), (1,)), ((), ())), preferred_element_type=F32)


def column(row):
    return jnp.broadcast_to(row, (LANES, LANES)).T


def swap_lanes(x, distance):
    lane = lax.broadcasted_iota(jnp.int32, x.shape, 1)
    after = pltpu.roll(x, LANES - distance, 1)
    before = pltpu.roll(x, distance, 1)
    return jnp.where((lane & distance) == 0, after, before)


def order_lists(ids):
    sub_even = (lax.axis_index("sub") & 1) == 0
    grp_even = (lax.axis_index("grp") & 1) == 0
    first, second = ids[:, :LANES], ids[:, LANES:]
    ids[:, :LANES] = jnp.where(sub_even, swap_lanes(first, NIS), first)
    lane = lax.broadcasted_iota(jnp.int32, second.shape, 1)
    groups = jnp.where(grp_even, swap_lanes(second, NIG), second)
    edges = jnp.where(sub_even, swap_lanes(second, 2 * NED), second)
    edges = jnp.where(grp_even, swap_lanes(edges, NED), edges)
    ids[:, LANES:] = jnp.where(lane < 2 * NIG, groups, edges)


def element_stress(terms, rows, onehot, scaled, sofar, store):
    step = 32
    pairs = onehot.shape[1] // (2 * LANES)
    for pair in range(pairs):
        operand = onehot[:, 2 * LANES * pair : 2 * LANES * (pair + 1)]
        elem = dot(terms[0], operand)
        for term in terms[1:]:
            elem = elem + dot(term, operand)
        for start in range(0, rows, step):
            sums = [None] * COMPS if pair == 0 else [sofar[i, start : start + step, :] for i in range(COMPS)]
            for half in range(2):
                for c in range(3):
                    x = elem[c * rows + start : c * rows + start + step, half * LANES : (half + 1) * LANES]
                    x = x.reshape(step // 8, 8, LANES)
                    for i in range(COMPS):
                        term = scaled[24 * i + 3 * (2 * pair + half) + c] * x
                        term = term.reshape(step, LANES)
                        sums[i] = term if sums[i] is None else sums[i] + term
            for i in range(COMPS):
                if pair < pairs - 1:
                    sofar[i, start : start + step, :] = sums[i]
                else:
                    store(i, start, sums[i])


def free_stress(free_t, first, rows, onehot, scaled, sofar, out):
    nodes = onehot.shape[0]
    parts = [free_t[first : first + rows, c * nodes : (c + 1) * nodes] for c in range(3)]

    def store(i, start, value):
        out[i, start : start + value.shape[0], :] = value

    element_stress(split_two(jnp.concatenate(parts, axis=0)), rows, onehot, scaled, sofar, store)


def start_copies(pairs, sems):
    copies = [pltpu.make_async_copy(src, dst, sems.at[k]) for k, (src, dst) in enumerate(pairs)]
    for copy in copies:
        copy.start()
    return copies


def prepare_lists(
    block_rows,
    members,
    corner_idx,
    connect,
    interface,
    strain_disp,
    modulus,
    volume,
    coarse,
    panel_nodes,
    force,
    panel_inv,
    own,
    panel_v,
    force_v,
    inverse,
    select,
    onehot,
    face,
    scaled,
    count,
    placing,
    placing_last,
    inverse_volume,
    corner_v,
    connect_v,
    interface_v,
    strain_v,
    modulus_v,
    volume_v,
    ids,
    sems,
):
    copies = start_copies(
        [
            (connect, connect_v),
            (interface, interface_v),
            (corner_idx, corner_v),
            (modulus, modulus_v),
            (strain_disp, strain_v),
            (volume, volume_v),
            (coarse, own),
            (panel_nodes, panel_v),
            (force, force_v),
            (panel_inv, inverse),
        ],
        sems,
    )
    nodes = onehot.shape[0]
    q = corner_idx.shape[1]

    copies[0].wait()
    node_of = lax.broadcasted_iota(jnp.int32, (nodes, LANES), 0)
    total = jnp.zeros((nodes, LANES), F32)
    for a in range(CORNERS):
        hit = jnp.where(connect_v[a : a + 1, :] == node_of, 1.0, 0.0)
        onehot[:, a * LANES : (a + 1) * LANES] = hit.astype(BF16)
        total = total + hit
    total = total.astype(BF16)
    count[:, :LANES] = total
    count[:, LANES:] = total

    copies[1].wait()
    ids[...] = jnp.full(ids.shape, -1.0, F32)
    ids[0:1, 0:NIF] = interface_v[...].astype(F32)
    order_lists(ids)
    lane = lax.broadcasted_iota(jnp.int32, (8, LANES), 1)
    edges = pltpu.roll(ids[:, LANES:], LANES - NIS, 1)
    again = pltpu.roll(ids[:, :LANES], LANES - NIS + 4 * NED, 1)
    last = jnp.where(lane < 4 * NED, edges, again)
    last = jnp.where(lane < LATE, last, pltpu.roll(edges, LATE, 1))
    for row, target in ((ids[0:1, LANES:], 0), (ids[0:1, :LANES], 1), (last[0:1], 2)):
        hit = jnp.where(row.astype(jnp.int32) == node_of, 1.0, 0.0).astype(BF16)
        if target == 0:
            placing[:, :LANES] = hit
            placing[:, LANES:] = hit
        else:
            placing_last[:, (target - 1) * LANES : target * LANES] = hit
    connect_f = connect_v[...].astype(F32)
    for half in range(2):
        id_col = column(ids[0:1, half * LANES : (half + 1) * LANES])
        rows = jnp.zeros((LANES, LANES), F32)
        for a in range(CORNERS):
            rows = rows + jnp.where(connect_f[a : a + 1, :] == id_col, 1.0, 0.0)
        rows = rows.astype(BF16)[: min(LANES, NIF - half * LANES)]
        face[half * LANES : half * LANES + rows.shape[0], :LANES] = rows
        face[half * LANES : half * LANES + rows.shape[0], LANES:] = rows

    copies[2].wait()
    ids[0:1, 0:q] = corner_v[...].astype(F32)
    wanted = column(ids[0:1, :LANES])[:TERM]
    lane = lax.broadcasted_iota(jnp.int32, (TERM, 3 * LANES), 1)
    entry = lax.broadcasted_iota(jnp.int32, (TERM, LANES), 0)
    s, g = lax.axis_index("sub"), lax.axis_index("grp")
    aside = 1 - 2 * (s & 1)
    row = jnp.full((TERM, 3 * LANES), -1, jnp.int32)
    base = 0
    for member in range(members):
        distance, bits, turn = members // 2, member, 0
        while distance:
            turn += (bits & 1) * distance
            distance, bits = distance // 2, bits >> 1
        for owner in (s, s - aside, s + aside):
            first = (owner * members + (g ^ turn)) * block_rows
            row = jnp.where((lane >= base) & (lane < base + block_rows), first - base + lane, row)
            base += block_rows
    for b in range(3):
        cols = slice(b * LANES, (b + 1) * LANES)
        hit = (wanted == row[:, cols].astype(F32)) & (entry < q)
        select[:, cols] = jnp.where(hit, 1.0, 0.0).astype(BF16)

    copies[3].wait()
    copies[4].wait()
    factor = modulus_v[...]
    whole = strain_v[...].astype(F32)
    rows = [whole[24 * i : 24 * (i + 1)] for i in range(COMPS)]
    trace = (rows[0] + rows[1] + rows[2]) * LAME
    for i in range(COMPS):
        value = trace + rows[i] * (2.0 * SHEAR) if i < 3 else rows[i] * SHEAR
        scaled[24 * i : 24 * (i + 1)] = jnp.broadcast_to((value * factor)[:, None, :], (24, 8, LANES))

    copies[5].wait()
    for k in range(nodes // LANES):
        inverse_volume[k * LANES : (k + 1) * LANES, :] = column(1.0 / volume_v[k : k + 1, :])
    for copy in copies[6:]:
        copy.wait()


def prepare_panels(
    coupling_v,
    panel_v,
    force_v,
    inverse,
    onehot,
    scaled,
    free_t,
    corner_t,
    stress_first,
    stress_corner,
    loads,
    solved,
    whole,
    sofar,
):
    panels, panel_rows, _ = inverse.shape
    panel_size = panel_rows // 3
    nodes = force_v.shape[1]
    q = coupling_v.shape[0]
    for c in range(3):
        loads[pl.ds(c, nodes, stride=3), :] = force_v[c].astype(F32)
    spare = corner_t.shape[0] - len(TERMS) * TERM
    stress_corner[len(TERMS) * TERM :, :] = jnp.zeros((spare, stress_corner.shape[1]), BF16)
    corner_t[len(TERMS) * TERM :, :] = jnp.zeros((spare, 3 * nodes), BF16)
    row_of = lax.broadcasted_iota(jnp.int32, (panel_rows, LANES), 0)
    for p in range(panels):
        start = p * panel_rows
        live = row_of < 3 * panel_v[0:1, p : p + 1]
        columns = []
        for k in range(panel_rows // LANES):
            part = coupling_v[:, start + k * LANES : start + (k + 1) * LANES].astype(F32)
            columns.append(jnp.concatenate([part, jnp.zeros((LANES - q, LANES), F32)], axis=0).T)
        sides = [loads[start : start + panel_rows, :], jnp.concatenate(columns, axis=0)]
        sides = jnp.concatenate([jnp.where(live, x, 0.0).astype(BF16) for x in sides], axis=1)
        result = dot(inverse[p], sides)
        for side in range(2):
            solved[side, :panel_rows, :] = jnp.where(live, result[:, side * LANES : (side + 1) * LANES], 0.0)
        for c in range(3):
            cols = slice(c * nodes + p * panel_size, c * nodes + (p + 1) * panel_size)
            free_t[:, cols] = solved[0, pl.ds(c, panel_size, stride=3), :].T
            value = solved[1, pl.ds(c, panel_size, stride=3), :].T[:TERM]
            whole[:, cols] = value
            pieces = split_three(value)
            for k, (piece, _) in enumerate(TERMS):
                corner_t[k * TERM : (k + 1) * TERM, cols] = pieces[piece]

    def store(i, start, value):
        pieces = split_three(value)
        for k, (piece, _) in enumerate(TERMS):
            stress_corner[k * TERM : (k + 1) * TERM, i * LANES : (i + 1) * LANES] = pieces[piece]

    parts = jnp.concatenate([whole[:, c * nodes : (c + 1) * nodes] for c in range(3)], axis=0)
    element_stress(split_two(parts), TERM, onehot, scaled, sofar, store)
    free_stress(free_t, 0, stress_first.shape[1], onehot, scaled, sofar, stress_first)


def stress_kernel(free_t, onehot, scaled, out, sofar):
    rows = out.shape[1]
    free_stress(free_t, free_t.shape[0] - rows, rows, onehot, scaled, sofar, out)


def join_kernel(*refs):
    *parts, out = refs
    start = 0
    for part in parts:
        out[start : start + part.shape[0], :] = part[...]
        start += part.shape[0]


def solve_kernel(
    near,
    across,
    select,
    stress_first,
    stress_rest,
    stress_corner,
    face,
    values,
    stress,
    sub_a,
    sub_b,
    grp_a,
    grp_b,
    terms,
):
    rows = near.shape[0]
    terms[:, 2 * rows :, :] = jnp.zeros((3, terms.shape[1] - 2 * rows, terms.shape[2]), BF16)
    for b, block in enumerate((near, across)):
        for t, value in enumerate(split_three(block[...])):
            terms[t, b * rows : (b + 1) * rows, :] = value
    picked = [dot(select[...], terms[t]) for t in range(3)]
    ordered = [picked[term] for _, term in TERMS]
    ordered += [jnp.zeros_like(picked[0])] * (stress_corner.shape[0] // TERM - len(ordered))
    per = LANES // TERM
    for k in range(0, len(ordered), per):
        block = jnp.concatenate(ordered[k : k + per], axis=0).T.astype(BF16)
        values[:, k * TERM : (k + per) * TERM] = block
    moved = dot(values[...], stress_corner[...])
    for i in range(COMPS):
        cols = slice(i * LANES, (i + 1) * LANES)
        free = jnp.concatenate([stress_first[i], stress_rest[i]], axis=0)
        high, low = split_two(free - moved[:, cols])
        stress[cols, 0:LANES] = high
        stress[cols, LANES : 2 * LANES] = low

    rows = dot_nt(face[...], stress[...])
    for i in range(COMPS):
        part = rows[:, i * LANES : (i + 1) * LANES]
        edge = [part[EDGES + NED * k : EDGES + NED * (k + 1)] for k in range(4)]
        sub_a[i] = part[:NIS]
        sub_b[i] = part[NIS : 2 * NIS]
        grp_a[i] = jnp.concatenate([part[2 * NIS : 2 * NIS + NIG], edge[0], edge[2]], axis=0)
        grp_b[i] = jnp.concatenate([part[2 * NIS + NIG : EDGES], edge[1], edge[3]], axis=0)


def edge_kernel(grp_a, grp_b, from_a, from_b, edge_b, edge_a):
    split = NIG + NED
    edge_a[:, :NED, :] = grp_a[:, NIG:split, :] + from_a[:, NIG:split, :]
    edge_a[:, NED:, :] = grp_b[:, NIG:split, :] + from_b[:, NIG:split, :]
    edge_b[:, :NED, :] = grp_a[:, split:, :] + from_a[:, split:, :]
    edge_b[:, NED:, :] = grp_b[:, split:, :] + from_b[:, split:, :]


def partial_kernel(
    count, stress, free_t, corner_t, values, placing, grp_a, grp_b, partial, disp_out, received
):
    nodes = disp_out.shape[1]
    for c in range(3):
        cols = slice(c * nodes, (c + 1) * nodes)
        part = free_t[:, cols] - dot(values[...], corner_t[:, cols])
        for k in range(0, nodes, LANES):
            disp_out[c, k : k + LANES, :] = part[:, k : k + LANES].T.astype(BF16)
    split = NIG + NED
    for i in range(COMPS):
        low, high = grp_a[i], grp_b[i]
        rows = [low[:NIG], high[:NIG], low[NIG:split], high[NIG:split], low[split:], high[split:]]
        rows.append(jnp.zeros((2 * LANES - NIF, LANES), F32))
        first, second = split_two(jnp.concatenate(rows, axis=0))
        received[:LANES, i * LANES : (i + 1) * LANES] = first
        received[LANES:, i * LANES : (i + 1) * LANES] = second
    for i in range(0, COMPS, 2):
        cols = slice(i * LANES, (i + 2) * LANES)
        own = dot_nt(count[...], stress[cols, :])
        total = own + dot(placing[...], received[:, cols])
        partial[i] = total[:, :LANES]
        partial[i + 1] = total[:, LANES:]


def finish_kernel(
    placing, partial, inverse_volume, sub_a, sub_b, edge_b, edge_a, out, received, nodal, sems
):
    scale = inverse_volume[...]
    copies = []
    for i in range(0, COMPS, 2):
        for k in (i, i + 1):
            cols = slice(k * LANES, (k + 1) * LANES)
            late = jnp.concatenate([sub_b[k], edge_a[k], edge_b[k]], axis=0)
            first, second = split_two(late)
            received[:NIS, cols] = sub_a[k].astype(BF16)
            received[NIS : NIS + LATE, cols] = first
            received[NIS + LATE :, cols] = second
        added = dot(placing[...], received[:, i * LANES : (i + 2) * LANES])
        nodal[i] = ((partial[i] + added[:, :LANES]) * scale).astype(BF16)
        nodal[i + 1] = ((partial[i + 1] + added[:, LANES:]) * scale).astype(BF16)
        copy = pltpu.make_async_copy(nodal.at[pl.ds(i, 2)], out.at[pl.ds(i, 2)], sems.at[i // 2])
        copy.start()
        copies.append(copy)
    for copy in copies:
        copy.wait()


def vmem(count):
    return [pl.BlockSpec(memory_space=pltpu.VMEM)] * count


def anywhere(count):
    return [pl.BlockSpec(memory_space=pl.ANY)] * count


def hbm(count):
    return [pl.BlockSpec(memory_space=pltpu.HBM)] * count


def array(shape, dtype=F32):
    return jax.ShapeDtypeStruct(shape, dtype)


def call(kernel, name, out_shape, in_specs, scratch=(), flops=0, moved=0, out_specs=None):
    return pl.pallas_call(
        kernel,
        name=name,
        out_shape=out_shape,
        in_specs=in_specs,
        out_specs=out_specs or vmem(len(out_shape)),
        scratch_shapes=list(scratch),
        compiler_params=pltpu.CompilerParams(vmem_limit_bytes=VMEM_LIMIT),
        cost_estimate=pl.CostEstimate(flops=flops, bytes_accessed=moved, transcendentals=0),
    )


def exchange(block, axis, first):
    count = lax.axis_size(axis)
    pairs = []
    for i in range(first, count - 1, 2):
        pairs += [(i, i + 1), (i + 1, i)]
    return lax.ppermute(block, axis, pairs)


def in_hbm(*arrays):
    return [pltpu.with_memory_space_constraint(x, pltpu.HBM) for x in arrays]


def gather_near(coarse, own, ahead):
    beyond = exchange(coarse, "sub", 1)
    beside = exchange(coarse, "sub", 0)
    parts = [own, beyond, beside]
    distance = lax.axis_size("grp") // 2
    while distance:
        rows = sum(x.shape[0] for x in parts)
        before, ahead = ahead[:1], ahead[1:]

        def join(*refs, skip=len(before)):
            join_kernel(*refs[: len(refs) - 1 - skip], refs[-1])

        (block,) = call(
            join,
            "join_blocks",
            (array((rows, parts[0].shape[1])),),
            vmem(len(parts)) + anywhere(len(before)),
        )(*parts, *before)
        pairs = [(i, i ^ distance) for i in range(lax.axis_size("grp"))]
        parts = [block, lax.ppermute(block, "grp", pairs)]
        distance //= 2
    return parts


def shards(
    coarse,
    corner_idx,
    coupling,
    force,
    panel_inv,
    panel_nodes,
    strain_disp,
    modulus,
    connect,
    interface,
    nodal_volume,
):
    nodes, _, cases = force.shape
    dofs = 3 * nodes
    q = corner_idx.shape[1]

    def lists(*refs):
        prepare_lists(coarse.shape[0], lax.axis_size("grp"), *refs)

    own, *panels, select, onehot, face, scaled, count, placing, placing_last, inverse_volume = call(
        lists,
        "prepare_lists",
        (
            array(coarse.shape),
            array(panel_nodes.shape, jnp.int32),
            array((3, nodes, cases), BF16),
            array(panel_inv.shape, BF16),
            array((TERM, 3 * LANES), BF16),
            array((nodes, CORNERS * LANES), BF16),
            array((NIF, 2 * LANES), BF16),
            array((COMPS * 24, 8, LANES)),
            array((nodes, 2 * LANES), BF16),
            array((nodes, 2 * LANES), BF16),
            array((nodes, 2 * LANES), BF16),
            array((nodes, LANES)),
        ),
        hbm(10),
        (
            pltpu.VMEM((1, q), jnp.int32),
            pltpu.VMEM(connect.shape, jnp.int32),
            pltpu.VMEM(interface.shape, jnp.int32),
            pltpu.VMEM((COMPS * 24, LANES), BF16),
            pltpu.VMEM((1, LANES), F32),
            pltpu.VMEM((nodes // LANES, LANES), F32),
            pltpu.VMEM((8, 2 * LANES), F32),
            pltpu.SemaphoreType.DMA((10,)),
        ),
        flops=100000000,
        moved=4000000,
    )(
        *in_hbm(
            corner_idx,
            connect,
            interface,
            strain_disp.reshape(COMPS * 24, LANES),
            modulus.reshape(1, -1),
            nodal_volume.reshape(-1, LANES),
            coarse,
            panel_nodes,
            jnp.transpose(force, (1, 0, 2)),
            panel_inv,
        )
    )
    first = 64
    free_t, corner_t, stress_first, stress_corner = call(
        prepare_panels,
        "prepare_panels",
        (
            array((cases, dofs)),
            array((2 * LANES, dofs), BF16),
            array((COMPS, first, LANES)),
            array((2 * LANES, COMPS * LANES), BF16),
        ),
        vmem(6),
        (
            pltpu.VMEM((dofs + SPARE, cases), F32),
            pltpu.VMEM((2, panel_inv.shape[1] + SPARE, LANES), F32),
            pltpu.VMEM((TERM, dofs), F32),
            pltpu.VMEM((COMPS, max(first, TERM), LANES), F32),
        ),
        flops=400000000,
        moved=4000000,
    )(coupling.T, *panels, onehot, scaled)
    (stress_rest,) = call(
        stress_kernel,
        "stress_of_loads",
        (array((COMPS, cases - first, LANES)),),
        vmem(3),
        (pltpu.VMEM((COMPS, cases - first, LANES), F32),),
        flops=400000000,
        moved=4000000,
    )(free_t, onehot, scaled)

    near = gather_near(coarse, own, [select, corner_t])
    values, stress, sub_a, sub_b, grp_a, grp_b = call(
        solve_kernel,
        "stress_and_rows",
        (
            array((cases, 2 * LANES), BF16),
            array((COMPS * cases, 2 * LANES), BF16),
            array((COMPS, NIS, cases)),
            array((COMPS, NIS, cases)),
            array((COMPS, NIG + 2 * NED, cases)),
            array((COMPS, NIG + 2 * NED, cases)),
        ),
        vmem(7),
        (pltpu.VMEM((3, 3 * LANES, cases), BF16),),
        flops=300000000,
        moved=3000000,
    )(*near, select, stress_first, stress_rest, stress_corner, face)
    from_sub_a = exchange(sub_a, "sub", 0)
    from_grp_a = exchange(grp_a, "grp", 0)
    from_grp_b = exchange(grp_b, "grp", 1)
    edge_b, edge_a = call(
        edge_kernel,
        "sum_edges",
        (array((COMPS, 2 * NED, cases)), array((COMPS, 2 * NED, cases))),
        vmem(4),
    )(grp_a, grp_b, from_grp_a, from_grp_b)
    from_sub_b = exchange(sub_b, "sub", 1)
    from_edge_b = exchange(edge_b, "sub", 1)
    from_edge_a = exchange(edge_a, "sub", 0)
    partial, disp = call(
        partial_kernel,
        "assemble_nodes",
        (array((COMPS, nodes, cases)), array((3, nodes, cases), BF16)),
        vmem(8),
        (pltpu.VMEM((2 * LANES, COMPS * cases), BF16),),
        flops=400000000,
        moved=2000000,
    )(count, stress, free_t, corner_t, values, placing, from_grp_a, from_grp_b)
    (nodal,) = call(
        finish_kernel,
        "add_last",
        (array((COMPS, nodes, cases), BF16),),
        vmem(7),
        (
            pltpu.VMEM((NIS + 2 * LATE, COMPS * cases), BF16),
            pltpu.VMEM((COMPS, nodes, cases), BF16),
            pltpu.SemaphoreType.DMA((COMPS // 2,)),
        ),
        flops=400000000,
        moved=3000000,
        out_specs=hbm(1),
    )(placing_last, partial, inverse_volume, from_sub_a, from_sub_b, from_edge_b, from_edge_a)
    return jnp.transpose(disp, (1, 0, 2)), jnp.transpose(nodal, (1, 0, 2))


def solution(mesh):
    owner = ("sub", "grp")
    placed = (
        P(owner, None),
        P(owner, None),
        P(owner, None),
        P(owner, None, None),
        P(owner, None, None),
        P(owner, None),
        P(None, None, owner),
        P(owner),
        P(None, owner),
        P(owner, None),
        P(owner),
    )
    return jax.shard_map(
        shards,
        mesh=mesh,
        in_specs=placed,
        out_specs=(P(owner, None, None), P(owner, None, None)),
        check_vma=False,
    )
```

```python
import jax
import jax.numpy as jnp
from jax import lax
from jax.experimental import pallas as pl
from jax.experimental.pallas import tpu as pltpu
from jax.sharding import PartitionSpec as P

NIS = 64
NIG = 32
NED = 8
EDGES = 2 * NIS + 2 * NIG
NIF = EDGES + 4 * NED
LATE = NIS + 4 * NED
CORNERS = 8
COMPS = 6
LANES = 128
TERM = 32
SPARE = 8
TERMS = ((0, 0), (0, 1), (0, 2), (1, 0), (1, 1), (2, 0))

POISSON = 0.3
LAME = POISSON / ((1.0 + POISSON) * (1.0 - 2.0 * POISSON))
SHEAR = 0.5 / (1.0 + POISSON)

F32 = jnp.float32
BF16 = jnp.bfloat16
VMEM_LIMIT = 24 * 1024 * 1024


def split_two(x):
    high = x.astype(BF16)
    return high, (x - high.astype(F32)).astype(BF16)


def split_three(x):
    high = x.astype(BF16)
    rest = x - high.astype(F32)
    middle = rest.astype(BF16)
    return high, middle, (rest - middle.astype(F32)).astype(BF16)


def dot(a, b):
    return jnp.dot(a, b, preferred_element_type=F32)


def dot_nt(a, b):
    return lax.dot_general(a, b, (((1,), (1,)), ((), ())), preferred_element_type=F32)


def column(row):
    return jnp.broadcast_to(row, (LANES, LANES)).T


def swap_lanes(x, distance):
    lane = lax.broadcasted_iota(jnp.int32, x.shape, 1)
    after = pltpu.roll(x, LANES - distance, 1)
    before = pltpu.roll(x, distance, 1)
    return jnp.where((lane & distance) == 0, after, before)


def order_lists(ids):
    sub_even = (lax.axis_index("sub") & 1) == 0
    grp_even = (lax.axis_index("grp") & 1) == 0
    first, second = ids[:, :LANES], ids[:, LANES:]
    ids[:, :LANES] = jnp.where(sub_even, swap_lanes(first, NIS), first)
    lane = lax.broadcasted_iota(jnp.int32, second.shape, 1)
    groups = jnp.where(grp_even, swap_lanes(second, NIG), second)
    edges = jnp.where(sub_even, swap_lanes(second, 2 * NED), second)
    edges = jnp.where(grp_even, swap_lanes(edges, NED), edges)
    ids[:, LANES:] = jnp.where(lane < 2 * NIG, groups, edges)


def element_stress(terms, rows, onehot, scaled, sofar, store):
    step = 32
    pairs = onehot.shape[1] // (2 * LANES)
    for pair in range(pairs):
        operand = onehot[:, 2 * LANES * pair : 2 * LANES * (pair + 1)]
        elem = dot(terms[0], operand)
        for term in terms[1:]:
            elem = elem + dot(term, operand)
        for start in range(0, rows, step):
            sums = [None] * COMPS if pair == 0 else [sofar[i, start : start + step, :] for i in range(COMPS)]
            for half in range(2):
                for c in range(3):
                    x = elem[c * rows + start : c * rows + start + step, half * LANES : (half + 1) * LANES]
                    x = x.reshape(step // 8, 8, LANES)
                    for i in range(COMPS):
                        term = scaled[24 * i + 3 * (2 * pair + half) + c] * x
                        term = term.reshape(step, LANES)
                        sums[i] = term if sums[i] is None else sums[i] + term
            for i in range(COMPS):
                if pair < pairs - 1:
                    sofar[i, start : start + step, :] = sums[i]
                else:
                    store(i, start, sums[i])


def free_stress(free_t, first, rows, onehot, scaled, sofar, out):
    nodes = onehot.shape[0]
    parts = [free_t[first : first + rows, c * nodes : (c + 1) * nodes] for c in range(3)]

    def store(i, start, value):
        out[i, start : start + value.shape[0], :] = value

    element_stress(split_two(jnp.concatenate(parts, axis=0)), rows, onehot, scaled, sofar, store)


def start_copies(pairs, sems):
    copies = [pltpu.make_async_copy(src, dst, sems.at[k]) for k, (src, dst) in enumerate(pairs)]
    for copy in copies:
        copy.start()
    return copies


def prepare_lists(
    block_rows,
    members,
    corner_idx,
    connect,
    interface,
    strain_disp,
    modulus,
    volume,
    coarse,
    panel_nodes,
    force,
    panel_inv,
    own,
    panel_v,
    force_v,
    inverse,
    select,
    onehot,
    face,
    scaled,
    count,
    placing,
    placing_last,
    inverse_volume,
    corner_v,
    connect_v,
    interface_v,
    strain_v,
    modulus_v,
    volume_v,
    ids,
    sems,
):
    copies = start_copies(
        [
            (connect, connect_v),
            (interface, interface_v),
            (corner_idx, corner_v),
            (modulus, modulus_v),
            (strain_disp, strain_v),
            (volume, volume_v),
            (coarse, own),
            (panel_nodes, panel_v),
            (force, force_v),
            (panel_inv, inverse),
        ],
        sems,
    )
    nodes = onehot.shape[0]
    q = corner_idx.shape[1]

    copies[0].wait()
    node_of = lax.broadcasted_iota(jnp.int32, (nodes, LANES), 0)
    total = jnp.zeros((nodes, LANES), F32)
    for a in range(CORNERS):
        hit = jnp.where(connect_v[a : a + 1, :] == node_of, 1.0, 0.0)
        onehot[:, a * LANES : (a + 1) * LANES] = hit.astype(BF16)
        total = total + hit
    total = total.astype(BF16)
    count[:, :LANES] = total
    count[:, LANES:] = total

    copies[1].wait()
    ids[...] = jnp.full(ids.shape, -1.0, F32)
    ids[0:1, 0:NIF] = interface_v[...].astype(F32)
    order_lists(ids)
    lane = lax.broadcasted_iota(jnp.int32, (8, LANES), 1)
    edges = pltpu.roll(ids[:, LANES:], LANES - NIS, 1)
    again = pltpu.roll(ids[:, :LANES], LANES - NIS + 4 * NED, 1)
    last = jnp.where(lane < 4 * NED, edges, again)
    last = jnp.where(lane < LATE, last, pltpu.roll(edges, LATE, 1))
    for row, target in ((ids[0:1, LANES:], 0), (ids[0:1, :LANES], 1), (last[0:1], 2)):
        hit = jnp.where(row.astype(jnp.int32) == node_of, 1.0, 0.0).astype(BF16)
        if target == 0:
            placing[:, :LANES] = hit
            placing[:, LANES:] = hit
        else:
            placing_last[:, (target - 1) * LANES : target * LANES] = hit
    connect_f = connect_v[...].astype(F32)
    for half in range(2):
        id_col = column(ids[0:1, half * LANES : (half + 1) * LANES])
        rows = jnp.zeros((LANES, LANES), F32)
        for a in range(CORNERS):
            rows = rows + jnp.where(connect_f[a : a + 1, :] == id_col, 1.0, 0.0)
        rows = rows.astype(BF16)[: min(LANES, NIF - half * LANES)]
        face[half * LANES : half * LANES + rows.shape[0], :LANES] = rows
        face[half * LANES : half * LANES + rows.shape[0], LANES:] = rows

    copies[2].wait()
    ids[0:1, 0:q] = corner_v[...].astype(F32)
    wanted = column(ids[0:1, :LANES])[:TERM]
    lane = lax.broadcasted_iota(jnp.int32, (TERM, 3 * LANES), 1)
    entry = lax.broadcasted_iota(jnp.int32, (TERM, LANES), 0)
    s, g = lax.axis_index("sub"), lax.axis_index("grp")
    aside = 1 - 2 * (s & 1)
    row = jnp.full((TERM, 3 * LANES), -1, jnp.int32)
    base = 0
    for member in range(members):
        distance, bits, turn = members // 2, member, 0
        while distance:
            turn += (bits & 1) * distance
            distance, bits = distance // 2, bits >> 1
        for owner in (s, s - aside, s + aside):
            first = (owner * members + (g ^ turn)) * block_rows
            row = jnp.where((lane >= base) & (lane < base + block_rows), first - base + lane, row)
            base += block_rows
    for b in range(3):
        cols = slice(b * LANES, (b + 1) * LANES)
        hit = (wanted == row[:, cols].astype(F32)) & (entry < q)
        select[:, cols] = jnp.where(hit, 1.0, 0.0).astype(BF16)

    copies[3].wait()
    copies[4].wait()
    factor = modulus_v[...]
    whole = strain_v[...].astype(F32)
    rows = [whole[24 * i : 24 * (i + 1)] for i in range(COMPS)]
    trace = (rows[0] + rows[1] + rows[2]) * LAME
    for i in range(COMPS):
        value = trace + rows[i] * (2.0 * SHEAR) if i < 3 else rows[i] * SHEAR
        scaled[24 * i : 24 * (i + 1)] = jnp.broadcast_to((value * factor)[:, None, :], (24, 8, LANES))

    copies[5].wait()
    for k in range(nodes // LANES):
        inverse_volume[k * LANES : (k + 1) * LANES, :] = column(1.0 / volume_v[k : k + 1, :])
    for copy in copies[6:]:
        copy.wait()


def prepare_panels(
    coupling_v,
    panel_v,
    force_v,
    inverse,
    onehot,
    scaled,
    free_t,
    corner_t,
    stress_first,
    stress_corner,
    loads,
    solved,
    whole,
    sofar,
):
    panels, panel_rows, _ = inverse.shape
    panel_size = panel_rows // 3
    nodes = force_v.shape[1]
    q = coupling_v.shape[0]
    for c in range(3):
        loads[pl.ds(c, nodes, stride=3), :] = force_v[c].astype(F32)
    spare = corner_t.shape[0] - len(TERMS) * TERM
    stress_corner[len(TERMS) * TERM :, :] = jnp.zeros((spare, stress_corner.shape[1]), BF16)
    corner_t[len(TERMS) * TERM :, :] = jnp.zeros((spare, 3 * nodes), BF16)
    row_of = lax.broadcasted_iota(jnp.int32, (panel_rows, LANES), 0)
    for p in range(panels):
        start = p * panel_rows
        live = row_of < 3 * panel_v[0:1, p : p + 1]
        columns = []
        for k in range(panel_rows // LANES):
            part = coupling_v[:, start + k * LANES : start + (k + 1) * LANES].astype(F32)
            columns.append(jnp.concatenate([part, jnp.zeros((LANES - q, LANES), F32)], axis=0).T)
        sides = [loads[start : start + panel_rows, :], jnp.concatenate(columns, axis=0)]
        sides = jnp.concatenate([jnp.where(live, x, 0.0).astype(BF16) for x in sides], axis=1)
        result = dot(inverse[p], sides)
        for side in range(2):
            solved[side, :panel_rows, :] = jnp.where(live, result[:, side * LANES : (side + 1) * LANES], 0.0)
        for c in range(3):
            cols = slice(c * nodes + p * panel_size, c * nodes + (p + 1) * panel_size)
            free_t[:, cols] = solved[0, pl.ds(c, panel_size, stride=3), :].T
            value = solved[1, pl.ds(c, panel_size, stride=3), :].T[:TERM]
            whole[:, cols] = value
            pieces = split_three(value)
            for k, (piece, _) in enumerate(TERMS):
                corner_t[k * TERM : (k + 1) * TERM, cols] = pieces[piece]

    def store(i, start, value):
        pieces = split_three(value)
        for k, (piece, _) in enumerate(TERMS):
            stress_corner[k * TERM : (k + 1) * TERM, i * LANES : (i + 1) * LANES] = pieces[piece]

    parts = jnp.concatenate([whole[:, c * nodes : (c + 1) * nodes] for c in range(3)], axis=0)
    element_stress(split_two(parts), TERM, onehot, scaled, sofar, store)
    free_stress(free_t, 0, stress_first.shape[1], onehot, scaled, sofar, stress_first)


def stress_kernel(free_t, onehot, scaled, out, sofar):
    rows = out.shape[1]
    free_stress(free_t, free_t.shape[0] - rows, rows, onehot, scaled, sofar, out)


def join_kernel(*refs):
    *parts, out = refs
    start = 0
    for part in parts:
        out[start : start + part.shape[0], :] = part[...]
        start += part.shape[0]


def solve_kernel(
    near,
    across,
    select,
    stress_first,
    stress_rest,
    stress_corner,
    face,
    values,
    stress,
    sub_a,
    sub_b,
    grp_a,
    grp_b,
    terms,
):
    rows = near.shape[0]
    terms[:, 2 * rows :, :] = jnp.zeros((3, terms.shape[1] - 2 * rows, terms.shape[2]), BF16)
    for b, block in enumerate((near, across)):
        for t, value in enumerate(split_three(block[...])):
            terms[t, b * rows : (b + 1) * rows, :] = value
    picked = [dot(select[...], terms[t]) for t in range(3)]
    ordered = [picked[term] for _, term in TERMS]
    ordered += [jnp.zeros_like(picked[0])] * (stress_corner.shape[0] // TERM - len(ordered))
    per = LANES // TERM
    for k in range(0, len(ordered), per):
        block = jnp.concatenate(ordered[k : k + per], axis=0).T.astype(BF16)
        values[:, k * TERM : (k + per) * TERM] = block
    moved = dot(values[...], stress_corner[...])
    for i in range(COMPS):
        cols = slice(i * LANES, (i + 1) * LANES)
        free = jnp.concatenate([stress_first[i], stress_rest[i]], axis=0)
        high, low = split_two(free - moved[:, cols])
        stress[cols, 0:LANES] = high
        stress[cols, LANES : 2 * LANES] = low

    rows = dot_nt(face[...], stress[...])
    for i in range(COMPS):
        part = rows[:, i * LANES : (i + 1) * LANES]
        edge = [part[EDGES + NED * k : EDGES + NED * (k + 1)] for k in range(4)]
        sub_a[i] = part[:NIS]
        sub_b[i] = part[NIS : 2 * NIS]
        grp_a[i] = jnp.concatenate([part[2 * NIS : 2 * NIS + NIG], edge[0], edge[2]], axis=0)
        grp_b[i] = jnp.concatenate([part[2 * NIS + NIG : EDGES], edge[1], edge[3]], axis=0)


def edge_kernel(grp_a, grp_b, from_a, from_b, edge_a, edge_b):
    split = NIG + NED
    edge_a[:, :NED, :] = grp_a[:, NIG:split, :] + from_a[:, NIG:split, :]
    edge_a[:, NED:, :] = grp_b[:, NIG:split, :] + from_b[:, NIG:split, :]
    edge_b[:, :NED, :] = grp_a[:, split:, :] + from_a[:, split:, :]
    edge_b[:, NED:, :] = grp_b[:, split:, :] + from_b[:, split:, :]


def partial_kernel(
    count, stress, free_t, corner_t, values, placing, grp_a, grp_b, partial, disp_out, received
):
    nodes = disp_out.shape[1]
    for c in range(3):
        cols = slice(c * nodes, (c + 1) * nodes)
        part = free_t[:, cols] - dot(values[...], corner_t[:, cols])
        for k in range(0, nodes, LANES):
            disp_out[c, k : k + LANES, :] = part[:, k : k + LANES].T.astype(BF16)
    split = NIG + NED
    for i in range(COMPS):
        low, high = grp_a[i], grp_b[i]
        rows = [low[:NIG], high[:NIG], low[NIG:split], high[NIG:split], low[split:], high[split:]]
        rows.append(jnp.zeros((2 * LANES - NIF, LANES), F32))
        first, second = split_two(jnp.concatenate(rows, axis=0))
        received[:LANES, i * LANES : (i + 1) * LANES] = first
        received[LANES:, i * LANES : (i + 1) * LANES] = second
    for i in range(0, COMPS, 2):
        cols = slice(i * LANES, (i + 2) * LANES)
        own = dot_nt(count[...], stress[cols, :])
        total = own + dot(placing[...], received[:, cols])
        partial[i] = total[:, :LANES]
        partial[i + 1] = total[:, LANES:]


def finish_kernel(
    placing, partial, inverse_volume, sub_a, sub_b, edge_a, edge_b, out, received, nodal, sems
):
    scale = inverse_volume[...]
    copies = []
    for i in range(0, COMPS, 2):
        for k in (i, i + 1):
            cols = slice(k * LANES, (k + 1) * LANES)
            late = jnp.concatenate([sub_b[k], edge_a[k], edge_b[k]], axis=0)
            first, second = split_two(late)
            received[:NIS, cols] = sub_a[k].astype(BF16)
            received[NIS : NIS + LATE, cols] = first
            received[NIS + LATE :, cols] = second
        added = dot(placing[...], received[:, i * LANES : (i + 2) * LANES])
        nodal[i] = ((partial[i] + added[:, :LANES]) * scale).astype(BF16)
        nodal[i + 1] = ((partial[i + 1] + added[:, LANES:]) * scale).astype(BF16)
        copy = pltpu.make_async_copy(nodal.at[pl.ds(i, 2)], out.at[pl.ds(i, 2)], sems.at[i // 2])
        copy.start()
        copies.append(copy)
    for copy in copies:
        copy.wait()


def vmem(count):
    return [pl.BlockSpec(memory_space=pltpu.VMEM)] * count


def anywhere(count):
    return [pl.BlockSpec(memory_space=pl.ANY)] * count


def hbm(count):
    return [pl.BlockSpec(memory_space=pltpu.HBM)] * count


def array(shape, dtype=F32):
    return jax.ShapeDtypeStruct(shape, dtype)


def call(kernel, name, out_shape, in_specs, scratch=(), flops=0, moved=0, out_specs=None):
    return pl.pallas_call(
        kernel,
        name=name,
        out_shape=out_shape,
        in_specs=in_specs,
        out_specs=out_specs or vmem(len(out_shape)),
        scratch_shapes=list(scratch),
        compiler_params=pltpu.CompilerParams(vmem_limit_bytes=VMEM_LIMIT),
        cost_estimate=pl.CostEstimate(flops=flops, bytes_accessed=moved, transcendentals=0),
    )


def exchange(block, axis, first):
    count = lax.axis_size(axis)
    pairs = []
    for i in range(first, count - 1, 2):
        pairs += [(i, i + 1), (i + 1, i)]
    return lax.ppermute(block, axis, pairs)


def in_hbm(*arrays):
    return [pltpu.with_memory_space_constraint(x, pltpu.HBM) for x in arrays]


def gather_near(coarse, own, ahead):
    beyond = exchange(coarse, "sub", 1)
    beside = exchange(coarse, "sub", 0)
    parts = [own, beyond, beside]
    distance = lax.axis_size("grp") // 2
    while distance:
        rows = sum(x.shape[0] for x in parts)
        before, ahead = ahead[:1], ahead[1:]

        def join(*refs, skip=len(before)):
            join_kernel(*refs[: len(refs) - 1 - skip], refs[-1])

        (block,) = call(
            join,
            "join_blocks",
            (array((rows, parts[0].shape[1])),),
            vmem(len(parts)) + anywhere(len(before)),
        )(*parts, *before)
        pairs = [(i, i ^ distance) for i in range(lax.axis_size("grp"))]
        parts = [block, lax.ppermute(block, "grp", pairs)]
        distance //= 2
    return parts


def shards(
    coarse,
    corner_idx,
    coupling,
    force,
    panel_inv,
    panel_nodes,
    strain_disp,
    modulus,
    connect,
    interface,
    nodal_volume,
):
    nodes, _, cases = force.shape
    dofs = 3 * nodes
    q = corner_idx.shape[1]

    def lists(*refs):
        prepare_lists(coarse.shape[0], lax.axis_size("grp"), *refs)

    own, *panels, select, onehot, face, scaled, count, placing, placing_last, inverse_volume = call(
        lists,
        "prepare_lists",
        (
            array(coarse.shape),
            array(panel_nodes.shape, jnp.int32),
            array((3, nodes, cases), BF16),
            array(panel_inv.shape, BF16),
            array((TERM, 3 * LANES), BF16),
            array((nodes, CORNERS * LANES), BF16),
            array((NIF, 2 * LANES), BF16),
            array((COMPS * 24, 8, LANES)),
            array((nodes, 2 * LANES), BF16),
            array((nodes, 2 * LANES), BF16),
            array((nodes, 2 * LANES), BF16),
            array((nodes, LANES)),
        ),
        hbm(10),
        (
            pltpu.VMEM((1, q), jnp.int32),
            pltpu.VMEM(connect.shape, jnp.int32),
            pltpu.VMEM(interface.shape, jnp.int32),
            pltpu.VMEM((COMPS * 24, LANES), BF16),
            pltpu.VMEM((1, LANES), F32),
            pltpu.VMEM((nodes // LANES, LANES), F32),
            pltpu.VMEM((8, 2 * LANES), F32),
            pltpu.SemaphoreType.DMA((10,)),
        ),
        flops=100000000,
        moved=4000000,
    )(
        *in_hbm(
            corner_idx,
            connect,
            interface,
            strain_disp.reshape(COMPS * 24, LANES),
            modulus.reshape(1, -1),
            nodal_volume.reshape(-1, LANES),
            coarse,
            panel_nodes,
            jnp.transpose(force, (1, 0, 2)),
            panel_inv,
        )
    )
    first = 64
    free_t, corner_t, stress_first, stress_corner = call(
        prepare_panels,
        "prepare_panels",
        (
            array((cases, dofs)),
            array((2 * LANES, dofs), BF16),
            array((COMPS, first, LANES)),
            array((2 * LANES, COMPS * LANES), BF16),
        ),
        vmem(6),
        (
            pltpu.VMEM((dofs + SPARE, cases), F32),
            pltpu.VMEM((2, panel_inv.shape[1] + SPARE, LANES), F32),
            pltpu.VMEM((TERM, dofs), F32),
            pltpu.VMEM((COMPS, max(first, TERM), LANES), F32),
        ),
        flops=400000000,
        moved=4000000,
    )(coupling.T, *panels, onehot, scaled)
    (stress_rest,) = call(
        stress_kernel,
        "stress_of_loads",
        (array((COMPS, cases - first, LANES)),),
        vmem(3),
        (pltpu.VMEM((COMPS, cases - first, LANES), F32),),
        flops=400000000,
        moved=4000000,
    )(free_t, onehot, scaled)

    near = gather_near(coarse, own, [select, corner_t])
    values, stress, sub_a, sub_b, grp_a, grp_b = call(
        solve_kernel,
        "stress_and_rows",
        (
            array((cases, 2 * LANES), BF16),
            array((COMPS * cases, 2 * LANES), BF16),
            array((COMPS, NIS, cases)),
            array((COMPS, NIS, cases)),
            array((COMPS, NIG + 2 * NED, cases)),
            array((COMPS, NIG + 2 * NED, cases)),
        ),
        vmem(7),
        (pltpu.VMEM((3, 3 * LANES, cases), BF16),),
        flops=300000000,
        moved=3000000,
    )(*near, select, stress_first, stress_rest, stress_corner, face)
    from_sub_a = exchange(sub_a, "sub", 0)
    from_grp_a = exchange(grp_a, "grp", 0)
    from_grp_b = exchange(grp_b, "grp", 1)
    edge_a, edge_b = call(
        edge_kernel,
        "sum_edges",
        (array((COMPS, 2 * NED, cases)), array((COMPS, 2 * NED, cases))),
        vmem(4),
    )(grp_a, grp_b, from_grp_a, from_grp_b)
    from_sub_b = exchange(sub_b, "sub", 1)
    from_edge_a = exchange(edge_a, "sub", 0)
    from_edge_b = exchange(edge_b, "sub", 1)
    partial, disp = call(
        partial_kernel,
        "assemble_nodes",
        (array((COMPS, nodes, cases)), array((3, nodes, cases), BF16)),
        vmem(8),
        (pltpu.VMEM((2 * LANES, COMPS * cases), BF16),),
        flops=400000000,
        moved=2000000,
    )(count, stress, free_t, corner_t, values, placing, from_grp_a, from_grp_b)
    (nodal,) = call(
        finish_kernel,
        "add_last",
        (array((COMPS, nodes, cases), BF16),),
        vmem(7),
        (
            pltpu.VMEM((NIS + 2 * LATE, COMPS * cases), BF16),
            pltpu.VMEM((COMPS, nodes, cases), BF16),
            pltpu.SemaphoreType.DMA((COMPS // 2,)),
        ),
        flops=400000000,
        moved=3000000,
        out_specs=hbm(1),
    )(placing_last, partial, inverse_volume, from_sub_a, from_sub_b, from_edge_a, from_edge_b)
    return jnp.transpose(disp, (1, 0, 2)), jnp.transpose(nodal, (1, 0, 2))


def solution(mesh):
    owner = ("sub", "grp")
    placed = (
        P(owner, None),
        P(owner, None),
        P(owner, None),
        P(owner, None, None),
        P(owner, None, None),
        P(owner, None),
        P(None, None, owner),
        P(owner),
        P(None, owner),
        P(owner, None),
        P(owner),
    )
    return jax.shard_map(
        shards,
        mesh=mesh,
        in_specs=placed,
        out_specs=(P(owner, None, None), P(owner, None, None)),
        check_vma=False,
    )
```

```python
import jax
import jax.numpy as jnp
from jax import lax
from jax.experimental import pallas as pl
from jax.experimental.pallas import tpu as pltpu
from jax.sharding import PartitionSpec as P

NIS = 64
NIG = 32
NED = 8
EDGES = 2 * NIS + 2 * NIG
NIF = EDGES + 4 * NED
LATE = NIS + 4 * NED
CORNERS = 8
COMPS = 6
LANES = 128
TERM = 32
SPARE = 8
TERMS = ((0, 0), (0, 1), (0, 2), (1, 0), (1, 1), (2, 0))

POISSON = 0.3
LAME = POISSON / ((1.0 + POISSON) * (1.0 - 2.0 * POISSON))
SHEAR = 0.5 / (1.0 + POISSON)

F32 = jnp.float32
BF16 = jnp.bfloat16
VMEM_LIMIT = 24 * 1024 * 1024


def split_two(x):
    high = x.astype(BF16)
    return high, (x - high.astype(F32)).astype(BF16)


def split_three(x):
    high = x.astype(BF16)
    rest = x - high.astype(F32)
    middle = rest.astype(BF16)
    return high, middle, (rest - middle.astype(F32)).astype(BF16)


def dot(a, b):
    return jnp.dot(a, b, preferred_element_type=F32)


def dot_nt(a, b):
    return lax.dot_general(a, b, (((1,), (1,)), ((), ())), preferred_element_type=F32)


def column(row):
    return jnp.broadcast_to(row, (LANES, LANES)).T


def swap_lanes(x, distance):
    lane = lax.broadcasted_iota(jnp.int32, x.shape, 1)
    after = pltpu.roll(x, LANES - distance, 1)
    before = pltpu.roll(x, distance, 1)
    return jnp.where((lane & distance) == 0, after, before)


def order_lists(ids):
    sub_even = (lax.axis_index("sub") & 1) == 0
    grp_even = (lax.axis_index("grp") & 1) == 0
    first, second = ids[:, :LANES], ids[:, LANES:]
    ids[:, :LANES] = jnp.where(sub_even, swap_lanes(first, NIS), first)
    lane = lax.broadcasted_iota(jnp.int32, second.shape, 1)
    groups = jnp.where(grp_even, swap_lanes(second, NIG), second)
    edges = jnp.where(sub_even, swap_lanes(second, 2 * NED), second)
    edges = jnp.where(grp_even, swap_lanes(edges, NED), edges)
    ids[:, LANES:] = jnp.where(lane < 2 * NIG, groups, edges)


def element_stress(terms, rows, onehot, scaled, sofar, store):
    step = 32
    pairs = onehot.shape[1] // (2 * LANES)
    for pair in range(pairs):
        operand = onehot[:, 2 * LANES * pair : 2 * LANES * (pair + 1)]
        elem = dot(terms[0], operand)
        for term in terms[1:]:
            elem = elem + dot(term, operand)
        for start in range(0, rows, step):
            sums = [None] * COMPS if pair == 0 else [sofar[i, start : start + step, :] for i in range(COMPS)]
            for half in range(2):
                for c in range(3):
                    x = elem[c * rows + start : c * rows + start + step, half * LANES : (half + 1) * LANES]
                    x = x.reshape(step // 8, 8, LANES)
                    for i in range(COMPS):
                        term = scaled[24 * i + 3 * (2 * pair + half) + c] * x
                        term = term.reshape(step, LANES)
                        sums[i] = term if sums[i] is None else sums[i] + term
            for i in range(COMPS):
                if pair < pairs - 1:
                    sofar[i, start : start + step, :] = sums[i]
                else:
                    store(i, start, sums[i])


def free_stress(free_t, first, rows, onehot, scaled, sofar, out):
    nodes = onehot.shape[0]
    parts = [free_t[first : first + rows, c * nodes : (c + 1) * nodes] for c in range(3)]

    def store(i, start, value):
        out[i, start : start + value.shape[0], :] = value

    element_stress(split_two(jnp.concatenate(parts, axis=0)), rows, onehot, scaled, sofar, store)


def start_copies(pairs, sems):
    copies = [pltpu.make_async_copy(src, dst, sems.at[k]) for k, (src, dst) in enumerate(pairs)]
    for copy in copies:
        copy.start()
    return copies


def prepare_lists(
    block_rows,
    members,
    corner_idx,
    connect,
    interface,
    strain_disp,
    modulus,
    volume,
    coarse,
    panel_nodes,
    force,
    panel_inv,
    own,
    panel_v,
    force_v,
    inverse,
    select,
    onehot,
    face,
    scaled,
    count,
    placing,
    placing_last,
    inverse_volume,
    corner_v,
    connect_v,
    interface_v,
    strain_v,
    modulus_v,
    volume_v,
    ids,
    sems,
):
    copies = start_copies(
        [
            (connect, connect_v),
            (interface, interface_v),
            (corner_idx, corner_v),
            (modulus, modulus_v),
            (strain_disp, strain_v),
            (volume, volume_v),
            (coarse, own),
            (panel_nodes, panel_v),
            (force, force_v),
            (panel_inv, inverse),
        ],
        sems,
    )
    nodes = onehot.shape[0]
    q = corner_idx.shape[1]

    copies[0].wait()
    node_of = lax.broadcasted_iota(jnp.int32, (nodes, LANES), 0)
    total = jnp.zeros((nodes, LANES), F32)
    for a in range(CORNERS):
        hit = jnp.where(connect_v[a : a + 1, :] == node_of, 1.0, 0.0)
        onehot[:, a * LANES : (a + 1) * LANES] = hit.astype(BF16)
        total = total + hit
    total = total.astype(BF16)
    count[:, :LANES] = total
    count[:, LANES:] = total

    copies[1].wait()
    ids[...] = jnp.full(ids.shape, -1.0, F32)
    ids[0:1, 0:NIF] = interface_v[...].astype(F32)
    order_lists(ids)
    lane = lax.broadcasted_iota(jnp.int32, (8, LANES), 1)
    edges = pltpu.roll(ids[:, LANES:], LANES - NIS, 1)
    again = pltpu.roll(ids[:, :LANES], LANES - NIS + 4 * NED, 1)
    last = jnp.where(lane < 4 * NED, edges, again)
    last = jnp.where(lane < LATE, last, pltpu.roll(edges, LATE, 1))
    for row, target in ((ids[0:1, LANES:], 0), (ids[0:1, :LANES], 1), (last[0:1], 2)):
        hit = jnp.where(row.astype(jnp.int32) == node_of, 1.0, 0.0).astype(BF16)
        if target == 0:
            placing[:, :LANES] = hit
            placing[:, LANES:] = hit
        else:
            placing_last[:, (target - 1) * LANES : target * LANES] = hit
    connect_f = connect_v[...].astype(F32)
    for half in range(2):
        id_col = column(ids[0:1, half * LANES : (half + 1) * LANES])
        rows = jnp.zeros((LANES, LANES), F32)
        for a in range(CORNERS):
            rows = rows + jnp.where(connect_f[a : a + 1, :] == id_col, 1.0, 0.0)
        rows = rows.astype(BF16)[: min(LANES, NIF - half * LANES)]
        face[half * LANES : half * LANES + rows.shape[0], :LANES] = rows
        face[half * LANES : half * LANES + rows.shape[0], LANES:] = rows

    copies[2].wait()
    ids[0:1, 0:q] = corner_v[...].astype(F32)
    wanted = column(ids[0:1, :LANES])[:TERM]
    lane = lax.broadcasted_iota(jnp.int32, (TERM, 3 * LANES), 1)
    entry = lax.broadcasted_iota(jnp.int32, (TERM, LANES), 0)
    s, g = lax.axis_index("sub"), lax.axis_index("grp")
    aside = 1 - 2 * (s & 1)
    row = jnp.full((TERM, 3 * LANES), -1, jnp.int32)
    base = 0
    for core in range(2):
        for owner in (s, s - aside, s + aside):
            for member in range(members // 2):
                distance, bits, turn = members // 2, member, core
                while distance > 1:
                    turn += (bits & 1) * distance
                    distance, bits = distance // 2, bits >> 1
                first = (owner * members + (g ^ turn)) * block_rows
                row = jnp.where((lane >= base) & (lane < base + block_rows), first - base + lane, row)
                base += block_rows
    for b in range(3):
        cols = slice(b * LANES, (b + 1) * LANES)
        hit = (wanted == row[:, cols].astype(F32)) & (entry < q)
        select[:, cols] = jnp.where(hit, 1.0, 0.0).astype(BF16)

    copies[3].wait()
    copies[4].wait()
    factor = modulus_v[...]
    whole = strain_v[...].astype(F32)
    rows = [whole[24 * i : 24 * (i + 1)] for i in range(COMPS)]
    trace = (rows[0] + rows[1] + rows[2]) * LAME
    for i in range(COMPS):
        value = trace + rows[i] * (2.0 * SHEAR) if i < 3 else rows[i] * SHEAR
        scaled[24 * i : 24 * (i + 1)] = jnp.broadcast_to((value * factor)[:, None, :], (24, 8, LANES))

    copies[5].wait()
    for k in range(nodes // LANES):
        inverse_volume[k * LANES : (k + 1) * LANES, :] = column(1.0 / volume_v[k : k + 1, :])
    for copy in copies[6:]:
        copy.wait()


def prepare_panels(
    coupling_v,
    panel_v,
    force_v,
    inverse,
    onehot,
    scaled,
    free_t,
    corner_t,
    stress_first,
    stress_corner,
    loads,
    solved,
    whole,
    sofar,
):
    panels, panel_rows, _ = inverse.shape
    panel_size = panel_rows // 3
    nodes = force_v.shape[1]
    q = coupling_v.shape[0]
    for c in range(3):
        loads[pl.ds(c, nodes, stride=3), :] = force_v[c].astype(F32)
    spare = corner_t.shape[0] - len(TERMS) * TERM
    stress_corner[len(TERMS) * TERM :, :] = jnp.zeros((spare, stress_corner.shape[1]), BF16)
    corner_t[len(TERMS) * TERM :, :] = jnp.zeros((spare, 3 * nodes), BF16)
    row_of = lax.broadcasted_iota(jnp.int32, (panel_rows, LANES), 0)
    for p in range(panels):
        start = p * panel_rows
        live = row_of < 3 * panel_v[0:1, p : p + 1]
        columns = []
        for k in range(panel_rows // LANES):
            part = coupling_v[:, start + k * LANES : start + (k + 1) * LANES].astype(F32)
            columns.append(jnp.concatenate([part, jnp.zeros((LANES - q, LANES), F32)], axis=0).T)
        sides = [loads[start : start + panel_rows, :], jnp.concatenate(columns, axis=0)]
        sides = jnp.concatenate([jnp.where(live, x, 0.0).astype(BF16) for x in sides], axis=1)
        result = dot(inverse[p], sides)
        for side in range(2):
            solved[side, :panel_rows, :] = jnp.where(live, result[:, side * LANES : (side + 1) * LANES], 0.0)
        for c in range(3):
            cols = slice(c * nodes + p * panel_size, c * nodes + (p + 1) * panel_size)
            free_t[:, cols] = solved[0, pl.ds(c, panel_size, stride=3), :].T
            value = solved[1, pl.ds(c, panel_size, stride=3), :].T[:TERM]
            whole[:, cols] = value
            pieces = split_three(value)
            for k, (piece, _) in enumerate(TERMS):
                corner_t[k * TERM : (k + 1) * TERM, cols] = pieces[piece]

    def store(i, start, value):
        pieces = split_three(value)
        for k, (piece, _) in enumerate(TERMS):
            stress_corner[k * TERM : (k + 1) * TERM, i * LANES : (i + 1) * LANES] = pieces[piece]

    parts = jnp.concatenate([whole[:, c * nodes : (c + 1) * nodes] for c in range(3)], axis=0)
    element_stress(split_two(parts), TERM, onehot, scaled, sofar, store)
    free_stress(free_t, 0, stress_first.shape[1], onehot, scaled, sofar, stress_first)


def stress_kernel(free_t, onehot, scaled, out, sofar):
    rows = out.shape[1]
    free_stress(free_t, free_t.shape[0] - rows, rows, onehot, scaled, sofar, out)


def join_kernel(*refs):
    *parts, out = refs
    start = 0
    for part in parts:
        out[start : start + part.shape[0], :] = part[...]
        start += part.shape[0]


def solve_kernel(
    near,
    across,
    select,
    stress_first,
    stress_rest,
    stress_corner,
    face,
    values,
    stress,
    sub_a,
    sub_b,
    grp_a,
    grp_b,
    terms,
):
    rows = near.shape[0]
    terms[:, 2 * rows :, :] = jnp.zeros((3, terms.shape[1] - 2 * rows, terms.shape[2]), BF16)
    for b, block in enumerate((near, across)):
        for t, value in enumerate(split_three(block[...])):
            terms[t, b * rows : (b + 1) * rows, :] = value
    picked = [dot(select[...], terms[t]) for t in range(3)]
    ordered = [picked[term] for _, term in TERMS]
    ordered += [jnp.zeros_like(picked[0])] * (stress_corner.shape[0] // TERM - len(ordered))
    per = LANES // TERM
    for k in range(0, len(ordered), per):
        block = jnp.concatenate(ordered[k : k + per], axis=0).T.astype(BF16)
        values[:, k * TERM : (k + per) * TERM] = block
    moved = dot(values[...], stress_corner[...])
    for i in range(COMPS):
        cols = slice(i * LANES, (i + 1) * LANES)
        free = jnp.concatenate([stress_first[i], stress_rest[i]], axis=0)
        high, low = split_two(free - moved[:, cols])
        stress[cols, 0:LANES] = high
        stress[cols, LANES : 2 * LANES] = low

    rows = dot_nt(face[...], stress[...])
    for i in range(COMPS):
        part = rows[:, i * LANES : (i + 1) * LANES]
        edge = [part[EDGES + NED * k : EDGES + NED * (k + 1)] for k in range(4)]
        sub_a[i] = part[:NIS]
        sub_b[i] = part[NIS : 2 * NIS]
        grp_a[i] = jnp.concatenate([part[2 * NIS : 2 * NIS + NIG], edge[0], edge[2]], axis=0)
        grp_b[i] = jnp.concatenate([part[2 * NIS + NIG : EDGES], edge[1], edge[3]], axis=0)


def edge_kernel(grp_a, grp_b, from_a, from_b, edge_b, edge_a):
    split = NIG + NED
    edge_a[:, :NED, :] = grp_a[:, NIG:split, :] + from_a[:, NIG:split, :]
    edge_a[:, NED:, :] = grp_b[:, NIG:split, :] + from_b[:, NIG:split, :]
    edge_b[:, :NED, :] = grp_a[:, split:, :] + from_a[:, split:, :]
    edge_b[:, NED:, :] = grp_b[:, split:, :] + from_b[:, split:, :]


def partial_kernel(
    count, stress, free_t, corner_t, values, placing, grp_a, grp_b, partial, disp_out, received
):
    nodes = disp_out.shape[1]
    for c in range(3):
        cols = slice(c * nodes, (c + 1) * nodes)
        part = free_t[:, cols] - dot(values[...], corner_t[:, cols])
        for k in range(0, nodes, LANES):
            disp_out[c, k : k + LANES, :] = part[:, k : k + LANES].T.astype(BF16)
    split = NIG + NED
    for i in range(COMPS):
        low, high = grp_a[i], grp_b[i]
        rows = [low[:NIG], high[:NIG], low[NIG:split], high[NIG:split], low[split:], high[split:]]
        rows.append(jnp.zeros((2 * LANES - NIF, LANES), F32))
        first, second = split_two(jnp.concatenate(rows, axis=0))
        received[:LANES, i * LANES : (i + 1) * LANES] = first
        received[LANES:, i * LANES : (i + 1) * LANES] = second
    for i in range(0, COMPS, 2):
        cols = slice(i * LANES, (i + 2) * LANES)
        own = dot_nt(count[...], stress[cols, :])
        total = own + dot(placing[...], received[:, cols])
        partial[i] = total[:, :LANES]
        partial[i + 1] = total[:, LANES:]


def finish_kernel(
    placing, partial, inverse_volume, sub_a, sub_b, edge_b, edge_a, out, received, nodal, sems
):
    scale = inverse_volume[...]
    copies = []
    for i in range(0, COMPS, 2):
        for k in (i, i + 1):
            cols = slice(k * LANES, (k + 1) * LANES)
            late = jnp.concatenate([sub_b[k], edge_a[k], edge_b[k]], axis=0)
            first, second = split_two(late)
            received[:NIS, cols] = sub_a[k].astype(BF16)
            received[NIS : NIS + LATE, cols] = first
            received[NIS + LATE :, cols] = second
        added = dot(placing[...], received[:, i * LANES : (i + 2) * LANES])
        nodal[i] = ((partial[i] + added[:, :LANES]) * scale).astype(BF16)
        nodal[i + 1] = ((partial[i + 1] + added[:, LANES:]) * scale).astype(BF16)
        copy = pltpu.make_async_copy(nodal.at[pl.ds(i, 2)], out.at[pl.ds(i, 2)], sems.at[i // 2])
        copy.start()
        copies.append(copy)
    for copy in copies:
        copy.wait()


def vmem(count):
    return [pl.BlockSpec(memory_space=pltpu.VMEM)] * count


def anywhere(count):
    return [pl.BlockSpec(memory_space=pl.ANY)] * count


def hbm(count):
    return [pl.BlockSpec(memory_space=pltpu.HBM)] * count


def array(shape, dtype=F32):
    return jax.ShapeDtypeStruct(shape, dtype)


def call(kernel, name, out_shape, in_specs, scratch=(), flops=0, moved=0, out_specs=None):
    return pl.pallas_call(
        kernel,
        name=name,
        out_shape=out_shape,
        in_specs=in_specs,
        out_specs=out_specs or vmem(len(out_shape)),
        scratch_shapes=list(scratch),
        compiler_params=pltpu.CompilerParams(vmem_limit_bytes=VMEM_LIMIT),
        cost_estimate=pl.CostEstimate(flops=flops, bytes_accessed=moved, transcendentals=0),
    )


def exchange(block, axis, first):
    count = lax.axis_size(axis)
    pairs = []
    for i in range(first, count - 1, 2):
        pairs += [(i, i + 1), (i + 1, i)]
    return lax.ppermute(block, axis, pairs)


def in_hbm(*arrays):
    return [pltpu.with_memory_space_constraint(x, pltpu.HBM) for x in arrays]


def gather_near(coarse, own, ahead):
    def join(parts, before):
        def kernel(*refs):
            join_kernel(*refs[: len(parts)], refs[-1])

        rows = sum(x.shape[0] for x in parts)
        (block,) = call(
            kernel,
            "join_blocks",
            (array((rows, parts[0].shape[1])),),
            vmem(len(parts)) + anywhere(1),
        )(*parts, before)
        return block

    def across(block, distance):
        return lax.ppermute(block, "grp", [(i, i ^ distance) for i in range(lax.axis_size("grp"))])

    distance = lax.axis_size("grp") // 2
    sent, block = coarse, own
    while distance > 1:
        block = join([block, across(sent, distance)], ahead[0])
        sent = block
        distance //= 2
    beyond = exchange(sent, "sub", 1)
    beside = exchange(sent, "sub", 0)
    block = join([block, beyond, beside], ahead[1])
    return [block, across(block, 1)]


def shards(
    coarse,
    corner_idx,
    coupling,
    force,
    panel_inv,
    panel_nodes,
    strain_disp,
    modulus,
    connect,
    interface,
    nodal_volume,
):
    nodes, _, cases = force.shape
    dofs = 3 * nodes
    q = corner_idx.shape[1]

    def lists(*refs):
        prepare_lists(coarse.shape[0], lax.axis_size("grp"), *refs)

    own, *panels, select, onehot, face, scaled, count, placing, placing_last, inverse_volume = call(
        lists,
        "prepare_lists",
        (
            array(coarse.shape),
            array(panel_nodes.shape, jnp.int32),
            array((3, nodes, cases), BF16),
            array(panel_inv.shape, BF16),
            array((TERM, 3 * LANES), BF16),
            array((nodes, CORNERS * LANES), BF16),
            array((NIF, 2 * LANES), BF16),
            array((COMPS * 24, 8, LANES)),
            array((nodes, 2 * LANES), BF16),
            array((nodes, 2 * LANES), BF16),
            array((nodes, 2 * LANES), BF16),
            array((nodes, LANES)),
        ),
        hbm(10),
        (
            pltpu.VMEM((1, q), jnp.int32),
            pltpu.VMEM(connect.shape, jnp.int32),
            pltpu.VMEM(interface.shape, jnp.int32),
            pltpu.VMEM((COMPS * 24, LANES), BF16),
            pltpu.VMEM((1, LANES), F32),
            pltpu.VMEM((nodes // LANES, LANES), F32),
            pltpu.VMEM((8, 2 * LANES), F32),
            pltpu.SemaphoreType.DMA((10,)),
        ),
        flops=100000000,
        moved=4000000,
    )(
        *in_hbm(
            corner_idx,
            connect,
            interface,
            strain_disp.reshape(COMPS * 24, LANES),
            modulus.reshape(1, -1),
            nodal_volume.reshape(-1, LANES),
            coarse,
            panel_nodes,
            jnp.transpose(force, (1, 0, 2)),
            panel_inv,
        )
    )
    first = 64
    free_t, corner_t, stress_first, stress_corner = call(
        prepare_panels,
        "prepare_panels",
        (
            array((cases, dofs)),
            array((2 * LANES, dofs), BF16),
            array((COMPS, first, LANES)),
            array((2 * LANES, COMPS * LANES), BF16),
        ),
        vmem(6),
        (
            pltpu.VMEM((dofs + SPARE, cases), F32),
            pltpu.VMEM((2, panel_inv.shape[1] + SPARE, LANES), F32),
            pltpu.VMEM((TERM, dofs), F32),
            pltpu.VMEM((COMPS, max(first, TERM), LANES), F32),
        ),
        flops=400000000,
        moved=4000000,
    )(coupling.T, *panels, onehot, scaled)
    (stress_rest,) = call(
        stress_kernel,
        "stress_of_loads",
        (array((COMPS, cases - first, LANES)),),
        vmem(3),
        (pltpu.VMEM((COMPS, cases - first, LANES), F32),),
        flops=400000000,
        moved=4000000,
    )(free_t, onehot, scaled)

    near = gather_near(coarse, own, [select, corner_t])
    values, stress, sub_a, sub_b, grp_a, grp_b = call(
        solve_kernel,
        "stress_and_rows",
        (
            array((cases, 2 * LANES), BF16),
            array((COMPS * cases, 2 * LANES), BF16),
            array((COMPS, NIS, cases)),
            array((COMPS, NIS, cases)),
            array((COMPS, NIG + 2 * NED, cases)),
            array((COMPS, NIG + 2 * NED, cases)),
        ),
        vmem(7),
        (pltpu.VMEM((3, 3 * LANES, cases), BF16),),
        flops=300000000,
        moved=3000000,
    )(*near, select, stress_first, stress_rest, stress_corner, face)
    from_sub_a = exchange(sub_a, "sub", 0)
    from_grp_a = exchange(grp_a, "grp", 0)
    from_grp_b = exchange(grp_b, "grp", 1)
    edge_b, edge_a = call(
        edge_kernel,
        "sum_edges",
        (array((COMPS, 2 * NED, cases)), array((COMPS, 2 * NED, cases))),
        vmem(4),
    )(grp_a, grp_b, from_grp_a, from_grp_b)
    from_sub_b = exchange(sub_b, "sub", 1)
    from_edge_b = exchange(edge_b, "sub", 1)
    from_edge_a = exchange(edge_a, "sub", 0)
    partial, disp = call(
        partial_kernel,
        "assemble_nodes",
        (array((COMPS, nodes, cases)), array((3, nodes, cases), BF16)),
        vmem(8),
        (pltpu.VMEM((2 * LANES, COMPS * cases), BF16),),
        flops=400000000,
        moved=2000000,
    )(count, stress, free_t, corner_t, values, placing, from_grp_a, from_grp_b)
    (nodal,) = call(
        finish_kernel,
        "add_last",
        (array((COMPS, nodes, cases), BF16),),
        vmem(7),
        (
            pltpu.VMEM((NIS + 2 * LATE, COMPS * cases), BF16),
            pltpu.VMEM((COMPS, nodes, cases), BF16),
            pltpu.SemaphoreType.DMA((COMPS // 2,)),
        ),
        flops=400000000,
        moved=3000000,
        out_specs=hbm(1),
    )(placing_last, partial, inverse_volume, from_sub_a, from_sub_b, from_edge_b, from_edge_a)
    return jnp.transpose(disp, (1, 0, 2)), jnp.transpose(nodal, (1, 0, 2))


def solution(mesh):
    owner = ("sub", "grp")
    placed = (
        P(owner, None),
        P(owner, None),
        P(owner, None),
        P(owner, None, None),
        P(owner, None, None),
        P(owner, None),
        P(None, None, owner),
        P(owner),
        P(None, owner),
        P(owner, None),
        P(owner),
    )
    return jax.shard_map(
        shards,
        mesh=mesh,
        in_specs=placed,
        out_specs=(P(owner, None, None), P(owner, None, None)),
        check_vma=False,
    )
```

```python
import jax
import jax.numpy as jnp
from jax import lax
from jax.experimental import pallas as pl
from jax.experimental.pallas import tpu as pltpu
from jax.sharding import PartitionSpec as P

NIS = 64
NIG = 32
NED = 8
EDGES = 2 * NIS + 2 * NIG
NIF = EDGES + 4 * NED
LATE = NIS + 4 * NED
CORNERS = 8
COMPS = 6
LANES = 128
TERM = 32
SPARE = 8
GRP_A = 64
TERMS = ((0, 0), (0, 1), (0, 2), (1, 0), (1, 1), (2, 0))

POISSON = 0.3
LAME = POISSON / ((1.0 + POISSON) * (1.0 - 2.0 * POISSON))
SHEAR = 0.5 / (1.0 + POISSON)

F32 = jnp.float32
BF16 = jnp.bfloat16
VMEM_LIMIT = 24 * 1024 * 1024


def split_two(x):
    high = x.astype(BF16)
    return high, (x - high.astype(F32)).astype(BF16)


def split_three(x):
    high = x.astype(BF16)
    rest = x - high.astype(F32)
    middle = rest.astype(BF16)
    return high, middle, (rest - middle.astype(F32)).astype(BF16)


def dot(a, b):
    return jnp.dot(a, b, preferred_element_type=F32)


def dot_nt(a, b):
    return lax.dot_general(a, b, (((1,), (1,)), ((), ())), preferred_element_type=F32)


def column(row):
    return jnp.broadcast_to(row, (LANES, LANES)).T


def swap_lanes(x, distance):
    lane = lax.broadcasted_iota(jnp.int32, x.shape, 1)
    after = pltpu.roll(x, LANES - distance, 1)
    before = pltpu.roll(x, distance, 1)
    return jnp.where((lane & distance) == 0, after, before)


def order_lists(ids):
    sub_even = (lax.axis_index("sub") & 1) == 0
    grp_even = (lax.axis_index("grp") & 1) == 0
    first, second = ids[:, :LANES], ids[:, LANES:]
    ids[:, :LANES] = jnp.where(sub_even, swap_lanes(first, NIS), first)
    lane = lax.broadcasted_iota(jnp.int32, second.shape, 1)
    groups = jnp.where(grp_even, swap_lanes(second, NIG), second)
    edges = jnp.where(sub_even, swap_lanes(second, 2 * NED), second)
    edges = jnp.where(grp_even, swap_lanes(edges, NED), edges)
    ids[:, LANES:] = jnp.where(lane < 2 * NIG, groups, edges)


def element_stress(terms, rows, onehot, scaled, sofar, store):
    step = 32
    pairs = onehot.shape[1] // (2 * LANES)
    for pair in range(pairs):
        operand = onehot[:, 2 * LANES * pair : 2 * LANES * (pair + 1)]
        elem = dot(terms[0], operand)
        for term in terms[1:]:
            elem = elem + dot(term, operand)
        for start in range(0, rows, step):
            sums = [None] * COMPS if pair == 0 else [sofar[i, start : start + step, :] for i in range(COMPS)]
            for half in range(2):
                for c in range(3):
                    x = elem[c * rows + start : c * rows + start + step, half * LANES : (half + 1) * LANES]
                    x = x.reshape(step // 8, 8, LANES)
                    for i in range(COMPS):
                        term = scaled[24 * i + 3 * (2 * pair + half) + c] * x
                        term = term.reshape(step, LANES)
                        sums[i] = term if sums[i] is None else sums[i] + term
            for i in range(COMPS):
                if pair < pairs - 1:
                    sofar[i, start : start + step, :] = sums[i]
                else:
                    store(i, start, sums[i])


def free_stress(free_t, first, rows, onehot, scaled, sofar, out):
    nodes = onehot.shape[0]
    parts = [free_t[first : first + rows, c * nodes : (c + 1) * nodes] for c in range(3)]

    def store(i, start, value):
        out[i, start : start + value.shape[0], :] = value

    element_stress(split_two(jnp.concatenate(parts, axis=0)), rows, onehot, scaled, sofar, store)


def start_copies(pairs, sems):
    copies = [pltpu.make_async_copy(src, dst, sems.at[k]) for k, (src, dst) in enumerate(pairs)]
    for copy in copies:
        copy.start()
    return copies


def prepare_lists(
    block_rows,
    members,
    corner_idx,
    connect,
    interface,
    strain_disp,
    modulus,
    volume,
    coarse,
    panel_nodes,
    force,
    panel_inv,
    own,
    panel_v,
    force_v,
    inverse,
    select,
    onehot,
    face,
    scaled,
    count,
    placing,
    placing_last,
    inverse_volume,
    corner_v,
    connect_v,
    interface_v,
    strain_v,
    modulus_v,
    volume_v,
    ids,
    sems,
):
    copies = start_copies(
        [
            (connect, connect_v),
            (interface, interface_v),
            (corner_idx, corner_v),
            (modulus, modulus_v),
            (strain_disp, strain_v),
            (volume, volume_v),
            (coarse, own),
            (panel_nodes, panel_v),
            (force, force_v),
            (panel_inv, inverse),
        ],
        sems,
    )
    nodes = onehot.shape[0]
    q = corner_idx.shape[1]

    copies[0].wait()
    node_of = lax.broadcasted_iota(jnp.int32, (nodes, LANES), 0)
    total = jnp.zeros((nodes, LANES), F32)
    for a in range(CORNERS):
        hit = jnp.where(connect_v[a : a + 1, :] == node_of, 1.0, 0.0)
        onehot[:, a * LANES : (a + 1) * LANES] = hit.astype(BF16)
        total = total + hit
    total = total.astype(BF16)
    count[:, :LANES] = total
    count[:, LANES:] = total

    copies[1].wait()
    ids[...] = jnp.full(ids.shape, -1.0, F32)
    ids[0:1, 0:NIF] = interface_v[...].astype(F32)
    order_lists(ids)
    lane = lax.broadcasted_iota(jnp.int32, (8, LANES), 1)
    faces, others = ids[:, :LANES], ids[:, LANES:]
    turned = pltpu.roll(others, NIS, 1)
    lists = (
        (placing, 0, jnp.where(lane < NIS, faces, turned)),
        (placing, 1, jnp.where(lane < 4 * NED, turned, pltpu.roll(others, 4 * NED, 1))),
        (
            placing_last,
            0,
            jnp.where(
                lane < NIS,
                pltpu.roll(faces, NIS, 1),
                jnp.where(lane < LATE, others, pltpu.roll(faces, 4 * NED, 1)),
            ),
        ),
        (
            placing_last,
            1,
            jnp.where(
                lane < 4 * NED,
                pltpu.roll(faces, 4 * NED, 1),
                jnp.where(lane < 8 * NED, pltpu.roll(others, LATE, 1), -1.0),
            ),
        ),
    )
    for target, half, row in lists:
        hit = jnp.where(row[0:1].astype(jnp.int32) == node_of, 1.0, 0.0).astype(BF16)
        target[:, half * LANES : (half + 1) * LANES] = hit
    connect_f = connect_v[...].astype(F32)
    for half in range(2):
        id_col = column(ids[0:1, half * LANES : (half + 1) * LANES])
        rows = jnp.zeros((LANES, LANES), F32)
        for a in range(CORNERS):
            rows = rows + jnp.where(connect_f[a : a + 1, :] == id_col, 1.0, 0.0)
        rows = rows.astype(BF16)[: min(LANES, NIF - half * LANES)]
        face[half * LANES : half * LANES + rows.shape[0], :LANES] = rows
        face[half * LANES : half * LANES + rows.shape[0], LANES:] = rows

    copies[2].wait()
    ids[0:1, 0:q] = corner_v[...].astype(F32)
    wanted = column(ids[0:1, :LANES])[:TERM]
    lane = lax.broadcasted_iota(jnp.int32, (TERM, 3 * LANES), 1)
    entry = lax.broadcasted_iota(jnp.int32, (TERM, LANES), 0)
    s, g = lax.axis_index("sub"), lax.axis_index("grp")
    aside = 1 - 2 * (s & 1)
    row = jnp.full((TERM, 3 * LANES), -1, jnp.int32)
    base = 0
    for core in range(2):
        for owner in (s, s - aside, s + aside):
            for member in range(members // 2):
                distance, bits, turn = members // 2, member, core
                while distance > 1:
                    turn += (bits & 1) * distance
                    distance, bits = distance // 2, bits >> 1
                first = (owner * members + (g ^ turn)) * block_rows
                row = jnp.where((lane >= base) & (lane < base + block_rows), first - base + lane, row)
                base += block_rows
    for b in range(3):
        cols = slice(b * LANES, (b + 1) * LANES)
        hit = (wanted == row[:, cols].astype(F32)) & (entry < q)
        select[:, cols] = jnp.where(hit, 1.0, 0.0).astype(BF16)

    copies[3].wait()
    copies[4].wait()
    factor = modulus_v[...]
    whole = strain_v[...].astype(F32)
    rows = [whole[24 * i : 24 * (i + 1)] for i in range(COMPS)]
    trace = (rows[0] + rows[1] + rows[2]) * LAME
    for i in range(COMPS):
        value = trace + rows[i] * (2.0 * SHEAR) if i < 3 else rows[i] * SHEAR
        scaled[24 * i : 24 * (i + 1)] = jnp.broadcast_to((value * factor)[:, None, :], (24, 8, LANES))

    copies[5].wait()
    for k in range(nodes // LANES):
        inverse_volume[k * LANES : (k + 1) * LANES, :] = column(1.0 / volume_v[k : k + 1, :])
    for copy in copies[6:]:
        copy.wait()


def prepare_panels(
    coupling_v,
    panel_v,
    force_v,
    inverse,
    onehot,
    scaled,
    free_t,
    corner_t,
    stress_first,
    stress_corner,
    loads,
    solved,
    whole,
    sofar,
):
    panels, panel_rows, _ = inverse.shape
    panel_size = panel_rows // 3
    nodes = force_v.shape[1]
    q = coupling_v.shape[0]
    for c in range(3):
        loads[pl.ds(c, nodes, stride=3), :] = force_v[c].astype(F32)
    spare = corner_t.shape[0] - len(TERMS) * TERM
    stress_corner[len(TERMS) * TERM :, :] = jnp.zeros((spare, stress_corner.shape[1]), BF16)
    corner_t[len(TERMS) * TERM :, :] = jnp.zeros((spare, 3 * nodes), BF16)
    row_of = lax.broadcasted_iota(jnp.int32, (panel_rows, LANES), 0)
    for p in range(panels):
        start = p * panel_rows
        live = row_of < 3 * panel_v[0:1, p : p + 1]
        columns = []
        for k in range(panel_rows // LANES):
            part = coupling_v[:, start + k * LANES : start + (k + 1) * LANES].astype(F32)
            columns.append(jnp.concatenate([part, jnp.zeros((LANES - q, LANES), F32)], axis=0).T)
        sides = [loads[start : start + panel_rows, :], jnp.concatenate(columns, axis=0)]
        sides = jnp.concatenate([jnp.where(live, x, 0.0).astype(BF16) for x in sides], axis=1)
        result = dot(inverse[p], sides)
        for side in range(2):
            solved[side, :panel_rows, :] = jnp.where(live, result[:, side * LANES : (side + 1) * LANES], 0.0)
        for c in range(3):
            cols = slice(c * nodes + p * panel_size, c * nodes + (p + 1) * panel_size)
            free_t[:, cols] = solved[0, pl.ds(c, panel_size, stride=3), :].T
            value = solved[1, pl.ds(c, panel_size, stride=3), :].T[:TERM]
            whole[:, cols] = value
            pieces = split_three(value)
            for k, (piece, _) in enumerate(TERMS):
                corner_t[k * TERM : (k + 1) * TERM, cols] = pieces[piece]

    def store(i, start, value):
        pieces = split_three(value)
        for k, (piece, _) in enumerate(TERMS):
            stress_corner[k * TERM : (k + 1) * TERM, i * LANES : (i + 1) * LANES] = pieces[piece]

    parts = jnp.concatenate([whole[:, c * nodes : (c + 1) * nodes] for c in range(3)], axis=0)
    element_stress(split_two(parts), TERM, onehot, scaled, sofar, store)
    free_stress(free_t, 0, stress_first.shape[1], onehot, scaled, sofar, stress_first)


def stress_kernel(free_t, onehot, scaled, out, sofar):
    rows = out.shape[1]
    free_stress(free_t, free_t.shape[0] - rows, rows, onehot, scaled, sofar, out)


def join_kernel(*refs):
    *parts, out = refs
    start = 0
    for part in parts:
        out[start : start + part.shape[0], :] = part[...]
        start += part.shape[0]


def solve_kernel(
    near,
    across,
    select,
    stress_first,
    stress_rest,
    stress_corner,
    face,
    values,
    stress,
    sub_a,
    sub_b,
    grp_a,
    grp_b,
    terms,
):
    rows = near.shape[0]
    terms[:, 2 * rows :, :] = jnp.zeros((3, terms.shape[1] - 2 * rows, terms.shape[2]), BF16)
    for b, block in enumerate((near, across)):
        for t, value in enumerate(split_three(block[...])):
            terms[t, b * rows : (b + 1) * rows, :] = value
    picked = [dot(select[...], terms[t]) for t in range(3)]
    ordered = [picked[term] for _, term in TERMS]
    ordered += [jnp.zeros_like(picked[0])] * (stress_corner.shape[0] // TERM - len(ordered))
    per = LANES // TERM
    for k in range(0, len(ordered), per):
        block = jnp.concatenate(ordered[k : k + per], axis=0).T.astype(BF16)
        values[:, k * TERM : (k + per) * TERM] = block
    moved = dot(values[...], stress_corner[...])
    for i in range(COMPS):
        cols = slice(i * LANES, (i + 1) * LANES)
        free = jnp.concatenate([stress_first[i], stress_rest[i]], axis=0)
        high, low = split_two(free - moved[:, cols])
        stress[cols, 0:LANES] = high
        stress[cols, LANES : 2 * LANES] = low

    rows = dot_nt(face[...], stress[...])
    for i in range(COMPS):
        part = rows[:, i * LANES : (i + 1) * LANES]
        edge = [part[EDGES + NED * k : EDGES + NED * (k + 1)] for k in range(4)]
        sub_a[i] = part[:NIS]
        sub_b[i] = part[NIS : 2 * NIS]
        gap = jnp.zeros((GRP_A - NIG - 2 * NED, LANES), F32)
        grp_a[i] = jnp.concatenate([part[2 * NIS : 2 * NIS + NIG], edge[0], edge[2], gap], axis=0)
        grp_b[i] = jnp.concatenate([part[2 * NIS + NIG : EDGES], edge[1], edge[3]], axis=0)


def edge_kernel(grp_a, grp_b, from_a, from_b, edge_b, edge_a):
    split = NIG + NED
    edge_a[:, :NED, :] = grp_a[:, NIG:split, :] + from_a[:, NIG:split, :]
    edge_a[:, NED:, :] = grp_b[:, NIG:split, :] + from_b[:, NIG:split, :]
    edge_b[:, :NED, :] = grp_a[:, split : split + NED, :] + from_a[:, split : split + NED, :]
    edge_b[:, NED:, :] = grp_b[:, split:, :] + from_b[:, split:, :]


def partial_kernel(
    count, stress, free_t, corner_t, values, placing, sub_a, grp_a, grp_b, partial, disp_out, received
):
    nodes = disp_out.shape[1]
    for c in range(3):
        cols = slice(c * nodes, (c + 1) * nodes)
        part = free_t[:, cols] - dot(values[...], corner_t[:, cols])
        for k in range(0, nodes, LANES):
            disp_out[c, k : k + LANES, :] = part[:, k : k + LANES].T.astype(BF16)
    split = NIG + NED
    for i in range(COMPS):
        low, high = grp_a[i], grp_b[i]
        rows = [low[:NIG], high[:NIG], low[NIG:split], high[NIG:split], low[split : split + NED], high[split:]]
        first, second = split_two(jnp.concatenate(rows, axis=0))
        cols = slice(i * LANES, (i + 1) * LANES)
        received[:NIS, cols] = sub_a[i].astype(BF16)
        received[NIS : NIS + LATE, cols] = first
        received[NIS + LATE :, cols] = second
    for i in range(0, COMPS, 2):
        cols = slice(i * LANES, (i + 2) * LANES)
        own = dot_nt(count[...], stress[cols, :])
        total = own + dot(placing[...], received[:, cols])
        partial[i] = total[:, :LANES]
        partial[i + 1] = total[:, LANES:]


def finish_kernel(
    placing, partial, inverse_volume, sub_b, edge_b, edge_a, out, received, nodal, sems
):
    received[2 * LATE :, :] = jnp.zeros((received.shape[0] - 2 * LATE, received.shape[1]), BF16)
    scale = inverse_volume[...]
    copies = []
    for i in range(0, COMPS, 2):
        for k in (i, i + 1):
            cols = slice(k * LANES, (k + 1) * LANES)
            late = jnp.concatenate([sub_b[k], edge_a[k], edge_b[k]], axis=0)
            first, second = split_two(late)
            received[:LATE, cols] = first
            received[LATE : 2 * LATE, cols] = second
        added = dot(placing[...], received[:, i * LANES : (i + 2) * LANES])
        nodal[i] = ((partial[i] + added[:, :LANES]) * scale).astype(BF16)
        nodal[i + 1] = ((partial[i + 1] + added[:, LANES:]) * scale).astype(BF16)
        copy = pltpu.make_async_copy(nodal.at[pl.ds(i, 2)], out.at[pl.ds(i, 2)], sems.at[i // 2])
        copy.start()
        copies.append(copy)
    for copy in copies:
        copy.wait()


def vmem(count):
    return [pl.BlockSpec(memory_space=pltpu.VMEM)] * count


def anywhere(count):
    return [pl.BlockSpec(memory_space=pl.ANY)] * count


def hbm(count):
    return [pl.BlockSpec(memory_space=pltpu.HBM)] * count


def array(shape, dtype=F32):
    return jax.ShapeDtypeStruct(shape, dtype)


def call(kernel, name, out_shape, in_specs, scratch=(), flops=0, moved=0, out_specs=None):
    return pl.pallas_call(
        kernel,
        name=name,
        out_shape=out_shape,
        in_specs=in_specs,
        out_specs=out_specs or vmem(len(out_shape)),
        scratch_shapes=list(scratch),
        compiler_params=pltpu.CompilerParams(vmem_limit_bytes=VMEM_LIMIT),
        cost_estimate=pl.CostEstimate(flops=flops, bytes_accessed=moved, transcendentals=0),
    )


def exchange(block, axis, first):
    count = lax.axis_size(axis)
    pairs = []
    for i in range(first, count - 1, 2):
        pairs += [(i, i + 1), (i + 1, i)]
    return lax.ppermute(block, axis, pairs)


def in_hbm(*arrays):
    return [pltpu.with_memory_space_constraint(x, pltpu.HBM) for x in arrays]


def gather_near(coarse, own, ahead):
    def join(parts, before):
        def kernel(*refs):
            join_kernel(*refs[: len(parts)], refs[-1])

        rows = sum(x.shape[0] for x in parts)
        (block,) = call(
            kernel,
            "join_blocks",
            (array((rows, parts[0].shape[1])),),
            vmem(len(parts)) + anywhere(1),
        )(*parts, before)
        return block

    def across(block, distance):
        return lax.ppermute(block, "grp", [(i, i ^ distance) for i in range(lax.axis_size("grp"))])

    distance = lax.axis_size("grp") // 2
    sent, block = coarse, own
    while distance > 1:
        block = join([block, across(sent, distance)], ahead[0])
        sent = block
        distance //= 2
    beyond = exchange(sent, "sub", 1)
    beside = exchange(sent, "sub", 0)
    block = join([block, beyond, beside], ahead[1])
    return [block, across(block, 1)]


def shards(
    coarse,
    corner_idx,
    coupling,
    force,
    panel_inv,
    panel_nodes,
    strain_disp,
    modulus,
    connect,
    interface,
    nodal_volume,
):
    nodes, _, cases = force.shape
    dofs = 3 * nodes
    q = corner_idx.shape[1]

    def lists(*refs):
        prepare_lists(coarse.shape[0], lax.axis_size("grp"), *refs)

    own, *panels, select, onehot, face, scaled, count, placing, placing_last, inverse_volume = call(
        lists,
        "prepare_lists",
        (
            array(coarse.shape),
            array(panel_nodes.shape, jnp.int32),
            array((3, nodes, cases), BF16),
            array(panel_inv.shape, BF16),
            array((TERM, 3 * LANES), BF16),
            array((nodes, CORNERS * LANES), BF16),
            array((NIF, 2 * LANES), BF16),
            array((COMPS * 24, 8, LANES)),
            array((nodes, 2 * LANES), BF16),
            array((nodes, 2 * LANES), BF16),
            array((nodes, 2 * LANES), BF16),
            array((nodes, LANES)),
        ),
        hbm(10),
        (
            pltpu.VMEM((1, q), jnp.int32),
            pltpu.VMEM(connect.shape, jnp.int32),
            pltpu.VMEM(interface.shape, jnp.int32),
            pltpu.VMEM((COMPS * 24, LANES), BF16),
            pltpu.VMEM((1, LANES), F32),
            pltpu.VMEM((nodes // LANES, LANES), F32),
            pltpu.VMEM((8, 2 * LANES), F32),
            pltpu.SemaphoreType.DMA((10,)),
        ),
        flops=100000000,
        moved=4000000,
    )(
        *in_hbm(
            corner_idx,
            connect,
            interface,
            strain_disp.reshape(COMPS * 24, LANES),
            modulus.reshape(1, -1),
            nodal_volume.reshape(-1, LANES),
            coarse,
            panel_nodes,
            jnp.transpose(force, (1, 0, 2)),
            panel_inv,
        )
    )
    first = 64
    free_t, corner_t, stress_first, stress_corner = call(
        prepare_panels,
        "prepare_panels",
        (
            array((cases, dofs)),
            array((2 * LANES, dofs), BF16),
            array((COMPS, first, LANES)),
            array((2 * LANES, COMPS * LANES), BF16),
        ),
        vmem(6),
        (
            pltpu.VMEM((dofs + SPARE, cases), F32),
            pltpu.VMEM((2, panel_inv.shape[1] + SPARE, LANES), F32),
            pltpu.VMEM((TERM, dofs), F32),
            pltpu.VMEM((COMPS, max(first, TERM), LANES), F32),
        ),
        flops=400000000,
        moved=4000000,
    )(coupling.T, *panels, onehot, scaled)
    (stress_rest,) = call(
        stress_kernel,
        "stress_of_loads",
        (array((COMPS, cases - first, LANES)),),
        vmem(3),
        (pltpu.VMEM((COMPS, cases - first, LANES), F32),),
        flops=400000000,
        moved=4000000,
    )(free_t, onehot, scaled)

    near = gather_near(coarse, own, [select, corner_t])
    values, stress, sub_a, sub_b, grp_a, grp_b = call(
        solve_kernel,
        "stress_and_rows",
        (
            array((cases, 2 * LANES), BF16),
            array((COMPS * cases, 2 * LANES), BF16),
            array((COMPS, NIS, cases)),
            array((COMPS, NIS, cases)),
            array((COMPS, GRP_A, cases)),
            array((COMPS, NIG + 2 * NED, cases)),
        ),
        vmem(7),
        (pltpu.VMEM((3, 3 * LANES, cases), BF16),),
        flops=300000000,
        moved=3000000,
    )(*near, select, stress_first, stress_rest, stress_corner, face)
    from_sub_a = exchange(sub_a, "sub", 0)
    from_grp_a = exchange(grp_a, "grp", 0)
    from_grp_b = exchange(grp_b, "grp", 1)
    edge_b, edge_a = call(
        edge_kernel,
        "sum_edges",
        (array((COMPS, 2 * NED, cases)), array((COMPS, 2 * NED, cases))),
        vmem(4),
    )(grp_a, grp_b, from_grp_a, from_grp_b)
    from_sub_b = exchange(sub_b, "sub", 1)
    from_edge_b = exchange(edge_b, "sub", 1)
    from_edge_a = exchange(edge_a, "sub", 0)
    partial, disp = call(
        partial_kernel,
        "assemble_nodes",
        (array((COMPS, nodes, cases)), array((3, nodes, cases), BF16)),
        vmem(9),
        (pltpu.VMEM((NIS + 2 * LATE, COMPS * cases), BF16),),
        flops=400000000,
        moved=2000000,
    )(count, stress, free_t, corner_t, values, placing, from_sub_a, from_grp_a, from_grp_b)
    (nodal,) = call(
        finish_kernel,
        "add_last",
        (array((COMPS, nodes, cases), BF16),),
        vmem(6),
        (
            pltpu.VMEM((2 * LANES, COMPS * cases), BF16),
            pltpu.VMEM((COMPS, nodes, cases), BF16),
            pltpu.SemaphoreType.DMA((COMPS // 2,)),
        ),
        flops=400000000,
        moved=3000000,
        out_specs=hbm(1),
    )(placing_last, partial, inverse_volume, from_sub_b, from_edge_b, from_edge_a)
    return jnp.transpose(disp, (1, 0, 2)), jnp.transpose(nodal, (1, 0, 2))


def solution(mesh):
    owner = ("sub", "grp")
    placed = (
        P(owner, None),
        P(owner, None),
        P(owner, None),
        P(owner, None, None),
        P(owner, None, None),
        P(owner, None),
        P(None, None, owner),
        P(owner),
        P(None, owner),
        P(owner, None),
        P(owner),
    )
    return jax.shard_map(
        shards,
        mesh=mesh,
        in_specs=placed,
        out_specs=(P(owner, None, None), P(owner, None, None)),
        check_vma=False,
    )
```

```python
import jax
import jax.numpy as jnp
from jax import lax
from jax.experimental import pallas as pl
from jax.experimental.pallas import tpu as pltpu
from jax.sharding import PartitionSpec as P

NIS = 64
NIG = 32
NED = 8
EDGES = 2 * NIS + 2 * NIG
NIF = EDGES + 4 * NED
LATE = NIS + 4 * NED
CORNERS = 8
COMPS = 6
LANES = 128
TERM = 32
SPARE = 8
HALF = 256
TERMS = ((0, 0), (0, 1), (0, 2), (1, 0), (1, 1), (2, 0))

POISSON = 0.3
LAME = POISSON / ((1.0 + POISSON) * (1.0 - 2.0 * POISSON))
SHEAR = 0.5 / (1.0 + POISSON)

F32 = jnp.float32
BF16 = jnp.bfloat16
VMEM_LIMIT = 24 * 1024 * 1024


def split_two(x):
    high = x.astype(BF16)
    return high, (x - high.astype(F32)).astype(BF16)


def split_three(x):
    high = x.astype(BF16)
    rest = x - high.astype(F32)
    middle = rest.astype(BF16)
    return high, middle, (rest - middle.astype(F32)).astype(BF16)


def dot(a, b):
    return jnp.dot(a, b, preferred_element_type=F32)


def dot_nt(a, b):
    return lax.dot_general(a, b, (((1,), (1,)), ((), ())), preferred_element_type=F32)


def column(row):
    return jnp.broadcast_to(row, (LANES, LANES)).T


def swap_lanes(x, distance):
    lane = lax.broadcasted_iota(jnp.int32, x.shape, 1)
    after = pltpu.roll(x, LANES - distance, 1)
    before = pltpu.roll(x, distance, 1)
    return jnp.where((lane & distance) == 0, after, before)


def order_lists(ids):
    sub_even = (lax.axis_index("sub") & 1) == 0
    grp_even = (lax.axis_index("grp") & 1) == 0
    first, second = ids[:, :LANES], ids[:, LANES:]
    ids[:, :LANES] = jnp.where(sub_even, swap_lanes(first, NIS), first)
    lane = lax.broadcasted_iota(jnp.int32, second.shape, 1)
    groups = jnp.where(grp_even, swap_lanes(second, NIG), second)
    edges = jnp.where(sub_even, swap_lanes(second, 2 * NED), second)
    edges = jnp.where(grp_even, swap_lanes(edges, NED), edges)
    ids[:, LANES:] = jnp.where(lane < 2 * NIG, groups, edges)


def element_stress(terms, rows, onehot, scaled, sofar, store):
    step = 32
    pairs = onehot.shape[1] // (2 * LANES)
    for pair in range(pairs):
        operand = onehot[:, 2 * LANES * pair : 2 * LANES * (pair + 1)]
        elem = dot(terms[0], operand)
        for term in terms[1:]:
            elem = elem + dot(term, operand)
        for start in range(0, rows, step):
            sums = [None] * COMPS if pair == 0 else [sofar[i, start : start + step, :] for i in range(COMPS)]
            for half in range(2):
                for c in range(3):
                    x = elem[c * rows + start : c * rows + start + step, half * LANES : (half + 1) * LANES]
                    x = x.reshape(step // 8, 8, LANES)
                    for i in range(COMPS):
                        term = scaled[24 * i + 3 * (2 * pair + half) + c] * x
                        term = term.reshape(step, LANES)
                        sums[i] = term if sums[i] is None else sums[i] + term
            for i in range(COMPS):
                if pair < pairs - 1:
                    sofar[i, start : start + step, :] = sums[i]
                else:
                    store(i, start, sums[i])


def free_stress(free_t, first, rows, onehot, scaled, sofar, out):
    nodes = onehot.shape[0]
    parts = [free_t[first : first + rows, c * nodes : (c + 1) * nodes] for c in range(3)]

    def store(i, start, value):
        out[i, start : start + value.shape[0], :] = value

    element_stress(split_two(jnp.concatenate(parts, axis=0)), rows, onehot, scaled, sofar, store)


def start_copies(pairs, sems):
    copies = [pltpu.make_async_copy(src, dst, sems.at[k]) for k, (src, dst) in enumerate(pairs)]
    for copy in copies:
        copy.start()
    return copies


def prepare_lists(
    block_rows,
    members,
    corner_idx,
    connect,
    interface,
    strain_disp,
    modulus,
    volume,
    coarse,
    panel_nodes,
    force,
    panel_inv,
    own,
    panel_v,
    force_v,
    inverse,
    select,
    onehot,
    face,
    scaled,
    count,
    placing,
    placing_last,
    inverse_volume,
    corner_v,
    connect_v,
    interface_v,
    strain_v,
    modulus_v,
    volume_v,
    ids,
    sems,
):
    copies = start_copies(
        [
            (connect, connect_v),
            (interface, interface_v),
            (corner_idx, corner_v),
            (modulus, modulus_v),
            (strain_disp, strain_v),
            (volume, volume_v),
            (coarse, own),
            (panel_nodes, panel_v),
            (force, force_v),
            (panel_inv, inverse),
        ],
        sems,
    )
    nodes = onehot.shape[0]
    q = corner_idx.shape[1]

    copies[0].wait()
    node_of = lax.broadcasted_iota(jnp.int32, (nodes, LANES), 0)
    total = jnp.zeros((nodes, LANES), F32)
    for a in range(CORNERS):
        hit = jnp.where(connect_v[a : a + 1, :] == node_of, 1.0, 0.0)
        onehot[:, a * LANES : (a + 1) * LANES] = hit.astype(BF16)
        total = total + hit
    total = total.astype(BF16)
    count[:, :LANES] = total
    count[:, LANES:] = total

    copies[1].wait()
    ids[...] = jnp.full(ids.shape, -1.0, F32)
    ids[0:1, 0:NIF] = interface_v[...].astype(F32)
    order_lists(ids)
    lane = lax.broadcasted_iota(jnp.int32, (8, LANES), 1)
    edges = pltpu.roll(ids[:, LANES:], LANES - NIS, 1)
    again = pltpu.roll(ids[:, :LANES], LANES - NIS + 4 * NED, 1)
    last = jnp.where(lane < 4 * NED, edges, again)
    last = jnp.where(lane < LATE, last, pltpu.roll(edges, LATE, 1))
    for row, target in ((ids[0:1, LANES:], 0), (ids[0:1, :LANES], 1), (last[0:1], 2)):
        hit = jnp.where(row.astype(jnp.int32) == node_of, 1.0, 0.0).astype(BF16)
        if target == 0:
            placing[:, :LANES] = hit
            placing[:, LANES:] = hit
        else:
            placing_last[:, (target - 1) * LANES : target * LANES] = hit
    connect_f = connect_v[...].astype(F32)
    for half in range(2):
        id_col = column(ids[0:1, half * LANES : (half + 1) * LANES])
        rows = jnp.zeros((LANES, LANES), F32)
        for a in range(CORNERS):
            rows = rows + jnp.where(connect_f[a : a + 1, :] == id_col, 1.0, 0.0)
        rows = rows.astype(BF16)[: min(LANES, NIF - half * LANES)]
        face[half * LANES : half * LANES + rows.shape[0], :LANES] = rows
        face[half * LANES : half * LANES + rows.shape[0], LANES:] = rows

    copies[2].wait()
    ids[0:1, 0:q] = corner_v[...].astype(F32)
    wanted = column(ids[0:1, :LANES])[:TERM]
    lane = lax.broadcasted_iota(jnp.int32, (TERM, 2 * HALF), 1)
    entry = lax.broadcasted_iota(jnp.int32, (TERM, LANES), 0)
    s, g = lax.axis_index("sub"), lax.axis_index("grp")
    aside = 1 - 2 * (s & 1)
    row = jnp.full((TERM, 2 * HALF), -1, jnp.int32)
    for core in range(2):
        base = core * HALF
        for owner in (s, s - aside, s + aside):
            for member in range(members // 2):
                distance, bits, turn = members // 2, member, core
                while distance > 1:
                    turn += (bits & 1) * distance
                    distance, bits = distance // 2, bits >> 1
                first = (owner * members + (g ^ turn)) * block_rows
                row = jnp.where((lane >= base) & (lane < base + block_rows), first - base + lane, row)
                base += block_rows
    for b in range(2 * HALF // LANES):
        cols = slice(b * LANES, (b + 1) * LANES)
        hit = (wanted == row[:, cols].astype(F32)) & (entry < q)
        select[:, cols] = jnp.where(hit, 1.0, 0.0).astype(BF16)

    copies[3].wait()
    copies[4].wait()
    factor = modulus_v[...]
    whole = strain_v[...].astype(F32)
    rows = [whole[24 * i : 24 * (i + 1)] for i in range(COMPS)]
    trace = (rows[0] + rows[1] + rows[2]) * LAME
    for i in range(COMPS):
        value = trace + rows[i] * (2.0 * SHEAR) if i < 3 else rows[i] * SHEAR
        scaled[24 * i : 24 * (i + 1)] = jnp.broadcast_to((value * factor)[:, None, :], (24, 8, LANES))

    copies[5].wait()
    for k in range(nodes // LANES):
        inverse_volume[k * LANES : (k + 1) * LANES, :] = column(1.0 / volume_v[k : k + 1, :])
    for copy in copies[6:]:
        copy.wait()


def prepare_panels(
    coupling_v,
    panel_v,
    force_v,
    inverse,
    onehot,
    scaled,
    free_t,
    corner_t,
    stress_first,
    stress_corner,
    loads,
    solved,
    whole,
    sofar,
):
    panels, panel_rows, _ = inverse.shape
    panel_size = panel_rows // 3
    nodes = force_v.shape[1]
    q = coupling_v.shape[0]
    for c in range(3):
        loads[pl.ds(c, nodes, stride=3), :] = force_v[c].astype(F32)
    spare = corner_t.shape[0] - len(TERMS) * TERM
    stress_corner[len(TERMS) * TERM :, :] = jnp.zeros((spare, stress_corner.shape[1]), BF16)
    corner_t[len(TERMS) * TERM :, :] = jnp.zeros((spare, 3 * nodes), BF16)
    row_of = lax.broadcasted_iota(jnp.int32, (panel_rows, LANES), 0)
    for p in range(panels):
        start = p * panel_rows
        live = row_of < 3 * panel_v[0:1, p : p + 1]
        columns = []
        for k in range(panel_rows // LANES):
            part = coupling_v[:, start + k * LANES : start + (k + 1) * LANES].astype(F32)
            columns.append(jnp.concatenate([part, jnp.zeros((LANES - q, LANES), F32)], axis=0).T)
        sides = [loads[start : start + panel_rows, :], jnp.concatenate(columns, axis=0)]
        sides = jnp.concatenate([jnp.where(live, x, 0.0).astype(BF16) for x in sides], axis=1)
        result = dot(inverse[p], sides)
        for side in range(2):
            solved[side, :panel_rows, :] = jnp.where(live, result[:, side * LANES : (side + 1) * LANES], 0.0)
        for c in range(3):
            cols = slice(c * nodes + p * panel_size, c * nodes + (p + 1) * panel_size)
            free_t[:, cols] = solved[0, pl.ds(c, panel_size, stride=3), :].T
            value = solved[1, pl.ds(c, panel_size, stride=3), :].T[:TERM]
            whole[:, cols] = value
            pieces = split_three(value)
            for k, (piece, _) in enumerate(TERMS):
                corner_t[k * TERM : (k + 1) * TERM, cols] = pieces[piece]

    def store(i, start, value):
        pieces = split_three(value)
        for k, (piece, _) in enumerate(TERMS):
            stress_corner[k * TERM : (k + 1) * TERM, i * LANES : (i + 1) * LANES] = pieces[piece]

    parts = jnp.concatenate([whole[:, c * nodes : (c + 1) * nodes] for c in range(3)], axis=0)
    element_stress(split_two(parts), TERM, onehot, scaled, sofar, store)
    free_stress(free_t, 0, stress_first.shape[1], onehot, scaled, sofar, stress_first)


def pick_rows(select, block, terms):
    rows = block.shape[0]
    terms[:, rows:, :] = jnp.zeros((3, terms.shape[1] - rows, terms.shape[2]), BF16)
    for t, value in enumerate(split_three(block[...])):
        terms[t, :rows, :] = value
    return [dot(select, terms[t]) for t in range(3)]


def stress_kernel(free_t, onehot, scaled, near, select, out, picked, sofar, terms):
    for t, value in enumerate(pick_rows(select[:, :HALF], near, terms)):
        picked[t] = value
    rows = out.shape[1]
    free_stress(free_t, free_t.shape[0] - rows, rows, onehot, scaled, sofar, out)


def join_kernel(*refs):
    *parts, out = refs
    start = 0
    for part in parts:
        out[start : start + part.shape[0], :] = part[...]
        start += part.shape[0]


def solve_kernel(
    across,
    picked_near,
    select,
    stress_first,
    stress_rest,
    stress_corner,
    face,
    values,
    stress,
    sub_a,
    sub_b,
    grp_a,
    grp_b,
    terms,
):
    picked = pick_rows(select[:, HALF:], across, terms)
    picked = [picked[t] + picked_near[t] for t in range(3)]
    ordered = [picked[term] for _, term in TERMS]
    ordered += [jnp.zeros_like(picked[0])] * (stress_corner.shape[0] // TERM - len(ordered))
    per = LANES // TERM
    for k in range(0, len(ordered), per):
        block = jnp.concatenate(ordered[k : k + per], axis=0).T.astype(BF16)
        values[:, k * TERM : (k + per) * TERM] = block
    moved = dot(values[...], stress_corner[...])
    for i in range(COMPS):
        cols = slice(i * LANES, (i + 1) * LANES)
        free = jnp.concatenate([stress_first[i], stress_rest[i]], axis=0)
        high, low = split_two(free - moved[:, cols])
        stress[cols, 0:LANES] = high
        stress[cols, LANES : 2 * LANES] = low

    rows = dot_nt(face[...], stress[...])
    for i in range(COMPS):
        part = rows[:, i * LANES : (i + 1) * LANES]
        edge = [part[EDGES + NED * k : EDGES + NED * (k + 1)] for k in range(4)]
        sub_a[i] = part[:NIS]
        sub_b[i] = part[NIS : 2 * NIS]
        grp_a[i] = jnp.concatenate([part[2 * NIS : 2 * NIS + NIG], edge[0], edge[2]], axis=0)
        grp_b[i] = jnp.concatenate([part[2 * NIS + NIG : EDGES], edge[1], edge[3]], axis=0)


def edge_kernel(grp_a, grp_b, from_a, from_b, edge_b, edge_a):
    split = NIG + NED
    edge_a[:, :NED, :] = grp_a[:, NIG:split, :] + from_a[:, NIG:split, :]
    edge_a[:, NED:, :] = grp_b[:, NIG:split, :] + from_b[:, NIG:split, :]
    edge_b[:, :NED, :] = grp_a[:, split:, :] + from_a[:, split:, :]
    edge_b[:, NED:, :] = grp_b[:, split:, :] + from_b[:, split:, :]


def partial_kernel(
    count, stress, free_t, corner_t, values, placing, grp_a, grp_b, partial, disp_out, received
):
    nodes = disp_out.shape[1]
    for c in range(3):
        cols = slice(c * nodes, (c + 1) * nodes)
        part = free_t[:, cols] - dot(values[...], corner_t[:, cols])
        for k in range(0, nodes, LANES):
            disp_out[c, k : k + LANES, :] = part[:, k : k + LANES].T.astype(BF16)
    split = NIG + NED
    for i in range(COMPS):
        low, high = grp_a[i], grp_b[i]
        rows = [low[:NIG], high[:NIG], low[NIG:split], high[NIG:split], low[split:], high[split:]]
        rows.append(jnp.zeros((2 * LANES - NIF, LANES), F32))
        first, second = split_two(jnp.concatenate(rows, axis=0))
        received[:LANES, i * LANES : (i + 1) * LANES] = first
        received[LANES:, i * LANES : (i + 1) * LANES] = second
    for i in range(0, COMPS, 2):
        cols = slice(i * LANES, (i + 2) * LANES)
        own = dot_nt(count[...], stress[cols, :])
        total = own + dot(placing[...], received[:, cols])
        partial[i] = total[:, :LANES]
        partial[i + 1] = total[:, LANES:]


def finish_kernel(
    placing, partial, inverse_volume, sub_a, sub_b, edge_b, edge_a, out, received, nodal, sems
):
    scale = inverse_volume[...]
    copies = []
    for i in range(0, COMPS, 2):
        for k in (i, i + 1):
            cols = slice(k * LANES, (k + 1) * LANES)
            late = jnp.concatenate([sub_b[k], edge_a[k], edge_b[k]], axis=0)
            first, second = split_two(late)
            received[:NIS, cols] = sub_a[k].astype(BF16)
            received[NIS : NIS + LATE, cols] = first
            received[NIS + LATE :, cols] = second
        added = dot(placing[...], received[:, i * LANES : (i + 2) * LANES])
        nodal[i] = ((partial[i] + added[:, :LANES]) * scale).astype(BF16)
        nodal[i + 1] = ((partial[i + 1] + added[:, LANES:]) * scale).astype(BF16)
        for k in (i, i + 1):
            copy = pltpu.make_async_copy(nodal.at[k], out.at[k], sems.at[k])
            copy.start()
            copies.append(copy)
    for copy in copies:
        copy.wait()


def vmem(count):
    return [pl.BlockSpec(memory_space=pltpu.VMEM)] * count


def anywhere(count):
    return [pl.BlockSpec(memory_space=pl.ANY)] * count


def hbm(count):
    return [pl.BlockSpec(memory_space=pltpu.HBM)] * count


def array(shape, dtype=F32):
    return jax.ShapeDtypeStruct(shape, dtype)


def call(kernel, name, out_shape, in_specs, scratch=(), flops=0, moved=0, out_specs=None):
    return pl.pallas_call(
        kernel,
        name=name,
        out_shape=out_shape,
        in_specs=in_specs,
        out_specs=out_specs or vmem(len(out_shape)),
        scratch_shapes=list(scratch),
        compiler_params=pltpu.CompilerParams(vmem_limit_bytes=VMEM_LIMIT),
        cost_estimate=pl.CostEstimate(flops=flops, bytes_accessed=moved, transcendentals=0),
    )


def exchange(block, axis, first):
    count = lax.axis_size(axis)
    pairs = []
    for i in range(first, count - 1, 2):
        pairs += [(i, i + 1), (i + 1, i)]
    return lax.ppermute(block, axis, pairs)


def in_hbm(*arrays):
    return [pltpu.with_memory_space_constraint(x, pltpu.HBM) for x in arrays]


def gather_near(coarse, own, ahead):
    def join(parts, before):
        def kernel(*refs):
            join_kernel(*refs[: len(parts)], refs[-1])

        rows = sum(x.shape[0] for x in parts)
        (block,) = call(
            kernel,
            "join_blocks",
            (array((rows, parts[0].shape[1])),),
            vmem(len(parts)) + anywhere(1),
        )(*parts, before)
        return block

    def across(block, distance):
        return lax.ppermute(block, "grp", [(i, i ^ distance) for i in range(lax.axis_size("grp"))])

    distance = lax.axis_size("grp") // 2
    sent, block = coarse, own
    while distance > 1:
        block = join([block, across(sent, distance)], ahead[0])
        sent = block
        distance //= 2
    beyond = exchange(sent, "sub", 1)
    beside = exchange(sent, "sub", 0)
    block = join([block, beyond, beside], ahead[1])
    return [block, across(block, 1)]


def shards(
    coarse,
    corner_idx,
    coupling,
    force,
    panel_inv,
    panel_nodes,
    strain_disp,
    modulus,
    connect,
    interface,
    nodal_volume,
):
    nodes, _, cases = force.shape
    dofs = 3 * nodes
    q = corner_idx.shape[1]

    def lists(*refs):
        prepare_lists(coarse.shape[0], lax.axis_size("grp"), *refs)

    own, *panels, select, onehot, face, scaled, count, placing, placing_last, inverse_volume = call(
        lists,
        "prepare_lists",
        (
            array(coarse.shape),
            array(panel_nodes.shape, jnp.int32),
            array((3, nodes, cases), BF16),
            array(panel_inv.shape, BF16),
            array((TERM, 2 * HALF), BF16),
            array((nodes, CORNERS * LANES), BF16),
            array((NIF, 2 * LANES), BF16),
            array((COMPS * 24, 8, LANES)),
            array((nodes, 2 * LANES), BF16),
            array((nodes, 2 * LANES), BF16),
            array((nodes, 2 * LANES), BF16),
            array((nodes, LANES)),
        ),
        hbm(10),
        (
            pltpu.VMEM((1, q), jnp.int32),
            pltpu.VMEM(connect.shape, jnp.int32),
            pltpu.VMEM(interface.shape, jnp.int32),
            pltpu.VMEM((COMPS * 24, LANES), BF16),
            pltpu.VMEM((1, LANES), F32),
            pltpu.VMEM((nodes // LANES, LANES), F32),
            pltpu.VMEM((8, 2 * LANES), F32),
            pltpu.SemaphoreType.DMA((10,)),
        ),
        flops=100000000,
        moved=4000000,
    )(
        *in_hbm(
            corner_idx,
            connect,
            interface,
            strain_disp.reshape(COMPS * 24, LANES),
            modulus.reshape(1, -1),
            nodal_volume.reshape(-1, LANES),
            coarse,
            panel_nodes,
            jnp.transpose(force, (1, 0, 2)),
            panel_inv,
        )
    )
    first = 64
    free_t, corner_t, stress_first, stress_corner = call(
        prepare_panels,
        "prepare_panels",
        (
            array((cases, dofs)),
            array((2 * LANES, dofs), BF16),
            array((COMPS, first, LANES)),
            array((2 * LANES, COMPS * LANES), BF16),
        ),
        vmem(6),
        (
            pltpu.VMEM((dofs + SPARE, cases), F32),
            pltpu.VMEM((2, panel_inv.shape[1] + SPARE, LANES), F32),
            pltpu.VMEM((TERM, dofs), F32),
            pltpu.VMEM((COMPS, max(first, TERM), LANES), F32),
        ),
        flops=400000000,
        moved=4000000,
    )(coupling.T, *panels, onehot, scaled)
    near, across = gather_near(coarse, own, [select, corner_t])
    stress_rest, picked_near = call(
        stress_kernel,
        "stress_of_loads",
        (array((COMPS, cases - first, LANES)), array((3, TERM, cases))),
        vmem(5),
        (
            pltpu.VMEM((COMPS, cases - first, LANES), F32),
            pltpu.VMEM((3, HALF, cases), BF16),
        ),
        flops=400000000,
        moved=4000000,
    )(free_t, onehot, scaled, near, select)
    values, stress, sub_a, sub_b, grp_a, grp_b = call(
        solve_kernel,
        "stress_and_rows",
        (
            array((cases, 2 * LANES), BF16),
            array((COMPS * cases, 2 * LANES), BF16),
            array((COMPS, NIS, cases)),
            array((COMPS, NIS, cases)),
            array((COMPS, NIG + 2 * NED, cases)),
            array((COMPS, NIG + 2 * NED, cases)),
        ),
        vmem(7),
        (pltpu.VMEM((3, HALF, cases), BF16),),
        flops=300000000,
        moved=3000000,
    )(across, picked_near, select, stress_first, stress_rest, stress_corner, face)
    from_sub_a = exchange(sub_a, "sub", 0)
    from_grp_a = exchange(grp_a, "grp", 0)
    from_grp_b = exchange(grp_b, "grp", 1)
    edge_b, edge_a = call(
        edge_kernel,
        "sum_edges",
        (array((COMPS, 2 * NED, cases)), array((COMPS, 2 * NED, cases))),
        vmem(4),
    )(grp_a, grp_b, from_grp_a, from_grp_b)
    from_sub_b = exchange(sub_b, "sub", 1)
    from_edge_b = exchange(edge_b, "sub", 1)
    from_edge_a = exchange(edge_a, "sub", 0)
    partial, disp = call(
        partial_kernel,
        "assemble_nodes",
        (array((COMPS, nodes, cases)), array((3, nodes, cases), BF16)),
        vmem(8),
        (pltpu.VMEM((2 * LANES, COMPS * cases), BF16),),
        flops=400000000,
        moved=2000000,
    )(count, stress, free_t, corner_t, values, placing, from_grp_a, from_grp_b)
    (nodal,) = call(
        finish_kernel,
        "add_last",
        (array((COMPS, nodes, cases), BF16),),
        vmem(7),
        (
            pltpu.VMEM((NIS + 2 * LATE, COMPS * cases), BF16),
            pltpu.VMEM((COMPS, nodes, cases), BF16),
            pltpu.SemaphoreType.DMA((COMPS,)),
        ),
        flops=400000000,
        moved=3000000,
        out_specs=hbm(1),
    )(placing_last, partial, inverse_volume, from_sub_a, from_sub_b, from_edge_b, from_edge_a)
    return jnp.transpose(disp, (1, 0, 2)), jnp.transpose(nodal, (1, 0, 2))


def solution(mesh):
    owner = ("sub", "grp")
    placed = (
        P(owner, None),
        P(owner, None),
        P(owner, None),
        P(owner, None, None),
        P(owner, None, None),
        P(owner, None),
        P(None, None, owner),
        P(owner),
        P(None, owner),
        P(owner, None),
        P(owner),
    )
    return jax.shard_map(
        shards,
        mesh=mesh,
        in_specs=placed,
        out_specs=(P(owner, None, None), P(owner, None, None)),
        check_vma=False,
    )
```

```python
import jax
import jax.numpy as jnp
from jax import lax
from jax.experimental import pallas as pl
from jax.experimental.pallas import tpu as pltpu
from jax.sharding import PartitionSpec as P

NIS = 64
NIG = 32
NED = 8
EDGES = 2 * NIS + 2 * NIG
NIF = EDGES + 4 * NED
LATE = NIS + 4 * NED
CORNERS = 8
COMPS = 6
LANES = 128
TERM = 32
SPARE = 8
HALF = 256
TERMS = ((0, 0), (0, 1), (0, 2), (1, 0), (1, 1), (2, 0))

POISSON = 0.3
LAME = POISSON / ((1.0 + POISSON) * (1.0 - 2.0 * POISSON))
SHEAR = 0.5 / (1.0 + POISSON)

F32 = jnp.float32
BF16 = jnp.bfloat16
VMEM_LIMIT = 24 * 1024 * 1024


def split_two(x):
    high = x.astype(BF16)
    return high, (x - high.astype(F32)).astype(BF16)


def split_three(x):
    high = x.astype(BF16)
    rest = x - high.astype(F32)
    middle = rest.astype(BF16)
    return high, middle, (rest - middle.astype(F32)).astype(BF16)


def dot(a, b):
    return jnp.dot(a, b, preferred_element_type=F32)


def dot_nt(a, b):
    return lax.dot_general(a, b, (((1,), (1,)), ((), ())), preferred_element_type=F32)


def column(row):
    return jnp.broadcast_to(row, (LANES, LANES)).T


def swap_lanes(x, distance):
    lane = lax.broadcasted_iota(jnp.int32, x.shape, 1)
    after = pltpu.roll(x, LANES - distance, 1)
    before = pltpu.roll(x, distance, 1)
    return jnp.where((lane & distance) == 0, after, before)


def order_lists(ids):
    sub_even = (lax.axis_index("sub") & 1) == 0
    grp_even = (lax.axis_index("grp") & 1) == 0
    first, second = ids[:, :LANES], ids[:, LANES:]
    ids[:, :LANES] = jnp.where(sub_even, swap_lanes(first, NIS), first)
    lane = lax.broadcasted_iota(jnp.int32, second.shape, 1)
    groups = jnp.where(grp_even, swap_lanes(second, NIG), second)
    edges = jnp.where(sub_even, swap_lanes(second, 2 * NED), second)
    edges = jnp.where(grp_even, swap_lanes(edges, NED), edges)
    ids[:, LANES:] = jnp.where(lane < 2 * NIG, groups, edges)


def element_stress(terms, rows, onehot, scaled, sofar, store):
    step = 32
    pairs = onehot.shape[1] // (2 * LANES)
    for pair in range(pairs):
        operand = onehot[:, 2 * LANES * pair : 2 * LANES * (pair + 1)]
        elem = dot(terms[0], operand)
        for term in terms[1:]:
            elem = elem + dot(term, operand)
        for start in range(0, rows, step):
            sums = [None] * COMPS if pair == 0 else [sofar[i, start : start + step, :] for i in range(COMPS)]
            for half in range(2):
                for c in range(3):
                    x = elem[c * rows + start : c * rows + start + step, half * LANES : (half + 1) * LANES]
                    x = x.reshape(step // 8, 8, LANES)
                    for i in range(COMPS):
                        term = scaled[24 * i + 3 * (2 * pair + half) + c] * x
                        term = term.reshape(step, LANES)
                        sums[i] = term if sums[i] is None else sums[i] + term
            for i in range(COMPS):
                if pair < pairs - 1:
                    sofar[i, start : start + step, :] = sums[i]
                else:
                    store(i, start, sums[i])


def free_stress(free_t, first, rows, onehot, scaled, sofar, out):
    nodes = onehot.shape[0]
    parts = [free_t[first : first + rows, c * nodes : (c + 1) * nodes] for c in range(3)]

    def store(i, start, value):
        out[i, start : start + value.shape[0], :] = value

    element_stress(split_two(jnp.concatenate(parts, axis=0)), rows, onehot, scaled, sofar, store)


def start_copies(pairs, sems):
    copies = [pltpu.make_async_copy(src, dst, sems.at[k]) for k, (src, dst) in enumerate(pairs)]
    for copy in copies:
        copy.start()
    return copies


def prepare_lists(
    block_rows,
    members,
    corner_idx,
    connect,
    interface,
    strain_disp,
    modulus,
    volume,
    coarse,
    panel_nodes,
    force,
    panel_inv,
    own,
    panel_v,
    force_v,
    inverse,
    select,
    onehot,
    face,
    scaled,
    count,
    placing,
    placing_last,
    inverse_volume,
    corner_v,
    connect_v,
    interface_v,
    strain_v,
    modulus_v,
    volume_v,
    ids,
    sems,
):
    copies = start_copies(
        [
            (connect, connect_v),
            (interface, interface_v),
            (corner_idx, corner_v),
            (modulus, modulus_v),
            (strain_disp, strain_v),
            (volume, volume_v),
            (coarse, own),
            (panel_nodes, panel_v),
            (force, force_v),
            (panel_inv, inverse),
        ],
        sems,
    )
    nodes = onehot.shape[0]
    q = corner_idx.shape[1]

    copies[0].wait()
    node_of = lax.broadcasted_iota(jnp.int32, (nodes, LANES), 0)
    total = jnp.zeros((nodes, LANES), F32)
    for a in range(CORNERS):
        hit = jnp.where(connect_v[a : a + 1, :] == node_of, 1.0, 0.0)
        onehot[:, a * LANES : (a + 1) * LANES] = hit.astype(BF16)
        total = total + hit
    total = total.astype(BF16)
    count[:, :LANES] = total
    count[:, LANES:] = total

    copies[1].wait()
    ids[...] = jnp.full(ids.shape, -1.0, F32)
    ids[0:1, 0:NIF] = interface_v[...].astype(F32)
    order_lists(ids)
    lane = lax.broadcasted_iota(jnp.int32, (8, LANES), 1)
    edges = pltpu.roll(ids[:, LANES:], LANES - NIS, 1)
    again = pltpu.roll(ids[:, :LANES], LANES - NIS + 4 * NED, 1)
    last = jnp.where(lane < 4 * NED, edges, again)
    last = jnp.where(lane < LATE, last, pltpu.roll(edges, LATE, 1))
    for row, target in ((ids[0:1, LANES:], 0), (ids[0:1, :LANES], 1), (last[0:1], 2)):
        hit = jnp.where(row.astype(jnp.int32) == node_of, 1.0, 0.0).astype(BF16)
        if target == 0:
            placing[:, :LANES] = hit
            placing[:, LANES:] = hit
        else:
            placing_last[:, (target - 1) * LANES : target * LANES] = hit
    connect_f = connect_v[...].astype(F32)
    for half in range(2):
        id_col = column(ids[0:1, half * LANES : (half + 1) * LANES])
        rows = jnp.zeros((LANES, LANES), F32)
        for a in range(CORNERS):
            rows = rows + jnp.where(connect_f[a : a + 1, :] == id_col, 1.0, 0.0)
        rows = rows.astype(BF16)[: min(LANES, NIF - half * LANES)]
        face[half * LANES : half * LANES + rows.shape[0], :LANES] = rows
        face[half * LANES : half * LANES + rows.shape[0], LANES:] = rows

    copies[2].wait()
    ids[0:1, 0:q] = corner_v[...].astype(F32)
    wanted = column(ids[0:1, :LANES])[:TERM]
    lane = lax.broadcasted_iota(jnp.int32, (TERM, 2 * HALF), 1)
    entry = lax.broadcasted_iota(jnp.int32, (TERM, LANES), 0)
    s, g = lax.axis_index("sub"), lax.axis_index("grp")
    aside = 1 - 2 * (s & 1)
    row = jnp.full((TERM, 2 * HALF), -1, jnp.int32)
    for core in range(2):
        base = core * HALF
        for owner in (s, s - aside, s + aside):
            for member in range(members // 2):
                distance, bits, turn = members // 2, member, core
                while distance > 1:
                    turn += (bits & 1) * distance
                    distance, bits = distance // 2, bits >> 1
                first = (owner * members + (g ^ turn)) * block_rows
                row = jnp.where((lane >= base) & (lane < base + block_rows), first - base + lane, row)
                base += block_rows
    for b in range(2 * HALF // LANES):
        cols = slice(b * LANES, (b + 1) * LANES)
        hit = (wanted == row[:, cols].astype(F32)) & (entry < q)
        select[:, cols] = jnp.where(hit, 1.0, 0.0).astype(BF16)

    copies[3].wait()
    copies[4].wait()
    factor = modulus_v[...]
    whole = strain_v[...].astype(F32)
    rows = [whole[24 * i : 24 * (i + 1)] for i in range(COMPS)]
    trace = (rows[0] + rows[1] + rows[2]) * LAME
    for i in range(COMPS):
        value = trace + rows[i] * (2.0 * SHEAR) if i < 3 else rows[i] * SHEAR
        scaled[24 * i : 24 * (i + 1)] = jnp.broadcast_to((value * factor)[:, None, :], (24, 8, LANES))

    copies[5].wait()
    for k in range(nodes // LANES):
        inverse_volume[k * LANES : (k + 1) * LANES, :] = column(1.0 / volume_v[k : k + 1, :])
    for copy in copies[6:]:
        copy.wait()


def prepare_panels(
    coupling_v,
    panel_v,
    force_v,
    inverse,
    onehot,
    scaled,
    free_t,
    corner_t,
    stress_first,
    stress_corner,
    loads,
    solved,
    whole,
    sofar,
):
    panels, panel_rows, _ = inverse.shape
    panel_size = panel_rows // 3
    nodes = force_v.shape[1]
    q = coupling_v.shape[0]
    for c in range(3):
        loads[pl.ds(c, nodes, stride=3), :] = force_v[c].astype(F32)
    spare = corner_t.shape[0] - len(TERMS) * TERM
    stress_corner[len(TERMS) * TERM :, :] = jnp.zeros((spare, stress_corner.shape[1]), BF16)
    corner_t[len(TERMS) * TERM :, :] = jnp.zeros((spare, 3 * nodes), BF16)
    row_of = lax.broadcasted_iota(jnp.int32, (panel_rows, LANES), 0)
    for p in range(panels):
        start = p * panel_rows
        live = row_of < 3 * panel_v[0:1, p : p + 1]
        columns = []
        for k in range(panel_rows // LANES):
            part = coupling_v[:, start + k * LANES : start + (k + 1) * LANES].astype(F32)
            columns.append(jnp.concatenate([part, jnp.zeros((LANES - q, LANES), F32)], axis=0).T)
        sides = [loads[start : start + panel_rows, :], jnp.concatenate(columns, axis=0)]
        sides = jnp.concatenate([jnp.where(live, x, 0.0).astype(BF16) for x in sides], axis=1)
        result = dot(inverse[p], sides)
        for side in range(2):
            solved[side, :panel_rows, :] = jnp.where(live, result[:, side * LANES : (side + 1) * LANES], 0.0)
        for c in range(3):
            cols = slice(c * nodes + p * panel_size, c * nodes + (p + 1) * panel_size)
            free_t[:, cols] = solved[0, pl.ds(c, panel_size, stride=3), :].T
            value = solved[1, pl.ds(c, panel_size, stride=3), :].T[:TERM]
            whole[:, cols] = value
            pieces = split_three(value)
            for k, (piece, _) in enumerate(TERMS):
                corner_t[k * TERM : (k + 1) * TERM, cols] = pieces[piece]

    def store(i, start, value):
        pieces = split_three(value)
        for k, (piece, _) in enumerate(TERMS):
            stress_corner[k * TERM : (k + 1) * TERM, i * LANES : (i + 1) * LANES] = pieces[piece]

    parts = jnp.concatenate([whole[:, c * nodes : (c + 1) * nodes] for c in range(3)], axis=0)
    element_stress(split_two(parts), TERM, onehot, scaled, sofar, store)
    free_stress(free_t, 0, stress_first.shape[1], onehot, scaled, sofar, stress_first)


def pick_rows(select, block, terms):
    rows = block.shape[0]
    terms[:, rows:, :] = jnp.zeros((3, terms.shape[1] - rows, terms.shape[2]), BF16)
    for t, value in enumerate(split_three(block[...])):
        terms[t, :rows, :] = value
    return [dot(select, terms[t]) for t in range(3)]


def stress_kernel(free_t, onehot, scaled, near, select, out, picked, sofar, terms):
    for t, value in enumerate(pick_rows(select[:, :HALF], near, terms)):
        picked[t] = value
    rows = out.shape[1]
    free_stress(free_t, free_t.shape[0] - rows, rows, onehot, scaled, sofar, out)


def join_kernel(*refs):
    *parts, out = refs
    start = 0
    for part in parts:
        out[start : start + part.shape[0], :] = part[...]
        start += part.shape[0]


def solve_kernel(
    across,
    picked_near,
    select,
    stress_first,
    stress_rest,
    stress_corner,
    face,
    values,
    stress,
    sub_a,
    sub_b,
    grp_a,
    grp_b,
    terms,
):
    picked = pick_rows(select[:, HALF:], across, terms)
    picked = [picked[t] + picked_near[t] for t in range(3)]
    ordered = [picked[term] for _, term in TERMS]
    ordered += [jnp.zeros_like(picked[0])] * (stress_corner.shape[0] // TERM - len(ordered))
    per = LANES // TERM
    for k in range(0, len(ordered), per):
        block = jnp.concatenate(ordered[k : k + per], axis=0).T.astype(BF16)
        values[:, k * TERM : (k + per) * TERM] = block
    moved = dot(values[...], stress_corner[...])
    for i in range(COMPS):
        cols = slice(i * LANES, (i + 1) * LANES)
        free = jnp.concatenate([stress_first[i], stress_rest[i]], axis=0)
        high, low = split_two(free - moved[:, cols])
        stress[cols, 0:LANES] = high
        stress[cols, LANES : 2 * LANES] = low

    rows = dot_nt(face[...], stress[...])
    for i in range(COMPS):
        part = rows[:, i * LANES : (i + 1) * LANES]
        edge = [part[EDGES + NED * k : EDGES + NED * (k + 1)] for k in range(4)]
        sub_a[i] = part[:NIS]
        sub_b[i] = part[NIS : 2 * NIS]
        grp_a[i] = jnp.concatenate([part[2 * NIS : 2 * NIS + NIG], edge[0], edge[2]], axis=0)
        grp_b[i] = jnp.concatenate([part[2 * NIS + NIG : EDGES], edge[1], edge[3]], axis=0)


def edge_kernel(grp_a, grp_b, from_a, from_b, edge_b, edge_a):
    split = NIG + NED
    edge_a[:, :NED, :] = grp_a[:, NIG:split, :] + from_a[:, NIG:split, :]
    edge_a[:, NED:, :] = grp_b[:, NIG:split, :] + from_b[:, NIG:split, :]
    edge_b[:, :NED, :] = grp_a[:, split:, :] + from_a[:, split:, :]
    edge_b[:, NED:, :] = grp_b[:, split:, :] + from_b[:, split:, :]


def partial_kernel(
    count, stress, free_t, corner_t, values, placing, grp_a, grp_b, partial, disp_out, received
):
    nodes = disp_out.shape[1]
    for c in range(3):
        cols = slice(c * nodes, (c + 1) * nodes)
        part = free_t[:, cols] - dot(values[...], corner_t[:, cols])
        for k in range(0, nodes, LANES):
            disp_out[c, k : k + LANES, :] = part[:, k : k + LANES].T.astype(BF16)
    split = NIG + NED
    for i in range(COMPS):
        low, high = grp_a[i], grp_b[i]
        rows = [low[:NIG], high[:NIG], low[NIG:split], high[NIG:split], low[split:], high[split:]]
        rows.append(jnp.zeros((2 * LANES - NIF, LANES), F32))
        first, second = split_two(jnp.concatenate(rows, axis=0))
        received[:LANES, i * LANES : (i + 1) * LANES] = first
        received[LANES:, i * LANES : (i + 1) * LANES] = second
    for i in range(0, COMPS, 2):
        cols = slice(i * LANES, (i + 2) * LANES)
        own = dot_nt(count[...], stress[cols, :])
        total = own + dot(placing[...], received[:, cols])
        partial[i] = total[:, :LANES]
        partial[i + 1] = total[:, LANES:]


def finish_kernel(
    placing, partial, inverse_volume, sub_a, sub_b, edge_b, edge_a, out, received, nodal, sems
):
    scale = inverse_volume[...]
    copies = []
    for i in range(0, COMPS, 3):
        for k in range(i, i + 3):
            cols = slice(k * LANES, (k + 1) * LANES)
            late = jnp.concatenate([sub_b[k], edge_a[k], edge_b[k]], axis=0)
            first, second = split_two(late)
            received[:NIS, cols] = sub_a[k].astype(BF16)
            received[NIS : NIS + LATE, cols] = first
            received[NIS + LATE :, cols] = second
        added = dot(placing[...], received[:, i * LANES : (i + 3) * LANES])
        for k in range(3):
            total = partial[i + k] + added[:, k * LANES : (k + 1) * LANES]
            nodal[i + k] = (total * scale).astype(BF16)
        copy = pltpu.make_async_copy(nodal.at[pl.ds(i, 3)], out.at[pl.ds(i, 3)], sems.at[i // 3])
        copy.start()
        copies.append(copy)
    for copy in copies:
        copy.wait()


def vmem(count):
    return [pl.BlockSpec(memory_space=pltpu.VMEM)] * count


def anywhere(count):
    return [pl.BlockSpec(memory_space=pl.ANY)] * count


def hbm(count):
    return [pl.BlockSpec(memory_space=pltpu.HBM)] * count


def array(shape, dtype=F32):
    return jax.ShapeDtypeStruct(shape, dtype)


def call(kernel, name, out_shape, in_specs, scratch=(), flops=0, moved=0, out_specs=None):
    return pl.pallas_call(
        kernel,
        name=name,
        out_shape=out_shape,
        in_specs=in_specs,
        out_specs=out_specs or vmem(len(out_shape)),
        scratch_shapes=list(scratch),
        compiler_params=pltpu.CompilerParams(vmem_limit_bytes=VMEM_LIMIT),
        cost_estimate=pl.CostEstimate(flops=flops, bytes_accessed=moved, transcendentals=0),
    )


def exchange(block, axis, first):
    count = lax.axis_size(axis)
    pairs = []
    for i in range(first, count - 1, 2):
        pairs += [(i, i + 1), (i + 1, i)]
    return lax.ppermute(block, axis, pairs)


def in_hbm(*arrays):
    return [pltpu.with_memory_space_constraint(x, pltpu.HBM) for x in arrays]


def gather_near(coarse, own, ahead):
    def join(parts, before):
        def kernel(*refs):
            join_kernel(*refs[: len(parts)], refs[-1])

        rows = sum(x.shape[0] for x in parts)
        (block,) = call(
            kernel,
            "join_blocks",
            (array((rows, parts[0].shape[1])),),
            vmem(len(parts)) + anywhere(1),
        )(*parts, before)
        return block

    def across(block, distance):
        return lax.ppermute(block, "grp", [(i, i ^ distance) for i in range(lax.axis_size("grp"))])

    distance = lax.axis_size("grp") // 2
    sent, block = coarse, own
    while distance > 1:
        block = join([block, across(sent, distance)], ahead[0])
        sent = block
        distance //= 2
    beyond = exchange(sent, "sub", 1)
    beside = exchange(sent, "sub", 0)
    block = join([block, beyond, beside], ahead[1])
    return [block, across(block, 1)]


def shards(
    coarse,
    corner_idx,
    coupling,
    force,
    panel_inv,
    panel_nodes,
    strain_disp,
    modulus,
    connect,
    interface,
    nodal_volume,
):
    nodes, _, cases = force.shape
    dofs = 3 * nodes
    q = corner_idx.shape[1]

    def lists(*refs):
        prepare_lists(coarse.shape[0], lax.axis_size("grp"), *refs)

    own, *panels, select, onehot, face, scaled, count, placing, placing_last, inverse_volume = call(
        lists,
        "prepare_lists",
        (
            array(coarse.shape),
            array(panel_nodes.shape, jnp.int32),
            array((3, nodes, cases), BF16),
            array(panel_inv.shape, BF16),
            array((TERM, 2 * HALF), BF16),
            array((nodes, CORNERS * LANES), BF16),
            array((NIF, 2 * LANES), BF16),
            array((COMPS * 24, 8, LANES)),
            array((nodes, 2 * LANES), BF16),
            array((nodes, 2 * LANES), BF16),
            array((nodes, 2 * LANES), BF16),
            array((nodes, LANES)),
        ),
        hbm(10),
        (
            pltpu.VMEM((1, q), jnp.int32),
            pltpu.VMEM(connect.shape, jnp.int32),
            pltpu.VMEM(interface.shape, jnp.int32),
            pltpu.VMEM((COMPS * 24, LANES), BF16),
            pltpu.VMEM((1, LANES), F32),
            pltpu.VMEM((nodes // LANES, LANES), F32),
            pltpu.VMEM((8, 2 * LANES), F32),
            pltpu.SemaphoreType.DMA((10,)),
        ),
        flops=100000000,
        moved=4000000,
    )(
        *in_hbm(
            corner_idx,
            connect,
            interface,
            strain_disp.reshape(COMPS * 24, LANES),
            modulus.reshape(1, -1),
            nodal_volume.reshape(-1, LANES),
            coarse,
            panel_nodes,
            jnp.transpose(force, (1, 0, 2)),
            panel_inv,
        )
    )
    first = 64
    free_t, corner_t, stress_first, stress_corner = call(
        prepare_panels,
        "prepare_panels",
        (
            array((cases, dofs)),
            array((2 * LANES, dofs), BF16),
            array((COMPS, first, LANES)),
            array((2 * LANES, COMPS * LANES), BF16),
        ),
        vmem(6),
        (
            pltpu.VMEM((dofs + SPARE, cases), F32),
            pltpu.VMEM((2, panel_inv.shape[1] + SPARE, LANES), F32),
            pltpu.VMEM((TERM, dofs), F32),
            pltpu.VMEM((COMPS, max(first, TERM), LANES), F32),
        ),
        flops=400000000,
        moved=4000000,
    )(coupling.T, *panels, onehot, scaled)
    near, across = gather_near(coarse, own, [select, corner_t])
    stress_rest, picked_near = call(
        stress_kernel,
        "stress_of_loads",
        (array((COMPS, cases - first, LANES)), array((3, TERM, cases))),
        vmem(5),
        (
            pltpu.VMEM((COMPS, cases - first, LANES), F32),
            pltpu.VMEM((3, HALF, cases), BF16),
        ),
        flops=400000000,
        moved=4000000,
    )(free_t, onehot, scaled, near, select)
    values, stress, sub_a, sub_b, grp_a, grp_b = call(
        solve_kernel,
        "stress_and_rows",
        (
            array((cases, 2 * LANES), BF16),
            array((COMPS * cases, 2 * LANES), BF16),
            array((COMPS, NIS, cases)),
            array((COMPS, NIS, cases)),
            array((COMPS, NIG + 2 * NED, cases)),
            array((COMPS, NIG + 2 * NED, cases)),
        ),
        vmem(7),
        (pltpu.VMEM((3, HALF, cases), BF16),),
        flops=300000000,
        moved=3000000,
    )(across, picked_near, select, stress_first, stress_rest, stress_corner, face)
    from_sub_a = exchange(sub_a, "sub", 0)
    from_grp_a = exchange(grp_a, "grp", 0)
    from_grp_b = exchange(grp_b, "grp", 1)
    edge_b, edge_a = call(
        edge_kernel,
        "sum_edges",
        (array((COMPS, 2 * NED, cases)), array((COMPS, 2 * NED, cases))),
        vmem(4),
    )(grp_a, grp_b, from_grp_a, from_grp_b)
    from_sub_b = exchange(sub_b, "sub", 1)
    from_edge_b = exchange(edge_b, "sub", 1)
    from_edge_a = exchange(edge_a, "sub", 0)
    partial, disp = call(
        partial_kernel,
        "assemble_nodes",
        (array((COMPS, nodes, cases)), array((3, nodes, cases), BF16)),
        vmem(8),
        (pltpu.VMEM((2 * LANES, COMPS * cases), BF16),),
        flops=400000000,
        moved=2000000,
    )(count, stress, free_t, corner_t, values, placing, from_grp_a, from_grp_b)
    (nodal,) = call(
        finish_kernel,
        "add_last",
        (array((COMPS, nodes, cases), BF16),),
        vmem(7),
        (
            pltpu.VMEM((NIS + 2 * LATE, COMPS * cases), BF16),
            pltpu.VMEM((COMPS, nodes, cases), BF16),
            pltpu.SemaphoreType.DMA((COMPS // 3,)),
        ),
        flops=400000000,
        moved=3000000,
        out_specs=hbm(1),
    )(placing_last, partial, inverse_volume, from_sub_a, from_sub_b, from_edge_b, from_edge_a)
    return jnp.transpose(disp, (1, 0, 2)), jnp.transpose(nodal, (1, 0, 2))


def solution(mesh):
    owner = ("sub", "grp")
    placed = (
        P(owner, None),
        P(owner, None),
        P(owner, None),
        P(owner, None, None),
        P(owner, None, None),
        P(owner, None),
        P(None, None, owner),
        P(owner),
        P(None, owner),
        P(owner, None),
        P(owner),
    )
    return jax.shard_map(
        shards,
        mesh=mesh,
        in_specs=placed,
        out_specs=(P(owner, None, None), P(owner, None, None)),
        check_vma=False,
    )
```

```python
import jax
import jax.numpy as jnp
from jax import lax
from jax.experimental import pallas as pl
from jax.experimental.pallas import tpu as pltpu
from jax.sharding import PartitionSpec as P

NIS = 64
NIG = 32
NED = 8
EDGES = 2 * NIS + 2 * NIG
NIF = EDGES + 4 * NED
LATE = NIS + 4 * NED
CORNERS = 8
COMPS = 6
LANES = 128
TERM = 32
SPARE = 8
HALF = 256
TERMS = ((0, 0), (0, 1), (0, 2), (1, 0), (1, 1), (2, 0))

POISSON = 0.3
LAME = POISSON / ((1.0 + POISSON) * (1.0 - 2.0 * POISSON))
SHEAR = 0.5 / (1.0 + POISSON)

F32 = jnp.float32
BF16 = jnp.bfloat16
VMEM_LIMIT = 24 * 1024 * 1024


def split_two(x):
    high = x.astype(BF16)
    return high, (x - high.astype(F32)).astype(BF16)


def split_three(x):
    high = x.astype(BF16)
    rest = x - high.astype(F32)
    middle = rest.astype(BF16)
    return high, middle, (rest - middle.astype(F32)).astype(BF16)


def dot(a, b):
    return jnp.dot(a, b, preferred_element_type=F32)


def dot_nt(a, b):
    return lax.dot_general(a, b, (((1,), (1,)), ((), ())), preferred_element_type=F32)


def column(row):
    return jnp.broadcast_to(row, (LANES, LANES)).T


def swap_lanes(x, distance):
    lane = lax.broadcasted_iota(jnp.int32, x.shape, 1)
    after = pltpu.roll(x, LANES - distance, 1)
    before = pltpu.roll(x, distance, 1)
    return jnp.where((lane & distance) == 0, after, before)


def order_lists(ids):
    sub_even = (lax.axis_index("sub") & 1) == 0
    grp_even = (lax.axis_index("grp") & 1) == 0
    first, second = ids[:, :LANES], ids[:, LANES:]
    ids[:, :LANES] = jnp.where(sub_even, swap_lanes(first, NIS), first)
    lane = lax.broadcasted_iota(jnp.int32, second.shape, 1)
    groups = jnp.where(grp_even, swap_lanes(second, NIG), second)
    edges = jnp.where(sub_even, swap_lanes(second, 2 * NED), second)
    edges = jnp.where(grp_even, swap_lanes(edges, NED), edges)
    ids[:, LANES:] = jnp.where(lane < 2 * NIG, groups, edges)


def element_stress(terms, rows, onehot, scaled, sofar, store):
    step = 32
    pairs = onehot.shape[1] // (2 * LANES)
    for pair in range(pairs):
        operand = onehot[:, 2 * LANES * pair : 2 * LANES * (pair + 1)]
        elem = dot(terms[0], operand)
        for term in terms[1:]:
            elem = elem + dot(term, operand)
        for start in range(0, rows, step):
            sums = [None] * COMPS if pair == 0 else [sofar[i, start : start + step, :] for i in range(COMPS)]
            for half in range(2):
                for c in range(3):
                    x = elem[c * rows + start : c * rows + start + step, half * LANES : (half + 1) * LANES]
                    x = x.reshape(step // 8, 8, LANES)
                    for i in range(COMPS):
                        term = scaled[24 * i + 3 * (2 * pair + half) + c] * x
                        term = term.reshape(step, LANES)
                        sums[i] = term if sums[i] is None else sums[i] + term
            for i in range(COMPS):
                if pair < pairs - 1:
                    sofar[i, start : start + step, :] = sums[i]
                else:
                    store(i, start, sums[i])


def free_stress(free_t, first, rows, onehot, scaled, sofar, out):
    nodes = onehot.shape[0]
    parts = [free_t[first : first + rows, c * nodes : (c + 1) * nodes] for c in range(3)]

    def store(i, start, value):
        out[i, start : start + value.shape[0], :] = value

    element_stress(split_two(jnp.concatenate(parts, axis=0)), rows, onehot, scaled, sofar, store)


def start_copies(pairs, sems):
    copies = [pltpu.make_async_copy(src, dst, sems.at[k]) for k, (src, dst) in enumerate(pairs)]
    for copy in copies:
        copy.start()
    return copies


def prepare_lists(
    block_rows,
    members,
    corner_idx,
    connect,
    interface,
    strain_disp,
    modulus,
    volume,
    coarse,
    panel_nodes,
    force,
    panel_inv,
    own,
    panel_v,
    force_v,
    inverse,
    select,
    onehot,
    face,
    scaled,
    count,
    placing,
    placing_last,
    inverse_volume,
    corner_v,
    connect_v,
    interface_v,
    strain_v,
    modulus_v,
    volume_v,
    ids,
    sems,
):
    copies = start_copies(
        [
            (connect, connect_v),
            (interface, interface_v),
            (corner_idx, corner_v),
            (modulus, modulus_v),
            (strain_disp, strain_v),
            (volume, volume_v),
            (coarse, own),
            (panel_nodes, panel_v),
            (force, force_v),
            (panel_inv, inverse),
        ],
        sems,
    )
    nodes = onehot.shape[0]
    q = corner_idx.shape[1]

    copies[0].wait()
    node_of = lax.broadcasted_iota(jnp.int32, (nodes, LANES), 0)
    total = jnp.zeros((nodes, LANES), F32)
    for a in range(CORNERS):
        hit = jnp.where(connect_v[a : a + 1, :] == node_of, 1.0, 0.0)
        onehot[:, a * LANES : (a + 1) * LANES] = hit.astype(BF16)
        total = total + hit
    total = total.astype(BF16)
    count[:, :LANES] = total
    count[:, LANES:] = total

    copies[1].wait()
    ids[...] = jnp.full(ids.shape, -1.0, F32)
    ids[0:1, 0:NIF] = interface_v[...].astype(F32)
    order_lists(ids)
    lane = lax.broadcasted_iota(jnp.int32, (8, LANES), 1)
    edges = pltpu.roll(ids[:, LANES:], LANES - NIS, 1)
    again = pltpu.roll(ids[:, :LANES], LANES - NIS + 4 * NED, 1)
    last = jnp.where(lane < 4 * NED, edges, again)
    last = jnp.where(lane < LATE, last, pltpu.roll(edges, LATE, 1))
    for row, target in ((ids[0:1, LANES:], 0), (ids[0:1, :LANES], 1), (last[0:1], 2)):
        hit = jnp.where(row.astype(jnp.int32) == node_of, 1.0, 0.0).astype(BF16)
        if target == 0:
            placing[:, :LANES] = hit
            placing[:, LANES:] = hit
        else:
            placing_last[:, (target - 1) * LANES : target * LANES] = hit
    connect_f = connect_v[...].astype(F32)
    for half in range(2):
        id_col = column(ids[0:1, half * LANES : (half + 1) * LANES])
        rows = jnp.zeros((LANES, LANES), F32)
        for a in range(CORNERS):
            rows = rows + jnp.where(connect_f[a : a + 1, :] == id_col, 1.0, 0.0)
        rows = rows.astype(BF16)[: min(LANES, NIF - half * LANES)]
        face[half * LANES : half * LANES + rows.shape[0], :LANES] = rows
        face[half * LANES : half * LANES + rows.shape[0], LANES:] = rows

    copies[2].wait()
    ids[0:1, 0:q] = corner_v[...].astype(F32)
    wanted = column(ids[0:1, :LANES])[:TERM]
    lane = lax.broadcasted_iota(jnp.int32, (TERM, 2 * HALF), 1)
    entry = lax.broadcasted_iota(jnp.int32, (TERM, LANES), 0)
    s, g = lax.axis_index("sub"), lax.axis_index("grp")
    aside = 1 - 2 * (s & 1)
    row = jnp.full((TERM, 2 * HALF), -1, jnp.int32)
    for core in range(2):
        base = core * HALF
        for owner in (s, s - aside, s + aside):
            for member in range(members // 2):
                distance, bits, turn = members // 2, member, core
                while distance > 1:
                    turn += (bits & 1) * distance
                    distance, bits = distance // 2, bits >> 1
                first = (owner * members + (g ^ turn)) * block_rows
                row = jnp.where((lane >= base) & (lane < base + block_rows), first - base + lane, row)
                base += block_rows
    for b in range(2 * HALF // LANES):
        cols = slice(b * LANES, (b + 1) * LANES)
        hit = (wanted == row[:, cols].astype(F32)) & (entry < q)
        select[:, cols] = jnp.where(hit, 1.0, 0.0).astype(BF16)

    copies[3].wait()
    copies[4].wait()
    factor = modulus_v[...]
    whole = strain_v[...].astype(F32)
    rows = [whole[24 * i : 24 * (i + 1)] for i in range(COMPS)]
    trace = (rows[0] + rows[1] + rows[2]) * LAME
    for i in range(COMPS):
        value = trace + rows[i] * (2.0 * SHEAR) if i < 3 else rows[i] * SHEAR
        scaled[24 * i : 24 * (i + 1)] = jnp.broadcast_to((value * factor)[:, None, :], (24, 8, LANES))

    copies[5].wait()
    for k in range(nodes // LANES):
        inverse_volume[k * LANES : (k + 1) * LANES, :] = column(1.0 / volume_v[k : k + 1, :])
    for copy in copies[6:]:
        copy.wait()


def prepare_panels(
    coupling_v,
    panel_v,
    force_v,
    inverse,
    onehot,
    scaled,
    free_t,
    corner_t,
    stress_first,
    stress_corner,
    loads,
    solved,
    whole,
    sofar,
):
    panels, panel_rows, _ = inverse.shape
    panel_size = panel_rows // 3
    nodes = force_v.shape[1]
    q = coupling_v.shape[0]
    for c in range(3):
        loads[pl.ds(c, nodes, stride=3), :] = force_v[c].astype(F32)
    spare = corner_t.shape[0] - len(TERMS) * TERM
    stress_corner[len(TERMS) * TERM :, :] = jnp.zeros((spare, stress_corner.shape[1]), BF16)
    corner_t[len(TERMS) * TERM :, :] = jnp.zeros((spare, 3 * nodes), BF16)
    row_of = lax.broadcasted_iota(jnp.int32, (panel_rows, LANES), 0)
    for p in range(panels):
        start = p * panel_rows
        live = row_of < 3 * panel_v[0:1, p : p + 1]
        columns = []
        for k in range(panel_rows // LANES):
            part = coupling_v[:, start + k * LANES : start + (k + 1) * LANES].astype(F32)
            columns.append(jnp.concatenate([part, jnp.zeros((LANES - q, LANES), F32)], axis=0).T)
        sides = [loads[start : start + panel_rows, :], jnp.concatenate(columns, axis=0)]
        sides = jnp.concatenate([jnp.where(live, x, 0.0).astype(BF16) for x in sides], axis=1)
        result = dot(inverse[p], sides)
        for side in range(2):
            solved[side, :panel_rows, :] = jnp.where(live, result[:, side * LANES : (side + 1) * LANES], 0.0)
        for c in range(3):
            cols = slice(c * nodes + p * panel_size, c * nodes + (p + 1) * panel_size)
            free_t[:, cols] = solved[0, pl.ds(c, panel_size, stride=3), :].T
            value = solved[1, pl.ds(c, panel_size, stride=3), :].T[:TERM]
            whole[:, cols] = value
            pieces = split_three(value)
            for k, (piece, _) in enumerate(TERMS):
                corner_t[k * TERM : (k + 1) * TERM, cols] = pieces[piece]

    def store(i, start, value):
        pieces = split_three(value)
        for k, (piece, _) in enumerate(TERMS):
            stress_corner[k * TERM : (k + 1) * TERM, i * LANES : (i + 1) * LANES] = pieces[piece]

    parts = jnp.concatenate([whole[:, c * nodes : (c + 1) * nodes] for c in range(3)], axis=0)
    element_stress(split_two(parts), TERM, onehot, scaled, sofar, store)
    free_stress(free_t, 0, stress_first.shape[1], onehot, scaled, sofar, stress_first)


def pick_rows(select, block, terms):
    rows = block.shape[0]
    terms[:, rows:, :] = jnp.zeros((3, terms.shape[1] - rows, terms.shape[2]), BF16)
    for t, value in enumerate(split_three(block[...])):
        terms[t, :rows, :] = value
    return [dot(select, terms[t]) for t in range(3)]


def stress_kernel(free_t, onehot, scaled, near, select, out, picked, sofar, terms):
    for t, value in enumerate(pick_rows(select[:, :HALF], near, terms)):
        picked[t] = value
    rows = out.shape[1]
    free_stress(free_t, free_t.shape[0] - rows, rows, onehot, scaled, sofar, out)


def join_kernel(*refs):
    *parts, out = refs
    start = 0
    for part in parts:
        out[start : start + part.shape[0], :] = part[...]
        start += part.shape[0]


def solve_kernel(
    across,
    picked_near,
    select,
    stress_first,
    stress_rest,
    stress_corner,
    face,
    values,
    stress,
    sub_a,
    sub_b,
    grp_a,
    grp_b,
    terms,
):
    picked = pick_rows(select[:, HALF:], across, terms)
    picked = [picked[t] + picked_near[t] for t in range(3)]
    ordered = [picked[term] for _, term in TERMS]
    ordered += [jnp.zeros_like(picked[0])] * (stress_corner.shape[0] // TERM - len(ordered))
    per = LANES // TERM
    for k in range(0, len(ordered), per):
        block = jnp.concatenate(ordered[k : k + per], axis=0).T.astype(BF16)
        values[:, k * TERM : (k + per) * TERM] = block
    moved = dot(values[...], stress_corner[...])
    for i in range(COMPS):
        cols = slice(i * LANES, (i + 1) * LANES)
        free = jnp.concatenate([stress_first[i], stress_rest[i]], axis=0)
        high, low = split_two(free - moved[:, cols])
        stress[cols, 0:LANES] = high
        stress[cols, LANES : 2 * LANES] = low

    rows = dot_nt(face[...], stress[...])
    for i in range(COMPS):
        part = rows[:, i * LANES : (i + 1) * LANES]
        edge = [part[EDGES + NED * k : EDGES + NED * (k + 1)] for k in range(4)]
        sub_a[i] = part[:NIS]
        sub_b[i] = part[NIS : 2 * NIS]
        grp_a[i] = jnp.concatenate([part[2 * NIS : 2 * NIS + NIG], edge[0], edge[2]], axis=0)
        grp_b[i] = jnp.concatenate([part[2 * NIS + NIG : EDGES], edge[1], edge[3]], axis=0)


def edge_kernel(grp_a, grp_b, from_a, from_b, edge_b, edge_a):
    split = NIG + NED
    edge_a[:, :NED, :] = grp_a[:, NIG:split, :] + from_a[:, NIG:split, :]
    edge_a[:, NED:, :] = grp_b[:, NIG:split, :] + from_b[:, NIG:split, :]
    edge_b[:, :NED, :] = grp_a[:, split:, :] + from_a[:, split:, :]
    edge_b[:, NED:, :] = grp_b[:, split:, :] + from_b[:, split:, :]


def partial_kernel(
    count, stress, free_t, corner_t, values, placing, grp_a, grp_b, partial, disp_out, received
):
    nodes = disp_out.shape[1]
    for c in range(3):
        cols = slice(c * nodes, (c + 1) * nodes)
        part = free_t[:, cols] - dot(values[...], corner_t[:, cols])
        for k in range(0, nodes, LANES):
            disp_out[c, k : k + LANES, :] = part[:, k : k + LANES].T.astype(BF16)
    split = NIG + NED
    for i in range(COMPS):
        low, high = grp_a[i], grp_b[i]
        rows = [low[:NIG], high[:NIG], low[NIG:split], high[NIG:split], low[split:], high[split:]]
        rows.append(jnp.zeros((2 * LANES - NIF, LANES), F32))
        first, second = split_two(jnp.concatenate(rows, axis=0))
        received[:LANES, i * LANES : (i + 1) * LANES] = first
        received[LANES:, i * LANES : (i + 1) * LANES] = second
    for i in range(0, COMPS, 2):
        cols = slice(i * LANES, (i + 2) * LANES)
        own = dot_nt(count[...], stress[cols, :])
        total = own + dot(placing[...], received[:, cols])
        partial[i] = total[:, :LANES]
        partial[i + 1] = total[:, LANES:]


def finish_kernel(
    placing, partial, inverse_volume, sub_a, sub_b, edge_b, edge_a, out, received, nodal, sems
):
    scale = inverse_volume[...]
    copies = []
    for i in range(0, COMPS, 2):
        for k in (i, i + 1):
            cols = slice(k * LANES, (k + 1) * LANES)
            late = jnp.concatenate([sub_b[k], edge_a[k], edge_b[k]], axis=0)
            first, second = split_two(late)
            received[:NIS, cols] = sub_a[k].astype(BF16)
            received[NIS : NIS + LATE, cols] = first
            received[NIS + LATE :, cols] = second
        added = dot(placing[...], received[:, i * LANES : (i + 2) * LANES])
        nodal[i] = ((partial[i] + added[:, :LANES]) * scale).astype(BF16)
        nodal[i + 1] = ((partial[i + 1] + added[:, LANES:]) * scale).astype(BF16)
        copy = pltpu.make_async_copy(nodal.at[pl.ds(i, 2)], out.at[pl.ds(i, 2)], sems.at[i // 2])
        copy.start()
        copies.append(copy)
    for copy in copies:
        copy.wait()


def vmem(count):
    return [pl.BlockSpec(memory_space=pltpu.VMEM)] * count


def anywhere(count):
    return [pl.BlockSpec(memory_space=pl.ANY)] * count


def hbm(count):
    return [pl.BlockSpec(memory_space=pltpu.HBM)] * count


def array(shape, dtype=F32):
    return jax.ShapeDtypeStruct(shape, dtype)


def call(kernel, name, out_shape, in_specs, scratch=(), flops=0, moved=0, out_specs=None):
    return pl.pallas_call(
        kernel,
        name=name,
        out_shape=out_shape,
        in_specs=in_specs,
        out_specs=out_specs or vmem(len(out_shape)),
        scratch_shapes=list(scratch),
        compiler_params=pltpu.CompilerParams(vmem_limit_bytes=VMEM_LIMIT),
        cost_estimate=pl.CostEstimate(flops=flops, bytes_accessed=moved, transcendentals=0),
    )


def exchange(block, axis, first):
    count = lax.axis_size(axis)
    pairs = []
    for i in range(first, count - 1, 2):
        pairs += [(i, i + 1), (i + 1, i)]
    return lax.ppermute(block, axis, pairs)


def in_hbm(*arrays):
    return [pltpu.with_memory_space_constraint(x, pltpu.HBM) for x in arrays]


def gather_near(coarse, own, ahead):
    def join(parts, before):
        def kernel(*refs):
            join_kernel(*refs[: len(parts)], refs[-1])

        rows = sum(x.shape[0] for x in parts)
        (block,) = call(
            kernel,
            "join_blocks",
            (array((rows, parts[0].shape[1])),),
            vmem(len(parts)) + anywhere(1),
        )(*parts, before)
        return block

    def across(block, distance):
        return lax.ppermute(block, "grp", [(i, i ^ distance) for i in range(lax.axis_size("grp"))])

    distance = lax.axis_size("grp") // 2
    sent, block = coarse, own
    while distance > 1:
        block = join([block, across(sent, distance)], ahead[0])
        sent = block
        distance //= 2
    beyond = exchange(sent, "sub", 1)
    beside = exchange(sent, "sub", 0)
    block = join([block, beyond, beside], ahead[1])
    return [block, across(block, 1)]


def shards(
    coarse,
    corner_idx,
    coupling,
    force,
    panel_inv,
    panel_nodes,
    strain_disp,
    modulus,
    connect,
    interface,
    nodal_volume,
):
    nodes, _, cases = force.shape
    dofs = 3 * nodes
    q = corner_idx.shape[1]

    def lists(*refs):
        prepare_lists(coarse.shape[0], lax.axis_size("grp"), *refs)

    own, *panels, select, onehot, face, scaled, count, placing, placing_last, inverse_volume = call(
        lists,
        "prepare_lists",
        (
            array(coarse.shape),
            array(panel_nodes.shape, jnp.int32),
            array((3, nodes, cases), BF16),
            array(panel_inv.shape, BF16),
            array((TERM, 2 * HALF), BF16),
            array((nodes, CORNERS * LANES), BF16),
            array((NIF, 2 * LANES), BF16),
            array((COMPS * 24, 8, LANES)),
            array((nodes, 2 * LANES), BF16),
            array((nodes, 2 * LANES), BF16),
            array((nodes, 2 * LANES), BF16),
            array((nodes, LANES)),
        ),
        hbm(10),
        (
            pltpu.VMEM((1, q), jnp.int32),
            pltpu.VMEM(connect.shape, jnp.int32),
            pltpu.VMEM(interface.shape, jnp.int32),
            pltpu.VMEM((COMPS * 24, LANES), BF16),
            pltpu.VMEM((1, LANES), F32),
            pltpu.VMEM((nodes // LANES, LANES), F32),
            pltpu.VMEM((8, 2 * LANES), F32),
            pltpu.SemaphoreType.DMA((10,)),
        ),
        flops=100000000,
        moved=4000000,
    )(
        *in_hbm(
            corner_idx,
            connect,
            interface,
            strain_disp.reshape(COMPS * 24, LANES),
            modulus.reshape(1, -1),
            nodal_volume.reshape(-1, LANES),
            coarse,
            panel_nodes,
            jnp.transpose(force, (1, 0, 2)),
            panel_inv,
        )
    )
    first = 64
    free_t, corner_t, stress_first, stress_corner = call(
        prepare_panels,
        "prepare_panels",
        (
            array((cases, dofs)),
            array((2 * LANES, dofs), BF16),
            array((COMPS, first, LANES)),
            array((2 * LANES, COMPS * LANES), BF16),
        ),
        vmem(6),
        (
            pltpu.VMEM((dofs + SPARE, cases), F32),
            pltpu.VMEM((2, panel_inv.shape[1] + SPARE, LANES), F32),
            pltpu.VMEM((TERM, dofs), F32),
            pltpu.VMEM((COMPS, max(first, TERM), LANES), F32),
        ),
        flops=400000000,
        moved=4000000,
    )(coupling.T, *panels, onehot, scaled)
    near, across = gather_near(coarse, own, [select, corner_t])
    stress_rest, picked_near = call(
        stress_kernel,
        "stress_of_loads",
        (array((COMPS, cases - first, LANES)), array((3, TERM, cases))),
        vmem(5),
        (
            pltpu.VMEM((COMPS, cases - first, LANES), F32),
            pltpu.VMEM((3, HALF, cases), BF16),
        ),
        flops=400000000,
        moved=4000000,
    )(free_t, onehot, scaled, near, select)
    values, stress, sub_a, sub_b, grp_a, grp_b = call(
        solve_kernel,
        "stress_and_rows",
        (
            array((cases, 2 * LANES), BF16),
            array((COMPS * cases, 2 * LANES), BF16),
            array((COMPS, NIS, cases)),
            array((COMPS, NIS, cases)),
            array((COMPS, NIG + 2 * NED, cases)),
            array((COMPS, NIG + 2 * NED, cases)),
        ),
        vmem(7),
        (pltpu.VMEM((3, HALF, cases), BF16),),
        flops=300000000,
        moved=3000000,
    )(across, picked_near, select, stress_first, stress_rest, stress_corner, face)
    from_sub_a = exchange(sub_a, "sub", 0)
    from_grp_a = exchange(grp_a, "grp", 0)
    from_grp_b = exchange(grp_b, "grp", 1)
    edge_b, edge_a = call(
        edge_kernel,
        "sum_edges",
        (array((COMPS, 2 * NED, cases)), array((COMPS, 2 * NED, cases))),
        vmem(4),
    )(grp_a, grp_b, from_grp_a, from_grp_b)
    from_sub_b = exchange(sub_b, "sub", 1)
    from_edge_b = exchange(edge_b, "sub", 1)
    from_edge_a = exchange(edge_a, "sub", 0)
    partial, disp = call(
        partial_kernel,
        "assemble_nodes",
        (array((COMPS, nodes, cases)), array((3, nodes, cases), BF16)),
        vmem(8),
        (pltpu.VMEM((2 * LANES, COMPS * cases), BF16),),
        flops=400000000,
        moved=2000000,
    )(count, stress, free_t, corner_t, values, placing, from_grp_a, from_grp_b)
    (nodal,) = call(
        finish_kernel,
        "add_last",
        (array((COMPS, nodes, cases), BF16),),
        vmem(7),
        (
            pltpu.VMEM((NIS + 2 * LATE, COMPS * cases), BF16),
            pltpu.VMEM((COMPS, nodes, cases), BF16),
            pltpu.SemaphoreType.DMA((COMPS // 2,)),
        ),
        flops=400000000,
        moved=3000000,
        out_specs=hbm(1),
    )(placing_last, partial, inverse_volume, from_sub_a, from_sub_b, from_edge_b, from_edge_a)
    return jnp.transpose(disp, (1, 0, 2)), jnp.transpose(nodal, (1, 0, 2))


def solution(mesh):
    owner = ("sub", "grp")
    placed = (
        P(owner, None),
        P(owner, None),
        P(owner, None),
        P(owner, None, None),
        P(owner, None, None),
        P(owner, None),
        P(None, None, owner),
        P(owner),
        P(None, owner),
        P(owner, None),
        P(owner),
    )
    return jax.shard_map(
        shards,
        mesh=mesh,
        in_specs=placed,
        out_specs=(P(owner, None, None), P(owner, None, None)),
        check_vma=False,
    )
```

```python
import jax
import jax.numpy as jnp
from jax import lax
from jax.experimental import pallas as pl
from jax.experimental.pallas import tpu as pltpu
from jax.sharding import PartitionSpec as P

NIS = 64
NIG = 32
NED = 8
EDGES = 2 * NIS + 2 * NIG
NIF = EDGES + 4 * NED
LATE = NIS + 4 * NED
CORNERS = 8
COMPS = 6
LANES = 128
TERM = 32
SPARE = 8
HALF = 256
TERMS = ((0, 0), (0, 1), (0, 2), (1, 0), (1, 1), (2, 0))

POISSON = 0.3
LAME = POISSON / ((1.0 + POISSON) * (1.0 - 2.0 * POISSON))
SHEAR = 0.5 / (1.0 + POISSON)

F32 = jnp.float32
BF16 = jnp.bfloat16
VMEM_LIMIT = 24 * 1024 * 1024


def split_two(x):
    high = x.astype(BF16)
    return high, (x - high.astype(F32)).astype(BF16)


def split_three(x):
    high = x.astype(BF16)
    rest = x - high.astype(F32)
    middle = rest.astype(BF16)
    return high, middle, (rest - middle.astype(F32)).astype(BF16)


def dot(a, b):
    return jnp.dot(a, b, preferred_element_type=F32)


def dot_nt(a, b):
    return lax.dot_general(a, b, (((1,), (1,)), ((), ())), preferred_element_type=F32)


def column(row):
    return jnp.broadcast_to(row, (LANES, LANES)).T


def swap_lanes(x, distance):
    lane = lax.broadcasted_iota(jnp.int32, x.shape, 1)
    after = pltpu.roll(x, LANES - distance, 1)
    before = pltpu.roll(x, distance, 1)
    return jnp.where((lane & distance) == 0, after, before)


def order_lists(ids):
    sub_even = (lax.axis_index("sub") & 1) == 0
    grp_even = (lax.axis_index("grp") & 1) == 0
    first, second = ids[:, :LANES], ids[:, LANES:]
    ids[:, :LANES] = jnp.where(sub_even, swap_lanes(first, NIS), first)
    lane = lax.broadcasted_iota(jnp.int32, second.shape, 1)
    groups = jnp.where(grp_even, swap_lanes(second, NIG), second)
    edges = jnp.where(sub_even, swap_lanes(second, 2 * NED), second)
    edges = jnp.where(grp_even, swap_lanes(edges, NED), edges)
    ids[:, LANES:] = jnp.where(lane < 2 * NIG, groups, edges)


def element_stress(terms, rows, onehot, scaled, sofar, store):
    step = 32
    pairs = onehot.shape[1] // (2 * LANES)
    for pair in range(pairs):
        operand = onehot[:, 2 * LANES * pair : 2 * LANES * (pair + 1)]
        elem = dot(terms[0], operand)
        for term in terms[1:]:
            elem = elem + dot(term, operand)
        for start in range(0, rows, step):
            sums = [None] * COMPS if pair == 0 else [sofar[i, start : start + step, :] for i in range(COMPS)]
            for half in range(2):
                for c in range(3):
                    x = elem[c * rows + start : c * rows + start + step, half * LANES : (half + 1) * LANES]
                    x = x.reshape(step // 8, 8, LANES)
                    for i in range(COMPS):
                        term = scaled[24 * i + 3 * (2 * pair + half) + c] * x
                        term = term.reshape(step, LANES)
                        sums[i] = term if sums[i] is None else sums[i] + term
            for i in range(COMPS):
                if pair < pairs - 1:
                    sofar[i, start : start + step, :] = sums[i]
                else:
                    store(i, start, sums[i])


def free_stress(free_t, first, rows, onehot, scaled, sofar, out):
    nodes = onehot.shape[0]
    parts = [free_t[first : first + rows, c * nodes : (c + 1) * nodes] for c in range(3)]

    def store(i, start, value):
        out[i, start : start + value.shape[0], :] = value

    element_stress(split_two(jnp.concatenate(parts, axis=0)), rows, onehot, scaled, sofar, store)


def start_copies(pairs, sems):
    copies = [pltpu.make_async_copy(src, dst, sems.at[k]) for k, (src, dst) in enumerate(pairs)]
    for copy in copies:
        copy.start()
    return copies


def prepare_lists(
    block_rows,
    members,
    corner_idx,
    connect,
    interface,
    strain_disp,
    modulus,
    volume,
    coarse,
    panel_nodes,
    force,
    panel_inv,
    own,
    panel_v,
    force_v,
    inverse,
    select,
    onehot,
    face,
    scaled,
    count,
    placing,
    placing_last,
    inverse_volume,
    corner_v,
    connect_v,
    interface_v,
    strain_v,
    modulus_v,
    volume_v,
    ids,
    sems,
):
    copies = start_copies(
        [
            (connect, connect_v),
            (interface, interface_v),
            (corner_idx, corner_v),
            (modulus, modulus_v),
            (strain_disp, strain_v),
            (volume, volume_v),
            (coarse, own),
            (panel_nodes, panel_v),
            (force, force_v),
            (panel_inv, inverse),
        ],
        sems,
    )
    nodes = onehot.shape[0]
    q = corner_idx.shape[1]

    copies[0].wait()
    node_of = lax.broadcasted_iota(jnp.int32, (nodes, LANES), 0)
    total = jnp.zeros((nodes, LANES), F32)
    for a in range(CORNERS):
        hit = jnp.where(connect_v[a : a + 1, :] == node_of, 1.0, 0.0)
        onehot[:, a * LANES : (a + 1) * LANES] = hit.astype(BF16)
        total = total + hit
    total = total.astype(BF16)
    count[:, :LANES] = total
    count[:, LANES:] = total

    copies[1].wait()
    ids[...] = jnp.full(ids.shape, -1.0, F32)
    ids[0:1, 0:NIF] = interface_v[...].astype(F32)
    order_lists(ids)
    lane = lax.broadcasted_iota(jnp.int32, (8, LANES), 1)
    edges = pltpu.roll(ids[:, LANES:], LANES - NIS, 1)
    again = pltpu.roll(ids[:, :LANES], LANES - NIS + 4 * NED, 1)
    last = jnp.where(lane < 4 * NED, edges, again)
    last = jnp.where(lane < LATE, last, pltpu.roll(edges, LATE, 1))
    for row, target in ((ids[0:1, LANES:], 0), (ids[0:1, :LANES], 1), (last[0:1], 2)):
        hit = jnp.where(row.astype(jnp.int32) == node_of, 1.0, 0.0).astype(BF16)
        if target == 0:
            placing[:, :LANES] = hit
            placing[:, LANES:] = hit
        else:
            placing_last[:, (target - 1) * LANES : target * LANES] = hit
    connect_f = connect_v[...].astype(F32)
    for half in range(2):
        id_col = column(ids[0:1, half * LANES : (half + 1) * LANES])
        rows = jnp.zeros((LANES, LANES), F32)
        for a in range(CORNERS):
            rows = rows + jnp.where(connect_f[a : a + 1, :] == id_col, 1.0, 0.0)
        rows = rows.astype(BF16)[: min(LANES, NIF - half * LANES)]
        face[half * LANES : half * LANES + rows.shape[0], :LANES] = rows
        face[half * LANES : half * LANES + rows.shape[0], LANES:] = rows

    copies[2].wait()
    ids[0:1, 0:q] = corner_v[...].astype(F32)
    wanted = column(ids[0:1, :LANES])[:TERM]
    lane = lax.broadcasted_iota(jnp.int32, (TERM, 2 * HALF), 1)
    entry = lax.broadcasted_iota(jnp.int32, (TERM, LANES), 0)
    s, g = lax.axis_index("sub"), lax.axis_index("grp")
    aside = 1 - 2 * (s & 1)
    row = jnp.full((TERM, 2 * HALF), -1, jnp.int32)
    for core in range(2):
        base = core * HALF
        for owner in (s, s - aside, s + aside):
            for member in range(members // 2):
                distance, bits, turn = members // 2, member, core
                while distance > 1:
                    turn += (bits & 1) * distance
                    distance, bits = distance // 2, bits >> 1
                first = (owner * members + (g ^ turn)) * block_rows
                row = jnp.where((lane >= base) & (lane < base + block_rows), first - base + lane, row)
                base += block_rows
    for b in range(2 * HALF // LANES):
        cols = slice(b * LANES, (b + 1) * LANES)
        hit = (wanted == row[:, cols].astype(F32)) & (entry < q)
        select[:, cols] = jnp.where(hit, 1.0, 0.0).astype(BF16)

    copies[3].wait()
    copies[4].wait()
    factor = modulus_v[...]
    whole = strain_v[...].astype(F32)
    rows = [whole[24 * i : 24 * (i + 1)] for i in range(COMPS)]
    trace = (rows[0] + rows[1] + rows[2]) * LAME
    for i in range(COMPS):
        value = trace + rows[i] * (2.0 * SHEAR) if i < 3 else rows[i] * SHEAR
        scaled[24 * i : 24 * (i + 1)] = jnp.broadcast_to((value * factor)[:, None, :], (24, 8, LANES))

    copies[5].wait()
    for k in range(nodes // LANES):
        inverse_volume[k * LANES : (k + 1) * LANES, :] = column(1.0 / volume_v[k : k + 1, :])
    for copy in copies[6:]:
        copy.wait()


def prepare_panels(
    coupling_v,
    panel_v,
    force_v,
    inverse,
    onehot,
    scaled,
    free_t,
    corner_t,
    stress_first,
    stress_corner,
    loads,
    solved,
    whole,
    sofar,
):
    panels, panel_rows, _ = inverse.shape
    panel_size = panel_rows // 3
    nodes = force_v.shape[1]
    q = coupling_v.shape[0]
    for c in range(3):
        loads[pl.ds(c, nodes, stride=3), :] = force_v[c].astype(F32)
    spare = corner_t.shape[0] - len(TERMS) * TERM
    stress_corner[len(TERMS) * TERM :, :] = jnp.zeros((spare, stress_corner.shape[1]), BF16)
    corner_t[len(TERMS) * TERM :, :] = jnp.zeros((spare, 3 * nodes), BF16)
    row_of = lax.broadcasted_iota(jnp.int32, (panel_rows, LANES), 0)
    for p in range(panels):
        start = p * panel_rows
        live = row_of < 3 * panel_v[0:1, p : p + 1]
        columns = []
        for k in range(panel_rows // LANES):
            part = coupling_v[:, start + k * LANES : start + (k + 1) * LANES].astype(F32)
            columns.append(jnp.concatenate([part, jnp.zeros((LANES - q, LANES), F32)], axis=0).T)
        sides = [loads[start : start + panel_rows, :], jnp.concatenate(columns, axis=0)]
        sides = jnp.concatenate([jnp.where(live, x, 0.0).astype(BF16) for x in sides], axis=1)
        result = dot(inverse[p], sides)
        for side in range(2):
            solved[side, :panel_rows, :] = jnp.where(live, result[:, side * LANES : (side + 1) * LANES], 0.0)
        for c in range(3):
            cols = slice(c * nodes + p * panel_size, c * nodes + (p + 1) * panel_size)
            free_t[:, cols] = solved[0, pl.ds(c, panel_size, stride=3), :].T
            value = solved[1, pl.ds(c, panel_size, stride=3), :].T[:TERM]
            whole[:, cols] = value
            pieces = split_three(value)
            for k, (piece, _) in enumerate(TERMS):
                corner_t[k * TERM : (k + 1) * TERM, cols] = pieces[piece]

    def store(i, start, value):
        pieces = split_three(value)
        for k, (piece, _) in enumerate(TERMS):
            stress_corner[k * TERM : (k + 1) * TERM, i * LANES : (i + 1) * LANES] = pieces[piece]

    parts = jnp.concatenate([whole[:, c * nodes : (c + 1) * nodes] for c in range(3)], axis=0)
    element_stress(split_two(parts), TERM, onehot, scaled, sofar, store)
    free_stress(free_t, 0, stress_first.shape[1], onehot, scaled, sofar, stress_first)


def pick_rows(select, block, terms):
    rows = block.shape[0]
    terms[:, rows:, :] = jnp.zeros((3, terms.shape[1] - rows, terms.shape[2]), BF16)
    for t, value in enumerate(split_three(block[...])):
        terms[t, :rows, :] = value
    return [dot(select, terms[t]) for t in range(3)]


def stress_kernel(free_t, onehot, scaled, near, select, out, picked, sofar, terms):
    for t, value in enumerate(pick_rows(select[:, :HALF], near, terms)):
        picked[t] = value
    rows = out.shape[1]
    free_stress(free_t, free_t.shape[0] - rows, rows, onehot, scaled, sofar, out)


def join_kernel(*refs):
    *parts, out = refs
    start = 0
    for part in parts:
        out[start : start + part.shape[0], :] = part[...]
        start += part.shape[0]


def solve_kernel(
    across,
    picked_near,
    select,
    stress_first,
    stress_rest,
    stress_corner,
    face,
    values,
    stress,
    sub_a,
    sub_b,
    grp_a,
    grp_b,
    terms,
):
    picked = pick_rows(select[:, HALF:], across, terms)
    picked = [picked[t] + picked_near[t] for t in range(3)]
    ordered = [picked[term] for _, term in TERMS]
    ordered += [jnp.zeros_like(picked[0])] * (stress_corner.shape[0] // TERM - len(ordered))
    per = LANES // TERM
    for k in range(0, len(ordered), per):
        block = jnp.concatenate(ordered[k : k + per], axis=0).T.astype(BF16)
        values[:, k * TERM : (k + per) * TERM] = block
    moved = dot(values[...], stress_corner[...])
    for pair in range(0, COMPS, 2):
        for i in (pair, pair + 1):
            cols = slice(i * LANES, (i + 1) * LANES)
            free = jnp.concatenate([stress_first[i], stress_rest[i]], axis=0)
            high, low = split_two(free - moved[:, cols])
            stress[cols, 0:LANES] = high
            stress[cols, LANES : 2 * LANES] = low
        rows = dot_nt(face[...], stress[pair * LANES : (pair + 2) * LANES, :])
        for i in (pair, pair + 1):
            part = rows[:, (i - pair) * LANES : (i - pair + 1) * LANES]
            edge = [part[EDGES + NED * k : EDGES + NED * (k + 1)] for k in range(4)]
            sub_a[i] = part[:NIS]
            sub_b[i] = part[NIS : 2 * NIS]
            grp_a[i] = jnp.concatenate([part[2 * NIS : 2 * NIS + NIG], edge[0], edge[2]], axis=0)
            grp_b[i] = jnp.concatenate([part[2 * NIS + NIG : EDGES], edge[1], edge[3]], axis=0)


def edge_kernel(grp_a, grp_b, from_a, from_b, edge_b, edge_a):
    split = NIG + NED
    edge_a[:, :NED, :] = grp_a[:, NIG:split, :] + from_a[:, NIG:split, :]
    edge_a[:, NED:, :] = grp_b[:, NIG:split, :] + from_b[:, NIG:split, :]
    edge_b[:, :NED, :] = grp_a[:, split:, :] + from_a[:, split:, :]
    edge_b[:, NED:, :] = grp_b[:, split:, :] + from_b[:, split:, :]


def partial_kernel(
    count, stress, free_t, corner_t, values, placing, grp_a, grp_b, partial, disp_out, received
):
    nodes = disp_out.shape[1]
    for c in range(3):
        cols = slice(c * nodes, (c + 1) * nodes)
        part = free_t[:, cols] - dot(values[...], corner_t[:, cols])
        for k in range(0, nodes, LANES):
            disp_out[c, k : k + LANES, :] = part[:, k : k + LANES].T.astype(BF16)
    split = NIG + NED
    for i in range(COMPS):
        low, high = grp_a[i], grp_b[i]
        rows = [low[:NIG], high[:NIG], low[NIG:split], high[NIG:split], low[split:], high[split:]]
        rows.append(jnp.zeros((2 * LANES - NIF, LANES), F32))
        first, second = split_two(jnp.concatenate(rows, axis=0))
        received[:LANES, i * LANES : (i + 1) * LANES] = first
        received[LANES:, i * LANES : (i + 1) * LANES] = second
    for i in range(0, COMPS, 2):
        cols = slice(i * LANES, (i + 2) * LANES)
        own = dot_nt(count[...], stress[cols, :])
        total = own + dot(placing[...], received[:, cols])
        partial[i] = total[:, :LANES]
        partial[i + 1] = total[:, LANES:]


def finish_kernel(
    placing, partial, inverse_volume, sub_a, sub_b, edge_b, edge_a, out, received, nodal, sems
):
    scale = inverse_volume[...]
    copies = []
    for i in range(0, COMPS, 2):
        for k in (i, i + 1):
            cols = slice(k * LANES, (k + 1) * LANES)
            late = jnp.concatenate([sub_b[k], edge_a[k], edge_b[k]], axis=0)
            first, second = split_two(late)
            received[:NIS, cols] = sub_a[k].astype(BF16)
            received[NIS : NIS + LATE, cols] = first
            received[NIS + LATE :, cols] = second
        added = dot(placing[...], received[:, i * LANES : (i + 2) * LANES])
        nodal[i] = ((partial[i] + added[:, :LANES]) * scale).astype(BF16)
        nodal[i + 1] = ((partial[i + 1] + added[:, LANES:]) * scale).astype(BF16)
        copy = pltpu.make_async_copy(nodal.at[pl.ds(i, 2)], out.at[pl.ds(i, 2)], sems.at[i // 2])
        copy.start()
        copies.append(copy)
    for copy in copies:
        copy.wait()


def vmem(count):
    return [pl.BlockSpec(memory_space=pltpu.VMEM)] * count


def anywhere(count):
    return [pl.BlockSpec(memory_space=pl.ANY)] * count


def hbm(count):
    return [pl.BlockSpec(memory_space=pltpu.HBM)] * count


def array(shape, dtype=F32):
    return jax.ShapeDtypeStruct(shape, dtype)


def call(kernel, name, out_shape, in_specs, scratch=(), flops=0, moved=0, out_specs=None):
    return pl.pallas_call(
        kernel,
        name=name,
        out_shape=out_shape,
        in_specs=in_specs,
        out_specs=out_specs or vmem(len(out_shape)),
        scratch_shapes=list(scratch),
        compiler_params=pltpu.CompilerParams(vmem_limit_bytes=VMEM_LIMIT),
        cost_estimate=pl.CostEstimate(flops=flops, bytes_accessed=moved, transcendentals=0),
    )


def exchange(block, axis, first):
    count = lax.axis_size(axis)
    pairs = []
    for i in range(first, count - 1, 2):
        pairs += [(i, i + 1), (i + 1, i)]
    return lax.ppermute(block, axis, pairs)


def in_hbm(*arrays):
    return [pltpu.with_memory_space_constraint(x, pltpu.HBM) for x in arrays]


def gather_near(coarse, own, ahead):
    def join(parts, before):
        def kernel(*refs):
            join_kernel(*refs[: len(parts)], refs[-1])

        rows = sum(x.shape[0] for x in parts)
        (block,) = call(
            kernel,
            "join_blocks",
            (array((rows, parts[0].shape[1])),),
            vmem(len(parts)) + anywhere(1),
        )(*parts, before)
        return block

    def across(block, distance):
        return lax.ppermute(block, "grp", [(i, i ^ distance) for i in range(lax.axis_size("grp"))])

    distance = lax.axis_size("grp") // 2
    sent, block = coarse, own
    while distance > 1:
        block = join([block, across(sent, distance)], ahead[0])
        sent = block
        distance //= 2
    beyond = exchange(sent, "sub", 1)
    beside = exchange(sent, "sub", 0)
    block = join([block, beyond, beside], ahead[1])
    return [block, across(block, 1)]


def shards(
    coarse,
    corner_idx,
    coupling,
    force,
    panel_inv,
    panel_nodes,
    strain_disp,
    modulus,
    connect,
    interface,
    nodal_volume,
):
    nodes, _, cases = force.shape
    dofs = 3 * nodes
    q = corner_idx.shape[1]

    def lists(*refs):
        prepare_lists(coarse.shape[0], lax.axis_size("grp"), *refs)

    own, *panels, select, onehot, face, scaled, count, placing, placing_last, inverse_volume = call(
        lists,
        "prepare_lists",
        (
            array(coarse.shape),
            array(panel_nodes.shape, jnp.int32),
            array((3, nodes, cases), BF16),
            array(panel_inv.shape, BF16),
            array((TERM, 2 * HALF), BF16),
            array((nodes, CORNERS * LANES), BF16),
            array((NIF, 2 * LANES), BF16),
            array((COMPS * 24, 8, LANES)),
            array((nodes, 2 * LANES), BF16),
            array((nodes, 2 * LANES), BF16),
            array((nodes, 2 * LANES), BF16),
            array((nodes, LANES)),
        ),
        hbm(10),
        (
            pltpu.VMEM((1, q), jnp.int32),
            pltpu.VMEM(connect.shape, jnp.int32),
            pltpu.VMEM(interface.shape, jnp.int32),
            pltpu.VMEM((COMPS * 24, LANES), BF16),
            pltpu.VMEM((1, LANES), F32),
            pltpu.VMEM((nodes // LANES, LANES), F32),
            pltpu.VMEM((8, 2 * LANES), F32),
            pltpu.SemaphoreType.DMA((10,)),
        ),
        flops=100000000,
        moved=4000000,
    )(
        *in_hbm(
            corner_idx,
            connect,
            interface,
            strain_disp.reshape(COMPS * 24, LANES),
            modulus.reshape(1, -1),
            nodal_volume.reshape(-1, LANES),
            coarse,
            panel_nodes,
            jnp.transpose(force, (1, 0, 2)),
            panel_inv,
        )
    )
    first = 64
    free_t, corner_t, stress_first, stress_corner = call(
        prepare_panels,
        "prepare_panels",
        (
            array((cases, dofs)),
            array((2 * LANES, dofs), BF16),
            array((COMPS, first, LANES)),
            array((2 * LANES, COMPS * LANES), BF16),
        ),
        vmem(6),
        (
            pltpu.VMEM((dofs + SPARE, cases), F32),
            pltpu.VMEM((2, panel_inv.shape[1] + SPARE, LANES), F32),
            pltpu.VMEM((TERM, dofs), F32),
            pltpu.VMEM((COMPS, max(first, TERM), LANES), F32),
        ),
        flops=400000000,
        moved=4000000,
    )(coupling.T, *panels, onehot, scaled)
    near, across = gather_near(coarse, own, [select, corner_t])
    stress_rest, picked_near = call(
        stress_kernel,
        "stress_of_loads",
        (array((COMPS, cases - first, LANES)), array((3, TERM, cases))),
        vmem(5),
        (
            pltpu.VMEM((COMPS, cases - first, LANES), F32),
            pltpu.VMEM((3, HALF, cases), BF16),
        ),
        flops=400000000,
        moved=4000000,
    )(free_t, onehot, scaled, near, select)
    values, stress, sub_a, sub_b, grp_a, grp_b = call(
        solve_kernel,
        "stress_and_rows",
        (
            array((cases, 2 * LANES), BF16),
            array((COMPS * cases, 2 * LANES), BF16),
            array((COMPS, NIS, cases)),
            array((COMPS, NIS, cases)),
            array((COMPS, NIG + 2 * NED, cases)),
            array((COMPS, NIG + 2 * NED, cases)),
        ),
        vmem(7),
        (pltpu.VMEM((3, HALF, cases), BF16),),
        flops=300000000,
        moved=3000000,
    )(across, picked_near, select, stress_first, stress_rest, stress_corner, face)
    from_sub_a = exchange(sub_a, "sub", 0)
    from_grp_a = exchange(grp_a, "grp", 0)
    from_grp_b = exchange(grp_b, "grp", 1)
    edge_b, edge_a = call(
        edge_kernel,
        "sum_edges",
        (array((COMPS, 2 * NED, cases)), array((COMPS, 2 * NED, cases))),
        vmem(4),
    )(grp_a, grp_b, from_grp_a, from_grp_b)
    from_sub_b = exchange(sub_b, "sub", 1)
    from_edge_b = exchange(edge_b, "sub", 1)
    from_edge_a = exchange(edge_a, "sub", 0)
    partial, disp = call(
        partial_kernel,
        "assemble_nodes",
        (array((COMPS, nodes, cases)), array((3, nodes, cases), BF16)),
        vmem(8),
        (pltpu.VMEM((2 * LANES, COMPS * cases), BF16),),
        flops=400000000,
        moved=2000000,
    )(count, stress, free_t, corner_t, values, placing, from_grp_a, from_grp_b)
    (nodal,) = call(
        finish_kernel,
        "add_last",
        (array((COMPS, nodes, cases), BF16),),
        vmem(7),
        (
            pltpu.VMEM((NIS + 2 * LATE, COMPS * cases), BF16),
            pltpu.VMEM((COMPS, nodes, cases), BF16),
            pltpu.SemaphoreType.DMA((COMPS // 2,)),
        ),
        flops=400000000,
        moved=3000000,
        out_specs=hbm(1),
    )(placing_last, partial, inverse_volume, from_sub_a, from_sub_b, from_edge_b, from_edge_a)
    return jnp.transpose(disp, (1, 0, 2)), jnp.transpose(nodal, (1, 0, 2))


def solution(mesh):
    owner = ("sub", "grp")
    placed = (
        P(owner, None),
        P(owner, None),
        P(owner, None),
        P(owner, None, None),
        P(owner, None, None),
        P(owner, None),
        P(None, None, owner),
        P(owner),
        P(None, owner),
        P(owner, None),
        P(owner),
    )
    return jax.shard_map(
        shards,
        mesh=mesh,
        in_specs=placed,
        out_specs=(P(owner, None, None), P(owner, None, None)),
        check_vma=False,
    )
```
